32 devices in a mesh: task: 4 (over y, x), space: 8 (over z, core).
Axes of the slice: x: 2, y: 2, z: 4, core: 2. Of those that a mesh axis runs over, the one named last changes fastest.
Arguments:
- features: bfloat16 [16, 128, 2048], P('space'), may hold values from -6 to 6
- row_width: int32 [16], replicated, may hold values from 32 to 128, as said below
- w_reduce: bfloat16 [2048, 512], replicated, may hold values from -0.125 to 0.125
- w_dilated: bfloat16 [512, 9, 512], replicated, may hold values from -0.09375 to 0.09375
- w_expand: bfloat16 [512, 2048], replicated, may hold values from -0.25 to 0.25
- trunk_gain: float32 [3072], replicated, may hold values from 0.5 to 1.5
- trunk_shift: float32 [3072], replicated, may hold values from -3 to 3
- branch_weight: bfloat16 [4, 2048, 512], P('task', 'space'), may hold values from -0.125 to 0.125
- rate_weight: bfloat16 [4, 2048, 6912], P('task', 'space'), may hold values from -0.046875 to 0.046875
- proj_weight: bfloat16 [4, 1280, 256], P('task'), may hold values from -0.15625 to 0.15625
- head_gain: float32 [4, 1280], P('task'), may hold values from 0.5 to 1.5
- head_shift: float32 [4, 1280], P('task'), may hold values from -3 to 3
- head_cot: bfloat16 [4, 16, 128, 256], P('task', 'space'), may hold values from -20 to 20
Outputs:
- head_out: bfloat16 [4, 16, 128, 256], P('task', 'space')
- features_grad: bfloat16 [16, 128, 2048], P('space')
- w_reduce_grad: float32 [2048, 512], P('space')
- w_dilated_grad: float32 [512, 9, 512], P('space')
- w_expand_grad: float32 [512, 2048], P('space')
- trunk_gain_grad: float32 [3072], replicated
- trunk_shift_grad: float32 [3072], replicated
- batch_stats: float32 [2, 3072], replicated
- branch_grad: float32 [4, 2048, 512], P('task', 'space')
- rate_grad: float32 [4, 2048, 6912], P('task', 'space')
- proj_grad: float32 [4, 1280, 256], P('task')
- head_gain_grad: float32 [4, 1280], P('task')
- head_shift_grad: float32 [4, 1280], P('task')
- task_weight: float32 [4], replicated
The draws below stay inside these ranges and needn't reach their ends.
Inputs may be any that keep to these rules, and one draw needn't show every extreme that they name: Columns 0 to row_width[r] - 1 of canvas row r are image, the rest padding; row 0 holds 32 columns and the last row is full.
All inputs are finite; a program needn't handle non-finite values.
Results may differ from the reference program's by a relative error of at most 0.02.
Values may be sent and summed in bfloat16 or wider, within the bound.
A program may use at most 384 MiB of HBM per device.

```python
import jax
import jax.numpy as jnp
from jax import lax

C_IN = 2048
C_MID = 512
C_HEAD = 256
COLS = 128
CONV_DILATION = 2
RATE = 12
TASKS = 4
H = 16


def draw_row_width(key, part):
    key = jax.random.fold_in(key, 11)
    row_ids = jnp.arange(H)
    base_width = COLS // 4 + 3 * COLS // 4 * row_ids // H
    extra_width = jax.random.randint(key, (H,), 0, COLS // 8 + 1)
    widths = jnp.minimum(base_width + extra_width, COLS)
    widths = jnp.where(row_ids == 0, COLS // 4, widths)
    widths = jnp.where(row_ids == H - 1, COLS, widths)
    return widths.astype(jnp.int32)


def row_profile(ratio):
    row_place = jnp.arange(H).astype(jnp.float32) / (H - 1.0) - 0.5
    direction = jnp.where(jnp.arange(TASKS) % 2 == 0, 1.0, -1.0)
    return jnp.exp(jnp.log(ratio) * direction[:, None] * row_place[None, :])


def draw_head_cot(key, part):
    key = jax.random.fold_in(key, 13)
    values = jnp.clip(jax.random.normal(key, (TASKS, H, COLS, C_HEAD), jnp.float32), -6.0, 6.0)
    profile = row_profile(10.0)
    return (values * jnp.sqrt(profile)[:, :, None, None]).astype(jnp.bfloat16)


def shard_levels(stream_key, dims, split, smallest, largest):
    level = 1.0
    for position, shards_of in split:
        steps = jax.random.uniform(jax.random.fold_in(jax.random.fold_in(stream_key, 6), position), (shards_of,), jnp.float32, smallest / len(split), largest / len(split))
        level = level * jnp.repeat(jnp.exp(steps), dims[position] // shards_of).reshape((-1,) + (1,) * (len(dims) - 1 - position))
    return level


def centred(key, dims, deviation, reach, cuts=(), held_as=jnp.bfloat16):
    entries = deviation * jax.random.normal(key, dims, jnp.float32)
    if cuts:
        entries = entries * shard_levels(key, dims, cuts, -0.22, 0.18)
    return jnp.clip(entries, -reach, reach).astype(held_as)


def setup_inputs(seed: int = 0) -> dict:
    arg_keys = jax.random.split(jax.random.key(seed), 14)
    return {
        "features": centred(arg_keys[0], (H, COLS, C_IN), 1.0, 6.0, ((0, 8),)),
        "row_width": draw_row_width(jax.random.fold_in(arg_keys[13], 71), 0),
        "w_reduce": centred(arg_keys[2], (C_IN, C_MID), C_IN ** -0.5, 0.125),
        "w_dilated": centred(arg_keys[3], (C_MID, 9, C_MID), (9 * C_MID) ** -0.5, 0.09375),
        "w_expand": centred(arg_keys[4], (C_MID, C_IN), C_MID ** -0.5, 0.25),
        "trunk_gain": jnp.clip(1.0 + 0.1 * jax.random.normal(arg_keys[5], (2 * C_MID + C_IN,), jnp.float32), 0.5, 1.5),
        "trunk_shift": centred(arg_keys[6], (2 * C_MID + C_IN,), 0.5, 3.0, (), jnp.float32),
        "branch_weight": centred(arg_keys[7], (TASKS, C_IN, 2 * C_HEAD), C_IN ** -0.5, 0.125, ((0, 4), (1, 8))),
        "rate_weight": centred(arg_keys[8], (TASKS, C_IN, 27 * C_HEAD), (9 * C_IN) ** -0.5, 0.046875, ((0, 4), (1, 8))),
        "proj_weight": centred(arg_keys[9], (TASKS, 5 * C_HEAD, C_HEAD), (5 * C_HEAD) ** -0.5, 0.15625, ((0, 4),)),
        "head_gain": jnp.clip(1.0 + 0.1 * jax.random.normal(arg_keys[10], (TASKS, 5 * C_HEAD), jnp.float32), 0.5, 1.5),
        "head_shift": centred(arg_keys[11], (TASKS, 5 * C_HEAD), 0.5, 3.0, ((0, 4),), jnp.float32),
        "head_cot": draw_head_cot(jax.random.fold_in(arg_keys[13], 71), 0),
    }


NORM_EPS = 1e-05
GRAM_EPS = 1e-06
PRECISE = lax.Precision.HIGHEST

@jax.custom_vjp
def low(v):
    return lax.optimization_barrier(v.astype(jnp.bfloat16)).astype(jnp.float32)

@jax.custom_vjp
def low_back(v):
    return v

def low_keep(v):
    return (low(v), None)

def low_pass(kept, grad):
    return (grad,)

def back_keep(v):
    return (v, None)

def back_low(kept, grad):
    return (low(grad),)
low.defvjp(low_keep, low_pass)
low_back.defvjp(back_keep, back_low)

def matmul(left_side, right_side):
    return jnp.dot(left_side, right_side, precision=PRECISE, preferred_element_type=jnp.float32)

def norm_apply(hidden, gain_vec, shift_vec, valid_mask, pixel_count):
    mean_value = lax.optimization_barrier(jnp.sum(hidden * valid_mask, axis=0)) / pixel_count
    variance = lax.optimization_barrier(jnp.sum(hidden * hidden * valid_mask, axis=0)) / pixel_count - mean_value * mean_value
    scaled = (hidden - mean_value) * lax.rsqrt(variance + NORM_EPS)
    return (gain_vec * scaled + shift_vec, mean_value, variance)

def displaced_kernel_taps(strip_image, reach_cells):
    image_height_rows, image_width_columns, channels = strip_image.shape
    padded = jnp.pad(strip_image, ((reach_cells, reach_cells), (reach_cells, reach_cells), (0, 0)))
    return [padded[row_tap * reach_cells:row_tap * reach_cells + image_height_rows, col_tap * reach_cells:col_tap * reach_cells + image_width_columns].reshape(image_height_rows * image_width_columns, channels) for row_tap in range(3) for col_tap in range(3)]

def small_solve(matrix, target):
    size_n = matrix.shape[0]
    rows_list = [matrix[number] for number in range(size_n)]
    values = [target[number] for number in range(size_n)]
    for pivot_row in range(size_n):
        for lower_row in range(pivot_row + 1, size_n):
            factor = rows_list[lower_row][pivot_row] / rows_list[pivot_row][pivot_row]
            rows_list[lower_row] = rows_list[lower_row] - factor * rows_list[pivot_row]
            values[lower_row] = values[lower_row] - factor * values[pivot_row]
    answer = [None] * size_n
    for pivot_row in reversed(range(size_n)):
        running = values[pivot_row]
        for later_row in range(pivot_row + 1, size_n):
            running = running - rows_list[pivot_row][later_row] * answer[later_row]
        answer[pivot_row] = running / rows_list[pivot_row][pivot_row]
    return jnp.stack(answer)

def imtl_weights(gram_matrix):
    grad_norms = jnp.sqrt(jnp.diagonal(gram_matrix) + GRAM_EPS)
    projections = gram_matrix / grad_norms[None, :]
    system = projections[0, 0] - projections[0:1, 1:] - projections[1:, 0:1] + projections[1:, 1:]
    target = projections[0, 0] - projections[0, 1:]
    other_weights = small_solve(jnp.transpose(system), target)
    return jnp.concatenate([(1.0 - jnp.sum(other_weights))[None], other_weights])

def trunk_forward(inputs, w_reduce, w_dilated, w_expand, trunk_gain, trunk_shift, valid_mask, pixel_count, image_height_rows, image_width_columns):
    middle_width = w_reduce.shape[1]
    hidden_one = low_back(matmul(inputs, w_reduce))
    normed_one, mean_one, var_one = norm_apply(hidden_one, trunk_gain[:middle_width], trunk_shift[:middle_width], valid_mask, pixel_count)
    first_active = low(jax.nn.gelu(normed_one) * valid_mask)
    kernel_taps = displaced_kernel_taps(first_active.reshape(image_height_rows, image_width_columns, middle_width), CONV_DILATION)
    hidden_two = low_back(sum((matmul(kernel_taps[number], w_dilated[:, number, :]) for number in range(9))))
    normed_two, mean_two, var_two = norm_apply(hidden_two, trunk_gain[middle_width:2 * middle_width], trunk_shift[middle_width:2 * middle_width], valid_mask, pixel_count)
    active_two = low(jax.nn.gelu(normed_two) * valid_mask)
    hidden_three = low_back(matmul(active_two, w_expand))
    normed_three, mean_three, var_three = norm_apply(hidden_three, trunk_gain[2 * middle_width:], trunk_shift[2 * middle_width:], valid_mask, pixel_count)
    shared = low_back(low(jax.nn.gelu(normed_three + inputs) * valid_mask))
    return (shared, (mean_one, mean_two, mean_three, var_one, var_two, var_three))

def make_branch(reach_cells, head_width, image_height_rows, image_width_columns):

    def rate_branch(values, weights):
        kernel_taps = displaced_kernel_taps(values.reshape(image_height_rows, image_width_columns, values.shape[1]), reach_cells)
        return sum((matmul(kernel_taps[number], weights[:, number * head_width:(number + 1) * head_width]) for number in range(9)))
    return jax.checkpoint(rate_branch)

def head_forward(shared, branch_local, rate_local, proj_local, gain_vec, shift_vec, valid_mask, pixel_count, image_height_rows, image_width_columns):
    head_width = proj_local.shape[1]
    shared_in = low_back(shared)
    pre_one = matmul(shared_in, branch_local[:, :head_width])
    pre_rates = [make_branch(level * RATE, head_width, image_height_rows, image_width_columns)(shared_in, rate_local[:, (level - 1) * 9 * head_width:level * 9 * head_width]) for level in (1, 2, 3)]
    pre_both = low_back(jnp.concatenate([pre_one] + pre_rates, axis=1))
    pooled = low_back(matmul(lax.optimization_barrier(jnp.sum(shared_in * valid_mask, axis=0))[None], branch_local[:, head_width:]) / pixel_count)
    normed_both = norm_apply(pre_both, gain_vec[:4 * head_width], shift_vec[:4 * head_width], valid_mask, pixel_count)[0]
    active_both = low(jax.nn.gelu(normed_both) * valid_mask)
    active_pool = low(jax.nn.gelu(pooled)) * valid_mask
    joined = jnp.concatenate([active_both, active_pool], axis=1)
    projected = low_back(matmul(joined, proj_local))
    normed_proj = norm_apply(projected, gain_vec[4 * head_width:], shift_vec[4 * head_width:], valid_mask, pixel_count)[0]
    return jax.nn.gelu(normed_proj) * valid_mask

def reference(features, row_width, w_reduce, w_dilated, w_expand, trunk_gain, trunk_shift, branch_weight, rate_weight, proj_weight, head_gain, head_shift, head_cot):
    image_height_rows, image_width_columns, in_width = features.shape
    head_width = proj_weight.shape[2]
    task_total = head_cot.shape[0]
    valid_mask = (jnp.arange(image_width_columns)[None, :] < row_width[:, None]).astype(jnp.float32).reshape(image_height_rows * image_width_columns, 1)
    pixel_count = jnp.sum(valid_mask)
    inputs = features.reshape(image_height_rows * image_width_columns, in_width).astype(jnp.float32)

    def trunk_apply(inputs_in, reduce_in, dilated_in, expand_in, gain_in, shift_in):
        return trunk_forward(inputs_in, reduce_in, dilated_in, expand_in, gain_in, shift_in, valid_mask, pixel_count, image_height_rows, image_width_columns)
    shared, trunk_back, stats = jax.vjp(trunk_apply, inputs, w_reduce.astype(jnp.float32), w_dilated.astype(jnp.float32), w_expand.astype(jnp.float32), trunk_gain, trunk_shift, has_aux=True)

    def head_apply(shared_in, branch_in, rate_in, proj_in, gain_in, shift_in):
        return head_forward(shared_in, branch_in, rate_in, proj_in, gain_in, shift_in, valid_mask, pixel_count, image_height_rows, image_width_columns)
    outputs_list, shared_grads, branch_list, rate_list, proj_list, gain_list, shift_list = ([], [], [], [], [], [], [])
    for task_index in range(task_total):
        result, head_back = jax.vjp(head_apply, shared, branch_weight[task_index].astype(jnp.float32), rate_weight[task_index].astype(jnp.float32), proj_weight[task_index].astype(jnp.float32), head_gain[task_index], head_shift[task_index])
        grads = head_back(head_cot[task_index].reshape(-1, head_width).astype(jnp.float32))
        outputs_list.append(result.astype(jnp.bfloat16))
        shared_grads.append(grads[0])
        branch_list.append(grads[1])
        rate_list.append(grads[2])
        proj_list.append(grads[3])
        gain_list.append(grads[4])
        shift_list.append(grads[5])
    gram_matrix = jnp.stack([jnp.stack([jnp.sum(shared_grads[first_task] * shared_grads[second_task]) for second_task in range(task_total)]) for first_task in range(task_total)])
    task_weight = imtl_weights(gram_matrix)
    combined = sum((task_weight[task_index] * shared_grads[task_index] for task_index in range(task_total)))
    trunk_grads = trunk_back(combined)
    means = jnp.concatenate([stats[0], stats[1], stats[2]])
    variances = jnp.concatenate([stats[3], stats[4], stats[5]]) * pixel_count / (pixel_count - 1.0)
    batch_stats = jnp.stack([means, variances])
    head_out = jnp.stack(outputs_list).reshape(task_total, image_height_rows, image_width_columns, head_width)
    return (head_out, trunk_grads[0].reshape(image_height_rows, image_width_columns, in_width).astype(jnp.bfloat16), trunk_grads[1], trunk_grads[2], trunk_grads[3], trunk_grads[4], trunk_grads[5], batch_stats, jnp.stack(branch_list), jnp.stack(rate_list), jnp.stack(proj_list), jnp.stack(gain_list), jnp.stack(shift_list), task_weight)
```

```python
import functools

import jax
import jax.numpy as jnp
from jax import lax
from jax.experimental import pallas as pl
from jax.experimental.pallas import tpu as pltpu
from jax.sharding import PartitionSpec as P

CONV_DILATION = 2
RATE = 12


NORM_EPS = 1e-05
GRAM_EPS = 1e-06
PRECISE = lax.Precision.HIGHEST


def with_halo(block, sides, width):
    for axis, dim in sides:
        count = lax.axis_size(axis)
        forward = [(i, i + 1) for i in range(count - 1)]
        backward = [(target, source) for source, target in forward]
        low = lax.ppermute(
            lax.slice_in_dim(block, block.shape[dim] - width, None, axis=dim), axis, forward
        )
        high = lax.ppermute(lax.slice_in_dim(block, 0, width, axis=dim), axis, backward)
        block = jnp.concatenate([low, block, high], axis=dim)
    return block


def from_behind(shard, axis, by):
    count = lax.axis_size(axis)
    pairs = [(i, i + by) for i in range(count) if 0 <= i + by < count]
    return lax.ppermute(shard, axis, pairs)


def small_solve(matrix, target):
    size_n = matrix.shape[0]
    rows_list = [matrix[number] for number in range(size_n)]
    values = [target[number] for number in range(size_n)]
    for pivot_row in range(size_n):
        for lower_row in range(pivot_row + 1, size_n):
            factor = rows_list[lower_row][pivot_row] / rows_list[pivot_row][pivot_row]
            rows_list[lower_row] = rows_list[lower_row] - factor * rows_list[pivot_row]
            values[lower_row] = values[lower_row] - factor * values[pivot_row]
    answer = [None] * size_n
    for pivot_row in reversed(range(size_n)):
        running = values[pivot_row]
        for later_row in range(pivot_row + 1, size_n):
            running = running - rows_list[pivot_row][later_row] * answer[later_row]
        answer[pivot_row] = running / rows_list[pivot_row][pivot_row]
    return jnp.stack(answer)


def imtl_weights(gram_matrix):
    grad_norms = jnp.sqrt(jnp.diagonal(gram_matrix) + GRAM_EPS)
    projections = gram_matrix / grad_norms[None, :]
    system = projections[0, 0] - projections[0:1, 1:] - projections[1:, 0:1] + projections[1:, 1:]
    target = projections[0, 0] - projections[0, 1:]
    other_weights = small_solve(jnp.transpose(system), target)
    return jnp.concatenate([(1.0 - jnp.sum(other_weights))[None], other_weights])


def gelu_back(value, upstream):
    return jax.vjp(jax.nn.gelu, value)[1](upstream)[0]


def channel_sums(members):
    return lax.psum(members, "space")


def norm_values(hidden, first_total, second_total, gain_vec, shift_vec, pixel_count):
    mean_value = first_total / pixel_count
    variance = second_total / pixel_count - mean_value * mean_value
    inv_std = lax.rsqrt(variance + NORM_EPS)
    scaled = (hidden - mean_value) * inv_std
    return (gain_vec * scaled + shift_vec, scaled, inv_std, mean_value, variance)


def norm_forward(hidden, gain_vec, shift_vec, valid_mask, pixel_count):
    totals = channel_sums(
        (jnp.sum(hidden * valid_mask, axis=0), jnp.sum(hidden * hidden * valid_mask, axis=0))
    )
    return norm_values(hidden, totals[0], totals[1], gain_vec, shift_vec, pixel_count)


def norm_finish(
    upstream, scaled, inv_std, gain_vec, gain_grad, shift_grad, valid_mask, pixel_count
):
    return (
        valid_mask
        * gain_vec
        * inv_std
        * (upstream - shift_grad / pixel_count - scaled * gain_grad / pixel_count)
    )


def norm_backward(upstream, scaled, inv_std, gain_vec, valid_mask, pixel_count):
    totals = channel_sums(
        (jnp.sum(upstream * valid_mask, axis=0), jnp.sum(upstream * scaled * valid_mask, axis=0))
    )
    hidden_grad = norm_finish(
        upstream, scaled, inv_std, gain_vec, totals[1], totals[0], valid_mask, pixel_count
    )
    return (hidden_grad, totals[1], totals[0])


def band_rim(strip_image):
    return with_halo(strip_image, (("space", 0),), CONV_DILATION)


def far_rows(strip_image, bands_away, upward):
    if bands_away >= lax.axis_size("space"):
        return jnp.zeros_like(strip_image)
    if upward:
        return from_behind(strip_image, "space", bands_away)
    return from_behind(strip_image, "space", -bands_away)


def trunk_taps(padded, reach_cells, rows_count, cols_count, flipped):
    col_padded = jnp.pad(padded, ((0, 0), (reach_cells, reach_cells), (0, 0)))
    pieces = []
    for row_tap in range(3):
        for col_tap in range(3):
            row_from = (2 - row_tap) * reach_cells if flipped else row_tap * reach_cells
            col_from = (2 - col_tap) * reach_cells if flipped else col_tap * reach_cells
            pieces.append(
                col_padded[
                    row_from : row_from + rows_count, col_from : col_from + cols_count
                ].reshape(rows_count * cols_count, -1)
            )
    return jnp.stack(pieces, axis=1)


def per_device(
    features,
    row_width,
    w_reduce,
    w_dilated,
    w_expand,
    trunk_gain,
    trunk_shift,
    branch_weight,
    rate_weight,
    proj_weight,
    head_gain,
    head_shift,
    head_cot,
):
    band_rows, cols_count, in_width = features.shape
    pixels = band_rows * cols_count
    middle_width = w_reduce.shape[1]
    head_width = proj_weight.shape[2]
    first_row = lax.axis_index("space") * band_rows
    widths = lax.dynamic_slice_in_dim(row_width, first_row, band_rows)
    valid_mask = (
        (jnp.arange(cols_count)[None, :] < widths[:, None]).astype(jnp.float32).reshape(pixels, 1)
    )
    pixel_count = jnp.sum(row_width).astype(jnp.float32)
    inputs = features.reshape(pixels, in_width)
    gain_one, shift_one = (trunk_gain[:middle_width], trunk_shift[:middle_width])
    gain_two, shift_two = (
        trunk_gain[middle_width : 2 * middle_width],
        trunk_shift[middle_width : 2 * middle_width],
    )
    gain_three, shift_three = (trunk_gain[2 * middle_width :], trunk_shift[2 * middle_width :])
    hidden_one = jnp.dot(inputs, w_reduce, preferred_element_type=jnp.float32)
    stats_one = norm_forward(hidden_one, gain_one, shift_one, valid_mask, pixel_count)
    first_active = (jax.nn.gelu(stats_one[0]) * valid_mask).astype(jnp.bfloat16)
    patches = trunk_taps(
        band_rim(first_active.reshape(band_rows, cols_count, middle_width)),
        CONV_DILATION,
        band_rows,
        cols_count,
        False,
    )
    hidden_two = jnp.einsum("pti,ito->po", patches, w_dilated, preferred_element_type=jnp.float32)
    stats_two = norm_forward(hidden_two, gain_two, shift_two, valid_mask, pixel_count)
    active_two = (jax.nn.gelu(stats_two[0]) * valid_mask).astype(jnp.bfloat16)
    hidden_three = jnp.dot(active_two, w_expand, preferred_element_type=jnp.float32)
    stats_three = norm_forward(hidden_three, gain_three, shift_three, valid_mask, pixel_count)
    before_act = stats_three[0] + inputs.astype(jnp.float32)
    shared = (jax.nn.gelu(before_act) * valid_mask).astype(jnp.bfloat16)
    proj_local = proj_weight[0]
    gain_local = head_gain[0]
    shift_local = head_shift[0]
    joined_weight = jnp.concatenate([branch_weight[0], rate_weight[0]], axis=1)
    pixel_sum = jnp.dot(
        valid_mask.reshape(1, pixels).astype(jnp.bfloat16),
        shared,
        preferred_element_type=jnp.float32,
    )[0]
    shared_image = shared.reshape(band_rows, cols_count, in_width)
    padded_sources = []
    for level in (1, 2, 3):
        reach = level * RATE
        bands_away = reach // band_rows
        triple = (
            far_rows(shared_image, bands_away, True),
            shared_image,
            far_rows(shared_image, bands_away, False),
        )
        padded_sources.append(
            [jnp.pad(source, ((0, 0), (reach, reach), (0, 0))) for source in triple]
        )
    zero_rows = jnp.zeros((pixels, head_width), jnp.float32)
    start_totals = (
        zero_rows,
        jnp.zeros((1, head_width), jnp.float32),
        zero_rows,
        zero_rows,
        zero_rows,
    )
    all_weights = lax.all_gather(joined_weight, "space", axis=0, tiled=True)
    width_now = all_weights.shape[0]
    one_acc = jnp.dot(shared, all_weights[:, :head_width], preferred_element_type=jnp.float32)
    pool_cols = pixel_sum[None]
    pool_acc = jnp.dot(
        pool_cols,
        all_weights[:, head_width : 2 * head_width].astype(jnp.float32),
        precision=PRECISE,
        preferred_element_type=jnp.float32,
    )
    rate_accs = []
    for fold_level_index in range(3):
        fold_reach = (fold_level_index + 1) * RATE
        running = start_totals[2 + fold_level_index]
        for fold_row_tap in range(3):
            fold_source = padded_sources[fold_level_index][fold_row_tap]
            for fold_col_tap in range(3):
                window = fold_source[
                    :, fold_col_tap * fold_reach : fold_col_tap * fold_reach + cols_count
                ].reshape(pixels, width_now)
                column = (2 + 9 * fold_level_index + 3 * fold_row_tap + fold_col_tap) * head_width
                running = running + jnp.dot(
                    window,
                    all_weights[:, column : column + head_width],
                    preferred_element_type=jnp.float32,
                )
        rate_accs.append(running)
    pre_both = jnp.concatenate([one_acc, rate_accs[0], rate_accs[1], rate_accs[2]], axis=1)
    gain_both, shift_both = (gain_local[: 4 * head_width], shift_local[: 4 * head_width])
    totals = channel_sums(
        (
            jnp.sum(pre_both * valid_mask, axis=0),
            jnp.sum(pre_both * pre_both * valid_mask, axis=0),
            pool_acc[0],
        )
    )
    stats_both = norm_values(pre_both, totals[0], totals[1], gain_both, shift_both, pixel_count)
    pooled = totals[2][None] / pixel_count
    active_both = (jax.nn.gelu(stats_both[0]) * valid_mask).astype(jnp.bfloat16)
    active_pool = jax.nn.gelu(pooled).astype(jnp.bfloat16)
    joined = jnp.concatenate(
        [active_both, (active_pool.astype(jnp.float32) * valid_mask).astype(jnp.bfloat16)], axis=1
    )
    projected = jnp.dot(joined, proj_local, preferred_element_type=jnp.float32)
    gain_proj = gain_local[4 * head_width :]
    stats_proj = norm_forward(
        projected, gain_proj, shift_local[4 * head_width :], valid_mask, pixel_count
    )
    head_result = (jax.nn.gelu(stats_proj[0]) * valid_mask).astype(jnp.bfloat16)
    cot_rows = head_cot[0].reshape(pixels, head_width).astype(jnp.float32)
    proj_upstream = gelu_back(stats_proj[0], cot_rows * valid_mask)
    proj_hidden, proj_gain_grad, proj_shift_grad = norm_backward(
        proj_upstream, stats_proj[1], stats_proj[2], gain_proj, valid_mask, pixel_count
    )
    proj_low = proj_hidden.astype(jnp.bfloat16)
    joined_grad = lax.dot_general(
        proj_low, proj_local, (((1,), (1,)), ((), ())), preferred_element_type=jnp.float32
    )
    proj_term = lax.dot_general(
        joined, proj_low, (((0,), (0,)), ((), ())), preferred_element_type=jnp.float32
    )
    both_upstream = gelu_back(stats_both[0], joined_grad[:, : 4 * head_width] * valid_mask)
    pool_total = jnp.sum(joined_grad[:, 4 * head_width :] * valid_mask, axis=0)
    back_totals = channel_sums(
        (
            proj_term,
            pool_total,
            jnp.sum(both_upstream * valid_mask, axis=0),
            jnp.sum(both_upstream * stats_both[1] * valid_mask, axis=0),
        )
    )
    pool_grad = gelu_back(pooled, back_totals[1][None]).astype(jnp.bfloat16)
    both_grad = norm_finish(
        both_upstream,
        stats_both[1],
        stats_both[2],
        gain_both,
        back_totals[3],
        back_totals[2],
        valid_mask,
        pixel_count,
    ).astype(jnp.bfloat16)
    tap_grads = []
    for level_index in range(3):
        reach = (level_index + 1) * RATE
        bands_away = reach // band_rows
        rate_image = both_grad[
            :, (1 + level_index) * head_width : (2 + level_index) * head_width
        ].reshape(band_rows, cols_count, head_width)
        back_sources = [
            jnp.pad(source, ((0, 0), (reach, reach), (0, 0)))
            for source in (
                far_rows(rate_image, bands_away, False),
                rate_image,
                far_rows(rate_image, bands_away, True),
            )
        ]
        for row_tap in range(3):
            for col_tap in range(3):
                tap_grads.append(
                    back_sources[row_tap][
                        :, (2 - col_tap) * reach : (2 - col_tap) * reach + cols_count
                    ].reshape(pixels, head_width)
                )
    right_side = jnp.concatenate([both_grad[:, :head_width]] + tap_grads, axis=1)
    used_rows = jnp.concatenate(
        [all_weights[:, :head_width], all_weights[:, 2 * head_width :]], axis=1
    )
    main_part = lax.dot_general(
        right_side, used_rows, (((1,), (1,)), ((), ())), preferred_element_type=jnp.float32
    )
    pool_part = lax.dot_general(
        pool_grad,
        all_weights[:, head_width : 2 * head_width],
        (((1,), (1,)), ((), ())),
        preferred_element_type=jnp.float32,
    )
    shared_grad = (main_part + valid_mask * pool_part / pixel_count).astype(jnp.bfloat16)
    head_term = lax.dot_general(
        shared, right_side, (((0,), (0,)), ((), ())), preferred_element_type=jnp.float32
    )
    pool_term = pixel_sum[:, None] * pool_grad.astype(jnp.float32) / pixel_count
    head_term = jnp.concatenate(
        [head_term[:, :head_width], pool_term, head_term[:, head_width:]], axis=1
    )
    all_grads = lax.all_gather(shared_grad[None], "task", axis=0, tiled=True)
    flat_grads = all_grads.reshape(all_grads.shape[0], -1)
    gram_matrix = lax.psum(
        lax.dot_general(
            flat_grads, flat_grads, (((1,), (1,)), ((), ())), preferred_element_type=jnp.float32
        ),
        "space",
    )
    task_weight = imtl_weights(gram_matrix)
    mixed_grad = task_weight[0] * all_grads[0].astype(jnp.float32)
    for task_index in range(1, all_grads.shape[0]):
        mixed_grad = mixed_grad + task_weight[task_index] * all_grads[task_index].astype(
            jnp.float32
        )
    combined = mixed_grad.astype(jnp.bfloat16)
    gate_grad = gelu_back(before_act, combined.astype(jnp.float32) * valid_mask)
    hidden_grad_three, gain_grad_three, shift_grad_three = norm_backward(
        gate_grad, stats_three[1], stats_three[2], gain_three, valid_mask, pixel_count
    )
    low_three = hidden_grad_three.astype(jnp.bfloat16)
    expand_term = lax.dot_general(
        active_two, low_three, (((0,), (0,)), ((), ())), preferred_element_type=jnp.float32
    )
    active_grad_two = lax.dot_general(
        low_three, w_expand, (((1,), (1,)), ((), ())), preferred_element_type=jnp.float32
    )
    upstream_two = gelu_back(stats_two[0], active_grad_two * valid_mask)
    hidden_grad_two, gain_grad_two, shift_grad_two = norm_backward(
        upstream_two, stats_two[1], stats_two[2], gain_two, valid_mask, pixel_count
    )
    low_two = hidden_grad_two.astype(jnp.bfloat16)
    dilated_term = jnp.einsum("pti,po->ito", patches, low_two, preferred_element_type=jnp.float32)
    back_patches = trunk_taps(
        band_rim(low_two.reshape(band_rows, cols_count, middle_width)),
        CONV_DILATION,
        band_rows,
        cols_count,
        True,
    )
    active_grad_one = jnp.einsum(
        "pto,ito->pi", back_patches, w_dilated, preferred_element_type=jnp.float32
    )
    upstream_one = gelu_back(stats_one[0], active_grad_one * valid_mask)
    hidden_grad_one, gain_grad_one, shift_grad_one = norm_backward(
        upstream_one, stats_one[1], stats_one[2], gain_one, valid_mask, pixel_count
    )
    low_one = hidden_grad_one.astype(jnp.bfloat16)
    reduce_term = lax.dot_general(
        inputs, low_one, (((0,), (0,)), ((), ())), preferred_element_type=jnp.float32
    )
    input_grad = (
        lax.dot_general(
            low_one, w_reduce, (((1,), (1,)), ((), ())), preferred_element_type=jnp.float32
        )
        + gate_grad
    )
    reduced = (
        lax.psum_scatter(head_term, "space", scatter_dimension=0, tiled=True),
        lax.psum_scatter(reduce_term, "space", scatter_dimension=0, tiled=True),
        lax.psum_scatter(dilated_term, "space", scatter_dimension=0, tiled=True),
        lax.psum_scatter(expand_term, "space", scatter_dimension=0, tiled=True),
    )
    means = jnp.concatenate([stats_one[3], stats_two[3], stats_three[3]])
    variances = (
        jnp.concatenate([stats_one[4], stats_two[4], stats_three[4]])
        * pixel_count
        / (pixel_count - 1.0)
    )
    batch_stats = jnp.stack([means, variances])
    head_gain_grad = jnp.concatenate([back_totals[3], proj_gain_grad])[None]
    head_shift_grad = jnp.concatenate([back_totals[2], proj_shift_grad])[None]
    return (
        head_result.reshape(1, band_rows, cols_count, head_width),
        input_grad.reshape(band_rows, cols_count, in_width).astype(jnp.bfloat16),
        reduced[1],
        reduced[2],
        reduced[3],
        jnp.concatenate([gain_grad_one, gain_grad_two, gain_grad_three]),
        jnp.concatenate([shift_grad_one, shift_grad_two, shift_grad_three]),
        batch_stats,
        reduced[0][:, : 2 * head_width][None],
        reduced[0][:, 2 * head_width :][None],
        back_totals[0][None],
        head_gain_grad,
        head_shift_grad,
        task_weight,
    )


MESH_ID = pl.DeviceIdType.MESH
LANE = 128


def meet_bands(place, count):
    barrier = pltpu.get_barrier_semaphore()
    for step in range(1, count):
        pl.semaphore_signal(
            barrier,
            inc=1,
            device_id={"space": lax.rem(place + step, count)},
            device_id_type=MESH_ID,
        )
    pl.semaphore_wait(barrier, count - 1)


def sum_kernel(count, own_ref, out_ref, landing, send_sem, recv_sem):
    place = lax.axis_index("space")
    meet_bands(place, count)
    copies = []
    for step in range(1, count):
        copy = pltpu.make_async_remote_copy(
            own_ref,
            landing.at[step],
            send_sem.at[step],
            recv_sem.at[step],
            device_id={"space": lax.rem(place + step, count)},
            device_id_type=MESH_ID,
        )
        copy.start()
        copies.append(copy)
    total = own_ref[...]
    for step in range(1, count):
        copies[step - 1].wait_recv()
        total = total + landing[step]
    out_ref[...] = total
    for copy in copies:
        copy.wait_send()


def gather_kernel(count, own_ref, out_ref, send_sem, recv_sem, local_sem):
    place = lax.axis_index("space")
    chips = count // 2
    chip = place // 2
    core = lax.rem(place, 2)
    twin = chip * 2 + 1 - core
    meet_bands(place, count)
    copies = []
    for step in range(1, chips):
        copy = pltpu.make_async_remote_copy(
            own_ref,
            out_ref.at[place],
            send_sem.at[step],
            recv_sem.at[step],
            device_id={"space": lax.rem(chip + step, chips) * 2 + core},
            device_id_type=MESH_ID,
        )
        copy.start()
        copies.append(copy)
    to_twin = pltpu.make_async_remote_copy(
        own_ref,
        out_ref.at[place],
        send_sem.at[0],
        recv_sem.at[0],
        device_id={"space": twin},
        device_id_type=MESH_ID,
    )
    to_twin.start()
    here = pltpu.make_async_copy(own_ref, out_ref.at[place], local_sem)
    here.start()
    passed = []
    for step in range(1, chips):
        copies[step - 1].wait_recv()
        source = lax.rem(chip + chips - step, chips) * 2 + core
        copy = pltpu.make_async_remote_copy(
            out_ref.at[source],
            out_ref.at[source],
            send_sem.at[chips - 1 + step],
            recv_sem.at[chips - 1 + step],
            device_id={"space": twin},
            device_id_type=MESH_ID,
        )
        copy.start()
        passed.append(copy)
    to_twin.wait()
    for copy in passed:
        copy.wait()
    for copy in copies:
        copy.wait_send()
    here.wait()


def swap_kernel(count, own_ref, out_ref, send_sem, recv_sem, local_sem):
    place = lax.axis_index("space")
    meet_bands(place, count)
    copies = []
    for step in range(1, count):
        target = lax.rem(place + step, count)
        copy = pltpu.make_async_remote_copy(
            own_ref.at[target],
            out_ref.at[place],
            send_sem.at[step],
            recv_sem.at[step],
            device_id={"space": target},
            device_id_type=MESH_ID,
        )
        copy.start()
        copies.append(copy)
    here = pltpu.make_async_copy(own_ref.at[place], out_ref.at[place], local_sem)
    here.start()
    for copy in copies:
        copy.wait()
    here.wait()


def scatter_kernel(count, own_ref, out_ref, twin_land, paired, landing, send_sem, recv_sem):
    place = lax.axis_index("space")
    chips = count // 2
    chip = place // 2
    core = lax.rem(place, 2)
    twin = chip * 2 + 1 - core
    meet_bands(place, count)
    from_twin = []
    for step in range(chips):
        other = lax.rem(chip + step, chips)
        copy = pltpu.make_async_remote_copy(
            own_ref.at[other * 2 + 1 - core],
            twin_land.at[step],
            send_sem.at[step],
            recv_sem.at[step],
            device_id={"space": twin},
            device_id_type=MESH_ID,
        )
        from_twin.append(copy)
    order = list(range(1, chips)) + [0]
    for step in order:
        from_twin[step].start()
    sent = []
    for step in order:
        from_twin[step].wait_recv()
        other = lax.rem(chip + step, chips)
        pair = own_ref[other * 2 + core].astype(jnp.float32) + twin_land[step].astype(jnp.float32)
        if step == 0:
            out_ref[...] = pair
            continue
        paired[step] = pair.astype(paired.dtype)
        copy = pltpu.make_async_remote_copy(
            paired.at[step],
            landing.at[step],
            send_sem.at[chips + step],
            recv_sem.at[chips + step],
            device_id={"space": other * 2 + core},
            device_id_type=MESH_ID,
        )
        copy.start()
        sent.append(copy)
    for step in range(1, chips):
        sent[step - 1].wait_recv()
        out_ref[...] += landing[step].astype(jnp.float32)
    for copy in sent:
        copy.wait_send()
    for copy in from_twin:
        copy.wait_send()


def tasks_kernel(count, own_ref, out_ref, send_sem, recv_sem, local_sem):
    place = lax.axis_index("task")
    barrier = pltpu.get_barrier_semaphore()
    for step in range(1, count):
        pl.semaphore_signal(
            barrier,
            inc=1,
            device_id={"task": lax.rem(place + step, count)},
            device_id_type=MESH_ID,
        )
    pl.semaphore_wait(barrier, count - 1)
    copies = []
    for step in range(1, count):
        copy = pltpu.make_async_remote_copy(
            own_ref,
            out_ref.at[place],
            send_sem.at[step],
            recv_sem.at[step],
            device_id={"task": lax.rem(place + step, count)},
            device_id_type=MESH_ID,
        )
        copy.start()
        copies.append(copy)
    here = pltpu.make_async_copy(own_ref, out_ref.at[place], local_sem)
    here.start()
    for copy in copies:
        copy.wait()
    here.wait()


class Links:
    def __init__(self):
        self.bands = lax.axis_size("space")
        self.tasks = lax.axis_size("task")
        self.used = 0

    def call(self, kernel, out, scratch, operand, label):
        self.used += 1
        in_vmem = pl.BlockSpec(memory_space=pltpu.VMEM)
        return pl.pallas_call(
            kernel,
            name=label,
            out_shape=out,
            in_specs=[in_vmem],
            out_specs=in_vmem,
            scratch_shapes=scratch,
            compiler_params=pltpu.CompilerParams(
                collective_id=self.used - 1, has_side_effects=True, vmem_limit_bytes=48 << 20
            ),
        )(operand)

    def sums(self, members, label):
        sizes = [member.size for member in members]
        flat = jnp.concatenate([member.reshape(-1) for member in members])
        tile = 8 * LANE
        padded = -(-flat.size // tile) * tile
        block = jnp.pad(flat, (0, padded - flat.size)).reshape(-1, LANE)
        sems = pltpu.SemaphoreType.DMA((self.bands,))
        total = self.call(
            functools.partial(sum_kernel, self.bands),
            jax.ShapeDtypeStruct(block.shape, block.dtype),
            [pltpu.VMEM((self.bands,) + block.shape, block.dtype), sems, sems],
            block,
            label,
        ).reshape(-1)
        out = []
        start = 0
        for member, size in zip(members, sizes):
            out.append(total[start : start + size].reshape(member.shape))
            start += size
        return out

    def gather(self, block, label):
        sems = pltpu.SemaphoreType.DMA((self.bands,))
        return self.call(
            functools.partial(gather_kernel, self.bands),
            jax.ShapeDtypeStruct((self.bands,) + block.shape, block.dtype),
            [sems, sems, pltpu.SemaphoreType.DMA],
            block,
            label,
        )

    def swap(self, blocks, label):
        sems = pltpu.SemaphoreType.DMA((self.bands,))
        return self.call(
            functools.partial(swap_kernel, self.bands),
            jax.ShapeDtypeStruct(blocks.shape, blocks.dtype),
            [sems, sems, pltpu.SemaphoreType.DMA],
            blocks,
            label,
        )

    def scatter(self, blocks, label):
        sems = pltpu.SemaphoreType.DMA((self.bands,))
        half = (self.bands // 2,) + blocks.shape[1:]
        return self.call(
            functools.partial(scatter_kernel, self.bands),
            jax.ShapeDtypeStruct(blocks.shape[1:], jnp.float32),
            [pltpu.VMEM(half, blocks.dtype)] * 3 + [sems, sems],
            blocks,
            label,
        )

    def over_tasks(self, block, label):
        sems = pltpu.SemaphoreType.DMA((self.tasks,))
        return self.call(
            functools.partial(tasks_kernel, self.tasks),
            jax.ShapeDtypeStruct((self.tasks,) + block.shape, block.dtype),
            [sems, sems, pltpu.SemaphoreType.DMA],
            block,
            label,
        )


def norm_scale(totals, pixel_count):
    mean_value = totals[0] / pixel_count
    variance = totals[1] / pixel_count - mean_value * mean_value
    return mean_value, variance, lax.rsqrt(variance + NORM_EPS)


def masked_sums(hidden, valid_mask):
    kept = hidden * valid_mask
    return [jnp.sum(kept, axis=0), jnp.sum(hidden * kept, axis=0)]


def shift_columns(image, by):
    if by == 0:
        return image
    cols = image.shape[1]
    if by > 0:
        return jnp.pad(image[:, by:], ((0, 0), (0, by), (0, 0)))
    return jnp.pad(image[:, : cols + by], ((0, 0), (-by, 0), (0, 0)))


def live_taps(rows, cols):
    taps = []
    for level in (1, 2, 3):
        for row_tap in range(3):
            for col_tap in range(3):
                down, right = (row_tap - 1) * level * RATE, (col_tap - 1) * level * RATE
                if abs(down) < rows and abs(right) < cols:
                    taps.append((level, row_tap, col_tap, down, right))
    return taps


def per_device_slices(
    features,
    row_width,
    w_reduce,
    w_dilated,
    w_expand,
    trunk_gain,
    trunk_shift,
    branch_weight,
    rate_weight,
    proj_weight,
    head_gain,
    head_shift,
    head_cot,
):
    links = Links()
    bands, tasks = links.bands, links.tasks
    low = jnp.bfloat16
    wide = jnp.float32
    band_rows, cols_count, in_width = features.shape
    rows_count = band_rows * bands
    pixels = band_rows * cols_count
    all_pixels = pixels * bands
    middle_width = w_reduce.shape[1]
    head_width = proj_weight.shape[2]
    slice_width = in_width // bands
    band = lax.axis_index("space")
    task = lax.axis_index("task")
    widths = lax.dynamic_slice_in_dim(row_width, band * band_rows, band_rows)

    def mask_of(some_widths):
        return (
            (jnp.arange(cols_count)[None, :] < some_widths[:, None]).astype(wide).reshape(-1, 1)
        )

    valid_mask = mask_of(widths)
    all_mask = mask_of(row_width)
    pixel_count = jnp.sum(row_width).astype(wide)
    inputs = features.reshape(pixels, in_width)
    gains = [
        trunk_gain[:middle_width],
        trunk_gain[middle_width : 2 * middle_width],
        trunk_gain[2 * middle_width :],
    ]
    shifts = [
        trunk_shift[:middle_width],
        trunk_shift[middle_width : 2 * middle_width],
        trunk_shift[2 * middle_width :],
    ]

    def norm(hidden, totals, gain_vec, shift_vec):
        mean_value, variance, inv_std = norm_scale(totals, pixel_count)
        scaled = (hidden - mean_value) * inv_std
        return gain_vec * scaled + shift_vec, scaled, inv_std, mean_value, variance

    hidden_one = jnp.dot(inputs, w_reduce, preferred_element_type=wide)
    stats_one = norm(
        hidden_one, links.sums(masked_sums(hidden_one, valid_mask), "sums_one"), gains[0], shifts[0]
    )
    first_active = (jax.nn.gelu(stats_one[0]) * valid_mask).astype(low)
    patches = trunk_taps(
        band_rim(first_active.reshape(band_rows, cols_count, middle_width)),
        CONV_DILATION,
        band_rows,
        cols_count,
        False,
    )
    hidden_two = jnp.einsum("pti,ito->po", patches, w_dilated, preferred_element_type=wide)
    stats_two = norm(
        hidden_two, links.sums(masked_sums(hidden_two, valid_mask), "sums_two"), gains[1], shifts[1]
    )
    active_two = (jax.nn.gelu(stats_two[0]) * valid_mask).astype(low)
    hidden_three = jnp.dot(active_two, w_expand, preferred_element_type=wide)
    stats_three = norm(
        hidden_three,
        links.sums(masked_sums(hidden_three, valid_mask), "sums_three"),
        gains[2],
        shifts[2],
    )
    before_act = stats_three[0] + inputs.astype(wide)
    shared = (jax.nn.gelu(before_act) * valid_mask).astype(low)

    shared_slice = links.swap(
        shared.reshape(pixels, bands, slice_width).transpose(1, 0, 2), "swap_shared"
    ).reshape(all_pixels, slice_width)
    pixel_sum = jnp.sum(shared_slice.astype(wide), axis=0)
    branch_local = branch_weight[0]
    rate_local = rate_weight[0]
    proj_local = proj_weight[0]
    gain_local = head_gain[0]
    shift_local = head_shift[0]

    def rate_columns(level, row_tap, col_tap):
        start = (9 * (level - 1) + 3 * row_tap + col_tap) * head_width
        return slice(start, start + head_width)

    taps = live_taps(rows_count, cols_count)
    shared_image = shared_slice.reshape(rows_count, cols_count, slice_width)
    pre_parts = [
        jnp.dot(shared_slice, branch_local[:, :head_width], preferred_element_type=wide).reshape(
            rows_count, cols_count, head_width
        )
    ]
    for level in (1, 2, 3):
        total = jnp.zeros((rows_count, cols_count, head_width), wide)
        for number, row_tap, col_tap, down, right in taps:
            if number != level:
                continue
            first, last = max(0, -down), rows_count - max(0, down)
            window = shift_columns(shared_image[first + down : last + down], right)
            term = jnp.dot(
                window.reshape(-1, slice_width),
                rate_local[:, rate_columns(level, row_tap, col_tap)],
                preferred_element_type=wide,
            ).reshape(last - first, cols_count, head_width)
            total = total + jnp.pad(term, ((first, rows_count - last), (0, 0), (0, 0)))
        pre_parts.append(total)
    pre_terms = jnp.concatenate(pre_parts, axis=2).astype(low)
    pre_both = links.scatter(pre_terms.reshape(bands, pixels, 4 * head_width), "scatter_pre")
    pool_term = jnp.dot(
        pixel_sum[None],
        branch_local[:, head_width:].astype(wide),
        precision=PRECISE,
        preferred_element_type=wide,
    )
    totals = links.sums(masked_sums(pre_both, valid_mask) + [pool_term], "sums_both")
    gain_both, shift_both = (gain_local[: 4 * head_width], shift_local[: 4 * head_width])
    stats_both = norm(pre_both, totals, gain_both, shift_both)
    pooled = totals[2] / pixel_count
    active_both = (jax.nn.gelu(stats_both[0]) * valid_mask).astype(low)
    active_pool = jax.nn.gelu(pooled).astype(low)
    joined = jnp.concatenate(
        [active_both, (active_pool.astype(wide) * valid_mask).astype(low)], axis=1
    )
    projected = jnp.dot(joined, proj_local, preferred_element_type=wide)
    gain_proj = gain_local[4 * head_width :]
    stats_proj = norm(
        projected,
        links.sums(masked_sums(projected, valid_mask), "sums_proj"),
        gain_proj,
        shift_local[4 * head_width :],
    )
    head_result = (jax.nn.gelu(stats_proj[0]) * valid_mask).astype(low)
    cot_rows = head_cot[0].reshape(pixels, head_width).astype(wide)

    def back_sums(upstream, scaled):
        kept = upstream * valid_mask
        return [jnp.sum(kept, axis=0), jnp.sum(kept * scaled, axis=0)]

    def finish(upstream, stats, gain_vec, sums):
        return norm_finish(
            upstream, stats[1], stats[2], gain_vec, sums[1], sums[0], valid_mask, pixel_count
        ).astype(low)

    proj_upstream = gelu_back(stats_proj[0], cot_rows * valid_mask)
    proj_sums = links.sums(back_sums(proj_upstream, stats_proj[1]), "back_proj")
    proj_low = finish(proj_upstream, stats_proj, gain_proj, proj_sums)
    joined_grad = lax.dot_general(
        proj_low, proj_local, (((1,), (1,)), ((), ())), preferred_element_type=wide
    )
    proj_term = lax.dot_general(
        joined, proj_low, (((0,), (0,)), ((), ())), preferred_element_type=wide
    )
    both_upstream = gelu_back(stats_both[0], joined_grad[:, : 4 * head_width] * valid_mask)
    pool_total = jnp.sum(joined_grad[:, 4 * head_width :] * valid_mask, axis=0)
    both_sums = links.sums(back_sums(both_upstream, stats_both[1]) + [pool_total], "back_both")
    pool_grad = gelu_back(pooled, both_sums[2][None]).astype(low)
    both_grad = finish(both_upstream, stats_both, gain_both, both_sums)
    proj_grad = lax.psum(proj_term, "space")

    both_all = links.gather(both_grad, "gather_both").reshape(
        rows_count, cols_count, 4 * head_width
    )
    turned = shared_slice.T

    def shared_back(first, last, grad_rows, weights):
        flat = grad_rows.reshape(-1, head_width)
        part = lax.dot_general(
            flat, weights, (((1,), (1,)), ((), ())), preferred_element_type=wide
        ).reshape(last - first, cols_count, slice_width)
        grad = jnp.dot(
            turned[:, first * cols_count : last * cols_count], flat, preferred_element_type=wide
        )
        return jnp.pad(part, ((first, rows_count - last), (0, 0), (0, 0))), grad

    slice_grad, one_grad = shared_back(
        0, rows_count, both_all[:, :, :head_width], branch_local[:, :head_width]
    )
    rate_grads = {}
    for level, row_tap, col_tap, down, right in taps:
        image = both_all[:, :, level * head_width : (level + 1) * head_width]
        first, last = max(0, down), rows_count - max(0, -down)
        window = shift_columns(image[first - down : last - down], -right)
        part, grad = shared_back(
            first, last, window, rate_local[:, rate_columns(level, row_tap, col_tap)]
        )
        slice_grad = slice_grad + part
        rate_grads[level, row_tap, col_tap] = grad
    nothing = jnp.zeros((slice_width, head_width), wide)
    rate_grad = jnp.concatenate(
        [
            rate_grads.get((level, row_tap, col_tap), nothing)
            for level in (1, 2, 3)
            for row_tap in range(3)
            for col_tap in range(3)
        ],
        axis=1,
    )
    pool_weight_grad = pixel_sum[:, None] * pool_grad.astype(wide) / pixel_count
    branch_grad = jnp.concatenate([one_grad, pool_weight_grad], axis=1)
    pool_part = lax.dot_general(
        pool_grad,
        branch_local[:, head_width:],
        (((1,), (1,)), ((), ())),
        preferred_element_type=wide,
    )
    shared_grad = (
        slice_grad.reshape(all_pixels, slice_width) + all_mask * pool_part / pixel_count
    ).astype(low)

    all_grads = links.over_tasks(shared_grad, "tasks_grads")
    flat_grads = all_grads.reshape(tasks, -1)
    gram_part = lax.dot_general(
        flat_grads, flat_grads, (((1,), (1,)), ((), ())), preferred_element_type=wide
    )
    gram_matrix = links.sums([gram_part], "sums_gram")[0]
    task_weight = imtl_weights(gram_matrix)
    mixed_grad = task_weight[0] * all_grads[0].astype(wide)
    for task_index in range(1, tasks):
        mixed_grad = mixed_grad + task_weight[task_index] * all_grads[task_index].astype(wide)
    combined = (
        links.swap(mixed_grad.astype(low).reshape(bands, pixels, slice_width), "swap_combined")
        .transpose(1, 0, 2)
        .reshape(pixels, in_width)
    )

    gate_grad = gelu_back(before_act, combined.astype(wide) * valid_mask)
    sums_three = links.sums(back_sums(gate_grad, stats_three[1]), "back_three")
    low_three = finish(gate_grad, stats_three, gains[2], sums_three)
    active_grad_two = lax.dot_general(
        low_three, w_expand, (((1,), (1,)), ((), ())), preferred_element_type=wide
    )
    upstream_two = gelu_back(stats_two[0], active_grad_two * valid_mask)
    sums_two = links.sums(back_sums(upstream_two, stats_two[1]), "back_two")
    low_two = finish(upstream_two, stats_two, gains[1], sums_two)
    back_patches = trunk_taps(
        band_rim(low_two.reshape(band_rows, cols_count, middle_width)),
        CONV_DILATION,
        band_rows,
        cols_count,
        True,
    )
    active_grad_one = jnp.einsum("pto,ito->pi", back_patches, w_dilated, preferred_element_type=wide)
    upstream_one = gelu_back(stats_one[0], active_grad_one * valid_mask)
    sums_one = links.sums(back_sums(upstream_one, stats_one[1]), "back_one")
    low_one = finish(upstream_one, stats_one, gains[0], sums_one)
    input_grad = (
        lax.dot_general(low_one, w_reduce, (((1,), (1,)), ((), ())), preferred_element_type=wide)
        + gate_grad
    ).astype(low)

    def share(low_grad):
        width = low_grad.shape[1] // tasks
        return lax.dynamic_slice_in_dim(low_grad, task * width, width, axis=1)

    def against(left_side, right_side):
        return lax.dot_general(
            left_side, right_side, (((0,), (0,)), ((), ())), preferred_element_type=wide
        ).astype(low)

    narrow = middle_width // tasks
    wide_share = in_width // tasks
    expand_term = against(active_two, share(low_three)).reshape(bands, -1, narrow)
    reduce_term = against(inputs, share(low_one)).reshape(bands, -1, narrow)
    dilated_term = against(
        patches.transpose(0, 2, 1).reshape(pixels, -1), share(low_two)
    ).reshape(bands, -1, narrow)
    terms = jnp.concatenate([expand_term, reduce_term, dilated_term], axis=1)
    shares = links.over_tasks(
        links.scatter(terms, "scatter_trunk").astype(low), "tasks_trunk"
    ).astype(wide)
    cut_one = expand_term.shape[1]
    cut_two = cut_one + reduce_term.shape[1]
    w_expand_grad = (
        shares[:, :cut_one].reshape(tasks, -1, wide_share).transpose(1, 0, 2).reshape(-1, in_width)
    )
    w_reduce_grad = shares[:, cut_one:cut_two].transpose(1, 0, 2).reshape(-1, middle_width)
    w_dilated_grad = (
        shares[:, cut_two:].transpose(1, 0, 2).reshape(-1, 9, middle_width)
    )
    means = jnp.concatenate([stats_one[3], stats_two[3], stats_three[3]])
    variances = (
        jnp.concatenate([stats_one[4], stats_two[4], stats_three[4]])
        * pixel_count
        / (pixel_count - 1.0)
    )
    return (
        head_result.reshape(1, band_rows, cols_count, head_width),
        input_grad.reshape(band_rows, cols_count, in_width),
        w_reduce_grad,
        w_dilated_grad,
        w_expand_grad,
        jnp.concatenate([sums_one[1], sums_two[1], sums_three[1]]),
        jnp.concatenate([sums_one[0], sums_two[0], sums_three[0]]),
        jnp.stack([means, variances]),
        branch_grad[None],
        rate_grad[None],
        proj_grad[None],
        jnp.concatenate([both_sums[1], proj_sums[1]])[None],
        jnp.concatenate([both_sums[0], proj_sums[0]])[None],
        task_weight,
    )


def solution(mesh):
    body = per_device_slices if mesh.shape["space"] == 8 else per_device
    return jax.shard_map(
        body,
        mesh=mesh,
        in_specs=(
            P("space", None, None),
            P(),
            P(),
            P(),
            P(),
            P(),
            P(),
            P("task", "space", None),
            P("task", "space", None),
            P("task", None, None),
            P("task", None),
            P("task", None),
            P("task", "space", None, None),
        ),
        out_specs=(
            P("task", "space", None, None),
            P("space", None, None),
            P("space", None),
            P("space", None, None),
            P("space", None),
            P(),
            P(),
            P(),
            P("task", "space", None),
            P("task", "space", None),
            P("task", None, None),
            P("task", None),
            P("task", None),
            P(),
        ),
        check_vma=False,
    )
```

```python
import functools

import jax
import jax.numpy as jnp
from jax import lax
from jax.experimental import pallas as pl
from jax.experimental.pallas import tpu as pltpu
from jax.sharding import PartitionSpec as P

CONV_DILATION = 2
RATE = 12


NORM_EPS = 1e-05
GRAM_EPS = 1e-06
PRECISE = lax.Precision.HIGHEST


def with_halo(block, sides, width):
    for axis, dim in sides:
        count = lax.axis_size(axis)
        forward = [(i, i + 1) for i in range(count - 1)]
        backward = [(target, source) for source, target in forward]
        low = lax.ppermute(
            lax.slice_in_dim(block, block.shape[dim] - width, None, axis=dim), axis, forward
        )
        high = lax.ppermute(lax.slice_in_dim(block, 0, width, axis=dim), axis, backward)
        block = jnp.concatenate([low, block, high], axis=dim)
    return block


def from_behind(shard, axis, by):
    count = lax.axis_size(axis)
    pairs = [(i, i + by) for i in range(count) if 0 <= i + by < count]
    return lax.ppermute(shard, axis, pairs)


def small_solve(matrix, target):
    size_n = matrix.shape[0]
    rows_list = [matrix[number] for number in range(size_n)]
    values = [target[number] for number in range(size_n)]
    for pivot_row in range(size_n):
        for lower_row in range(pivot_row + 1, size_n):
            factor = rows_list[lower_row][pivot_row] / rows_list[pivot_row][pivot_row]
            rows_list[lower_row] = rows_list[lower_row] - factor * rows_list[pivot_row]
            values[lower_row] = values[lower_row] - factor * values[pivot_row]
    answer = [None] * size_n
    for pivot_row in reversed(range(size_n)):
        running = values[pivot_row]
        for later_row in range(pivot_row + 1, size_n):
            running = running - rows_list[pivot_row][later_row] * answer[later_row]
        answer[pivot_row] = running / rows_list[pivot_row][pivot_row]
    return jnp.stack(answer)


def imtl_weights(gram_matrix):
    grad_norms = jnp.sqrt(jnp.diagonal(gram_matrix) + GRAM_EPS)
    projections = gram_matrix / grad_norms[None, :]
    system = projections[0, 0] - projections[0:1, 1:] - projections[1:, 0:1] + projections[1:, 1:]
    target = projections[0, 0] - projections[0, 1:]
    other_weights = small_solve(jnp.transpose(system), target)
    return jnp.concatenate([(1.0 - jnp.sum(other_weights))[None], other_weights])


def gelu_back(value, upstream):
    return jax.vjp(jax.nn.gelu, value)[1](upstream)[0]


def channel_sums(members):
    return lax.psum(members, "space")


def norm_values(hidden, first_total, second_total, gain_vec, shift_vec, pixel_count):
    mean_value = first_total / pixel_count
    variance = second_total / pixel_count - mean_value * mean_value
    inv_std = lax.rsqrt(variance + NORM_EPS)
    scaled = (hidden - mean_value) * inv_std
    return (gain_vec * scaled + shift_vec, scaled, inv_std, mean_value, variance)


def norm_forward(hidden, gain_vec, shift_vec, valid_mask, pixel_count):
    totals = channel_sums(
        (jnp.sum(hidden * valid_mask, axis=0), jnp.sum(hidden * hidden * valid_mask, axis=0))
    )
    return norm_values(hidden, totals[0], totals[1], gain_vec, shift_vec, pixel_count)


def norm_finish(
    upstream, scaled, inv_std, gain_vec, gain_grad, shift_grad, valid_mask, pixel_count
):
    return (
        valid_mask
        * gain_vec
        * inv_std
        * (upstream - shift_grad / pixel_count - scaled * gain_grad / pixel_count)
    )


def norm_backward(upstream, scaled, inv_std, gain_vec, valid_mask, pixel_count):
    totals = channel_sums(
        (jnp.sum(upstream * valid_mask, axis=0), jnp.sum(upstream * scaled * valid_mask, axis=0))
    )
    hidden_grad = norm_finish(
        upstream, scaled, inv_std, gain_vec, totals[1], totals[0], valid_mask, pixel_count
    )
    return (hidden_grad, totals[1], totals[0])


def band_rim(strip_image):
    return with_halo(strip_image, (("space", 0),), CONV_DILATION)


def far_rows(strip_image, bands_away, upward):
    if bands_away >= lax.axis_size("space"):
        return jnp.zeros_like(strip_image)
    if upward:
        return from_behind(strip_image, "space", bands_away)
    return from_behind(strip_image, "space", -bands_away)


def trunk_taps(padded, reach_cells, rows_count, cols_count, flipped):
    col_padded = jnp.pad(padded, ((0, 0), (reach_cells, reach_cells), (0, 0)))
    pieces = []
    for row_tap in range(3):
        for col_tap in range(3):
            row_from = (2 - row_tap) * reach_cells if flipped else row_tap * reach_cells
            col_from = (2 - col_tap) * reach_cells if flipped else col_tap * reach_cells
            pieces.append(
                col_padded[
                    row_from : row_from + rows_count, col_from : col_from + cols_count
                ].reshape(rows_count * cols_count, -1)
            )
    return jnp.stack(pieces, axis=1)


def per_device(
    features,
    row_width,
    w_reduce,
    w_dilated,
    w_expand,
    trunk_gain,
    trunk_shift,
    branch_weight,
    rate_weight,
    proj_weight,
    head_gain,
    head_shift,
    head_cot,
):
    band_rows, cols_count, in_width = features.shape
    pixels = band_rows * cols_count
    middle_width = w_reduce.shape[1]
    head_width = proj_weight.shape[2]
    first_row = lax.axis_index("space") * band_rows
    widths = lax.dynamic_slice_in_dim(row_width, first_row, band_rows)
    valid_mask = (
        (jnp.arange(cols_count)[None, :] < widths[:, None]).astype(jnp.float32).reshape(pixels, 1)
    )
    pixel_count = jnp.sum(row_width).astype(jnp.float32)
    inputs = features.reshape(pixels, in_width)
    gain_one, shift_one = (trunk_gain[:middle_width], trunk_shift[:middle_width])
    gain_two, shift_two = (
        trunk_gain[middle_width : 2 * middle_width],
        trunk_shift[middle_width : 2 * middle_width],
    )
    gain_three, shift_three = (trunk_gain[2 * middle_width :], trunk_shift[2 * middle_width :])
    hidden_one = jnp.dot(inputs, w_reduce, preferred_element_type=jnp.float32)
    stats_one = norm_forward(hidden_one, gain_one, shift_one, valid_mask, pixel_count)
    first_active = (jax.nn.gelu(stats_one[0]) * valid_mask).astype(jnp.bfloat16)
    patches = trunk_taps(
        band_rim(first_active.reshape(band_rows, cols_count, middle_width)),
        CONV_DILATION,
        band_rows,
        cols_count,
        False,
    )
    hidden_two = jnp.einsum("pti,ito->po", patches, w_dilated, preferred_element_type=jnp.float32)
    stats_two = norm_forward(hidden_two, gain_two, shift_two, valid_mask, pixel_count)
    active_two = (jax.nn.gelu(stats_two[0]) * valid_mask).astype(jnp.bfloat16)
    hidden_three = jnp.dot(active_two, w_expand, preferred_element_type=jnp.float32)
    stats_three = norm_forward(hidden_three, gain_three, shift_three, valid_mask, pixel_count)
    before_act = stats_three[0] + inputs.astype(jnp.float32)
    shared = (jax.nn.gelu(before_act) * valid_mask).astype(jnp.bfloat16)
    proj_local = proj_weight[0]
    gain_local = head_gain[0]
    shift_local = head_shift[0]
    joined_weight = jnp.concatenate([branch_weight[0], rate_weight[0]], axis=1)
    pixel_sum = jnp.dot(
        valid_mask.reshape(1, pixels).astype(jnp.bfloat16),
        shared,
        preferred_element_type=jnp.float32,
    )[0]
    shared_image = shared.reshape(band_rows, cols_count, in_width)
    padded_sources = []
    for level in (1, 2, 3):
        reach = level * RATE
        bands_away = reach // band_rows
        triple = (
            far_rows(shared_image, bands_away, True),
            shared_image,
            far_rows(shared_image, bands_away, False),
        )
        padded_sources.append(
            [jnp.pad(source, ((0, 0), (reach, reach), (0, 0))) for source in triple]
        )
    zero_rows = jnp.zeros((pixels, head_width), jnp.float32)
    start_totals = (
        zero_rows,
        jnp.zeros((1, head_width), jnp.float32),
        zero_rows,
        zero_rows,
        zero_rows,
    )
    all_weights = lax.all_gather(joined_weight, "space", axis=0, tiled=True)
    width_now = all_weights.shape[0]
    one_acc = jnp.dot(shared, all_weights[:, :head_width], preferred_element_type=jnp.float32)
    pool_cols = pixel_sum[None]
    pool_acc = jnp.dot(
        pool_cols,
        all_weights[:, head_width : 2 * head_width].astype(jnp.float32),
        precision=PRECISE,
        preferred_element_type=jnp.float32,
    )
    rate_accs = []
    for fold_level_index in range(3):
        fold_reach = (fold_level_index + 1) * RATE
        running = start_totals[2 + fold_level_index]
        for fold_row_tap in range(3):
            fold_source = padded_sources[fold_level_index][fold_row_tap]
            for fold_col_tap in range(3):
                window = fold_source[
                    :, fold_col_tap * fold_reach : fold_col_tap * fold_reach + cols_count
                ].reshape(pixels, width_now)
                column = (2 + 9 * fold_level_index + 3 * fold_row_tap + fold_col_tap) * head_width
                running = running + jnp.dot(
                    window,
                    all_weights[:, column : column + head_width],
                    preferred_element_type=jnp.float32,
                )
        rate_accs.append(running)
    pre_both = jnp.concatenate([one_acc, rate_accs[0], rate_accs[1], rate_accs[2]], axis=1)
    gain_both, shift_both = (gain_local[: 4 * head_width], shift_local[: 4 * head_width])
    totals = channel_sums(
        (
            jnp.sum(pre_both * valid_mask, axis=0),
            jnp.sum(pre_both * pre_both * valid_mask, axis=0),
            pool_acc[0],
        )
    )
    stats_both = norm_values(pre_both, totals[0], totals[1], gain_both, shift_both, pixel_count)
    pooled = totals[2][None] / pixel_count
    active_both = (jax.nn.gelu(stats_both[0]) * valid_mask).astype(jnp.bfloat16)
    active_pool = jax.nn.gelu(pooled).astype(jnp.bfloat16)
    joined = jnp.concatenate(
        [active_both, (active_pool.astype(jnp.float32) * valid_mask).astype(jnp.bfloat16)], axis=1
    )
    projected = jnp.dot(joined, proj_local, preferred_element_type=jnp.float32)
    gain_proj = gain_local[4 * head_width :]
    stats_proj = norm_forward(
        projected, gain_proj, shift_local[4 * head_width :], valid_mask, pixel_count
    )
    head_result = (jax.nn.gelu(stats_proj[0]) * valid_mask).astype(jnp.bfloat16)
    cot_rows = head_cot[0].reshape(pixels, head_width).astype(jnp.float32)
    proj_upstream = gelu_back(stats_proj[0], cot_rows * valid_mask)
    proj_hidden, proj_gain_grad, proj_shift_grad = norm_backward(
        proj_upstream, stats_proj[1], stats_proj[2], gain_proj, valid_mask, pixel_count
    )
    proj_low = proj_hidden.astype(jnp.bfloat16)
    joined_grad = lax.dot_general(
        proj_low, proj_local, (((1,), (1,)), ((), ())), preferred_element_type=jnp.float32
    )
    proj_term = lax.dot_general(
        joined, proj_low, (((0,), (0,)), ((), ())), preferred_element_type=jnp.float32
    )
    both_upstream = gelu_back(stats_both[0], joined_grad[:, : 4 * head_width] * valid_mask)
    pool_total = jnp.sum(joined_grad[:, 4 * head_width :] * valid_mask, axis=0)
    back_totals = channel_sums(
        (
            proj_term,
            pool_total,
            jnp.sum(both_upstream * valid_mask, axis=0),
            jnp.sum(both_upstream * stats_both[1] * valid_mask, axis=0),
        )
    )
    pool_grad = gelu_back(pooled, back_totals[1][None]).astype(jnp.bfloat16)
    both_grad = norm_finish(
        both_upstream,
        stats_both[1],
        stats_both[2],
        gain_both,
        back_totals[3],
        back_totals[2],
        valid_mask,
        pixel_count,
    ).astype(jnp.bfloat16)
    tap_grads = []
    for level_index in range(3):
        reach = (level_index + 1) * RATE
        bands_away = reach // band_rows
        rate_image = both_grad[
            :, (1 + level_index) * head_width : (2 + level_index) * head_width
        ].reshape(band_rows, cols_count, head_width)
        back_sources = [
            jnp.pad(source, ((0, 0), (reach, reach), (0, 0)))
            for source in (
                far_rows(rate_image, bands_away, False),
                rate_image,
                far_rows(rate_image, bands_away, True),
            )
        ]
        for row_tap in range(3):
            for col_tap in range(3):
                tap_grads.append(
                    back_sources[row_tap][
                        :, (2 - col_tap) * reach : (2 - col_tap) * reach + cols_count
                    ].reshape(pixels, head_width)
                )
    right_side = jnp.concatenate([both_grad[:, :head_width]] + tap_grads, axis=1)
    used_rows = jnp.concatenate(
        [all_weights[:, :head_width], all_weights[:, 2 * head_width :]], axis=1
    )
    main_part = lax.dot_general(
        right_side, used_rows, (((1,), (1,)), ((), ())), preferred_element_type=jnp.float32
    )
    pool_part = lax.dot_general(
        pool_grad,
        all_weights[:, head_width : 2 * head_width],
        (((1,), (1,)), ((), ())),
        preferred_element_type=jnp.float32,
    )
    shared_grad = (main_part + valid_mask * pool_part / pixel_count).astype(jnp.bfloat16)
    head_term = lax.dot_general(
        shared, right_side, (((0,), (0,)), ((), ())), preferred_element_type=jnp.float32
    )
    pool_term = pixel_sum[:, None] * pool_grad.astype(jnp.float32) / pixel_count
    head_term = jnp.concatenate(
        [head_term[:, :head_width], pool_term, head_term[:, head_width:]], axis=1
    )
    all_grads = lax.all_gather(shared_grad[None], "task", axis=0, tiled=True)
    flat_grads = all_grads.reshape(all_grads.shape[0], -1)
    gram_matrix = lax.psum(
        lax.dot_general(
            flat_grads, flat_grads, (((1,), (1,)), ((), ())), preferred_element_type=jnp.float32
        ),
        "space",
    )
    task_weight = imtl_weights(gram_matrix)
    mixed_grad = task_weight[0] * all_grads[0].astype(jnp.float32)
    for task_index in range(1, all_grads.shape[0]):
        mixed_grad = mixed_grad + task_weight[task_index] * all_grads[task_index].astype(
            jnp.float32
        )
    combined = mixed_grad.astype(jnp.bfloat16)
    gate_grad = gelu_back(before_act, combined.astype(jnp.float32) * valid_mask)
    hidden_grad_three, gain_grad_three, shift_grad_three = norm_backward(
        gate_grad, stats_three[1], stats_three[2], gain_three, valid_mask, pixel_count
    )
    low_three = hidden_grad_three.astype(jnp.bfloat16)
    expand_term = lax.dot_general(
        active_two, low_three, (((0,), (0,)), ((), ())), preferred_element_type=jnp.float32
    )
    active_grad_two = lax.dot_general(
        low_three, w_expand, (((1,), (1,)), ((), ())), preferred_element_type=jnp.float32
    )
    upstream_two = gelu_back(stats_two[0], active_grad_two * valid_mask)
    hidden_grad_two, gain_grad_two, shift_grad_two = norm_backward(
        upstream_two, stats_two[1], stats_two[2], gain_two, valid_mask, pixel_count
    )
    low_two = hidden_grad_two.astype(jnp.bfloat16)
    dilated_term = jnp.einsum("pti,po->ito", patches, low_two, preferred_element_type=jnp.float32)
    back_patches = trunk_taps(
        band_rim(low_two.reshape(band_rows, cols_count, middle_width)),
        CONV_DILATION,
        band_rows,
        cols_count,
        True,
    )
    active_grad_one = jnp.einsum(
        "pto,ito->pi", back_patches, w_dilated, preferred_element_type=jnp.float32
    )
    upstream_one = gelu_back(stats_one[0], active_grad_one * valid_mask)
    hidden_grad_one, gain_grad_one, shift_grad_one = norm_backward(
        upstream_one, stats_one[1], stats_one[2], gain_one, valid_mask, pixel_count
    )
    low_one = hidden_grad_one.astype(jnp.bfloat16)
    reduce_term = lax.dot_general(
        inputs, low_one, (((0,), (0,)), ((), ())), preferred_element_type=jnp.float32
    )
    input_grad = (
        lax.dot_general(
            low_one, w_reduce, (((1,), (1,)), ((), ())), preferred_element_type=jnp.float32
        )
        + gate_grad
    )
    reduced = (
        lax.psum_scatter(head_term, "space", scatter_dimension=0, tiled=True),
        lax.psum_scatter(reduce_term, "space", scatter_dimension=0, tiled=True),
        lax.psum_scatter(dilated_term, "space", scatter_dimension=0, tiled=True),
        lax.psum_scatter(expand_term, "space", scatter_dimension=0, tiled=True),
    )
    means = jnp.concatenate([stats_one[3], stats_two[3], stats_three[3]])
    variances = (
        jnp.concatenate([stats_one[4], stats_two[4], stats_three[4]])
        * pixel_count
        / (pixel_count - 1.0)
    )
    batch_stats = jnp.stack([means, variances])
    head_gain_grad = jnp.concatenate([back_totals[3], proj_gain_grad])[None]
    head_shift_grad = jnp.concatenate([back_totals[2], proj_shift_grad])[None]
    return (
        head_result.reshape(1, band_rows, cols_count, head_width),
        input_grad.reshape(band_rows, cols_count, in_width).astype(jnp.bfloat16),
        reduced[1],
        reduced[2],
        reduced[3],
        jnp.concatenate([gain_grad_one, gain_grad_two, gain_grad_three]),
        jnp.concatenate([shift_grad_one, shift_grad_two, shift_grad_three]),
        batch_stats,
        reduced[0][:, : 2 * head_width][None],
        reduced[0][:, 2 * head_width :][None],
        back_totals[0][None],
        head_gain_grad,
        head_shift_grad,
        task_weight,
    )


MESH_ID = pl.DeviceIdType.MESH
LANE = 128


def meet_bands(place, count):
    barrier = pltpu.get_barrier_semaphore()
    for step in range(1, count):
        pl.semaphore_signal(
            barrier,
            inc=1,
            device_id={"space": lax.rem(place + step, count)},
            device_id_type=MESH_ID,
        )
    pl.semaphore_wait(barrier, count - 1)


def sum_kernel(count, own_ref, out_ref, landing, send_sem, recv_sem):
    place = lax.axis_index("space")
    meet_bands(place, count)
    copies = []
    for step in range(1, count):
        copy = pltpu.make_async_remote_copy(
            own_ref,
            landing.at[step],
            send_sem.at[step],
            recv_sem.at[step],
            device_id={"space": lax.rem(place + step, count)},
            device_id_type=MESH_ID,
        )
        copy.start()
        copies.append(copy)
    total = own_ref[...]
    for step in range(1, count):
        copies[step - 1].wait_recv()
        total = total + landing[step]
    out_ref[...] = total
    for copy in copies:
        copy.wait_send()


def gather_kernel(count, own_ref, out_ref, send_sem, recv_sem, local_sem):
    place = lax.axis_index("space")
    chips = count // 2
    chip = place // 2
    core = lax.rem(place, 2)
    twin = chip * 2 + 1 - core
    meet_bands(place, count)
    copies = []
    for step in range(1, chips):
        copy = pltpu.make_async_remote_copy(
            own_ref,
            out_ref.at[place],
            send_sem.at[step],
            recv_sem.at[step],
            device_id={"space": lax.rem(chip + step, chips) * 2 + core},
            device_id_type=MESH_ID,
        )
        copy.start()
        copies.append(copy)
    to_twin = pltpu.make_async_remote_copy(
        own_ref,
        out_ref.at[place],
        send_sem.at[0],
        recv_sem.at[0],
        device_id={"space": twin},
        device_id_type=MESH_ID,
    )
    to_twin.start()
    here = pltpu.make_async_copy(own_ref, out_ref.at[place], local_sem)
    here.start()
    passed = []
    for step in range(1, chips):
        copies[step - 1].wait_recv()
        source = lax.rem(chip + chips - step, chips) * 2 + core
        copy = pltpu.make_async_remote_copy(
            out_ref.at[source],
            out_ref.at[source],
            send_sem.at[chips - 1 + step],
            recv_sem.at[chips - 1 + step],
            device_id={"space": twin},
            device_id_type=MESH_ID,
        )
        copy.start()
        passed.append(copy)
    to_twin.wait()
    for copy in passed:
        copy.wait()
    for copy in copies:
        copy.wait_send()
    here.wait()


def swap_kernel(count, own_ref, out_ref, send_sem, recv_sem, local_sem):
    place = lax.axis_index("space")
    meet_bands(place, count)
    copies = []
    for step in range(1, count):
        target = lax.rem(place + step, count)
        copy = pltpu.make_async_remote_copy(
            own_ref.at[target],
            out_ref.at[place],
            send_sem.at[step],
            recv_sem.at[step],
            device_id={"space": target},
            device_id_type=MESH_ID,
        )
        copy.start()
        copies.append(copy)
    here = pltpu.make_async_copy(own_ref.at[place], out_ref.at[place], local_sem)
    here.start()
    for copy in copies:
        copy.wait()
    here.wait()


def scatter_kernel(count, own_ref, out_ref, twin_land, paired, landing, send_sem, recv_sem):
    place = lax.axis_index("space")
    chips = count // 2
    chip = place // 2
    core = lax.rem(place, 2)
    twin = chip * 2 + 1 - core
    meet_bands(place, count)
    from_twin = []
    for step in range(chips):
        other = lax.rem(chip + step, chips)
        copy = pltpu.make_async_remote_copy(
            own_ref.at[other * 2 + 1 - core],
            twin_land.at[step],
            send_sem.at[step],
            recv_sem.at[step],
            device_id={"space": twin},
            device_id_type=MESH_ID,
        )
        from_twin.append(copy)
    order = list(range(1, chips)) + [0]
    for step in order:
        from_twin[step].start()
    sent = []
    for step in order:
        from_twin[step].wait_recv()
        other = lax.rem(chip + step, chips)
        pair = own_ref[other * 2 + core].astype(jnp.float32) + twin_land[step].astype(jnp.float32)
        if step == 0:
            out_ref[...] = pair
            continue
        paired[step] = pair.astype(paired.dtype)
        copy = pltpu.make_async_remote_copy(
            paired.at[step],
            landing.at[step],
            send_sem.at[chips + step],
            recv_sem.at[chips + step],
            device_id={"space": other * 2 + core},
            device_id_type=MESH_ID,
        )
        copy.start()
        sent.append(copy)
    for step in range(1, chips):
        sent[step - 1].wait_recv()
        out_ref[...] += landing[step].astype(jnp.float32)
    for copy in sent:
        copy.wait_send()
    for copy in from_twin:
        copy.wait_send()


def tasks_kernel(count, own_ref, out_ref, send_sem, recv_sem, local_sem):
    place = lax.axis_index("task")
    barrier = pltpu.get_barrier_semaphore()
    for step in range(1, count):
        pl.semaphore_signal(
            barrier,
            inc=1,
            device_id={"task": lax.rem(place + step, count)},
            device_id_type=MESH_ID,
        )
    pl.semaphore_wait(barrier, count - 1)
    copies = []
    for step in range(1, count):
        copy = pltpu.make_async_remote_copy(
            own_ref,
            out_ref.at[place],
            send_sem.at[step],
            recv_sem.at[step],
            device_id={"task": lax.rem(place + step, count)},
            device_id_type=MESH_ID,
        )
        copy.start()
        copies.append(copy)
    here = pltpu.make_async_copy(own_ref, out_ref.at[place], local_sem)
    here.start()
    for copy in copies:
        copy.wait()
    here.wait()


class Links:
    def __init__(self):
        self.bands = lax.axis_size("space")
        self.tasks = lax.axis_size("task")
        self.used = 0

    def call(self, kernel, out, scratch, operand, label):
        self.used += 1
        in_vmem = pl.BlockSpec(memory_space=pltpu.VMEM)
        return pl.pallas_call(
            kernel,
            name=label,
            out_shape=out,
            in_specs=[in_vmem],
            out_specs=in_vmem,
            scratch_shapes=scratch,
            compiler_params=pltpu.CompilerParams(
                collective_id=self.used - 1, has_side_effects=True, vmem_limit_bytes=48 << 20
            ),
        )(operand)

    def sums(self, members, label):
        sizes = [member.size for member in members]
        flat = jnp.concatenate([member.reshape(-1) for member in members])
        tile = 8 * LANE
        padded = -(-flat.size // tile) * tile
        block = jnp.pad(flat, (0, padded - flat.size)).reshape(-1, LANE)
        sems = pltpu.SemaphoreType.DMA((self.bands,))
        total = self.call(
            functools.partial(sum_kernel, self.bands),
            jax.ShapeDtypeStruct(block.shape, block.dtype),
            [pltpu.VMEM((self.bands,) + block.shape, block.dtype), sems, sems],
            block,
            label,
        ).reshape(-1)
        out = []
        start = 0
        for member, size in zip(members, sizes):
            out.append(total[start : start + size].reshape(member.shape))
            start += size
        return out

    def gather(self, block, label):
        sems = pltpu.SemaphoreType.DMA((self.bands,))
        return self.call(
            functools.partial(gather_kernel, self.bands),
            jax.ShapeDtypeStruct((self.bands,) + block.shape, block.dtype),
            [sems, sems, pltpu.SemaphoreType.DMA],
            block,
            label,
        )

    def swap(self, blocks, label):
        sems = pltpu.SemaphoreType.DMA((self.bands,))
        return self.call(
            functools.partial(swap_kernel, self.bands),
            jax.ShapeDtypeStruct(blocks.shape, blocks.dtype),
            [sems, sems, pltpu.SemaphoreType.DMA],
            blocks,
            label,
        )

    def scatter(self, blocks, label):
        sems = pltpu.SemaphoreType.DMA((self.bands,))
        half = (self.bands // 2,) + blocks.shape[1:]
        return self.call(
            functools.partial(scatter_kernel, self.bands),
            jax.ShapeDtypeStruct(blocks.shape[1:], jnp.float32),
            [pltpu.VMEM(half, blocks.dtype)] * 3 + [sems, sems],
            blocks,
            label,
        )

    def over_tasks(self, block, label):
        sems = pltpu.SemaphoreType.DMA((self.tasks,))
        return self.call(
            functools.partial(tasks_kernel, self.tasks),
            jax.ShapeDtypeStruct((self.tasks,) + block.shape, block.dtype),
            [sems, sems, pltpu.SemaphoreType.DMA],
            block,
            label,
        )


GELU_A = 0.7978845608028654
GELU_B = 0.044715


def gelu_of(value):
    return 0.5 * value * (1.0 + jnp.tanh(GELU_A * (value + GELU_B * value * value * value)))


def gelu_slope(value):
    square = value * value
    bend = jnp.tanh(GELU_A * value * (1.0 + GELU_B * square))
    return 0.5 * (1.0 + bend) + 0.5 * value * (1.0 - bend * bend) * (
        GELU_A * (1.0 + 3.0 * GELU_B * square)
    )


def dot_nn(left_side, right_side):
    return jnp.dot(left_side, right_side, preferred_element_type=jnp.float32)


def dot_nt(left_side, right_side):
    return lax.dot_general(
        left_side, right_side, (((1,), (1,)), ((), ())), preferred_element_type=jnp.float32
    )


def shift_pixels(value, by, cols):
    if by == 0:
        return value
    rows = value.shape[0]
    column = lax.rem(lax.broadcasted_iota(jnp.int32, value.shape, 0), cols) + by
    rolled = pltpu.roll(value, (-by) % rows, 0)
    return jnp.where((column >= 0) & (column < cols), rolled, 0.0)


class Post:
    def __init__(self, send_sem, recv_sem):
        self.send_sem, self.recv_sem = send_sem, recv_sem
        self.used = 0
        self.sent = []

    def copy(self, source, target, device):
        made = pltpu.make_async_remote_copy(
            source,
            target,
            self.send_sem.at[self.used],
            self.recv_sem.at[self.used],
            device_id=device,
            device_id_type=MESH_ID,
        )
        self.used += 1
        return made

    def push(self, source, target, device):
        made = self.copy(source, target, device)
        made.start()
        self.sent.append(made)
        return made

    def close(self):
        for made in self.sent:
            made.wait_send()


class Place:
    def __init__(self, tasks, bands):
        self.tasks, self.bands, self.chips = tasks, bands, bands // 2
        self.task = lax.axis_index("task")
        self.band = lax.axis_index("space")
        self.chip = self.band // 2
        self.core = lax.rem(self.band, 2)
        self.twin = {"space": self.chip * 2 + 1 - self.core}
        low, high = lax.rem(self.task, 2), self.task // 2
        self.other_tasks = [(1 - high) * 2 + 1 - low, high * 2 + 1 - low, (1 - high) * 2 + low]
        self.other_bands = [lax.rem(self.band + step, bands) for step in range(1, bands)]

    def meet(self, with_tasks, with_bands):
        barrier = pltpu.get_barrier_semaphore()
        greeted = []
        if with_tasks:
            greeted += [{"task": task} for task in self.other_tasks]
        if with_bands:
            greeted += [{"space": band} for band in self.other_bands]
        for device in greeted:
            pl.semaphore_signal(barrier, inc=1, device_id=device, device_id_type=MESH_ID)
        pl.semaphore_wait(barrier, len(greeted))

    def sum_over(self, post, axis, own_ref, land_ref):
        mine = self.task if axis == "task" else self.band
        others = self.other_tasks if axis == "task" else self.other_bands
        copies = [post.push(own_ref, land_ref.at[mine], {axis: other}) for other in others]
        land_ref[pl.ds(mine, 1)] = own_ref[...][None]
        for made in copies:
            made.wait_recv()
        total = land_ref[0]
        for slot in range(1, len(others) + 1):
            total = total + land_ref[slot]
        return total


def trunk_back_kernel(
    sizes,
    sg_ref,
    h3_ref,
    x_ref,
    v3_ref,
    h2_ref,
    v2_ref,
    h1_ref,
    v1_ref,
    a1_ref,
    a2_ref,
    mask_ref,
    inv_ref,
    we_hbm,
    wd_hbm,
    wr_hbm,
    pt_ref,
    tw_out,
    ig_out,
    rg_out,
    dg_out,
    eg_out,
    s3_out,
    s2_out,
    s1_out,
    pg_out,
    we,
    wd,
    wr,
    h3q,
    xq,
    xg,
    gram_own,
    gram_land,
    gram_mid,
    gram_land_b,
    comb,
    comb_land,
    gate,
    scaled,
    gate_low,
    gate_band,
    st3,
    st3_land,
    st3_mid,
    st3_land_b,
    l3,
    l3x,
    st2,
    st2_land,
    st2_mid,
    st2_land_b,
    l2,
    l2_halo,
    ag1,
    st1,
    st1_land,
    l1,
    xt,
    a1t,
    a2t,
    e_term,
    e_twin,
    e_land,
    e_share,
    e_tasks,
    d_term,
    d_twin,
    d_land,
    d_share,
    d_tasks,
    r_term,
    r_twin,
    r_land,
    r_share,
    r_tasks,
    p_twin,
    p_land,
    p_all,
    send_sem,
    recv_sem,
    local_sem,
):
    tasks, bands, cols, quarter, mid, wide, piece = sizes
    low = jnp.bfloat16
    f32 = jnp.float32
    at = Place(tasks, bands)
    post = Post(send_sem, recv_sem)
    task, band = at.task, at.band
    my_rows = pl.ds(pl.multiple_of(task * quarter, quarter), quarter)
    loads = [
        pltpu.make_async_copy(h3_ref.at[my_rows], h3q, local_sem.at[0]),
        pltpu.make_async_copy(x_ref.at[my_rows], xq, local_sem.at[1]),
        pltpu.make_async_copy(we_hbm, we, local_sem.at[2]),
        pltpu.make_async_copy(wd_hbm, wd, local_sem.at[3]),
        pltpu.make_async_copy(wr_hbm, wr, local_sem.at[4]),
    ]
    for load in loads:
        load.start()
    at.meet(True, True)

    grads_in = []
    for other in at.other_tasks:
        theirs = pl.ds(pl.multiple_of(other * quarter, quarter), quarter)
        grads_in.append(post.push(sg_ref.at[:, theirs], xg.at[task], {"task": other}))
    own_copy = pltpu.make_async_copy(sg_ref.at[:, my_rows], xg.at[task], local_sem.at[5])
    own_copy.start()

    p_pair = [
        post.push(pt_ref.at[2 * number + 1 - at.core], p_twin.at[number], at.twin)
        for number in range(at.chips)
    ]

    for number in range(3):
        a1t[number] = a1_ref[number].T
    a2t[...] = a2_ref[...].T

    def turn_inputs(number, carry):
        lanes = pl.ds(pl.multiple_of(number * piece, piece), piece)
        xt[lanes, :] = x_ref[:, lanes].T
        return carry

    lax.fori_loop(0, wide // piece, turn_inputs, 0)
    for made in p_pair:
        made.wait_recv()
    p_in = []
    for step in range(1, at.chips):
        other = lax.rem(at.chip + step, at.chips)
        both = pt_ref[2 * other + at.core].astype(f32) + p_twin[other].astype(f32)
        p_twin[other] = both.astype(low)
        p_in.append(
            post.push(p_twin.at[other], p_land.at[at.chip], {"space": other * 2 + at.core})
        )
    own_copy.wait()
    for made in grads_in:
        made.wait_recv()

    pairs = [(a, b) for a in range(tasks) for b in range(a, tasks)]

    def gram_step(number, totals):
        grads = [xg[a, number].astype(f32) for a in range(tasks)]
        out = []
        for (a, b), total in zip(pairs, totals):
            product = grads[a] * grads[b]
            product = product.reshape(quarter // 8, 8, piece).sum(axis=0)
            for start in range(0, piece, LANE):
                total = total + product[:, start : start + LANE]
            out.append(total)
        return tuple(out)

    totals = lax.fori_loop(
        0, bands, gram_step, tuple(jnp.zeros((8, LANE), f32) for _ in pairs)
    )
    gram_own[...] = jnp.zeros_like(gram_own)
    for number, total in enumerate(totals):
        gram_own[number : number + 1] = jnp.sum(total, axis=0, keepdims=True)
    p_total = pt_ref[band].astype(f32) + p_twin[at.chip].astype(f32)
    for made in p_in:
        made.wait_recv()
    for step in range(1, at.chips):
        p_total = p_total + p_land[lax.rem(at.chip + step, at.chips)].astype(f32)
    p_all[pl.ds(band, 1)] = p_total.astype(low)[None]
    p_block = p_all.at[band]
    p_near = post.push(p_block, p_block, at.twin)
    p_far = [
        post.push(
            p_block,
            p_block,
            {"space": lax.rem(at.chip + step, at.chips) * 2 + at.core},
        )
        for step in range(1, at.chips)
    ]
    gram_mid[...] = at.sum_over(post, "task", gram_own, gram_land)
    gram_sum = at.sum_over(post, "space", gram_mid, gram_land_b)
    gram_sum = jnp.broadcast_to(jnp.sum(gram_sum, axis=1, keepdims=True), gram_sum.shape)
    gram = [[None] * tasks for _ in range(tasks)]
    for number, (a, b) in enumerate(pairs):
        gram[a][b] = gram[b][a] = gram_sum[number : number + 1]
    norms = [jnp.sqrt(gram[a][a] + GRAM_EPS) for a in range(tasks)]
    cos = [[gram[a][b] / norms[b] for b in range(tasks)] for a in range(tasks)]
    rows_list = [
        [cos[0][0] - cos[0][l] - cos[k][0] + cos[k][l] for k in range(1, tasks)]
        for l in range(1, tasks)
    ]
    values = [cos[0][0] - cos[0][l] for l in range(1, tasks)]
    count = tasks - 1
    for pivot in range(count):
        for lower in range(pivot + 1, count):
            factor = rows_list[lower][pivot] / rows_list[pivot][pivot]
            rows_list[lower] = [
                under - factor * over for under, over in zip(rows_list[lower], rows_list[pivot])
            ]
            values[lower] = values[lower] - factor * values[pivot]
    answer = [None] * count
    for pivot in reversed(range(count)):
        running = values[pivot]
        for later in range(pivot + 1, count):
            running = running - rows_list[pivot][later] * answer[later]
        answer[pivot] = running / rows_list[pivot][pivot]
    rest = answer[0]
    for value in answer[1:]:
        rest = rest + value
    task_weight = [1.0 - rest] + answer
    for number in range(tasks):
        tw_out[number : number + 1] = task_weight[number]
    weights = [jnp.concatenate([value] * (piece // LANE), axis=1) for value in task_weight]

    def mixed(number):
        total = weights[0] * xg[0, number].astype(f32)
        for a in range(1, tasks):
            total = total + weights[a] * xg[a, number].astype(f32)
        return total.astype(low)

    comb_in = []
    for other in at.other_bands:
        comb[other] = mixed(other)
        comb_in.append(post.push(comb.at[other], comb_land.at[band], {"space": other}))
    comb_land[pl.ds(band, 1)] = mixed(band)[None]
    for load in loads[:2]:
        load.wait()
    for made in comb_in:
        made.wait_recv()

    mask_quarter = mask_ref[my_rows]
    mask_piece = jnp.concatenate([mask_quarter] * (piece // LANE), axis=1)
    inv_count = inv_ref[0:1]
    inv_piece = jnp.concatenate([inv_count] * (piece // LANE), axis=1)
    per_row = st3.shape[1] // piece
    half = st3.shape[0] // 2

    def gate_step(number, carry):
        lanes = pl.ds(pl.multiple_of(number * piece, piece), piece)
        hat = (h3q[:, lanes] - v3_ref[0:1, lanes]) * v3_ref[1:2, lanes]
        before = v3_ref[2:3, lanes] * hat + v3_ref[3:4, lanes] + xq[:, lanes].astype(f32)
        grad = gelu_slope(before) * comb_land[number].astype(f32) * mask_piece
        gate[number] = grad
        scaled[number] = hat
        gate_low[number] = grad.astype(low)
        row = number // per_row
        spot = pl.ds(pl.multiple_of(lax.rem(number, per_row) * piece, piece), piece)
        st3[pl.ds(row, 1), spot] = jnp.sum(grad, axis=0, keepdims=True)
        st3[pl.ds(half + row, 1), spot] = jnp.sum(grad * hat, axis=0, keepdims=True)
        return carry

    lax.fori_loop(0, bands, gate_step, 0)
    st3_mid[...] = at.sum_over(post, "task", st3, st3_land)
    gate_in = [
        post.push(gate_low, gate_band.at[task], {"task": other}) for other in at.other_tasks
    ]
    gate_band[pl.ds(task, 1)] = gate_low[...][None]
    s3_out[...] = at.sum_over(post, "space", st3_mid, st3_land_b)

    def third_step(number, carry):
        lanes = pl.ds(pl.multiple_of(number * piece, piece), piece)
        row = number // per_row
        spot = pl.ds(pl.multiple_of(lax.rem(number, per_row) * piece, piece), piece)
        shift_grad = s3_out[pl.ds(row, 1), spot] * inv_piece
        gain_grad = s3_out[pl.ds(half + row, 1), spot] * inv_piece
        l3[number] = (
            mask_piece
            * (v3_ref[2:3, lanes] * v3_ref[1:2, lanes])
            * (gate[number] - shift_grad - scaled[number] * gain_grad)
        ).astype(low)
        return carry

    lax.fori_loop(0, bands, third_step, 0)
    per_task = bands // tasks
    l3_in = []
    for other in at.other_tasks:
        l3_in.append(
            post.push(l3.at[pl.ds(other * per_task, per_task)], l3x.at[task], {"task": other})
        )
    l3x[pl.ds(task, 1)] = l3[pl.ds(task * per_task, per_task)][None]
    loads[2].wait()

    def expand_step(number, total):
        lanes = pl.ds(pl.multiple_of(number * piece, piece), piece)
        return total + dot_nt(l3[number], we[:, lanes])

    ag2 = lax.fori_loop(0, bands, expand_step, jnp.zeros((quarter, mid), f32))

    mask_mid = jnp.concatenate([mask_quarter] * (mid // LANE), axis=1)
    inv_mid = jnp.concatenate([inv_count] * (mid // LANE), axis=1)
    hat = (h2_ref[my_rows] - v2_ref[0:1]) * v2_ref[1:2]
    grad = gelu_slope(v2_ref[2:3] * hat + v2_ref[3:4]) * ag2 * mask_mid
    spread = mid // LANE

    def put_sums(target, first, second):
        for number in range(spread):
            lanes = slice(number * LANE, (number + 1) * LANE)
            target[number : number + 1] = first[:, lanes]
            target[spread + number : spread + number + 1] = second[:, lanes]

    def get_sums(total):
        return [
            jnp.concatenate([total[base + k : base + k + 1] for k in range(spread)], axis=1)
            for base in (0, spread)
        ]

    put_sums(
        st2, jnp.sum(grad, axis=0, keepdims=True), jnp.sum(grad * hat, axis=0, keepdims=True)
    )
    st2_mid[...] = at.sum_over(post, "task", st2, st2_land)
    s2_out[...] = at.sum_over(post, "space", st2_mid, st2_land_b)
    shift_grad, gain_grad = get_sums(s2_out[...])
    l2[my_rows] = (
        mask_mid
        * (v2_ref[2:3] * v2_ref[1:2])
        * (grad - shift_grad * inv_mid - hat * (gain_grad * inv_mid))
    ).astype(low)
    l2_in = [post.push(l2.at[my_rows], l2.at[my_rows], {"task": other}) for other in at.other_tasks]
    for made in l2_in:
        made.wait_recv()
    has_above, has_below = band > 0, band < bands - 1
    up = post.copy(l2, l2_halo.at[1], {"space": lax.rem(band + bands - 1, bands)})
    down = post.copy(l2, l2_halo.at[0], {"space": lax.rem(band + 1, bands)})

    @pl.when(has_above)
    def _():
        up.start()

    @pl.when(has_below)
    def _():
        down.start()

    @pl.when(jnp.logical_not(has_above))
    def _():
        l2_halo[0] = jnp.zeros_like(l2)

    @pl.when(jnp.logical_not(has_below))
    def _():
        l2_halo[1] = jnp.zeros_like(l2)

    p_passed = []
    for step, made in enumerate(p_far, start=1):
        made.wait_recv()
        block = p_all.at[lax.rem(at.chip + at.chips - step, at.chips) * 2 + at.core]
        p_passed.append(post.push(block, block, at.twin))
    loads[3].wait()
    halves = [slice(start, start + piece) for start in range(0, mid, piece)]
    for lanes in halves:
        total = None
        for col_tap in range(3):
            part = shift_pixels(
                dot_nt(l2[...], wd[3 + col_tap, lanes, :]), -CONV_DILATION * (col_tap - 1), cols
            )
            total = part if total is None else total + part
        ag1[:, lanes] = total

    for made in l3_in:
        made.wait_recv()
    share_e = [
        jnp.concatenate([l3x[a, number] for a in range(tasks)], axis=0)
        for number in range(per_task)
    ]
    for number in range(per_task):
        part = dot_nn(a2t[...], share_e[number]).astype(low)
        per_band = part.shape[0] // bands
        for target in range(bands):
            e_term[target % 2, target // 2, :, number * piece : (number + 1) * piece] = part[
                target * per_band : (target + 1) * per_band
            ]

    def to_twin(term, landing):
        return post.push(term.at[1 - at.core], landing, at.twin)

    e_pair = to_twin(e_term, e_twin)
    narrow = mid // tasks
    my_lanes = pl.ds(pl.multiple_of(task * narrow, narrow), narrow)

    @pl.when(has_below)
    def _():
        up.wait_recv()

    @pl.when(has_above)
    def _():
        down.wait_recv()

    for lanes in halves:
        total = None
        for col_tap in range(3):
            part = dot_nt(l2_halo[1], wd[col_tap, lanes, :]) + dot_nt(
                l2_halo[0], wd[6 + col_tap, lanes, :]
            )
            part = shift_pixels(part, -CONV_DILATION * (col_tap - 1), cols)
            total = part if total is None else total + part
        ag1[:, lanes] += total

    pixels = ag1.shape[0]
    chunk = pixels // 8

    def first_rows(number):
        return pl.ds(pl.multiple_of(number * chunk, chunk), chunk)

    def first_step(number, sums):
        rows = first_rows(number)
        hat = (h1_ref[rows] - v1_ref[0:1]) * v1_ref[1:2]
        keep = jnp.concatenate([mask_ref[rows]] * spread, axis=1)
        grad = gelu_slope(v1_ref[2:3] * hat + v1_ref[3:4]) * ag1[rows] * keep
        ag1[rows] = grad
        return (
            sums[0] + jnp.sum(grad, axis=0, keepdims=True),
            sums[1] + jnp.sum(grad * hat, axis=0, keepdims=True),
        )

    nothing = jnp.zeros((1, mid), f32)
    first, second = lax.fori_loop(0, 8, first_step, (nothing, nothing))
    put_sums(st1, first, second)
    s1_out[...] = at.sum_over(post, "space", st1, st1_land)
    shift_grad, gain_grad = get_sums(s1_out[...])
    shift_grad, gain_grad = shift_grad * inv_mid, gain_grad * inv_mid

    def first_finish(number, carry):
        rows = first_rows(number)
        hat = (h1_ref[rows] - v1_ref[0:1]) * v1_ref[1:2]
        keep = jnp.concatenate([mask_ref[rows]] * spread, axis=1)
        l1[rows] = (
            keep * (v1_ref[2:3] * v1_ref[1:2]) * (ag1[rows] - shift_grad - hat * gain_grad)
        ).astype(low)
        return carry

    lax.fori_loop(0, 8, first_finish, 0)

    share_r = l1[:, my_lanes]
    per_band_r = wide // bands

    def reduce_step(number, carry):
        rows = pl.ds(pl.multiple_of(number * per_band_r, per_band_r), per_band_r)
        r_term[lax.rem(number, 2), number // 2] = dot_nn(xt[rows, :], share_r).astype(low)
        return carry

    lax.fori_loop(0, bands, reduce_step, 0)
    r_pair = to_twin(r_term, r_twin)
    share_d = l2[:, my_lanes].astype(f32)
    for col_tap in range(3):
        moved = shift_pixels(share_d, -CONV_DILATION * (col_tap - 1), cols).astype(low)
        for row_tap in range(3):
            part = dot_nn(a1t[row_tap], moved).astype(low)
            per_band = part.shape[0] // bands
            for target in range(bands):
                d_term[target % 2, target // 2, 3 * row_tap + col_tap] = part[
                    target * per_band : (target + 1) * per_band
                ]

    def along(pair, term, twin, landing):
        pair.wait_recv()
        arrivals = []
        for step in range(1, at.chips):
            other = lax.rem(at.chip + step, at.chips)
            both = term[at.core, other].astype(f32) + twin[other].astype(f32)
            twin[other] = both.astype(low)
            arrivals.append(
                post.push(twin.at[other], landing.at[at.chip], {"space": other * 2 + at.core})
            )
        return arrivals

    def settle(arrivals, term, twin, landing):
        total = term[at.core, at.chip].astype(f32) + twin[at.chip].astype(f32)
        for made in arrivals:
            made.wait_recv()
        for step in range(1, at.chips):
            total = total + landing[lax.rem(at.chip + step, at.chips)].astype(f32)
        return total.astype(low)

    def to_tasks(share, landing):
        arrivals = [post.push(share, landing.at[task], {"task": other}) for other in at.other_tasks]
        landing[pl.ds(task, 1)] = share[...][None]
        return arrivals

    r_in = along(r_pair, r_term, r_twin, r_land)
    e_in = along(e_pair, e_term, e_twin, e_land)
    d_pair = to_twin(d_term, d_twin)
    r_share[...] = settle(r_in, r_term, r_twin, r_land)
    r_back = to_tasks(r_share, r_tasks)
    d_in = along(d_pair, d_term, d_twin, d_land)
    e_share[...] = settle(e_in, e_term, e_twin, e_land)
    e_back = to_tasks(e_share, e_tasks)

    loads[4].wait()
    for made in gate_in:
        made.wait_recv()

    def input_step(number, carry):
        lanes = pl.ds(pl.multiple_of(number * piece, piece), piece)
        gates = jnp.concatenate([gate_band[a, number] for a in range(tasks)], axis=0).astype(f32)
        ig_out[:, lanes] = (dot_nt(l1[...], wr[lanes, :]) + gates).astype(low)
        return carry

    lax.fori_loop(0, bands, input_step, 0)
    d_share[...] = settle(d_in, d_term, d_twin, d_land)
    d_back = to_tasks(d_share, d_tasks)
    for made in [p_near] + p_passed:
        made.wait_recv()
    pg_out[...] = p_all[...].astype(f32)
    for made in r_back:
        made.wait_recv()
    for a in range(tasks):
        rg_out[:, a * narrow : (a + 1) * narrow] = r_tasks[a].astype(f32)
    for made in e_back:
        made.wait_recv()
    broad = wide // tasks
    for a in range(tasks):
        eg_out[:, a * broad : (a + 1) * broad] = e_tasks[a].astype(f32)
    for made in d_back:
        made.wait_recv()
    for a in range(tasks):
        dg_out[:, :, a * narrow : (a + 1) * narrow] = d_tasks[a].astype(f32)
    post.close()

    @pl.when(has_above)
    def _():
        up.wait_send()

    @pl.when(has_below)
    def _():
        down.wait_send()


def trunk_back(
    tasks, bands, cols, collective, sg, h3, x, v3, h2, v2, h1, v1, a1, a2, mask, inv, we, wd, wr, pt
):
    low, f32 = jnp.bfloat16, jnp.float32
    pixels, wide = x.shape
    mid = a2.shape[1]
    quarter = pixels // tasks
    piece = wide // bands
    narrow, broad = mid // tasks, wide // tasks
    chips = bands // 2
    part = mid // bands
    in_vmem = pl.BlockSpec(memory_space=pltpu.VMEM)
    anywhere = pl.BlockSpec(memory_space=pl.ANY)
    shape = jax.ShapeDtypeStruct

    def stats(rows, lanes):
        return [
            pltpu.VMEM((rows, lanes), f32),
            pltpu.VMEM((tasks, rows, lanes), f32),
            pltpu.VMEM((rows, lanes), f32),
            pltpu.VMEM((bands, rows, lanes), f32),
        ]

    def terms(*dims):
        return [
            pltpu.VMEM((2, chips) + dims, low),
            pltpu.VMEM((chips,) + dims, low),
            pltpu.VMEM((chips,) + dims, low),
            pltpu.VMEM(dims, low),
            pltpu.VMEM((tasks,) + dims, low),
        ]

    stat_wide = 2 * wide // 8
    scratch = (
        [
            pltpu.VMEM(we.shape, low),
            pltpu.VMEM(wd.shape, low),
            pltpu.VMEM(wr.shape, low),
            pltpu.VMEM((quarter, wide), f32),
            pltpu.VMEM((quarter, wide), low),
            pltpu.VMEM((tasks, bands, quarter, piece), low),
        ]
        + stats(16, LANE)
        + [
            pltpu.VMEM((bands, quarter, piece), low),
            pltpu.VMEM((bands, quarter, piece), low),
            pltpu.VMEM((bands, quarter, piece), f32),
            pltpu.VMEM((bands, quarter, piece), f32),
            pltpu.VMEM((bands, quarter, piece), low),
            pltpu.VMEM((tasks, bands, quarter, piece), low),
        ]
        + stats(8, stat_wide)
        + [
            pltpu.VMEM((bands, quarter, piece), low),
            pltpu.VMEM((tasks, bands // tasks, quarter, piece), low),
        ]
        + stats(2 * mid // LANE, LANE)
        + [
            pltpu.VMEM((pixels, mid), low),
            pltpu.VMEM((2, pixels, mid), low),
            pltpu.VMEM((pixels, mid), f32),
            pltpu.VMEM((2 * mid // LANE, LANE), f32),
            pltpu.VMEM((bands, 2 * mid // LANE, LANE), f32),
            pltpu.VMEM((pixels, mid), low),
            pltpu.VMEM((wide, pixels), low),
            pltpu.VMEM((3, mid, pixels), low),
            pltpu.VMEM((mid, pixels), low),
        ]
        + terms(part, broad)
        + terms(9, part, narrow)
        + terms(piece, narrow)
        + [
            pltpu.VMEM((chips,) + pt.shape[1:], low),
            pltpu.VMEM((chips,) + pt.shape[1:], low),
            pltpu.VMEM(pt.shape, low),
            pltpu.SemaphoreType.DMA((96,)),
            pltpu.SemaphoreType.DMA((96,)),
            pltpu.SemaphoreType.DMA((6,)),
        ]
    )
    out_shapes = (
        shape((8, LANE), f32),
        shape((pixels, wide), low),
        shape((piece, mid), f32),
        shape((9, part, mid), f32),
        shape((part, wide), f32),
        shape((8, stat_wide), f32),
        shape((2 * mid // LANE, LANE), f32),
        shape((2 * mid // LANE, LANE), f32),
        shape(pt.shape, f32),
    )
    return pl.pallas_call(
        functools.partial(trunk_back_kernel, (tasks, bands, cols, quarter, mid, wide, piece)),
        name="trunk_back",
        out_shape=out_shapes,
        in_specs=[in_vmem, anywhere, in_vmem] + [in_vmem] * 9 + [anywhere] * 3 + [in_vmem],
        out_specs=(in_vmem,) * 9,
        scratch_shapes=scratch,
        compiler_params=pltpu.CompilerParams(
            collective_id=collective, has_side_effects=True, vmem_limit_bytes=56 << 20
        ),
    )(sg, h3, x, v3, h2, v2, h1, v1, a1, a2, mask, inv, we, wd, wr, pt)


def head_kernel(
    plan,
    sh_ref,
    mask_ref,
    inv_ref,
    gain_ref,
    shift_ref,
    cot_ref,
    bw_ref,
    pw_ref,
    rate_hbm,
    head_out,
    sg_out,
    grads_out,
    proj_out,
    pool_out,
    both_sums_out,
    proj_sums_out,
    rate,
    turned,
    extra,
    term,
    twin_land,
    right_land,
    left_land,
    pre,
    joined,
    upstream,
    st_both,
    st_both_sum,
    st_both_land,
    st_proj,
    st_proj_sum,
    st_proj_land,
    st_pback,
    st_pback_land,
    st_back,
    st_back_land,
    both_all,
    moved,
    grads,
    back,
    send_sem,
    recv_sem,
    rate_sem,
):
    tasks, bands, cols, pixels, width, taps, extras = plan
    low, f32 = jnp.bfloat16, jnp.float32
    at = Place(tasks, bands)
    post = Post(send_sem, recv_sem)
    chips, chip, core, band = at.chips, at.chip, at.core, at.band
    last = chips - 1
    group = 2 * pixels
    number_of = {tap[:3]: number for number, tap in enumerate(taps)}
    loads = []
    for number, (level, row_tap, col_tap, _, _) in enumerate(taps):
        start = (9 * (level - 1) + 3 * row_tap + col_tap) * width
        load = pltpu.make_async_copy(
            rate_hbm.at[:, start : start + width], rate.at[number], rate_sem.at[number]
        )
        load.start()
        loads.append(load)
    at.meet(False, True)
    for load in loads:
        load.wait()

    def rows_of(ref, number):
        return jnp.concatenate([ref[2 * number], ref[2 * number + 1]], axis=0)

    def right_of(level, col_tap):
        return (col_tap - 1) * level * RATE

    def forward_taps(source, level, row_tap):
        total = None
        for col_tap in range(3):
            number = number_of.get((level, row_tap, col_tap))
            if number is None:
                continue
            part = shift_pixels(
                dot_nn(source, rate[number]), right_of(level, col_tap), cols
            )
            total = part if total is None else total + part
        return total

    extra[...] = jnp.zeros_like(extra)
    for level, target, source, row_tap in extras:
        extra[level - 1, target] += forward_taps(rows_of(sh_ref, source), level, row_tap)

    def twin_term(number):
        return pltpu.make_async_remote_copy(
            term.at[number, 1 - core],
            twin_land.at[number],
            send_sem.at[number],
            recv_sem.at[number],
            device_id=at.twin,
            device_id_type=MESH_ID,
        )

    post.used = chips

    def forward_group(step, carry):
        number = lax.rem(step, 2) * (last - step // 2) + (1 - lax.rem(step, 2)) * (step // 2)
        source = rows_of(sh_ref, number)

        def put(branch, value):
            value = value.astype(low)
            term[number, 0, branch] = value[:pixels]
            term[number, 1, branch] = value[pixels:]

        put(0, dot_nn(source, bw_ref[:, :width]))
        for level in (1, 2, 3):
            total = forward_taps(source, level, 1)
            if any(level == entry[0] for entry in extras):
                total = total + extra[level - 1, number]
            put(level, total)
        twin_term(number).start()
        turned[:, pl.ds(pl.multiple_of(number * group, group), group)] = source.T
        return carry + jnp.sum(source.astype(f32), axis=0, keepdims=True)

    pixel_sum = lax.fori_loop(0, chips, forward_group, jnp.zeros((1, width), f32))

    def hop(source, landing, device_chip, number):
        return pltpu.make_async_remote_copy(
            source,
            landing,
            send_sem.at[number],
            recv_sem.at[number],
            device_id={"space": device_chip * 2 + core},
            device_id_type=MESH_ID,
        )

    base_right, base_left = post.used, post.used + chips
    post.used += 2 * chips
    next_chip = lax.rem(chip + 1, chips)
    prev_chip = lax.rem(chip + last, chips)

    def go_right(number):
        return hop(twin_land.at[number], right_land.at[number], next_chip, base_right + number)

    def go_left(number):
        return hop(twin_land.at[number], left_land.at[number], prev_chip, base_left + number)

    def pass_on(number, copy, landing, has_incoming):
        twin_term(number).wait_recv()

        @pl.when(has_incoming)
        def _():
            copy.wait_recv()

            def add(branch, carry):
                twin_land[number, branch] = (
                    term[number, core, branch].astype(f32)
                    + twin_land[number, branch].astype(f32)
                    + landing[number, branch].astype(f32)
                ).astype(low)
                return carry

            lax.fori_loop(0, 4, add, 0)

        @pl.when(jnp.logical_not(has_incoming))
        def _():
            def add(branch, carry):
                twin_land[number, branch] = (
                    term[number, core, branch].astype(f32) + twin_land[number, branch].astype(f32)
                ).astype(low)
                return carry

            lax.fori_loop(0, 4, add, 0)

        copy.start()

    for number in range(last):
        to_right, to_left = last - number, number

        @pl.when(chip < to_right)
        def _():
            pass_on(to_right, go_right(to_right), right_land, chip > 0)

        @pl.when(chip > to_left)
        def _():
            pass_on(to_left, go_left(to_left), left_land, chip < last)

    mask_own = mask_ref[pl.ds(pl.multiple_of(band * pixels, pixels), pixels)]
    mask_own = jnp.concatenate([mask_own] * (width // LANE), axis=1)
    inv_count = jnp.concatenate([inv_ref[0:1]] * (width // LANE), axis=1)
    spread = width // LANE

    def put_rows(target, number, value):
        for part in range(spread):
            target[pl.ds(number * spread + part, 1), :] = value[:, part * LANE : (part + 1) * LANE]

    def get_rows(target, number):
        return jnp.concatenate(
            [target[pl.ds(number * spread + part, 1), :] for part in range(spread)], axis=1
        )

    def column_sum(value):
        return jnp.sum(value, axis=0, keepdims=True)

    twin_term(chip).wait_recv()

    @pl.when(chip > 0)
    def _():
        go_right(chip).wait_recv()

    @pl.when(chip < last)
    def _():
        go_left(chip).wait_recv()

    @pl.when(chip == 0)
    def _():
        right_land[0] = jnp.zeros(right_land.shape[1:], low)

    @pl.when(chip == last)
    def _():
        left_land[last] = jnp.zeros(left_land.shape[1:], low)

    st_both[...] = jnp.zeros_like(st_both)

    def settle(branch, carry):
        value = (
            term[chip, core, branch].astype(f32)
            + twin_land[chip, branch].astype(f32)
            + right_land[chip, branch].astype(f32)
            + left_land[chip, branch].astype(f32)
        )
        pre[branch] = value
        kept = value * mask_own
        put_rows(st_both, branch, column_sum(kept))
        put_rows(st_both, 4 + branch, column_sum(kept * value))
        return carry

    lax.fori_loop(0, 4, settle, 0)
    high = pixel_sum.astype(low)
    rest = pixel_sum - high.astype(f32)
    middle = rest.astype(low)
    tail = (rest - middle.astype(f32)).astype(low)
    pieces = jnp.concatenate(
        [high.astype(f32), middle.astype(f32), tail.astype(f32), jnp.zeros((13, width), f32)],
        axis=0,
    ).astype(low)
    put_rows(st_both, 8, column_sum(dot_nn(pieces, bw_ref[:, width:])))
    st_both_sum[...] = at.sum_over(post, "space", st_both, st_both_land)
    pooled = get_rows(st_both_sum, 8) * inv_count

    def lanes_of(number):
        return pl.ds(pl.multiple_of(number * width, width), width)

    def scale_of(target, first, second):
        mean_value = get_rows(target, first) * inv_count
        variance = get_rows(target, second) * inv_count - mean_value * mean_value
        return mean_value, lax.rsqrt(variance + NORM_EPS)

    def activate(branch, projected):
        mean_value, inv_std = scale_of(st_both_sum, branch, 4 + branch)
        hat = (pre[branch] - mean_value) * inv_std
        pre[branch] = hat
        normed = gain_ref[:, lanes_of(branch)] * hat + shift_ref[:, lanes_of(branch)]
        active = (gelu_of(normed) * mask_own).astype(low)
        joined[branch] = active
        return projected + dot_nn(active, pw_ref[lanes_of(branch), :])

    joined[4] = (gelu_of(pooled).astype(low).astype(f32) * mask_own).astype(low)
    projected = dot_nn(joined[4], pw_ref[4 * width : 5 * width, :])
    projected = lax.fori_loop(0, 4, activate, projected)
    kept = projected * mask_own
    st_proj[...] = jnp.zeros_like(st_proj)
    put_rows(st_proj, 0, column_sum(kept))
    put_rows(st_proj, 1, column_sum(kept * projected))
    st_proj_sum[...] = at.sum_over(post, "space", st_proj, st_proj_land)
    mean_value, inv_std = scale_of(st_proj_sum, 0, 1)
    hat = (projected - mean_value) * inv_std
    gain_proj = gain_ref[:, 4 * width : 5 * width]
    normed = gain_proj * hat + shift_ref[:, 4 * width : 5 * width]
    proj_up = gelu_slope(normed) * cot_ref[...].astype(f32) * mask_own
    st_pback[...] = jnp.zeros_like(st_pback)
    put_rows(st_pback, 0, column_sum(proj_up))
    put_rows(st_pback, 1, column_sum(proj_up * hat))
    proj_sums_out[...] = at.sum_over(post, "space", st_pback, st_pback_land)
    head_out[...] = (gelu_of(normed) * mask_own).astype(low)
    shift_grad, gain_grad = get_rows(proj_sums_out, 0), get_rows(proj_sums_out, 1)
    proj_low = (
        mask_own
        * (gain_proj * inv_std)
        * (proj_up - shift_grad * inv_count - hat * (gain_grad * inv_count))
    ).astype(low)
    st_back[...] = jnp.zeros_like(st_back)

    def back_step(branch, carry):
        joined_grad = dot_nt(proj_low, pw_ref[lanes_of(branch), :])
        hat = pre[branch]
        normed = gain_ref[:, lanes_of(branch)] * hat + shift_ref[:, lanes_of(branch)]
        up = gelu_slope(normed) * joined_grad * mask_own
        upstream[branch] = up
        put_rows(st_back, branch, column_sum(up))
        put_rows(st_back, 4 + branch, column_sum(up * hat))
        return carry

    lax.fori_loop(0, 4, back_step, 0)
    pool_total = column_sum(dot_nt(proj_low, pw_ref[4 * width : 5 * width, :]) * mask_own)
    put_rows(st_back, 8, pool_total)
    both_sums_out[...] = at.sum_over(post, "space", st_back, st_back_land)
    pool_grad = (gelu_slope(pooled) * get_rows(both_sums_out, 8)).astype(low)
    pool_out[...] = jnp.broadcast_to(pool_grad.astype(f32), pool_out.shape)

    def both_step(branch, carry):
        _, inv_std = scale_of(st_both_sum, branch, 4 + branch)
        shift_grad = get_rows(both_sums_out, branch) * inv_count
        gain_grad = get_rows(both_sums_out, 4 + branch) * inv_count
        both_all[band, branch] = (
            mask_own
            * (gain_ref[:, lanes_of(branch)] * inv_std)
            * (upstream[branch] - shift_grad - pre[branch] * gain_grad)
        ).astype(low)
        return carry

    lax.fori_loop(0, 4, both_step, 0)

    all_right = post.used
    all_left = all_right + chips
    all_twin = all_left + chips

    def send_right(step):
        block = both_all.at[lax.rem(chip - step + 1 + chips, chips) * 2 + core]
        return hop(block, block, next_chip, all_right + step)

    def send_left(step):
        block = both_all.at[lax.rem(chip + step - 1, chips) * 2 + core]
        return hop(block, block, prev_chip, all_left + step)

    def hand_over(number):
        block = both_all.at[number * 2 + core]
        return pltpu.make_async_remote_copy(
            block,
            block,
            send_sem.at[all_twin + number],
            recv_sem.at[all_twin + number],
            device_id=at.twin,
            device_id_type=MESH_ID,
        )

    def from_left(step):
        block = both_all.at[lax.rem(chip - step + chips, chips) * 2 + core]
        return hop(block, block, next_chip, all_right + step)

    def from_right(step):
        block = both_all.at[lax.rem(chip + step, chips) * 2 + core]
        return hop(block, block, prev_chip, all_left + step)

    @pl.when(chip < last)
    def _():
        send_right(1).start()

    @pl.when(chip > 0)
    def _():
        send_left(1).start()

    hand_over(chip).start()

    def proj_step(branch, carry):
        proj_out[lanes_of(branch), :] = dot_nn(joined[branch].T, proj_low).astype(low)
        return carry

    lax.fori_loop(0, 5, proj_step, 0)
    grads[...] = jnp.zeros_like(grads)
    pool_row = dot_nt(
        jnp.broadcast_to(pool_grad, (16, width)), bw_ref[:, width:]
    )[0:1] * inv_count
    moved_levels = sorted({entry[0] for entry in extras})

    def back_group(step, carry):
        number = group_at(step)
        hand_over(number).wait_recv()
        columns = turned[:, pl.ds(pl.multiple_of(number * group, group), group)]

        def both_of(branch):
            return jnp.concatenate(
                [both_all[2 * number, branch], both_all[2 * number + 1, branch]], axis=0
            )

        part = both_of(0)
        total = dot_nt(part, bw_ref[:, :width])
        grads[len(taps)] += dot_nn(columns, part)
        for level in (1, 2, 3):
            image = both_of(level).astype(f32)
            for col_tap in range(3):
                tap = number_of.get((level, 1, col_tap))
                if tap is None:
                    continue
                part = shift_pixels(image, -right_of(level, col_tap), cols).astype(low)
                if level in moved_levels:
                    moved[moved_levels.index(level), number, col_tap] = part
                total = total + dot_nt(part, rate[tap])
                grads[tap] += dot_nn(columns, part)
        back[number] = total
        return carry

    mirror = chip // 2
    near = chip * (1 - mirror) + (last - chip) * mirror

    def group_at(step):
        place = step + near * (1 - 2 * step) * ((last - step) // 2)
        return place * (1 - mirror) + (last - place) * mirror

    lax.fori_loop(0, 1, back_group, 0)
    done = 1
    for step in range(1, chips):
        @pl.when(chip >= step)
        def _():
            from_left(step).wait_recv()
            if step < last:

                @pl.when(chip < last)
                def _():
                    send_right(step + 1).start()

            hand_over(lax.rem(chip - step + chips, chips)).start()

        @pl.when(chip + step <= last)
        def _():
            from_right(step).wait_recv()
            if step < last:

                @pl.when(chip > 0)
                def _():
                    send_left(step + 1).start()

            hand_over(lax.rem(chip + step, chips)).start()

        upto = chips if step == last else step + 1 + near
        lax.fori_loop(done, upto, back_group, 0)
        done = upto

    for level, target, source, row_tap in extras:
        columns = turned[:, source * group : (source + 1) * group]
        total = back[source]
        for col_tap in range(3):
            tap = number_of.get((level, row_tap, col_tap))
            if tap is None:
                continue
            part = moved[moved_levels.index(level), target, col_tap]
            total = total + dot_nt(part, rate[tap])
            grads[tap] += dot_nn(columns, part)
        back[source] = total

    def finish_group(number, carry):
        rows = pl.ds(pl.multiple_of(number * group, group), group)
        keep = jnp.concatenate([mask_ref[rows]] * spread, axis=1)
        value = (back[number] + keep * pool_row).astype(low)
        sg_out[2 * number] = value[:pixels]
        sg_out[2 * number + 1] = value[pixels:]
        return carry

    lax.fori_loop(0, chips, finish_group, 0)

    def finish_tap(number, carry):
        grads_out[number] = grads[number].astype(low)
        return carry

    lax.fori_loop(0, len(taps) + 1, finish_tap, 0)

    post.close()

    def twin_left(number, carry):
        twin_term(number).wait_send()
        hand_over(number).wait_send()
        return carry

    lax.fori_loop(0, chips, twin_left, 0)
    for number in range(last):
        to_right, to_left = last - number, number

        @pl.when(chip < to_right)
        def _():
            go_right(to_right).wait_send()

        @pl.when(chip > to_left)
        def _():
            go_left(to_left).wait_send()

    for step in range(1, chips):

        @pl.when((chip < last) & (chip - step + 1 >= 0))
        def _():
            send_right(step).wait_send()

        @pl.when((chip > 0) & (chip + step - 1 <= last))
        def _():
            send_left(step).wait_send()


def head(tasks, bands, cols, rows, collective, sh, mask, inv, gain, shift, cot, bw, pw, rate):
    low, f32 = jnp.bfloat16, jnp.float32
    pixels, width = sh.shape[1], pw.shape[1]
    chips = bands // 2
    group_rows = rows // chips
    taps = live_taps(rows, cols)
    extras = []
    for level in (1, 2, 3):
        for row_tap in (0, 2):
            if (level, row_tap, 1) in [tap[:3] for tap in taps]:
                away = (row_tap - 1) * level * RATE // group_rows
                extras += [
                    (level, target, target + away, row_tap)
                    for target in range(chips)
                    if 0 <= target + away < chips
                ]
    levels = max([entry[0] for entry in extras], default=1)
    in_vmem = pl.BlockSpec(memory_space=pltpu.VMEM)
    anywhere = pl.BlockSpec(memory_space=pl.ANY)
    shape = jax.ShapeDtypeStruct
    block = (pixels, width)
    both_rows, proj_rows = -(-9 * width // LANE // 8) * 8, 8

    def stats(count):
        return [pltpu.VMEM((count, LANE), f32), pltpu.VMEM((bands, count, LANE), f32)]

    scratch = (
        [
            pltpu.VMEM((len(taps), sh.shape[2], width), low),
            pltpu.VMEM((sh.shape[2], bands * pixels), low),
            pltpu.VMEM((levels, chips, 2 * pixels, width), f32),
            pltpu.VMEM((chips, 2, 4) + block, low),
            pltpu.VMEM((chips, 4) + block, low),
            pltpu.VMEM((chips, 4) + block, low),
            pltpu.VMEM((chips, 4) + block, low),
            pltpu.VMEM((4,) + block, f32),
            pltpu.VMEM((5,) + block, low),
            pltpu.VMEM((4,) + block, f32),
        ]
        + [pltpu.VMEM((both_rows, LANE), f32)]
        + stats(both_rows)
        + [pltpu.VMEM((proj_rows, LANE), f32)]
        + stats(proj_rows)
        + stats(proj_rows)
        + stats(both_rows)
        + [
            pltpu.VMEM((bands, 4) + block, low),
            pltpu.VMEM((levels, chips, 3, 2 * pixels, width), low),
            pltpu.VMEM((len(taps) + 1, sh.shape[2], width), f32),
            pltpu.VMEM((chips, 2 * pixels, width), f32),
            pltpu.SemaphoreType.DMA((80,)),
            pltpu.SemaphoreType.DMA((80,)),
            pltpu.SemaphoreType.DMA((len(taps),)),
        ]
    )
    out_shapes = (
        shape(block, low),
        shape(sh.shape, low),
        shape((len(taps) + 1, sh.shape[2], width), low),
        shape(pw.shape, low),
        shape((8, width), f32),
        shape((both_rows, LANE), f32),
        shape((proj_rows, LANE), f32),
    )
    return taps, pl.pallas_call(
        functools.partial(
            head_kernel, (tasks, bands, cols, pixels, width, tuple(taps), tuple(extras))
        ),
        name="head",
        out_shape=out_shapes,
        in_specs=[in_vmem] * 8 + [anywhere],
        out_specs=(in_vmem,) * 7,
        scratch_shapes=scratch,
        compiler_params=pltpu.CompilerParams(
            collective_id=collective, has_side_effects=True, vmem_limit_bytes=60 << 20
        ),
    )(sh, mask, inv, gain, shift, cot, bw, pw, rate)


def norm_scale(totals, pixel_count):
    mean_value = totals[0] / pixel_count
    variance = totals[1] / pixel_count - mean_value * mean_value
    return mean_value, variance, lax.rsqrt(variance + NORM_EPS)


def masked_sums(hidden, valid_mask):
    kept = hidden * valid_mask
    return [jnp.sum(kept, axis=0), jnp.sum(hidden * kept, axis=0)]


def shift_columns(image, by):
    if by == 0:
        return image
    cols = image.shape[1]
    if by > 0:
        return jnp.pad(image[:, by:], ((0, 0), (0, by), (0, 0)))
    return jnp.pad(image[:, : cols + by], ((0, 0), (-by, 0), (0, 0)))


def live_taps(rows, cols):
    taps = []
    for level in (1, 2, 3):
        for row_tap in range(3):
            for col_tap in range(3):
                down, right = (row_tap - 1) * level * RATE, (col_tap - 1) * level * RATE
                if abs(down) < rows and abs(right) < cols:
                    taps.append((level, row_tap, col_tap, down, right))
    return taps


def per_device_slices(
    features,
    row_width,
    w_reduce,
    w_dilated,
    w_expand,
    trunk_gain,
    trunk_shift,
    branch_weight,
    rate_weight,
    proj_weight,
    head_gain,
    head_shift,
    head_cot,
):
    links = Links()
    bands, tasks = links.bands, links.tasks
    low = jnp.bfloat16
    wide = jnp.float32
    band_rows, cols_count, in_width = features.shape
    rows_count = band_rows * bands
    pixels = band_rows * cols_count
    all_pixels = pixels * bands
    middle_width = w_reduce.shape[1]
    head_width = proj_weight.shape[2]
    slice_width = in_width // bands
    band = lax.axis_index("space")
    task = lax.axis_index("task")
    widths = lax.dynamic_slice_in_dim(row_width, band * band_rows, band_rows)

    def mask_of(some_widths):
        return (
            (jnp.arange(cols_count)[None, :] < some_widths[:, None]).astype(wide).reshape(-1, 1)
        )

    valid_mask = mask_of(widths)
    all_mask = mask_of(row_width)
    pixel_count = jnp.sum(row_width).astype(wide)
    inputs = features.reshape(pixels, in_width)
    gains = [
        trunk_gain[:middle_width],
        trunk_gain[middle_width : 2 * middle_width],
        trunk_gain[2 * middle_width :],
    ]
    shifts = [
        trunk_shift[:middle_width],
        trunk_shift[middle_width : 2 * middle_width],
        trunk_shift[2 * middle_width :],
    ]

    def norm(hidden, totals, gain_vec, shift_vec):
        mean_value, variance, inv_std = norm_scale(totals, pixel_count)
        scaled = (hidden - mean_value) * inv_std
        return gain_vec * scaled + shift_vec, scaled, inv_std, mean_value, variance

    hidden_one = jnp.dot(inputs, w_reduce, preferred_element_type=wide)
    stats_one = norm(
        hidden_one, links.sums(masked_sums(hidden_one, valid_mask), "sums_one"), gains[0], shifts[0]
    )
    first_active = (jax.nn.gelu(stats_one[0]) * valid_mask).astype(low)
    rim = band_rim(first_active.reshape(band_rows, cols_count, middle_width))
    patches = trunk_taps(rim, CONV_DILATION, band_rows, cols_count, False)
    hidden_two = jnp.einsum("pti,ito->po", patches, w_dilated, preferred_element_type=wide)
    stats_two = norm(
        hidden_two, links.sums(masked_sums(hidden_two, valid_mask), "sums_two"), gains[1], shifts[1]
    )
    active_two = (jax.nn.gelu(stats_two[0]) * valid_mask).astype(low)
    hidden_three = jnp.dot(active_two, w_expand, preferred_element_type=wide)
    stats_three = norm(
        hidden_three,
        links.sums(masked_sums(hidden_three, valid_mask), "sums_three"),
        gains[2],
        shifts[2],
    )
    before_act = stats_three[0] + inputs.astype(wide)
    shared = (jax.nn.gelu(before_act) * valid_mask).astype(low)

    shared_slice = links.swap(
        shared.reshape(pixels, bands, slice_width).transpose(1, 0, 2), "swap_shared"
    ).reshape(all_pixels, slice_width)
    pixel_sum = jnp.sum(shared_slice.astype(wide), axis=0)
    branch_local = branch_weight[0]
    inv_block = jnp.broadcast_to(1.0 / pixel_count, (8, LANE))
    links.used += 1
    taps, (
        head_result,
        shared_grad,
        tap_grads,
        proj_term,
        pool_rows,
        both_sums,
        proj_sums,
    ) = head(
        tasks,
        bands,
        cols_count,
        rows_count,
        links.used - 1,
        shared_slice.reshape(bands, pixels, slice_width),
        jnp.broadcast_to(all_mask, (all_pixels, LANE)),
        inv_block,
        head_gain,
        head_shift,
        head_cot.reshape(pixels, head_width),
        branch_local,
        proj_weight[0],
        rate_weight[0],
    )
    pool_weight_grad = pixel_sum[:, None] * pool_rows[0:1] / pixel_count
    branch_grad = jnp.concatenate([tap_grads[len(taps)].astype(wide), pool_weight_grad], axis=1)
    place_of = {tap[:3]: number for number, tap in enumerate(taps)}
    nothing = jnp.zeros((slice_width, head_width), wide)
    rate_grad = jnp.concatenate(
        [
            tap_grads[place_of[level, row_tap, col_tap]].astype(wide)
            if (level, row_tap, col_tap) in place_of
            else nothing
            for level in (1, 2, 3)
            for row_tap in range(3)
            for col_tap in range(3)
        ],
        axis=1,
    )
    head_sums = [
        jnp.concatenate([both, proj])
        for both, proj in zip(
            both_sums.reshape(-1)[: 8 * head_width].reshape(2, -1),
            proj_sums.reshape(-1)[: 2 * head_width].reshape(2, -1),
        )
    ]

    def vectors(stats, number):
        return jnp.concatenate(
            [
                jnp.stack([stats[3], stats[2], gains[number], shifts[number]]),
                jnp.zeros((4, stats[3].size), wide),
            ]
        )

    links.used += 1
    (
        weight_rows,
        input_grad,
        w_reduce_grad,
        dilated_grad,
        w_expand_grad,
        sums_three,
        sums_two,
        sums_one,
        proj_grad,
    ) = trunk_back(
        tasks,
        bands,
        cols_count,
        links.used - 1,
        shared_grad,
        hidden_three,
        inputs,
        vectors(stats_three, 2),
        hidden_two,
        vectors(stats_two, 1),
        hidden_one,
        vectors(stats_one, 0),
        rim.reshape(3, pixels, middle_width),
        active_two,
        jnp.broadcast_to(valid_mask, (pixels, LANE)),
        inv_block,
        w_expand,
        w_dilated.transpose(1, 0, 2),
        w_reduce,
        proj_term.reshape(bands, -1, head_width),
    )
    proj_grad = proj_grad.reshape(-1, head_width)
    task_weight = weight_rows[:tasks, 0]
    w_dilated_grad = dilated_grad.transpose(1, 0, 2)
    sums_three, sums_two, sums_one = (
        value.reshape(2, -1) for value in (sums_three, sums_two, sums_one)
    )
    means = jnp.concatenate([stats_one[3], stats_two[3], stats_three[3]])
    variances = (
        jnp.concatenate([stats_one[4], stats_two[4], stats_three[4]])
        * pixel_count
        / (pixel_count - 1.0)
    )
    return (
        head_result.reshape(1, band_rows, cols_count, head_width),
        input_grad.reshape(band_rows, cols_count, in_width),
        w_reduce_grad,
        w_dilated_grad,
        w_expand_grad,
        jnp.concatenate([sums_one[1], sums_two[1], sums_three[1]]),
        jnp.concatenate([sums_one[0], sums_two[0], sums_three[0]]),
        jnp.stack([means, variances]),
        branch_grad[None],
        rate_grad[None],
        proj_grad[None],
        head_sums[1][None],
        head_sums[0][None],
        task_weight,
    )


def solution(mesh):
    body = per_device_slices if mesh.shape["space"] == 8 else per_device
    return jax.shard_map(
        body,
        mesh=mesh,
        in_specs=(
            P("space", None, None),
            P(),
            P(),
            P(),
            P(),
            P(),
            P(),
            P("task", "space", None),
            P("task", "space", None),
            P("task", None, None),
            P("task", None),
            P("task", None),
            P("task", "space", None, None),
        ),
        out_specs=(
            P("task", "space", None, None),
            P("space", None, None),
            P("space", None),
            P("space", None, None),
            P("space", None),
            P(),
            P(),
            P(),
            P("task", "space", None),
            P("task", "space", None),
            P("task", None, None),
            P("task", None),
            P("task", None),
            P(),
        ),
        check_vma=False,
    )
```

```python
import functools

import jax
import jax.numpy as jnp
from jax import lax
from jax.experimental import pallas as pl
from jax.experimental.pallas import tpu as pltpu
from jax.sharding import PartitionSpec as P

CONV_DILATION = 2
RATE = 12


NORM_EPS = 1e-05
GRAM_EPS = 1e-06
PRECISE = lax.Precision.HIGHEST


def with_halo(block, sides, width):
    for axis, dim in sides:
        count = lax.axis_size(axis)
        forward = [(i, i + 1) for i in range(count - 1)]
        backward = [(target, source) for source, target in forward]
        low = lax.ppermute(
            lax.slice_in_dim(block, block.shape[dim] - width, None, axis=dim), axis, forward
        )
        high = lax.ppermute(lax.slice_in_dim(block, 0, width, axis=dim), axis, backward)
        block = jnp.concatenate([low, block, high], axis=dim)
    return block


def from_behind(shard, axis, by):
    count = lax.axis_size(axis)
    pairs = [(i, i + by) for i in range(count) if 0 <= i + by < count]
    return lax.ppermute(shard, axis, pairs)


def small_solve(matrix, target):
    size_n = matrix.shape[0]
    rows_list = [matrix[number] for number in range(size_n)]
    values = [target[number] for number in range(size_n)]
    for pivot_row in range(size_n):
        for lower_row in range(pivot_row + 1, size_n):
            factor = rows_list[lower_row][pivot_row] / rows_list[pivot_row][pivot_row]
            rows_list[lower_row] = rows_list[lower_row] - factor * rows_list[pivot_row]
            values[lower_row] = values[lower_row] - factor * values[pivot_row]
    answer = [None] * size_n
    for pivot_row in reversed(range(size_n)):
        running = values[pivot_row]
        for later_row in range(pivot_row + 1, size_n):
            running = running - rows_list[pivot_row][later_row] * answer[later_row]
        answer[pivot_row] = running / rows_list[pivot_row][pivot_row]
    return jnp.stack(answer)


def imtl_weights(gram_matrix):
    grad_norms = jnp.sqrt(jnp.diagonal(gram_matrix) + GRAM_EPS)
    projections = gram_matrix / grad_norms[None, :]
    system = projections[0, 0] - projections[0:1, 1:] - projections[1:, 0:1] + projections[1:, 1:]
    target = projections[0, 0] - projections[0, 1:]
    other_weights = small_solve(jnp.transpose(system), target)
    return jnp.concatenate([(1.0 - jnp.sum(other_weights))[None], other_weights])


def gelu_back(value, upstream):
    return jax.vjp(jax.nn.gelu, value)[1](upstream)[0]


def channel_sums(members):
    return lax.psum(members, "space")


def norm_values(hidden, first_total, second_total, gain_vec, shift_vec, pixel_count):
    mean_value = first_total / pixel_count
    variance = second_total / pixel_count - mean_value * mean_value
    inv_std = lax.rsqrt(variance + NORM_EPS)
    scaled = (hidden - mean_value) * inv_std
    return (gain_vec * scaled + shift_vec, scaled, inv_std, mean_value, variance)


def norm_forward(hidden, gain_vec, shift_vec, valid_mask, pixel_count):
    totals = channel_sums(
        (jnp.sum(hidden * valid_mask, axis=0), jnp.sum(hidden * hidden * valid_mask, axis=0))
    )
    return norm_values(hidden, totals[0], totals[1], gain_vec, shift_vec, pixel_count)


def norm_finish(
    upstream, scaled, inv_std, gain_vec, gain_grad, shift_grad, valid_mask, pixel_count
):
    return (
        valid_mask
        * gain_vec
        * inv_std
        * (upstream - shift_grad / pixel_count - scaled * gain_grad / pixel_count)
    )


def norm_backward(upstream, scaled, inv_std, gain_vec, valid_mask, pixel_count):
    totals = channel_sums(
        (jnp.sum(upstream * valid_mask, axis=0), jnp.sum(upstream * scaled * valid_mask, axis=0))
    )
    hidden_grad = norm_finish(
        upstream, scaled, inv_std, gain_vec, totals[1], totals[0], valid_mask, pixel_count
    )
    return (hidden_grad, totals[1], totals[0])


def band_rim(strip_image):
    return with_halo(strip_image, (("space", 0),), CONV_DILATION)


def far_rows(strip_image, bands_away, upward):
    if bands_away >= lax.axis_size("space"):
        return jnp.zeros_like(strip_image)
    if upward:
        return from_behind(strip_image, "space", bands_away)
    return from_behind(strip_image, "space", -bands_away)


def trunk_taps(padded, reach_cells, rows_count, cols_count, flipped):
    col_padded = jnp.pad(padded, ((0, 0), (reach_cells, reach_cells), (0, 0)))
    pieces = []
    for row_tap in range(3):
        for col_tap in range(3):
            row_from = (2 - row_tap) * reach_cells if flipped else row_tap * reach_cells
            col_from = (2 - col_tap) * reach_cells if flipped else col_tap * reach_cells
            pieces.append(
                col_padded[
                    row_from : row_from + rows_count, col_from : col_from + cols_count
                ].reshape(rows_count * cols_count, -1)
            )
    return jnp.stack(pieces, axis=1)


def per_device(
    features,
    row_width,
    w_reduce,
    w_dilated,
    w_expand,
    trunk_gain,
    trunk_shift,
    branch_weight,
    rate_weight,
    proj_weight,
    head_gain,
    head_shift,
    head_cot,
):
    band_rows, cols_count, in_width = features.shape
    pixels = band_rows * cols_count
    middle_width = w_reduce.shape[1]
    head_width = proj_weight.shape[2]
    first_row = lax.axis_index("space") * band_rows
    widths = lax.dynamic_slice_in_dim(row_width, first_row, band_rows)
    valid_mask = (
        (jnp.arange(cols_count)[None, :] < widths[:, None]).astype(jnp.float32).reshape(pixels, 1)
    )
    pixel_count = jnp.sum(row_width).astype(jnp.float32)
    inputs = features.reshape(pixels, in_width)
    gain_one, shift_one = (trunk_gain[:middle_width], trunk_shift[:middle_width])
    gain_two, shift_two = (
        trunk_gain[middle_width : 2 * middle_width],
        trunk_shift[middle_width : 2 * middle_width],
    )
    gain_three, shift_three = (trunk_gain[2 * middle_width :], trunk_shift[2 * middle_width :])
    hidden_one = jnp.dot(inputs, w_reduce, preferred_element_type=jnp.float32)
    stats_one = norm_forward(hidden_one, gain_one, shift_one, valid_mask, pixel_count)
    first_active = (jax.nn.gelu(stats_one[0]) * valid_mask).astype(jnp.bfloat16)
    patches = trunk_taps(
        band_rim(first_active.reshape(band_rows, cols_count, middle_width)),
        CONV_DILATION,
        band_rows,
        cols_count,
        False,
    )
    hidden_two = jnp.einsum("pti,ito->po", patches, w_dilated, preferred_element_type=jnp.float32)
    stats_two = norm_forward(hidden_two, gain_two, shift_two, valid_mask, pixel_count)
    active_two = (jax.nn.gelu(stats_two[0]) * valid_mask).astype(jnp.bfloat16)
    hidden_three = jnp.dot(active_two, w_expand, preferred_element_type=jnp.float32)
    stats_three = norm_forward(hidden_three, gain_three, shift_three, valid_mask, pixel_count)
    before_act = stats_three[0] + inputs.astype(jnp.float32)
    shared = (jax.nn.gelu(before_act) * valid_mask).astype(jnp.bfloat16)
    proj_local = proj_weight[0]
    gain_local = head_gain[0]
    shift_local = head_shift[0]
    joined_weight = jnp.concatenate([branch_weight[0], rate_weight[0]], axis=1)
    pixel_sum = jnp.dot(
        valid_mask.reshape(1, pixels).astype(jnp.bfloat16),
        shared,
        preferred_element_type=jnp.float32,
    )[0]
    shared_image = shared.reshape(band_rows, cols_count, in_width)
    padded_sources = []
    for level in (1, 2, 3):
        reach = level * RATE
        bands_away = reach // band_rows
        triple = (
            far_rows(shared_image, bands_away, True),
            shared_image,
            far_rows(shared_image, bands_away, False),
        )
        padded_sources.append(
            [jnp.pad(source, ((0, 0), (reach, reach), (0, 0))) for source in triple]
        )
    zero_rows = jnp.zeros((pixels, head_width), jnp.float32)
    start_totals = (
        zero_rows,
        jnp.zeros((1, head_width), jnp.float32),
        zero_rows,
        zero_rows,
        zero_rows,
    )
    all_weights = lax.all_gather(joined_weight, "space", axis=0, tiled=True)
    width_now = all_weights.shape[0]
    one_acc = jnp.dot(shared, all_weights[:, :head_width], preferred_element_type=jnp.float32)
    pool_cols = pixel_sum[None]
    pool_acc = jnp.dot(
        pool_cols,
        all_weights[:, head_width : 2 * head_width].astype(jnp.float32),
        precision=PRECISE,
        preferred_element_type=jnp.float32,
    )
    rate_accs = []
    for fold_level_index in range(3):
        fold_reach = (fold_level_index + 1) * RATE
        running = start_totals[2 + fold_level_index]
        for fold_row_tap in range(3):
            fold_source = padded_sources[fold_level_index][fold_row_tap]
            for fold_col_tap in range(3):
                window = fold_source[
                    :, fold_col_tap * fold_reach : fold_col_tap * fold_reach + cols_count
                ].reshape(pixels, width_now)
                column = (2 + 9 * fold_level_index + 3 * fold_row_tap + fold_col_tap) * head_width
                running = running + jnp.dot(
                    window,
                    all_weights[:, column : column + head_width],
                    preferred_element_type=jnp.float32,
                )
        rate_accs.append(running)
    pre_both = jnp.concatenate([one_acc, rate_accs[0], rate_accs[1], rate_accs[2]], axis=1)
    gain_both, shift_both = (gain_local[: 4 * head_width], shift_local[: 4 * head_width])
    totals = channel_sums(
        (
            jnp.sum(pre_both * valid_mask, axis=0),
            jnp.sum(pre_both * pre_both * valid_mask, axis=0),
            pool_acc[0],
        )
    )
    stats_both = norm_values(pre_both, totals[0], totals[1], gain_both, shift_both, pixel_count)
    pooled = totals[2][None] / pixel_count
    active_both = (jax.nn.gelu(stats_both[0]) * valid_mask).astype(jnp.bfloat16)
    active_pool = jax.nn.gelu(pooled).astype(jnp.bfloat16)
    joined = jnp.concatenate(
        [active_both, (active_pool.astype(jnp.float32) * valid_mask).astype(jnp.bfloat16)], axis=1
    )
    projected = jnp.dot(joined, proj_local, preferred_element_type=jnp.float32)
    gain_proj = gain_local[4 * head_width :]
    stats_proj = norm_forward(
        projected, gain_proj, shift_local[4 * head_width :], valid_mask, pixel_count
    )
    head_result = (jax.nn.gelu(stats_proj[0]) * valid_mask).astype(jnp.bfloat16)
    cot_rows = head_cot[0].reshape(pixels, head_width).astype(jnp.float32)
    proj_upstream = gelu_back(stats_proj[0], cot_rows * valid_mask)
    proj_hidden, proj_gain_grad, proj_shift_grad = norm_backward(
        proj_upstream, stats_proj[1], stats_proj[2], gain_proj, valid_mask, pixel_count
    )
    proj_low = proj_hidden.astype(jnp.bfloat16)
    joined_grad = lax.dot_general(
        proj_low, proj_local, (((1,), (1,)), ((), ())), preferred_element_type=jnp.float32
    )
    proj_term = lax.dot_general(
        joined, proj_low, (((0,), (0,)), ((), ())), preferred_element_type=jnp.float32
    )
    both_upstream = gelu_back(stats_both[0], joined_grad[:, : 4 * head_width] * valid_mask)
    pool_total = jnp.sum(joined_grad[:, 4 * head_width :] * valid_mask, axis=0)
    back_totals = channel_sums(
        (
            proj_term,
            pool_total,
            jnp.sum(both_upstream * valid_mask, axis=0),
            jnp.sum(both_upstream * stats_both[1] * valid_mask, axis=0),
        )
    )
    pool_grad = gelu_back(pooled, back_totals[1][None]).astype(jnp.bfloat16)
    both_grad = norm_finish(
        both_upstream,
        stats_both[1],
        stats_both[2],
        gain_both,
        back_totals[3],
        back_totals[2],
        valid_mask,
        pixel_count,
    ).astype(jnp.bfloat16)
    tap_grads = []
    for level_index in range(3):
        reach = (level_index + 1) * RATE
        bands_away = reach // band_rows
        rate_image = both_grad[
            :, (1 + level_index) * head_width : (2 + level_index) * head_width
        ].reshape(band_rows, cols_count, head_width)
        back_sources = [
            jnp.pad(source, ((0, 0), (reach, reach), (0, 0)))
            for source in (
                far_rows(rate_image, bands_away, False),
                rate_image,
                far_rows(rate_image, bands_away, True),
            )
        ]
        for row_tap in range(3):
            for col_tap in range(3):
                tap_grads.append(
                    back_sources[row_tap][
                        :, (2 - col_tap) * reach : (2 - col_tap) * reach + cols_count
                    ].reshape(pixels, head_width)
                )
    right_side = jnp.concatenate([both_grad[:, :head_width]] + tap_grads, axis=1)
    used_rows = jnp.concatenate(
        [all_weights[:, :head_width], all_weights[:, 2 * head_width :]], axis=1
    )
    main_part = lax.dot_general(
        right_side, used_rows, (((1,), (1,)), ((), ())), preferred_element_type=jnp.float32
    )
    pool_part = lax.dot_general(
        pool_grad,
        all_weights[:, head_width : 2 * head_width],
        (((1,), (1,)), ((), ())),
        preferred_element_type=jnp.float32,
    )
    shared_grad = (main_part + valid_mask * pool_part / pixel_count).astype(jnp.bfloat16)
    head_term = lax.dot_general(
        shared, right_side, (((0,), (0,)), ((), ())), preferred_element_type=jnp.float32
    )
    pool_term = pixel_sum[:, None] * pool_grad.astype(jnp.float32) / pixel_count
    head_term = jnp.concatenate(
        [head_term[:, :head_width], pool_term, head_term[:, head_width:]], axis=1
    )
    all_grads = lax.all_gather(shared_grad[None], "task", axis=0, tiled=True)
    flat_grads = all_grads.reshape(all_grads.shape[0], -1)
    gram_matrix = lax.psum(
        lax.dot_general(
            flat_grads, flat_grads, (((1,), (1,)), ((), ())), preferred_element_type=jnp.float32
        ),
        "space",
    )
    task_weight = imtl_weights(gram_matrix)
    mixed_grad = task_weight[0] * all_grads[0].astype(jnp.float32)
    for task_index in range(1, all_grads.shape[0]):
        mixed_grad = mixed_grad + task_weight[task_index] * all_grads[task_index].astype(
            jnp.float32
        )
    combined = mixed_grad.astype(jnp.bfloat16)
    gate_grad = gelu_back(before_act, combined.astype(jnp.float32) * valid_mask)
    hidden_grad_three, gain_grad_three, shift_grad_three = norm_backward(
        gate_grad, stats_three[1], stats_three[2], gain_three, valid_mask, pixel_count
    )
    low_three = hidden_grad_three.astype(jnp.bfloat16)
    expand_term = lax.dot_general(
        active_two, low_three, (((0,), (0,)), ((), ())), preferred_element_type=jnp.float32
    )
    active_grad_two = lax.dot_general(
        low_three, w_expand, (((1,), (1,)), ((), ())), preferred_element_type=jnp.float32
    )
    upstream_two = gelu_back(stats_two[0], active_grad_two * valid_mask)
    hidden_grad_two, gain_grad_two, shift_grad_two = norm_backward(
        upstream_two, stats_two[1], stats_two[2], gain_two, valid_mask, pixel_count
    )
    low_two = hidden_grad_two.astype(jnp.bfloat16)
    dilated_term = jnp.einsum("pti,po->ito", patches, low_two, preferred_element_type=jnp.float32)
    back_patches = trunk_taps(
        band_rim(low_two.reshape(band_rows, cols_count, middle_width)),
        CONV_DILATION,
        band_rows,
        cols_count,
        True,
    )
    active_grad_one = jnp.einsum(
        "pto,ito->pi", back_patches, w_dilated, preferred_element_type=jnp.float32
    )
    upstream_one = gelu_back(stats_one[0], active_grad_one * valid_mask)
    hidden_grad_one, gain_grad_one, shift_grad_one = norm_backward(
        upstream_one, stats_one[1], stats_one[2], gain_one, valid_mask, pixel_count
    )
    low_one = hidden_grad_one.astype(jnp.bfloat16)
    reduce_term = lax.dot_general(
        inputs, low_one, (((0,), (0,)), ((), ())), preferred_element_type=jnp.float32
    )
    input_grad = (
        lax.dot_general(
            low_one, w_reduce, (((1,), (1,)), ((), ())), preferred_element_type=jnp.float32
        )
        + gate_grad
    )
    reduced = (
        lax.psum_scatter(head_term, "space", scatter_dimension=0, tiled=True),
        lax.psum_scatter(reduce_term, "space", scatter_dimension=0, tiled=True),
        lax.psum_scatter(dilated_term, "space", scatter_dimension=0, tiled=True),
        lax.psum_scatter(expand_term, "space", scatter_dimension=0, tiled=True),
    )
    means = jnp.concatenate([stats_one[3], stats_two[3], stats_three[3]])
    variances = (
        jnp.concatenate([stats_one[4], stats_two[4], stats_three[4]])
        * pixel_count
        / (pixel_count - 1.0)
    )
    batch_stats = jnp.stack([means, variances])
    head_gain_grad = jnp.concatenate([back_totals[3], proj_gain_grad])[None]
    head_shift_grad = jnp.concatenate([back_totals[2], proj_shift_grad])[None]
    return (
        head_result.reshape(1, band_rows, cols_count, head_width),
        input_grad.reshape(band_rows, cols_count, in_width).astype(jnp.bfloat16),
        reduced[1],
        reduced[2],
        reduced[3],
        jnp.concatenate([gain_grad_one, gain_grad_two, gain_grad_three]),
        jnp.concatenate([shift_grad_one, shift_grad_two, shift_grad_three]),
        batch_stats,
        reduced[0][:, : 2 * head_width][None],
        reduced[0][:, 2 * head_width :][None],
        back_totals[0][None],
        head_gain_grad,
        head_shift_grad,
        task_weight,
    )


MESH_ID = pl.DeviceIdType.MESH
LANE = 128


GELU_A = 0.7978845608028654
GELU_B = 0.044715


def gelu_of(value):
    return 0.5 * value * (1.0 + jnp.tanh(GELU_A * (value + GELU_B * value * value * value)))


def gelu_slope(value):
    square = value * value
    bend = jnp.tanh(GELU_A * value * (1.0 + GELU_B * square))
    return 0.5 * (1.0 + bend) + 0.5 * value * (1.0 - bend * bend) * (
        GELU_A * (1.0 + 3.0 * GELU_B * square)
    )


def dot_nn(left_side, right_side):
    return jnp.dot(left_side, right_side, preferred_element_type=jnp.float32)


def dot_nt(left_side, right_side):
    return lax.dot_general(
        left_side, right_side, (((1,), (1,)), ((), ())), preferred_element_type=jnp.float32
    )


def shift_pixels(value, by, cols):
    if by == 0:
        return value
    rows = value.shape[0]
    column = lax.rem(lax.broadcasted_iota(jnp.int32, value.shape, 0), cols) + by
    rolled = pltpu.roll(value, (-by) % rows, 0)
    return jnp.where((column >= 0) & (column < cols), rolled, 0.0)


def row_mask(widths_ref, first_row, rows, cols):
    column = lax.broadcasted_iota(jnp.int32, (cols, LANE), 0)
    return jnp.concatenate(
        [
            jnp.where(column < widths_ref[first_row + number], 1.0, 0.0).astype(jnp.float32)
            for number in range(rows)
        ],
        axis=0,
    )


def count_pixels(widths_ref):
    total = widths_ref[0]
    for number in range(1, widths_ref.shape[0]):
        total = total + widths_ref[number]
    return jnp.full((1, LANE), total.astype(jnp.float32), jnp.float32)


class Post:
    def __init__(self, send_sem, recv_sem):
        self.send_sem, self.recv_sem = send_sem, recv_sem
        self.used = 0
        self.sent = []

    def copy(self, source, target, device):
        made = pltpu.make_async_remote_copy(
            source,
            target,
            self.send_sem.at[self.used],
            self.recv_sem.at[self.used],
            device_id=device,
            device_id_type=MESH_ID,
        )
        self.used += 1
        return made

    def push(self, source, target, device):
        made = self.copy(source, target, device)
        made.start()
        self.sent.append(made)
        return made

    def close(self):
        for made in self.sent:
            made.wait_send()


class Place:
    def __init__(self, tasks, bands):
        self.tasks, self.bands, self.chips = tasks, bands, bands // 2
        self.task = lax.axis_index("task")
        self.band = lax.axis_index("space")
        self.chip = self.band // 2
        self.core = lax.rem(self.band, 2)
        self.twin = {"space": self.chip * 2 + 1 - self.core}
        low, high = lax.rem(self.task, 2), self.task // 2
        self.other_tasks = [(1 - high) * 2 + 1 - low, high * 2 + 1 - low, (1 - high) * 2 + low]
        self.other_bands = [lax.rem(self.band + step, bands) for step in range(1, bands)]

    def meet(self, with_tasks, with_bands):
        barrier = pltpu.get_barrier_semaphore()
        greeted = []
        if with_tasks:
            greeted += [{"task": task} for task in self.other_tasks]
        if with_bands:
            greeted += [{"space": band} for band in self.other_bands]
        for device in greeted:
            pl.semaphore_signal(barrier, inc=1, device_id=device, device_id_type=MESH_ID)
        pl.semaphore_wait(barrier, len(greeted))

    def sum_begin(self, post, axis, own_ref, land_ref):
        mine = self.task if axis == "task" else self.band
        others = self.other_tasks if axis == "task" else self.other_bands
        copies = [post.push(own_ref, land_ref.at[mine], {axis: other}) for other in others]
        land_ref[pl.ds(mine, 1)] = own_ref[...][None]
        return copies, land_ref

    def sum_end(self, begun):
        copies, land_ref = begun
        for made in copies:
            made.wait_recv()
        total = land_ref[0]
        for slot in range(1, len(copies) + 1):
            total = total + land_ref[slot]
        return total

    def sum_over(self, post, axis, own_ref, land_ref):
        return self.sum_end(self.sum_begin(post, axis, own_ref, land_ref))


def trunk_back_kernel(
    sizes,
    sg_ref,
    h3q,
    x_ref,
    v3_ref,
    h2_ref,
    v2_ref,
    h1_ref,
    v1_ref,
    a1_ref,
    a2_ref,
    widths_ref,
    we_hbm,
    wd_hbm,
    wr_hbm,
    pt_ref,
    tw_out,
    ig_out,
    rg_out,
    dg_out,
    eg_out,
    s3_out,
    s2_out,
    s1_out,
    pg_out,
    we,
    wd,
    wr,
    mask_ref,
    xq,
    xg,
    gram_own,
    gram_land,
    gram_mid,
    gram_land_b,
    comb,
    comb_land,
    gate,
    scaled,
    gate_low,
    gate_band,
    st3,
    st3_land,
    st3_mid,
    st3_land_b,
    l3,
    l3x,
    st2,
    st2_land,
    st2_mid,
    st2_land_b,
    l2,
    l2_halo,
    ag1,
    st1,
    st1_land,
    l1,
    xt,
    a1t,
    a2t,
    e_term,
    e_twin,
    e_land,
    e_share,
    e_tasks,
    d_term,
    d_twin,
    d_land,
    d_share,
    d_tasks,
    r_term,
    r_twin,
    r_land,
    r_share,
    r_tasks,
    p_twin,
    p_land,
    p_all,
    send_sem,
    recv_sem,
    local_sem,
):
    tasks, bands, cols, quarter, mid, wide, piece = sizes
    low = jnp.bfloat16
    f32 = jnp.float32
    at = Place(tasks, bands)
    post = Post(send_sem, recv_sem)
    task, band = at.task, at.band
    my_rows = pl.ds(pl.multiple_of(task * quarter, quarter), quarter)
    loads = [
        pltpu.make_async_copy(x_ref.at[my_rows], xq, local_sem.at[0]),
        pltpu.make_async_copy(we_hbm, we, local_sem.at[1]),
        pltpu.make_async_copy(wd_hbm, wd, local_sem.at[2]),
        pltpu.make_async_copy(wr_hbm, wr, local_sem.at[3]),
    ]
    for load in loads:
        load.start()
    at.meet(True, True)

    grads_in = []
    for other in at.other_tasks:
        theirs = pl.ds(pl.multiple_of(other * quarter, quarter), quarter)
        grads_in.append(post.push(sg_ref.at[:, theirs], xg.at[task], {"task": other}))
    own_copy = pltpu.make_async_copy(sg_ref.at[:, my_rows], xg.at[task], local_sem.at[4])
    own_copy.start()

    p_pair = [
        post.push(pt_ref.at[2 * number + 1 - at.core], p_twin.at[number], at.twin)
        for number in range(at.chips)
    ]

    band_rows = x_ref.shape[0] // cols
    mask_ref[...] = row_mask(widths_ref, band * band_rows, band_rows, cols)

    for number in range(3):
        a1t[number] = a1_ref[number].T
    a2t[...] = a2_ref[...].T

    def turn_inputs(number, carry):
        lanes = pl.ds(pl.multiple_of(number * piece, piece), piece)
        xt[lanes, :] = x_ref[:, lanes].T
        return carry

    lax.fori_loop(0, wide // piece, turn_inputs, 0)
    for made in p_pair:
        made.wait_recv()
    p_in = []
    for step in range(1, at.chips):
        other = lax.rem(at.chip + step, at.chips)
        both = pt_ref[2 * other + at.core].astype(f32) + p_twin[other].astype(f32)
        p_twin[other] = both.astype(low)
        p_in.append(
            post.push(p_twin.at[other], p_land.at[at.chip], {"space": other * 2 + at.core})
        )
    own_copy.wait()
    for made in grads_in:
        made.wait_recv()

    pairs = [(a, b) for a in range(tasks) for b in range(a, tasks)]

    def gram_step(number, totals):
        grads = [xg[a, number].astype(f32) for a in range(tasks)]
        out = []
        for (a, b), total in zip(pairs, totals):
            product = grads[a] * grads[b]
            product = product.reshape(quarter // 8, 8, piece).sum(axis=0)
            for start in range(0, piece, LANE):
                total = total + product[:, start : start + LANE]
            out.append(total)
        return tuple(out)

    totals = lax.fori_loop(
        0, bands, gram_step, tuple(jnp.zeros((8, LANE), f32) for _ in pairs)
    )
    gram_own[...] = jnp.zeros_like(gram_own)
    for number, total in enumerate(totals):
        gram_own[number : number + 1] = jnp.sum(total, axis=0, keepdims=True)
    p_total = pt_ref[band].astype(f32) + p_twin[at.chip].astype(f32)
    for made in p_in:
        made.wait_recv()
    for step in range(1, at.chips):
        p_total = p_total + p_land[lax.rem(at.chip + step, at.chips)].astype(f32)
    p_all[pl.ds(band, 1)] = p_total.astype(low)[None]
    p_block = p_all.at[band]
    p_near = post.push(p_block, p_block, at.twin)
    p_far = [
        post.push(
            p_block,
            p_block,
            {"space": lax.rem(at.chip + step, at.chips) * 2 + at.core},
        )
        for step in range(1, at.chips)
    ]
    gram_mid[...] = at.sum_over(post, "task", gram_own, gram_land)
    gram_sum = at.sum_over(post, "space", gram_mid, gram_land_b)
    gram_sum = jnp.broadcast_to(jnp.sum(gram_sum, axis=1, keepdims=True), gram_sum.shape)
    gram = [[None] * tasks for _ in range(tasks)]
    for number, (a, b) in enumerate(pairs):
        gram[a][b] = gram[b][a] = gram_sum[number : number + 1]
    norms = [jnp.sqrt(gram[a][a] + GRAM_EPS) for a in range(tasks)]
    cos = [[gram[a][b] / norms[b] for b in range(tasks)] for a in range(tasks)]
    rows_list = [
        [cos[0][0] - cos[0][l] - cos[k][0] + cos[k][l] for k in range(1, tasks)]
        for l in range(1, tasks)
    ]
    values = [cos[0][0] - cos[0][l] for l in range(1, tasks)]
    count = tasks - 1
    for pivot in range(count):
        for lower in range(pivot + 1, count):
            factor = rows_list[lower][pivot] / rows_list[pivot][pivot]
            rows_list[lower] = [
                under - factor * over for under, over in zip(rows_list[lower], rows_list[pivot])
            ]
            values[lower] = values[lower] - factor * values[pivot]
    answer = [None] * count
    for pivot in reversed(range(count)):
        running = values[pivot]
        for later in range(pivot + 1, count):
            running = running - rows_list[pivot][later] * answer[later]
        answer[pivot] = running / rows_list[pivot][pivot]
    rest = answer[0]
    for value in answer[1:]:
        rest = rest + value
    task_weight = [1.0 - rest] + answer
    for number in range(tasks):
        tw_out[number : number + 1] = task_weight[number]
    weights = [jnp.concatenate([value] * (piece // LANE), axis=1) for value in task_weight]

    def mixed(number):
        total = weights[0] * xg[0, number].astype(f32)
        for a in range(1, tasks):
            total = total + weights[a] * xg[a, number].astype(f32)
        return total.astype(low)

    comb_in = []
    for other in at.other_bands:
        comb[other] = mixed(other)
        comb_in.append(post.push(comb.at[other], comb_land.at[band], {"space": other}))
    comb_land[pl.ds(band, 1)] = mixed(band)[None]
    loads[0].wait()
    for made in comb_in:
        made.wait_recv()

    mask_quarter = mask_ref[my_rows]
    mask_piece = jnp.concatenate([mask_quarter] * (piece // LANE), axis=1)
    inv_count = 1.0 / count_pixels(widths_ref)
    inv_piece = jnp.concatenate([inv_count] * (piece // LANE), axis=1)
    per_row = st3.shape[1] // piece
    half = st3.shape[0] // 2

    def gate_step(number, carry):
        lanes = pl.ds(pl.multiple_of(number * piece, piece), piece)
        hat = (h3q[:, lanes] - v3_ref[0:1, lanes]) * v3_ref[1:2, lanes]
        before = v3_ref[2:3, lanes] * hat + v3_ref[3:4, lanes] + xq[:, lanes].astype(f32)
        grad = gelu_slope(before) * comb_land[number].astype(f32) * mask_piece
        gate[number] = grad
        scaled[number] = hat
        gate_low[number] = grad.astype(low)
        row = number // per_row
        spot = pl.ds(pl.multiple_of(lax.rem(number, per_row) * piece, piece), piece)
        st3[pl.ds(row, 1), spot] = jnp.sum(grad, axis=0, keepdims=True)
        st3[pl.ds(half + row, 1), spot] = jnp.sum(grad * hat, axis=0, keepdims=True)
        return carry

    lax.fori_loop(0, bands, gate_step, 0)
    st3_mid[...] = at.sum_over(post, "task", st3, st3_land)
    s3_out[...] = at.sum_over(post, "space", st3_mid, st3_land_b)

    def third_step(number, carry):
        lanes = pl.ds(pl.multiple_of(number * piece, piece), piece)
        row = number // per_row
        spot = pl.ds(pl.multiple_of(lax.rem(number, per_row) * piece, piece), piece)
        shift_grad = s3_out[pl.ds(row, 1), spot] * inv_piece
        gain_grad = s3_out[pl.ds(half + row, 1), spot] * inv_piece
        l3[number] = (
            mask_piece
            * (v3_ref[2:3, lanes] * v3_ref[1:2, lanes])
            * (gate[number] - shift_grad - scaled[number] * gain_grad)
        ).astype(low)
        return carry

    lax.fori_loop(0, bands, third_step, 0)
    per_task = bands // tasks
    l3_in = []
    for other in at.other_tasks:
        l3_in.append(
            post.push(l3.at[pl.ds(other * per_task, per_task)], l3x.at[task], {"task": other})
        )
    l3x[pl.ds(task, 1)] = l3[pl.ds(task * per_task, per_task)][None]
    loads[1].wait()

    def expand_step(number, total):
        lanes = pl.ds(pl.multiple_of(number * piece, piece), piece)
        return total + dot_nt(l3[number], we[:, lanes])

    ag2 = lax.fori_loop(0, bands, expand_step, jnp.zeros((quarter, mid), f32))

    mask_mid = jnp.concatenate([mask_quarter] * (mid // LANE), axis=1)
    inv_mid = jnp.concatenate([inv_count] * (mid // LANE), axis=1)
    hat = (h2_ref[my_rows] - v2_ref[0:1]) * v2_ref[1:2]
    grad = gelu_slope(v2_ref[2:3] * hat + v2_ref[3:4]) * ag2 * mask_mid
    spread = mid // LANE

    def put_sums(target, first, second):
        for number in range(spread):
            lanes = slice(number * LANE, (number + 1) * LANE)
            target[number : number + 1] = first[:, lanes]
            target[spread + number : spread + number + 1] = second[:, lanes]

    def get_sums(total):
        return [
            jnp.concatenate([total[base + k : base + k + 1] for k in range(spread)], axis=1)
            for base in (0, spread)
        ]

    def to_twin(term, landing):
        return post.push(term.at[1 - at.core], landing, at.twin)

    def both_cores(pair, term, twin):
        pair.wait_recv()
        for step in range(1, at.chips):
            other = lax.rem(at.chip + step, at.chips)
            both = term[at.core, other].astype(f32) + twin[other].astype(f32)
            twin[other] = both.astype(low)

    def along(twin, landing):
        return [
            post.push(
                twin.at[other], landing.at[at.chip], {"space": other * 2 + at.core}
            )
            for other in [lax.rem(at.chip + step, at.chips) for step in range(1, at.chips)]
        ]

    def settle(arrivals, term, twin, landing):
        total = term[at.core, at.chip].astype(f32) + twin[at.chip].astype(f32)
        for made in arrivals:
            made.wait_recv()
        for step in range(1, at.chips):
            total = total + landing[lax.rem(at.chip + step, at.chips)].astype(f32)
        return total.astype(low)

    def to_tasks(share, landing):
        arrivals = [post.push(share, landing.at[task], {"task": other}) for other in at.other_tasks]
        landing[pl.ds(task, 1)] = share[...][None]
        return arrivals

    def expand_part(number):
        share = jnp.concatenate([l3x[a, number] for a in range(tasks)], axis=0)
        part = dot_nn(a2t[...], share).astype(low)
        per_band = part.shape[0] // bands
        for target in range(bands):
            e_term[target % 2, target // 2, :, number * piece : (number + 1) * piece] = part[
                target * per_band : (target + 1) * per_band
            ]

    narrow = mid // tasks
    my_lanes = pl.ds(pl.multiple_of(task * narrow, narrow), narrow)
    put_sums(
        st2, jnp.sum(grad, axis=0, keepdims=True), jnp.sum(grad * hat, axis=0, keepdims=True)
    )
    begun = at.sum_begin(post, "task", st2, st2_land)
    for made in l3_in:
        made.wait_recv()
    expand_part(0)
    st2_mid[...] = at.sum_end(begun)
    begun = at.sum_begin(post, "space", st2_mid, st2_land_b)
    for number in range(1, per_task):
        expand_part(number)
    e_pair = to_twin(e_term, e_twin)
    s2_out[...] = at.sum_end(begun)
    shift_grad, gain_grad = get_sums(s2_out[...])
    l2[my_rows] = (
        mask_mid
        * (v2_ref[2:3] * v2_ref[1:2])
        * (grad - shift_grad * inv_mid - hat * (gain_grad * inv_mid))
    ).astype(low)
    l2_in = [post.push(l2.at[my_rows], l2.at[my_rows], {"task": other}) for other in at.other_tasks]
    both_cores(e_pair, e_term, e_twin)
    e_in = along(e_twin, e_land)
    for made in l2_in:
        made.wait_recv()
    gate_in = [
        post.push(gate_low, gate_band.at[task], {"task": other}) for other in at.other_tasks
    ]
    gate_band[pl.ds(task, 1)] = gate_low[...][None]
    has_above, has_below = band > 0, band < bands - 1
    up = post.copy(l2, l2_halo.at[1], {"space": lax.rem(band + bands - 1, bands)})
    down = post.copy(l2, l2_halo.at[0], {"space": lax.rem(band + 1, bands)})

    @pl.when(has_above)
    def _():
        up.start()

    @pl.when(has_below)
    def _():
        down.start()

    @pl.when(jnp.logical_not(has_above))
    def _():
        l2_halo[0] = jnp.zeros_like(l2)

    @pl.when(jnp.logical_not(has_below))
    def _():
        l2_halo[1] = jnp.zeros_like(l2)

    p_passed = []
    for step, made in enumerate(p_far, start=1):
        made.wait_recv()
        block = p_all.at[lax.rem(at.chip + at.chips - step, at.chips) * 2 + at.core]
        p_passed.append(post.push(block, block, at.twin))
    loads[2].wait()
    halves = [slice(start, start + piece) for start in range(0, mid, piece)]
    for lanes in halves:
        total = None
        for col_tap in range(3):
            part = shift_pixels(
                dot_nt(l2[...], wd[3 + col_tap, lanes, :]), -CONV_DILATION * (col_tap - 1), cols
            )
            total = part if total is None else total + part
        ag1[:, lanes] = total

    share_d = l2[:, my_lanes].astype(f32)
    for col_tap in range(3):
        moved = shift_pixels(share_d, -CONV_DILATION * (col_tap - 1), cols).astype(low)
        for row_tap in range(3):
            part = dot_nn(a1t[row_tap], moved).astype(low)
            per_band = part.shape[0] // bands
            for target in range(bands):
                d_term[target % 2, target // 2, 3 * row_tap + col_tap] = part[
                    target * per_band : (target + 1) * per_band
                ]
    d_pair = to_twin(d_term, d_twin)

    @pl.when(has_below)
    def _():
        up.wait_recv()

    @pl.when(has_above)
    def _():
        down.wait_recv()

    for lanes in halves:
        total = None
        for col_tap in range(3):
            part = dot_nt(l2_halo[1], wd[col_tap, lanes, :]) + dot_nt(
                l2_halo[0], wd[6 + col_tap, lanes, :]
            )
            part = shift_pixels(part, -CONV_DILATION * (col_tap - 1), cols)
            total = part if total is None else total + part
        ag1[:, lanes] += total

    pixels = ag1.shape[0]
    chunk = pixels // 8

    def first_rows(number):
        return pl.ds(pl.multiple_of(number * chunk, chunk), chunk)

    def first_step(number, sums):
        rows = first_rows(number)
        hat = (h1_ref[rows] - v1_ref[0:1]) * v1_ref[1:2]
        keep = jnp.concatenate([mask_ref[rows]] * spread, axis=1)
        grad = gelu_slope(v1_ref[2:3] * hat + v1_ref[3:4]) * ag1[rows] * keep
        ag1[rows] = grad
        return (
            sums[0] + jnp.sum(grad, axis=0, keepdims=True),
            sums[1] + jnp.sum(grad * hat, axis=0, keepdims=True),
        )

    nothing = jnp.zeros((1, mid), f32)
    first, second = lax.fori_loop(0, 8, first_step, (nothing, nothing))
    put_sums(st1, first, second)
    begun = at.sum_begin(post, "space", st1, st1_land)
    both_cores(d_pair, d_term, d_twin)
    e_share[...] = settle(e_in, e_term, e_twin, e_land)
    s1_out[...] = at.sum_end(begun)
    d_in = along(d_twin, d_land)
    shift_grad, gain_grad = get_sums(s1_out[...])
    shift_grad, gain_grad = shift_grad * inv_mid, gain_grad * inv_mid

    def first_finish(number, carry):
        rows = first_rows(number)
        hat = (h1_ref[rows] - v1_ref[0:1]) * v1_ref[1:2]
        keep = jnp.concatenate([mask_ref[rows]] * spread, axis=1)
        l1[rows] = (
            keep * (v1_ref[2:3] * v1_ref[1:2]) * (ag1[rows] - shift_grad - hat * gain_grad)
        ).astype(low)
        return carry

    lax.fori_loop(0, 8, first_finish, 0)

    share_r = l1[:, my_lanes]
    per_band_r = wide // bands

    def reduce_step(number, carry):
        rows = pl.ds(pl.multiple_of(number * per_band_r, per_band_r), per_band_r)
        r_term[lax.rem(number, 2), number // 2] = dot_nn(xt[rows, :], share_r).astype(low)
        return carry

    lax.fori_loop(0, bands, reduce_step, 0)
    r_pair = to_twin(r_term, r_twin)
    e_back = to_tasks(e_share, e_tasks)
    both_cores(r_pair, r_term, r_twin)
    r_in = along(r_twin, r_land)

    loads[3].wait()
    for made in gate_in:
        made.wait_recv()

    def input_step(number, carry):
        lanes = pl.ds(pl.multiple_of(number * piece, piece), piece)
        gates = jnp.concatenate([gate_band[a, number] for a in range(tasks)], axis=0).astype(f32)
        ig_out[:, lanes] = (dot_nt(l1[...], wr[lanes, :]) + gates).astype(low)
        return carry

    lax.fori_loop(0, bands, input_step, 0)
    d_share[...] = settle(d_in, d_term, d_twin, d_land)
    d_back = to_tasks(d_share, d_tasks)
    r_share[...] = settle(r_in, r_term, r_twin, r_land)
    r_back = to_tasks(r_share, r_tasks)
    for made in [p_near] + p_passed:
        made.wait_recv()
    pg_out[...] = p_all[...]
    for made in e_back:
        made.wait_recv()
    broad = wide // tasks
    for a in range(tasks):
        eg_out[:, a * broad : (a + 1) * broad] = e_tasks[a].astype(f32)
    for made in d_back:
        made.wait_recv()
    for a in range(tasks):
        dg_out[:, :, a * narrow : (a + 1) * narrow] = d_tasks[a].astype(f32)
    for made in r_back:
        made.wait_recv()
    for a in range(tasks):
        rg_out[:, a * narrow : (a + 1) * narrow] = r_tasks[a].astype(f32)
    post.close()

    @pl.when(has_above)
    def _():
        up.wait_send()

    @pl.when(has_below)
    def _():
        down.wait_send()


def trunk_back(
    tasks, bands, cols, collective, sg, h3, x, v3, h2, v2, h1, v1, a1, a2, widths, we, wd, wr, pt
):
    low, f32 = jnp.bfloat16, jnp.float32
    pixels, wide = x.shape
    mid = a2.shape[1]
    quarter = pixels // tasks
    piece = wide // bands
    narrow, broad = mid // tasks, wide // tasks
    chips = bands // 2
    part = mid // bands
    in_vmem = pl.BlockSpec(memory_space=pltpu.VMEM)
    anywhere = pl.BlockSpec(memory_space=pl.ANY)
    shape = jax.ShapeDtypeStruct

    def stats(rows, lanes):
        return [
            pltpu.VMEM((rows, lanes), f32),
            pltpu.VMEM((tasks, rows, lanes), f32),
            pltpu.VMEM((rows, lanes), f32),
            pltpu.VMEM((bands, rows, lanes), f32),
        ]

    def terms(*dims):
        return [
            pltpu.VMEM((2, chips) + dims, low),
            pltpu.VMEM((chips,) + dims, low),
            pltpu.VMEM((chips,) + dims, low),
            pltpu.VMEM(dims, low),
            pltpu.VMEM((tasks,) + dims, low),
        ]

    stat_wide = 2 * wide // 8
    scratch = (
        [
            pltpu.VMEM(we.shape, low),
            pltpu.VMEM(wd.shape, low),
            pltpu.VMEM(wr.shape, low),
            pltpu.VMEM((pixels, LANE), f32),
            pltpu.VMEM((quarter, wide), low),
            pltpu.VMEM((tasks, bands, quarter, piece), low),
        ]
        + stats(16, LANE)
        + [
            pltpu.VMEM((bands, quarter, piece), low),
            pltpu.VMEM((bands, quarter, piece), low),
            pltpu.VMEM((bands, quarter, piece), f32),
            pltpu.VMEM((bands, quarter, piece), f32),
            pltpu.VMEM((bands, quarter, piece), low),
            pltpu.VMEM((tasks, bands, quarter, piece), low),
        ]
        + stats(8, stat_wide)
        + [
            pltpu.VMEM((bands, quarter, piece), low),
            pltpu.VMEM((tasks, bands // tasks, quarter, piece), low),
        ]
        + stats(2 * mid // LANE, LANE)
        + [
            pltpu.VMEM((pixels, mid), low),
            pltpu.VMEM((2, pixels, mid), low),
            pltpu.VMEM((pixels, mid), f32),
            pltpu.VMEM((2 * mid // LANE, LANE), f32),
            pltpu.VMEM((bands, 2 * mid // LANE, LANE), f32),
            pltpu.VMEM((pixels, mid), low),
            pltpu.VMEM((wide, pixels), low),
            pltpu.VMEM((3, mid, pixels), low),
            pltpu.VMEM((mid, pixels), low),
        ]
        + terms(part, broad)
        + terms(9, part, narrow)
        + terms(piece, narrow)
        + [
            pltpu.VMEM((chips,) + pt.shape[1:], low),
            pltpu.VMEM((chips,) + pt.shape[1:], low),
            pltpu.VMEM(pt.shape, low),
            pltpu.SemaphoreType.DMA((96,)),
            pltpu.SemaphoreType.DMA((96,)),
            pltpu.SemaphoreType.DMA((6,)),
        ]
    )
    out_shapes = (
        shape((8, LANE), f32),
        shape((pixels, wide), low),
        shape((piece, mid), f32),
        shape((9, part, mid), f32),
        shape((part, wide), f32),
        shape((8, stat_wide), f32),
        shape((2 * mid // LANE, LANE), f32),
        shape((2 * mid // LANE, LANE), f32),
        shape(pt.shape, low),
    )
    return pl.pallas_call(
        functools.partial(trunk_back_kernel, (tasks, bands, cols, quarter, mid, wide, piece)),
        name="trunk_back",
        out_shape=out_shapes,
        in_specs=[in_vmem] * 10
        + [pl.BlockSpec(memory_space=pltpu.SMEM)]
        + [anywhere] * 3
        + [in_vmem],
        out_specs=(in_vmem,) * 9,
        scratch_shapes=scratch,
        compiler_params=pltpu.CompilerParams(
            collective_id=collective, has_side_effects=True, vmem_limit_bytes=27 << 20
        ),
    )(sg, h3, x, v3, h2, v2, h1, v1, a1, a2, widths, we, wd, wr, pt)


def head_kernel(
    plan,
    sh_ref,
    widths_ref,
    gain_ref,
    shift_ref,
    cot_ref,
    bw_ref,
    pw_ref,
    rate_hbm,
    head_out,
    sg_out,
    grads_out,
    proj_out,
    both_sums_out,
    proj_sums_out,
    rate,
    turned,
    extra,
    term,
    twin_land,
    right_land,
    left_land,
    pre,
    joined,
    upstream,
    st_both,
    st_both_sum,
    st_both_land,
    st_proj,
    st_proj_sum,
    st_proj_land,
    st_pback,
    st_pback_land,
    st_back,
    st_back_land,
    both_all,
    moved,
    grads,
    back,
    send_sem,
    recv_sem,
    rate_sem,
):
    tasks, bands, cols, pixels, width, taps, extras = plan
    low, f32 = jnp.bfloat16, jnp.float32
    at = Place(tasks, bands)
    post = Post(send_sem, recv_sem)
    chips, chip, core, band = at.chips, at.chip, at.core, at.band
    last = chips - 1
    group = 2 * pixels
    number_of = {tap[:3]: number for number, tap in enumerate(taps)}
    loads = []
    for number, (level, row_tap, col_tap, _, _) in enumerate(taps):
        start = (9 * (level - 1) + 3 * row_tap + col_tap) * width
        load = pltpu.make_async_copy(
            rate_hbm.at[:, start : start + width], rate.at[number], rate_sem.at[number]
        )
        load.start()
        loads.append(load)
    at.meet(False, True)
    for load in loads:
        load.wait()

    def rows_of(ref, number):
        return jnp.concatenate([ref[2 * number], ref[2 * number + 1]], axis=0)

    def right_of(level, col_tap):
        return (col_tap - 1) * level * RATE

    def forward_taps(source, level, row_tap):
        total = None
        for col_tap in range(3):
            number = number_of.get((level, row_tap, col_tap))
            if number is None:
                continue
            part = shift_pixels(
                dot_nn(source, rate[number]), right_of(level, col_tap), cols
            )
            total = part if total is None else total + part
        return total

    extra[...] = jnp.zeros_like(extra)
    for level, target, source, row_tap in extras:
        extra[level - 1, target] += forward_taps(rows_of(sh_ref, source), level, row_tap)

    def twin_term(number):
        return pltpu.make_async_remote_copy(
            term.at[number, 1 - core],
            twin_land.at[number],
            send_sem.at[number],
            recv_sem.at[number],
            device_id=at.twin,
            device_id_type=MESH_ID,
        )

    post.used = chips

    def forward_group(step, carry):
        number = lax.rem(step, 2) * (last - step // 2) + (1 - lax.rem(step, 2)) * (step // 2)
        source = rows_of(sh_ref, number)

        def put(branch, value):
            value = value.astype(low)
            term[number, 0, branch] = value[:pixels]
            term[number, 1, branch] = value[pixels:]

        put(0, dot_nn(source, bw_ref[:, :width]))
        for level in (1, 2, 3):
            total = forward_taps(source, level, 1)
            if any(level == entry[0] for entry in extras):
                total = total + extra[level - 1, number]
            put(level, total)
        twin_term(number).start()
        return carry

    lax.fori_loop(0, 2, forward_group, 0)

    def hop(source, landing, device_chip, number):
        return pltpu.make_async_remote_copy(
            source,
            landing,
            send_sem.at[number],
            recv_sem.at[number],
            device_id={"space": device_chip * 2 + core},
            device_id_type=MESH_ID,
        )

    base_right, base_left = post.used, post.used + chips
    post.used += 2 * chips
    next_chip = lax.rem(chip + 1, chips)
    prev_chip = lax.rem(chip + last, chips)

    def go_right(number):
        return hop(twin_land.at[number], right_land.at[number], next_chip, base_right + number)

    def go_left(number):
        return hop(twin_land.at[number], left_land.at[number], prev_chip, base_left + number)

    def start_off(number, copy):
        twin_term(number).wait_recv()

        def add(branch, carry):
            twin_land[number, branch] = (
                term[number, core, branch].astype(f32) + twin_land[number, branch].astype(f32)
            ).astype(low)
            return carry

        lax.fori_loop(0, 4, add, 0)
        copy.start()

    def pass_on(number, copy, landing, has_incoming):

        @pl.when(jnp.logical_not(has_incoming))
        def _():
            start_off(number, copy)

        @pl.when(has_incoming)
        def _():
            twin_term(number).wait_recv()
            copy.wait_recv()

            def add(branch, carry):
                twin_land[number, branch] = (
                    term[number, core, branch].astype(f32)
                    + twin_land[number, branch].astype(f32)
                    + landing[number, branch].astype(f32)
                ).astype(low)
                return carry

            lax.fori_loop(0, 4, add, 0)
            copy.start()

    @pl.when(chip == 0)
    def _():
        start_off(last, go_right(last))

    @pl.when(chip == last)
    def _():
        start_off(0, go_left(0))

    lax.fori_loop(2, chips, forward_group, 0)

    def pass_right(number):
        there = (chip < number) if number < last else ((chip < number) & (chip > 0))

        @pl.when(there)
        def _():
            pass_on(number, go_right(number), right_land, chip > 0)

    def pass_left(number):
        there = (chip > number) if number > 0 else ((chip > number) & (chip < last))

        @pl.when(there)
        def _():
            pass_on(number, go_left(number), left_land, chip < last)

    def turn_group(number, carry):
        source = rows_of(sh_ref, number)
        turned[:, pl.ds(pl.multiple_of(number * group, group), group)] = source.T
        return carry + jnp.sum(source.astype(f32), axis=0, keepdims=True)

    pixel_sum = lax.fori_loop(0, chips, turn_group, jnp.zeros((1, width), f32))

    @pl.when(chip < chips // 2)
    def _():
        for number in range(last):
            pass_right(last - number)
            pass_left(number)

    @pl.when(chip >= chips // 2)
    def _():
        for number in range(last):
            pass_left(number)
            pass_right(last - number)

    band_rows = pixels // cols
    mask_own = row_mask(widths_ref, band * band_rows, band_rows, cols)
    mask_own = jnp.concatenate([mask_own] * (width // LANE), axis=1)
    inv_count = jnp.concatenate([1.0 / count_pixels(widths_ref)] * (width // LANE), axis=1)
    spread = width // LANE

    def put_rows(target, number, value):
        for part in range(spread):
            target[pl.ds(number * spread + part, 1), :] = value[:, part * LANE : (part + 1) * LANE]

    def get_rows(target, number):
        return jnp.concatenate(
            [target[pl.ds(number * spread + part, 1), :] for part in range(spread)], axis=1
        )

    def column_sum(value):
        return jnp.sum(value, axis=0, keepdims=True)

    twin_term(chip).wait_recv()

    @pl.when(chip > 0)
    def _():
        go_right(chip).wait_recv()

    @pl.when(chip < last)
    def _():
        go_left(chip).wait_recv()

    @pl.when(chip == 0)
    def _():
        right_land[0] = jnp.zeros(right_land.shape[1:], low)

    @pl.when(chip == last)
    def _():
        left_land[last] = jnp.zeros(left_land.shape[1:], low)

    st_both[...] = jnp.zeros_like(st_both)

    def settle(branch, carry):
        value = (
            term[chip, core, branch].astype(f32)
            + twin_land[chip, branch].astype(f32)
            + right_land[chip, branch].astype(f32)
            + left_land[chip, branch].astype(f32)
        )
        pre[branch] = value
        kept = value * mask_own
        put_rows(st_both, branch, column_sum(kept))
        put_rows(st_both, 4 + branch, column_sum(kept * value))
        return carry

    lax.fori_loop(0, 4, settle, 0)
    high = pixel_sum.astype(low)
    rest = pixel_sum - high.astype(f32)
    middle = rest.astype(low)
    tail = (rest - middle.astype(f32)).astype(low)
    pieces = jnp.concatenate(
        [high.astype(f32), middle.astype(f32), tail.astype(f32), jnp.zeros((13, width), f32)],
        axis=0,
    ).astype(low)
    put_rows(st_both, 8, column_sum(dot_nn(pieces, bw_ref[:, width:])))
    st_both_sum[...] = at.sum_over(post, "space", st_both, st_both_land)
    pooled = get_rows(st_both_sum, 8) * inv_count

    def lanes_of(number):
        return pl.ds(pl.multiple_of(number * width, width), width)

    def scale_of(target, first, second):
        mean_value = get_rows(target, first) * inv_count
        variance = get_rows(target, second) * inv_count - mean_value * mean_value
        return mean_value, lax.rsqrt(variance + NORM_EPS)

    def activate(branch, projected):
        mean_value, inv_std = scale_of(st_both_sum, branch, 4 + branch)
        hat = (pre[branch] - mean_value) * inv_std
        pre[branch] = hat
        normed = gain_ref[:, lanes_of(branch)] * hat + shift_ref[:, lanes_of(branch)]
        active = (gelu_of(normed) * mask_own).astype(low)
        joined[branch] = active
        return projected + dot_nn(active, pw_ref[lanes_of(branch), :])

    joined[4] = (gelu_of(pooled).astype(low).astype(f32) * mask_own).astype(low)
    projected = dot_nn(joined[4], pw_ref[4 * width : 5 * width, :])
    projected = lax.fori_loop(0, 4, activate, projected)
    kept = projected * mask_own
    st_proj[...] = jnp.zeros_like(st_proj)
    put_rows(st_proj, 0, column_sum(kept))
    put_rows(st_proj, 1, column_sum(kept * projected))
    st_proj_sum[...] = at.sum_over(post, "space", st_proj, st_proj_land)
    mean_value, inv_std = scale_of(st_proj_sum, 0, 1)
    hat = (projected - mean_value) * inv_std
    gain_proj = gain_ref[:, 4 * width : 5 * width]
    normed = gain_proj * hat + shift_ref[:, 4 * width : 5 * width]
    proj_up = gelu_slope(normed) * cot_ref[...].astype(f32) * mask_own
    st_pback[...] = jnp.zeros_like(st_pback)
    put_rows(st_pback, 0, column_sum(proj_up))
    put_rows(st_pback, 1, column_sum(proj_up * hat))
    proj_sums_out[...] = at.sum_over(post, "space", st_pback, st_pback_land)
    head_out[...] = (gelu_of(normed) * mask_own).astype(low)
    shift_grad, gain_grad = get_rows(proj_sums_out, 0), get_rows(proj_sums_out, 1)
    proj_low = (
        mask_own
        * (gain_proj * inv_std)
        * (proj_up - shift_grad * inv_count - hat * (gain_grad * inv_count))
    ).astype(low)
    st_back[...] = jnp.zeros_like(st_back)

    def back_step(branch, carry):
        joined_grad = dot_nt(proj_low, pw_ref[lanes_of(branch), :])
        hat = pre[branch]
        normed = gain_ref[:, lanes_of(branch)] * hat + shift_ref[:, lanes_of(branch)]
        up = gelu_slope(normed) * joined_grad * mask_own
        upstream[branch] = up
        put_rows(st_back, branch, column_sum(up))
        put_rows(st_back, 4 + branch, column_sum(up * hat))
        return carry

    lax.fori_loop(0, 4, back_step, 0)
    pool_total = column_sum(dot_nt(proj_low, pw_ref[4 * width : 5 * width, :]) * mask_own)
    put_rows(st_back, 8, pool_total)
    both_sums_out[...] = at.sum_over(post, "space", st_back, st_back_land)
    pool_grad = (gelu_slope(pooled) * get_rows(both_sums_out, 8)).astype(low)
    column = jnp.broadcast_to(pixel_sum, (8, width)).T[:, 0:1]
    grads_out[len(taps) + 1] = (
        column * (pool_grad.astype(f32) * inv_count)
    ).astype(low)

    def both_step(branch, carry):
        _, inv_std = scale_of(st_both_sum, branch, 4 + branch)
        shift_grad = get_rows(both_sums_out, branch) * inv_count
        gain_grad = get_rows(both_sums_out, 4 + branch) * inv_count
        both_all[band, branch] = (
            mask_own
            * (gain_ref[:, lanes_of(branch)] * inv_std)
            * (upstream[branch] - shift_grad - pre[branch] * gain_grad)
        ).astype(low)
        return carry

    lax.fori_loop(0, 4, both_step, 0)

    all_right = post.used
    all_left = all_right + chips
    all_twin = all_left + chips

    def send_right(step):
        block = both_all.at[lax.rem(chip - step + 1 + chips, chips) * 2 + core]
        return hop(block, block, next_chip, all_right + step)

    def send_left(step):
        block = both_all.at[lax.rem(chip + step - 1, chips) * 2 + core]
        return hop(block, block, prev_chip, all_left + step)

    def hand_over(number):
        block = both_all.at[number * 2 + core]
        return pltpu.make_async_remote_copy(
            block,
            block,
            send_sem.at[all_twin + number],
            recv_sem.at[all_twin + number],
            device_id=at.twin,
            device_id_type=MESH_ID,
        )

    def from_left(step):
        block = both_all.at[lax.rem(chip - step + chips, chips) * 2 + core]
        return hop(block, block, next_chip, all_right + step)

    def from_right(step):
        block = both_all.at[lax.rem(chip + step, chips) * 2 + core]
        return hop(block, block, prev_chip, all_left + step)

    @pl.when(chip < last)
    def _():
        send_right(1).start()

    @pl.when(chip > 0)
    def _():
        send_left(1).start()

    hand_over(chip).start()

    def proj_step(branch, carry):
        proj_out[lanes_of(branch), :] = dot_nn(joined[branch].T, proj_low).astype(low)
        return carry

    lax.fori_loop(0, 5, proj_step, 0)
    grads[...] = jnp.zeros_like(grads)
    pool_row = dot_nt(
        jnp.broadcast_to(pool_grad, (16, width)), bw_ref[:, width:]
    )[0:1] * inv_count
    moved_levels = sorted({entry[0] for entry in extras})

    def back_group(step, carry):
        number = group_at(step)
        hand_over(number).wait_recv()
        columns = turned[:, pl.ds(pl.multiple_of(number * group, group), group)]

        def both_of(branch):
            return jnp.concatenate(
                [both_all[2 * number, branch], both_all[2 * number + 1, branch]], axis=0
            )

        part = both_of(0)
        total = dot_nt(part, bw_ref[:, :width])
        grads[len(taps)] += dot_nn(columns, part)
        for level in (1, 2, 3):
            image = both_of(level).astype(f32)
            for col_tap in range(3):
                tap = number_of.get((level, 1, col_tap))
                if tap is None:
                    continue
                part = shift_pixels(image, -right_of(level, col_tap), cols).astype(low)
                if level in moved_levels:
                    moved[moved_levels.index(level), number, col_tap] = part
                total = total + dot_nt(part, rate[tap])
                grads[tap] += dot_nn(columns, part)
        back[number] = total
        return carry

    mirror = chip // 2
    near = chip * (1 - mirror) + (last - chip) * mirror

    def group_at(step):
        place = step + near * (1 - 2 * step) * ((last - step) // 2)
        return place * (1 - mirror) + (last - place) * mirror

    lax.fori_loop(0, 1, back_group, 0)
    done = 1
    for step in range(1, chips):
        @pl.when(chip >= step)
        def _():
            from_left(step).wait_recv()
            if step < last:

                @pl.when(chip < last)
                def _():
                    send_right(step + 1).start()

            hand_over(lax.rem(chip - step + chips, chips)).start()

        @pl.when(chip + step <= last)
        def _():
            from_right(step).wait_recv()
            if step < last:

                @pl.when(chip > 0)
                def _():
                    send_left(step + 1).start()

            hand_over(lax.rem(chip + step, chips)).start()

        upto = chips if step == last else step + 1 + near
        lax.fori_loop(done, upto, back_group, 0)
        done = upto

    for level, target, source, row_tap in extras:
        columns = turned[:, source * group : (source + 1) * group]
        total = back[source]
        for col_tap in range(3):
            tap = number_of.get((level, row_tap, col_tap))
            if tap is None:
                continue
            part = moved[moved_levels.index(level), target, col_tap]
            total = total + dot_nt(part, rate[tap])
            grads[tap] += dot_nn(columns, part)
        back[source] = total

    def finish_group(number, carry):
        keep = row_mask(widths_ref, number * 2 * band_rows, 2 * band_rows, cols)
        keep = jnp.concatenate([keep] * spread, axis=1)
        value = (back[number] + keep * pool_row).astype(low)
        sg_out[2 * number] = value[:pixels]
        sg_out[2 * number + 1] = value[pixels:]
        return carry

    lax.fori_loop(0, chips, finish_group, 0)

    def finish_tap(number, carry):
        grads_out[number] = grads[number].astype(low)
        return carry

    lax.fori_loop(0, len(taps) + 1, finish_tap, 0)

    post.close()

    def twin_left(number, carry):
        twin_term(number).wait_send()
        hand_over(number).wait_send()
        return carry

    lax.fori_loop(0, chips, twin_left, 0)
    for number in range(last):
        to_right, to_left = last - number, number

        @pl.when(chip < to_right)
        def _():
            go_right(to_right).wait_send()

        @pl.when(chip > to_left)
        def _():
            go_left(to_left).wait_send()

    for step in range(1, chips):

        @pl.when((chip < last) & (chip - step + 1 >= 0))
        def _():
            send_right(step).wait_send()

        @pl.when((chip > 0) & (chip + step - 1 <= last))
        def _():
            send_left(step).wait_send()


def head(tasks, bands, cols, rows, collective, sh, widths, gain, shift, cot, bw, pw, rate):
    low, f32 = jnp.bfloat16, jnp.float32
    pixels, width = sh.shape[1], pw.shape[1]
    chips = bands // 2
    group_rows = rows // chips
    taps = live_taps(rows, cols)
    extras = []
    for level in (1, 2, 3):
        for row_tap in (0, 2):
            if (level, row_tap, 1) in [tap[:3] for tap in taps]:
                away = (row_tap - 1) * level * RATE // group_rows
                extras += [
                    (level, target, target + away, row_tap)
                    for target in range(chips)
                    if 0 <= target + away < chips
                ]
    levels = max([entry[0] for entry in extras], default=1)
    in_vmem = pl.BlockSpec(memory_space=pltpu.VMEM)
    anywhere = pl.BlockSpec(memory_space=pl.ANY)
    shape = jax.ShapeDtypeStruct
    block = (pixels, width)
    both_rows, proj_rows = -(-9 * width // LANE // 8) * 8, 8

    def stats(count):
        return [pltpu.VMEM((count, LANE), f32), pltpu.VMEM((bands, count, LANE), f32)]

    scratch = (
        [
            pltpu.VMEM((len(taps), sh.shape[2], width), low),
            pltpu.VMEM((sh.shape[2], bands * pixels), low),
            pltpu.VMEM((levels, chips, 2 * pixels, width), f32),
            pltpu.VMEM((chips, 2, 4) + block, low),
            pltpu.VMEM((chips, 4) + block, low),
            pltpu.VMEM((chips, 4) + block, low),
            pltpu.VMEM((chips, 4) + block, low),
            pltpu.VMEM((4,) + block, f32),
            pltpu.VMEM((5,) + block, low),
            pltpu.VMEM((4,) + block, f32),
        ]
        + [pltpu.VMEM((both_rows, LANE), f32)]
        + stats(both_rows)
        + [pltpu.VMEM((proj_rows, LANE), f32)]
        + stats(proj_rows)
        + stats(proj_rows)
        + stats(both_rows)
        + [
            pltpu.VMEM((bands, 4) + block, low),
            pltpu.VMEM((levels, chips, 3, 2 * pixels, width), low),
            pltpu.VMEM((len(taps) + 1, sh.shape[2], width), f32),
            pltpu.VMEM((chips, 2 * pixels, width), f32),
            pltpu.SemaphoreType.DMA((80,)),
            pltpu.SemaphoreType.DMA((80,)),
            pltpu.SemaphoreType.DMA((len(taps),)),
        ]
    )
    out_shapes = (
        shape(block, low),
        shape(sh.shape, low),
        shape((len(taps) + 2, sh.shape[2], width), low),
        shape(pw.shape, low),
        shape((both_rows, LANE), f32),
        shape((proj_rows, LANE), f32),
    )
    return taps, pl.pallas_call(
        functools.partial(
            head_kernel, (tasks, bands, cols, pixels, width, tuple(taps), tuple(extras))
        ),
        name="head",
        out_shape=out_shapes,
        in_specs=[in_vmem, pl.BlockSpec(memory_space=pltpu.SMEM)] + [in_vmem] * 5 + [anywhere],
        out_specs=(in_vmem,) * 6,
        scratch_shapes=scratch,
        compiler_params=pltpu.CompilerParams(
            collective_id=collective, has_side_effects=True, vmem_limit_bytes=36 << 20
        ),
    )(sh, widths, gain, shift, cot, bw, pw, rate)


def trunk_kernel(
    sizes,
    x_hbm,
    widths_ref,
    gain_ref,
    shift_ref,
    wr_hbm,
    wd_hbm,
    we_hbm,
    sh_out,
    rim,
    h1,
    h2,
    a2,
    h3q,
    v1,
    v2,
    v3,
    stats_out,
    x,
    wr,
    wd,
    we,
    h3,
    blocks,
    mask_own,
    st1,
    st1_land,
    st2,
    st2_land,
    st3,
    st3_land,
    send_sem,
    recv_sem,
    local_sem,
):
    tasks, bands, cols, quarter, mid, wide, piece = sizes
    low, f32 = jnp.bfloat16, jnp.float32
    at = Place(tasks, bands)
    post = Post(send_sem, recv_sem)
    task, band = at.task, at.band
    my_rows = pl.ds(pl.multiple_of(task * quarter, quarter), quarter)
    loads = [
        pltpu.make_async_copy(source, target, local_sem.at[number])
        for number, (source, target) in enumerate(
            ((x_hbm, x), (wr_hbm, wr), (wd_hbm, wd), (we_hbm, we))
        )
    ]
    for load in loads:
        load.start()
    at.meet(True, True)
    pixels = x.shape[0]
    band_rows = pixels // cols
    mask = row_mask(widths_ref, band * band_rows, band_rows, cols)
    count = count_pixels(widths_ref)
    spread = mid // LANE

    def across(value, lanes):
        return jnp.concatenate([value] * (lanes // LANE), axis=1)

    def put_sums(target, value, keep):
        kept = value * keep
        first = jnp.sum(kept, axis=0, keepdims=True)
        second = jnp.sum(kept * value, axis=0, keepdims=True)
        for number in range(spread):
            lanes = slice(number * LANE, (number + 1) * LANE)
            target[number : number + 1] = first[:, lanes]
            target[spread + number : spread + number + 1] = second[:, lanes]

    def get_sums(total):
        return [
            jnp.concatenate([total[base + k : base + k + 1] for k in range(spread)], axis=1)
            for base in (0, spread)
        ]

    def put_norm(vectors, lanes, first, second, start):
        width = first.shape[1]
        inv = across(1.0 / count, width)
        mean_value = first * inv
        variance = second * inv - mean_value * mean_value
        vectors[0:1, lanes] = mean_value
        vectors[1:2, lanes] = lax.rsqrt(variance + NORM_EPS)
        vectors[2:3, lanes] = gain_ref[:, start : start + width]
        vectors[3:4, lanes] = shift_ref[:, start : start + width]
        stats_out[0:1, start : start + width] = mean_value
        stats_out[1:2, start : start + width] = variance * across(count / (count - 1.0), width)

    def activate(hidden, vectors, keep):
        normed = vectors[2:3] * ((hidden - vectors[0:1]) * vectors[1:2]) + vectors[3:4]
        return (gelu_of(normed) * keep).astype(low)

    mask_mid = across(mask, mid)
    for load in loads[:2]:
        load.wait()
    h1[...] = dot_nn(x[...], wr[...])
    put_sums(st1, h1[...], mask_mid)
    first, second = get_sums(at.sum_over(post, "space", st1, st1_land))
    put_norm(v1, slice(0, mid), first, second, 0)
    rim[1] = activate(h1[...], v1, mask_mid)

    has_above, has_below = band > 0, band < bands - 1
    up = post.copy(rim.at[1], rim.at[2], {"space": lax.rem(band + bands - 1, bands)})
    down = post.copy(rim.at[1], rim.at[0], {"space": lax.rem(band + 1, bands)})

    @pl.when(has_above)
    def _():
        up.start()

    @pl.when(has_below)
    def _():
        down.start()

    @pl.when(jnp.logical_not(has_above))
    def _():
        rim[0] = jnp.zeros(rim.shape[1:], low)

    @pl.when(jnp.logical_not(has_below))
    def _():
        rim[2] = jnp.zeros(rim.shape[1:], low)

    loads[2].wait()
    halves = [slice(start, start + piece) for start in range(0, mid, piece)]

    def tap_sum(row_taps, lanes):
        total = None
        for col_tap in range(3):
            part = None
            for row_tap in row_taps:
                term = dot_nn(rim[row_tap], wd[3 * row_tap + col_tap, :, lanes])
                part = term if part is None else part + term
            part = shift_pixels(part, CONV_DILATION * (col_tap - 1), cols)
            total = part if total is None else total + part
        return total

    for lanes in halves:
        h2[:, lanes] = tap_sum((1,), lanes)

    @pl.when(has_below)
    def _():
        up.wait_recv()

    @pl.when(has_above)
    def _():
        down.wait_recv()

    for lanes in halves:
        h2[:, lanes] += tap_sum((0, 2), lanes)

    put_sums(st2, h2[...], mask_mid)
    first, second = get_sums(at.sum_over(post, "space", st2, st2_land))
    put_norm(v2, slice(0, mid), first, second, mid)
    a2[...] = activate(h2[...], v2, mask_mid)

    loads[3].wait()
    mask_piece = across(mask, piece)
    per_row = st3.shape[1] // piece
    half = st3.shape[0] // 2

    def expand_step(number, carry):
        lanes = pl.ds(pl.multiple_of(number * piece, piece), piece)
        value = dot_nn(a2[...], we[:, lanes])
        h3[:, lanes] = value
        kept = value * mask_piece
        row = number // per_row
        spot = pl.ds(pl.multiple_of(lax.rem(number, per_row) * piece, piece), piece)
        st3[pl.ds(row, 1), spot] = jnp.sum(kept, axis=0, keepdims=True)
        st3[pl.ds(half + row, 1), spot] = jnp.sum(kept * value, axis=0, keepdims=True)
        return carry

    lax.fori_loop(0, bands, expand_step, 0)
    begun = at.sum_begin(post, "space", st3, st3_land)
    h3q[...] = h3[my_rows]
    total = at.sum_end(begun)
    lanes_in = st3.shape[1]
    for row in range(half):
        put_norm(
            v3,
            slice(row * lanes_in, (row + 1) * lanes_in),
            total[row : row + 1],
            total[half + row : half + row + 1],
            2 * mid + row * lanes_in,
        )

    mask_own[...] = mask
    mask_quarter = across(mask_own[my_rows], piece)

    def shared_of(number):
        lanes = pl.ds(pl.multiple_of(number * piece, piece), piece)
        hat = (h3q[:, lanes] - v3[0:1, lanes]) * v3[1:2, lanes]
        before = v3[2:3, lanes] * hat + v3[3:4, lanes] + x[my_rows, lanes].astype(f32)
        return (gelu_of(before) * mask_quarter).astype(low)

    slices_in = []
    for other in at.other_bands:
        blocks[other] = shared_of(other)
        slices_in.append(
            post.push(blocks.at[other], sh_out.at[band, my_rows], {"space": other})
        )
    sh_out[band, my_rows] = shared_of(band)

    def to_tasks(number):
        block = sh_out.at[number, my_rows]
        return [post.push(block, block, {"task": other}) for other in at.other_tasks]

    quarters_in = to_tasks(band)
    for step, made in enumerate(slices_in, start=1):
        made.wait_recv()
        quarters_in += to_tasks(lax.rem(band + bands - step, bands))
    for made in quarters_in:
        made.wait_recv()
    post.close()

    @pl.when(has_above)
    def _():
        up.wait_send()

    @pl.when(has_below)
    def _():
        down.wait_send()


def trunk(tasks, bands, cols, collective, x, widths, gain, shift, wr, wd, we):
    low, f32 = jnp.bfloat16, jnp.float32
    pixels, wide = x.shape
    mid = wr.shape[1]
    quarter, piece = pixels // tasks, wide // bands
    in_vmem = pl.BlockSpec(memory_space=pltpu.VMEM)
    anywhere = pl.BlockSpec(memory_space=pl.ANY)
    shape = jax.ShapeDtypeStruct
    narrow_stats = [
        pltpu.VMEM((2 * mid // LANE, LANE), f32),
        pltpu.VMEM((bands, 2 * mid // LANE, LANE), f32),
    ]
    return pl.pallas_call(
        functools.partial(trunk_kernel, (tasks, bands, cols, quarter, mid, wide, piece)),
        name="trunk",
        out_shape=(
            shape((bands, pixels, piece), low),
            shape((3, pixels, mid), low),
            shape((pixels, mid), f32),
            shape((pixels, mid), f32),
            shape((pixels, mid), low),
            shape((quarter, wide), f32),
            shape((8, mid), f32),
            shape((8, mid), f32),
            shape((8, wide), f32),
            shape((2, 2 * mid + wide), f32),
        ),
        in_specs=[anywhere, pl.BlockSpec(memory_space=pltpu.SMEM), in_vmem, in_vmem]
        + [anywhere] * 3,
        out_specs=(in_vmem,) * 10,
        scratch_shapes=[
            pltpu.VMEM(x.shape, low),
            pltpu.VMEM(wr.shape, low),
            pltpu.VMEM(wd.shape, low),
            pltpu.VMEM(we.shape, low),
            pltpu.VMEM((pixels, wide), f32),
            pltpu.VMEM((bands, quarter, piece), low),
            pltpu.VMEM((pixels, LANE), f32),
        ]
        + narrow_stats
        + narrow_stats
        + [
            pltpu.VMEM((8, wide // 4), f32),
            pltpu.VMEM((bands, 8, wide // 4), f32),
            pltpu.SemaphoreType.DMA((64,)),
            pltpu.SemaphoreType.DMA((64,)),
            pltpu.SemaphoreType.DMA((4,)),
        ],
        compiler_params=pltpu.CompilerParams(
            collective_id=collective, has_side_effects=True, vmem_limit_bytes=54 << 20
        ),
    )(x, widths, gain, shift, wr, wd, we)


def finish_kernel(
    places,
    tap_ref,
    ho_in,
    ig_in,
    rg_in,
    dg_in,
    eg_in,
    pg_ref,
    s3_ref,
    s2_ref,
    s1_ref,
    both_ref,
    proj_ref,
    ho_out,
    ig_out,
    rg_out,
    dg_out,
    eg_out,
    branch_out,
    rate_out,
    pg_out,
    tg_out,
    ts_out,
    hg_out,
    hs_out,
    branch,
    rate,
    sems,
):
    f32 = jnp.float32
    width = tap_ref.shape[2]
    copies = [
        pltpu.make_async_copy(source, target, sems.at[number])
        for number, (source, target) in enumerate(
            (
                (ho_in, ho_out),
                (ig_in, ig_out),
                (rg_in, rg_out),
                (dg_in, dg_out),
                (eg_in, eg_out),
            )
        )
    ]
    for copy in copies:
        copy.start()
    per_level = len(places) // 3
    for level in range(3):
        for number in range(level * per_level, (level + 1) * per_level):
            lanes = slice(number * width, (number + 1) * width)
            if places[number] is None:
                rate[:, lanes] = jnp.zeros((rate.shape[0], width), f32)
            else:
                rate[:, lanes] = tap_ref[places[number]].astype(f32)
        lanes = slice(level * per_level * width, (level + 1) * per_level * width)
        copy = pltpu.make_async_copy(
            rate.at[:, lanes], rate_out.at[:, lanes], sems.at[len(copies)]
        )
        copy.start()
        copies.append(copy)
    count = tap_ref.shape[0]
    branch[:, :width] = tap_ref[count - 2].astype(f32)
    branch[:, width:] = tap_ref[count - 1].astype(f32)
    copy = pltpu.make_async_copy(branch, branch_out, sems.at[len(copies)])
    copy.start()
    copies.append(copy)
    pg_out[...] = pg_ref[...].astype(f32)
    rows = s1_ref.shape[0] // 2
    ts_out[0:rows] = s1_ref[0:rows]
    tg_out[0:rows] = s1_ref[rows : 2 * rows]
    ts_out[rows : 2 * rows] = s2_ref[0:rows]
    tg_out[rows : 2 * rows] = s2_ref[rows : 2 * rows]
    half, lanes_in = s3_ref.shape[0] // 2, s3_ref.shape[1]
    for row in range(half):
        for part in range(lanes_in // LANE):
            target = 2 * rows + row * (lanes_in // LANE) + part
            lanes = slice(part * LANE, (part + 1) * LANE)
            ts_out[target : target + 1] = s3_ref[row : row + 1, lanes]
            tg_out[target : target + 1] = s3_ref[half + row : half + row + 1, lanes]
    spread = width // LANE
    hs_out[0 : 4 * spread] = both_ref[0 : 4 * spread]
    hg_out[0 : 4 * spread] = both_ref[4 * spread : 8 * spread]
    hs_out[4 * spread : 5 * spread] = proj_ref[0:spread]
    hg_out[4 * spread : 5 * spread] = proj_ref[spread : 2 * spread]
    for copy in copies:
        copy.wait()


def finish(places, taps, ho, ig, rg, dg, eg, pg, s3, s2, s1, both, proj):
    f32 = jnp.float32
    in_vmem = pl.BlockSpec(memory_space=pltpu.VMEM)
    anywhere = pl.BlockSpec(memory_space=pl.ANY)
    shape = jax.ShapeDtypeStruct
    depth, width = taps.shape[1:]
    rows = (s1.size + s2.size + s3.size) // 2 // LANE
    head_rows = 5 * width // LANE
    return pl.pallas_call(
        functools.partial(finish_kernel, places),
        name="finish",
        out_shape=(
            shape(ho.shape, ho.dtype),
            shape(ig.shape, ig.dtype),
            shape(rg.shape, rg.dtype),
            shape(dg.shape, dg.dtype),
            shape(eg.shape, eg.dtype),
            shape((depth, 2 * width), f32),
            shape((depth, len(places) * width), f32),
            shape(pg.shape, f32),
            shape((rows, LANE), f32),
            shape((rows, LANE), f32),
            shape((head_rows, LANE), f32),
            shape((head_rows, LANE), f32),
        ),
        in_specs=[in_vmem] + [anywhere] * 5 + [in_vmem] * 6,
        out_specs=(anywhere,) * 7 + (in_vmem,) * 5,
        scratch_shapes=[
            pltpu.VMEM((depth, 2 * width), f32),
            pltpu.VMEM((depth, len(places) * width), f32),
            pltpu.SemaphoreType.DMA((9,)),
        ],
        compiler_params=pltpu.CompilerParams(vmem_limit_bytes=40 << 20),
    )(taps, ho, ig, rg, dg, eg, pg, s3, s2, s1, both, proj)


def live_taps(rows, cols):
    taps = []
    for level in (1, 2, 3):
        for row_tap in range(3):
            for col_tap in range(3):
                down, right = (row_tap - 1) * level * RATE, (col_tap - 1) * level * RATE
                if abs(down) < rows and abs(right) < cols:
                    taps.append((level, row_tap, col_tap, down, right))
    return taps


def per_device_slices(
    features,
    row_width,
    w_reduce,
    w_dilated,
    w_expand,
    trunk_gain,
    trunk_shift,
    branch_weight,
    rate_weight,
    proj_weight,
    head_gain,
    head_shift,
    head_cot,
):
    bands, tasks = lax.axis_size("space"), lax.axis_size("task")
    band_rows, cols, in_width = features.shape
    rows = band_rows * bands
    pixels = band_rows * cols
    head_width = proj_weight.shape[2]
    inputs = features.reshape(pixels, in_width)
    dilated = w_dilated.transpose(1, 0, 2)
    shared, rim, h1, h2, a2, h3q, v1, v2, v3, batch_stats = trunk(
        tasks,
        bands,
        cols,
        0,
        inputs,
        row_width,
        trunk_gain.reshape(1, -1),
        trunk_shift.reshape(1, -1),
        w_reduce,
        dilated,
        w_expand,
    )
    taps, (head_out, shared_grad, tap_grads, proj_term, both_sums, proj_sums) = head(
        tasks,
        bands,
        cols,
        rows,
        1,
        shared,
        row_width,
        head_gain,
        head_shift,
        head_cot.reshape(pixels, head_width),
        branch_weight[0],
        proj_weight[0],
        rate_weight[0],
    )
    (
        weight_rows,
        input_grad,
        reduce_grad,
        dilated_grad,
        expand_grad,
        sums_three,
        sums_two,
        sums_one,
        proj_grad,
    ) = trunk_back(
        tasks,
        bands,
        cols,
        2,
        shared_grad,
        h3q,
        inputs,
        v3,
        h2,
        v2,
        h1,
        v1,
        rim,
        a2,
        row_width,
        w_expand,
        dilated,
        w_reduce,
        proj_term.reshape(bands, -1, head_width),
    )
    place_of = {tap[:3]: number for number, tap in enumerate(taps)}
    places = tuple(
        place_of.get((level, row_tap, col_tap))
        for level in (1, 2, 3)
        for row_tap in range(3)
        for col_tap in range(3)
    )
    (
        head_out,
        input_grad,
        reduce_grad,
        dilated_grad,
        expand_grad,
        branch_grad,
        rate_grad,
        proj_grad,
        trunk_gains,
        trunk_shifts,
        head_gains,
        head_shifts,
    ) = finish(
        places,
        tap_grads,
        head_out,
        input_grad,
        reduce_grad,
        dilated_grad,
        expand_grad,
        proj_grad.reshape(-1, head_width),
        sums_three,
        sums_two,
        sums_one,
        both_sums,
        proj_sums,
    )
    return (
        head_out.reshape(1, band_rows, cols, head_width),
        input_grad.reshape(features.shape),
        reduce_grad,
        dilated_grad.transpose(1, 0, 2),
        expand_grad,
        trunk_gains.reshape(-1),
        trunk_shifts.reshape(-1),
        batch_stats,
        branch_grad[None],
        rate_grad[None],
        proj_grad[None],
        head_gains.reshape(1, -1),
        head_shifts.reshape(1, -1),
        weight_rows[:tasks, 0],
    )


def solution(mesh):
    body = per_device_slices if mesh.shape["space"] == 8 else per_device
    return jax.shard_map(
        body,
        mesh=mesh,
        in_specs=(
            P("space", None, None),
            P(),
            P(),
            P(),
            P(),
            P(),
            P(),
            P("task", "space", None),
            P("task", "space", None),
            P("task", None, None),
            P("task", None),
            P("task", None),
            P("task", "space", None, None),
        ),
        out_specs=(
            P("task", "space", None, None),
            P("space", None, None),
            P("space", None),
            P("space", None, None),
            P("space", None),
            P(),
            P(),
            P(),
            P("task", "space", None),
            P("task", "space", None),
            P("task", None, None),
            P("task", None),
            P("task", None),
            P(),
        ),
        check_vma=False,
    )
```

```python
import functools

import jax
import jax.numpy as jnp
from jax import lax
from jax.experimental import pallas as pl
from jax.experimental.pallas import tpu as pltpu
from jax.sharding import PartitionSpec as P

CONV_DILATION = 2
RATE = 12


NORM_EPS = 1e-05
GRAM_EPS = 1e-06
PRECISE = lax.Precision.HIGHEST


def with_halo(block, sides, width):
    for axis, dim in sides:
        count = lax.axis_size(axis)
        forward = [(i, i + 1) for i in range(count - 1)]
        backward = [(target, source) for source, target in forward]
        low = lax.ppermute(
            lax.slice_in_dim(block, block.shape[dim] - width, None, axis=dim), axis, forward
        )
        high = lax.ppermute(lax.slice_in_dim(block, 0, width, axis=dim), axis, backward)
        block = jnp.concatenate([low, block, high], axis=dim)
    return block


def from_behind(shard, axis, by):
    count = lax.axis_size(axis)
    pairs = [(i, i + by) for i in range(count) if 0 <= i + by < count]
    return lax.ppermute(shard, axis, pairs)


def small_solve(matrix, target):
    size_n = matrix.shape[0]
    rows_list = [matrix[number] for number in range(size_n)]
    values = [target[number] for number in range(size_n)]
    for pivot_row in range(size_n):
        for lower_row in range(pivot_row + 1, size_n):
            factor = rows_list[lower_row][pivot_row] / rows_list[pivot_row][pivot_row]
            rows_list[lower_row] = rows_list[lower_row] - factor * rows_list[pivot_row]
            values[lower_row] = values[lower_row] - factor * values[pivot_row]
    answer = [None] * size_n
    for pivot_row in reversed(range(size_n)):
        running = values[pivot_row]
        for later_row in range(pivot_row + 1, size_n):
            running = running - rows_list[pivot_row][later_row] * answer[later_row]
        answer[pivot_row] = running / rows_list[pivot_row][pivot_row]
    return jnp.stack(answer)


def imtl_weights(gram_matrix):
    grad_norms = jnp.sqrt(jnp.diagonal(gram_matrix) + GRAM_EPS)
    projections = gram_matrix / grad_norms[None, :]
    system = projections[0, 0] - projections[0:1, 1:] - projections[1:, 0:1] + projections[1:, 1:]
    target = projections[0, 0] - projections[0, 1:]
    other_weights = small_solve(jnp.transpose(system), target)
    return jnp.concatenate([(1.0 - jnp.sum(other_weights))[None], other_weights])


def gelu_back(value, upstream):
    return jax.vjp(jax.nn.gelu, value)[1](upstream)[0]


def channel_sums(members):
    return lax.psum(members, "space")


def norm_values(hidden, first_total, second_total, gain_vec, shift_vec, pixel_count):
    mean_value = first_total / pixel_count
    variance = second_total / pixel_count - mean_value * mean_value
    inv_std = lax.rsqrt(variance + NORM_EPS)
    scaled = (hidden - mean_value) * inv_std
    return (gain_vec * scaled + shift_vec, scaled, inv_std, mean_value, variance)


def norm_forward(hidden, gain_vec, shift_vec, valid_mask, pixel_count):
    totals = channel_sums(
        (jnp.sum(hidden * valid_mask, axis=0), jnp.sum(hidden * hidden * valid_mask, axis=0))
    )
    return norm_values(hidden, totals[0], totals[1], gain_vec, shift_vec, pixel_count)


def norm_finish(
    upstream, scaled, inv_std, gain_vec, gain_grad, shift_grad, valid_mask, pixel_count
):
    return (
        valid_mask
        * gain_vec
        * inv_std
        * (upstream - shift_grad / pixel_count - scaled * gain_grad / pixel_count)
    )


def norm_backward(upstream, scaled, inv_std, gain_vec, valid_mask, pixel_count):
    totals = channel_sums(
        (jnp.sum(upstream * valid_mask, axis=0), jnp.sum(upstream * scaled * valid_mask, axis=0))
    )
    hidden_grad = norm_finish(
        upstream, scaled, inv_std, gain_vec, totals[1], totals[0], valid_mask, pixel_count
    )
    return (hidden_grad, totals[1], totals[0])


def band_rim(strip_image):
    return with_halo(strip_image, (("space", 0),), CONV_DILATION)


def far_rows(strip_image, bands_away, upward):
    if bands_away >= lax.axis_size("space"):
        return jnp.zeros_like(strip_image)
    if upward:
        return from_behind(strip_image, "space", bands_away)
    return from_behind(strip_image, "space", -bands_away)


def trunk_taps(padded, reach_cells, rows_count, cols_count, flipped):
    col_padded = jnp.pad(padded, ((0, 0), (reach_cells, reach_cells), (0, 0)))
    pieces = []
    for row_tap in range(3):
        for col_tap in range(3):
            row_from = (2 - row_tap) * reach_cells if flipped else row_tap * reach_cells
            col_from = (2 - col_tap) * reach_cells if flipped else col_tap * reach_cells
            pieces.append(
                col_padded[
                    row_from : row_from + rows_count, col_from : col_from + cols_count
                ].reshape(rows_count * cols_count, -1)
            )
    return jnp.stack(pieces, axis=1)


def per_device(
    features,
    row_width,
    w_reduce,
    w_dilated,
    w_expand,
    trunk_gain,
    trunk_shift,
    branch_weight,
    rate_weight,
    proj_weight,
    head_gain,
    head_shift,
    head_cot,
):
    band_rows, cols_count, in_width = features.shape
    pixels = band_rows * cols_count
    middle_width = w_reduce.shape[1]
    head_width = proj_weight.shape[2]
    first_row = lax.axis_index("space") * band_rows
    widths = lax.dynamic_slice_in_dim(row_width, first_row, band_rows)
    valid_mask = (
        (jnp.arange(cols_count)[None, :] < widths[:, None]).astype(jnp.float32).reshape(pixels, 1)
    )
    pixel_count = jnp.sum(row_width).astype(jnp.float32)
    inputs = features.reshape(pixels, in_width)
    gain_one, shift_one = (trunk_gain[:middle_width], trunk_shift[:middle_width])
    gain_two, shift_two = (
        trunk_gain[middle_width : 2 * middle_width],
        trunk_shift[middle_width : 2 * middle_width],
    )
    gain_three, shift_three = (trunk_gain[2 * middle_width :], trunk_shift[2 * middle_width :])
    hidden_one = jnp.dot(inputs, w_reduce, preferred_element_type=jnp.float32)
    stats_one = norm_forward(hidden_one, gain_one, shift_one, valid_mask, pixel_count)
    first_active = (jax.nn.gelu(stats_one[0]) * valid_mask).astype(jnp.bfloat16)
    patches = trunk_taps(
        band_rim(first_active.reshape(band_rows, cols_count, middle_width)),
        CONV_DILATION,
        band_rows,
        cols_count,
        False,
    )
    hidden_two = jnp.einsum("pti,ito->po", patches, w_dilated, preferred_element_type=jnp.float32)
    stats_two = norm_forward(hidden_two, gain_two, shift_two, valid_mask, pixel_count)
    active_two = (jax.nn.gelu(stats_two[0]) * valid_mask).astype(jnp.bfloat16)
    hidden_three = jnp.dot(active_two, w_expand, preferred_element_type=jnp.float32)
    stats_three = norm_forward(hidden_three, gain_three, shift_three, valid_mask, pixel_count)
    before_act = stats_three[0] + inputs.astype(jnp.float32)
    shared = (jax.nn.gelu(before_act) * valid_mask).astype(jnp.bfloat16)
    proj_local = proj_weight[0]
    gain_local = head_gain[0]
    shift_local = head_shift[0]
    joined_weight = jnp.concatenate([branch_weight[0], rate_weight[0]], axis=1)
    pixel_sum = jnp.dot(
        valid_mask.reshape(1, pixels).astype(jnp.bfloat16),
        shared,
        preferred_element_type=jnp.float32,
    )[0]
    shared_image = shared.reshape(band_rows, cols_count, in_width)
    padded_sources = []
    for level in (1, 2, 3):
        reach = level * RATE
        bands_away = reach // band_rows
        triple = (
            far_rows(shared_image, bands_away, True),
            shared_image,
            far_rows(shared_image, bands_away, False),
        )
        padded_sources.append(
            [jnp.pad(source, ((0, 0), (reach, reach), (0, 0))) for source in triple]
        )
    zero_rows = jnp.zeros((pixels, head_width), jnp.float32)
    start_totals = (
        zero_rows,
        jnp.zeros((1, head_width), jnp.float32),
        zero_rows,
        zero_rows,
        zero_rows,
    )
    all_weights = lax.all_gather(joined_weight, "space", axis=0, tiled=True)
    width_now = all_weights.shape[0]
    one_acc = jnp.dot(shared, all_weights[:, :head_width], preferred_element_type=jnp.float32)
    pool_cols = pixel_sum[None]
    pool_acc = jnp.dot(
        pool_cols,
        all_weights[:, head_width : 2 * head_width].astype(jnp.float32),
        precision=PRECISE,
        preferred_element_type=jnp.float32,
    )
    rate_accs = []
    for fold_level_index in range(3):
        fold_reach = (fold_level_index + 1) * RATE
        running = start_totals[2 + fold_level_index]
        for fold_row_tap in range(3):
            fold_source = padded_sources[fold_level_index][fold_row_tap]
            for fold_col_tap in range(3):
                window = fold_source[
                    :, fold_col_tap * fold_reach : fold_col_tap * fold_reach + cols_count
                ].reshape(pixels, width_now)
                column = (2 + 9 * fold_level_index + 3 * fold_row_tap + fold_col_tap) * head_width
                running = running + jnp.dot(
                    window,
                    all_weights[:, column : column + head_width],
                    preferred_element_type=jnp.float32,
                )
        rate_accs.append(running)
    pre_both = jnp.concatenate([one_acc, rate_accs[0], rate_accs[1], rate_accs[2]], axis=1)
    gain_both, shift_both = (gain_local[: 4 * head_width], shift_local[: 4 * head_width])
    totals = channel_sums(
        (
            jnp.sum(pre_both * valid_mask, axis=0),
            jnp.sum(pre_both * pre_both * valid_mask, axis=0),
            pool_acc[0],
        )
    )
    stats_both = norm_values(pre_both, totals[0], totals[1], gain_both, shift_both, pixel_count)
    pooled = totals[2][None] / pixel_count
    active_both = (jax.nn.gelu(stats_both[0]) * valid_mask).astype(jnp.bfloat16)
    active_pool = jax.nn.gelu(pooled).astype(jnp.bfloat16)
    joined = jnp.concatenate(
        [active_both, (active_pool.astype(jnp.float32) * valid_mask).astype(jnp.bfloat16)], axis=1
    )
    projected = jnp.dot(joined, proj_local, preferred_element_type=jnp.float32)
    gain_proj = gain_local[4 * head_width :]
    stats_proj = norm_forward(
        projected, gain_proj, shift_local[4 * head_width :], valid_mask, pixel_count
    )
    head_result = (jax.nn.gelu(stats_proj[0]) * valid_mask).astype(jnp.bfloat16)
    cot_rows = head_cot[0].reshape(pixels, head_width).astype(jnp.float32)
    proj_upstream = gelu_back(stats_proj[0], cot_rows * valid_mask)
    proj_hidden, proj_gain_grad, proj_shift_grad = norm_backward(
        proj_upstream, stats_proj[1], stats_proj[2], gain_proj, valid_mask, pixel_count
    )
    proj_low = proj_hidden.astype(jnp.bfloat16)
    joined_grad = lax.dot_general(
        proj_low, proj_local, (((1,), (1,)), ((), ())), preferred_element_type=jnp.float32
    )
    proj_term = lax.dot_general(
        joined, proj_low, (((0,), (0,)), ((), ())), preferred_element_type=jnp.float32
    )
    both_upstream = gelu_back(stats_both[0], joined_grad[:, : 4 * head_width] * valid_mask)
    pool_total = jnp.sum(joined_grad[:, 4 * head_width :] * valid_mask, axis=0)
    back_totals = channel_sums(
        (
            proj_term,
            pool_total,
            jnp.sum(both_upstream * valid_mask, axis=0),
            jnp.sum(both_upstream * stats_both[1] * valid_mask, axis=0),
        )
    )
    pool_grad = gelu_back(pooled, back_totals[1][None]).astype(jnp.bfloat16)
    both_grad = norm_finish(
        both_upstream,
        stats_both[1],
        stats_both[2],
        gain_both,
        back_totals[3],
        back_totals[2],
        valid_mask,
        pixel_count,
    ).astype(jnp.bfloat16)
    tap_grads = []
    for level_index in range(3):
        reach = (level_index + 1) * RATE
        bands_away = reach // band_rows
        rate_image = both_grad[
            :, (1 + level_index) * head_width : (2 + level_index) * head_width
        ].reshape(band_rows, cols_count, head_width)
        back_sources = [
            jnp.pad(source, ((0, 0), (reach, reach), (0, 0)))
            for source in (
                far_rows(rate_image, bands_away, False),
                rate_image,
                far_rows(rate_image, bands_away, True),
            )
        ]
        for row_tap in range(3):
            for col_tap in range(3):
                tap_grads.append(
                    back_sources[row_tap][
                        :, (2 - col_tap) * reach : (2 - col_tap) * reach + cols_count
                    ].reshape(pixels, head_width)
                )
    right_side = jnp.concatenate([both_grad[:, :head_width]] + tap_grads, axis=1)
    used_rows = jnp.concatenate(
        [all_weights[:, :head_width], all_weights[:, 2 * head_width :]], axis=1
    )
    main_part = lax.dot_general(
        right_side, used_rows, (((1,), (1,)), ((), ())), preferred_element_type=jnp.float32
    )
    pool_part = lax.dot_general(
        pool_grad,
        all_weights[:, head_width : 2 * head_width],
        (((1,), (1,)), ((), ())),
        preferred_element_type=jnp.float32,
    )
    shared_grad = (main_part + valid_mask * pool_part / pixel_count).astype(jnp.bfloat16)
    head_term = lax.dot_general(
        shared, right_side, (((0,), (0,)), ((), ())), preferred_element_type=jnp.float32
    )
    pool_term = pixel_sum[:, None] * pool_grad.astype(jnp.float32) / pixel_count
    head_term = jnp.concatenate(
        [head_term[:, :head_width], pool_term, head_term[:, head_width:]], axis=1
    )
    all_grads = lax.all_gather(shared_grad[None], "task", axis=0, tiled=True)
    flat_grads = all_grads.reshape(all_grads.shape[0], -1)
    gram_matrix = lax.psum(
        lax.dot_general(
            flat_grads, flat_grads, (((1,), (1,)), ((), ())), preferred_element_type=jnp.float32
        ),
        "space",
    )
    task_weight = imtl_weights(gram_matrix)
    mixed_grad = task_weight[0] * all_grads[0].astype(jnp.float32)
    for task_index in range(1, all_grads.shape[0]):
        mixed_grad = mixed_grad + task_weight[task_index] * all_grads[task_index].astype(
            jnp.float32
        )
    combined = mixed_grad.astype(jnp.bfloat16)
    gate_grad = gelu_back(before_act, combined.astype(jnp.float32) * valid_mask)
    hidden_grad_three, gain_grad_three, shift_grad_three = norm_backward(
        gate_grad, stats_three[1], stats_three[2], gain_three, valid_mask, pixel_count
    )
    low_three = hidden_grad_three.astype(jnp.bfloat16)
    expand_term = lax.dot_general(
        active_two, low_three, (((0,), (0,)), ((), ())), preferred_element_type=jnp.float32
    )
    active_grad_two = lax.dot_general(
        low_three, w_expand, (((1,), (1,)), ((), ())), preferred_element_type=jnp.float32
    )
    upstream_two = gelu_back(stats_two[0], active_grad_two * valid_mask)
    hidden_grad_two, gain_grad_two, shift_grad_two = norm_backward(
        upstream_two, stats_two[1], stats_two[2], gain_two, valid_mask, pixel_count
    )
    low_two = hidden_grad_two.astype(jnp.bfloat16)
    dilated_term = jnp.einsum("pti,po->ito", patches, low_two, preferred_element_type=jnp.float32)
    back_patches = trunk_taps(
        band_rim(low_two.reshape(band_rows, cols_count, middle_width)),
        CONV_DILATION,
        band_rows,
        cols_count,
        True,
    )
    active_grad_one = jnp.einsum(
        "pto,ito->pi", back_patches, w_dilated, preferred_element_type=jnp.float32
    )
    upstream_one = gelu_back(stats_one[0], active_grad_one * valid_mask)
    hidden_grad_one, gain_grad_one, shift_grad_one = norm_backward(
        upstream_one, stats_one[1], stats_one[2], gain_one, valid_mask, pixel_count
    )
    low_one = hidden_grad_one.astype(jnp.bfloat16)
    reduce_term = lax.dot_general(
        inputs, low_one, (((0,), (0,)), ((), ())), preferred_element_type=jnp.float32
    )
    input_grad = (
        lax.dot_general(
            low_one, w_reduce, (((1,), (1,)), ((), ())), preferred_element_type=jnp.float32
        )
        + gate_grad
    )
    reduced = (
        lax.psum_scatter(head_term, "space", scatter_dimension=0, tiled=True),
        lax.psum_scatter(reduce_term, "space", scatter_dimension=0, tiled=True),
        lax.psum_scatter(dilated_term, "space", scatter_dimension=0, tiled=True),
        lax.psum_scatter(expand_term, "space", scatter_dimension=0, tiled=True),
    )
    means = jnp.concatenate([stats_one[3], stats_two[3], stats_three[3]])
    variances = (
        jnp.concatenate([stats_one[4], stats_two[4], stats_three[4]])
        * pixel_count
        / (pixel_count - 1.0)
    )
    batch_stats = jnp.stack([means, variances])
    head_gain_grad = jnp.concatenate([back_totals[3], proj_gain_grad])[None]
    head_shift_grad = jnp.concatenate([back_totals[2], proj_shift_grad])[None]
    return (
        head_result.reshape(1, band_rows, cols_count, head_width),
        input_grad.reshape(band_rows, cols_count, in_width).astype(jnp.bfloat16),
        reduced[1],
        reduced[2],
        reduced[3],
        jnp.concatenate([gain_grad_one, gain_grad_two, gain_grad_three]),
        jnp.concatenate([shift_grad_one, shift_grad_two, shift_grad_three]),
        batch_stats,
        reduced[0][:, : 2 * head_width][None],
        reduced[0][:, 2 * head_width :][None],
        back_totals[0][None],
        head_gain_grad,
        head_shift_grad,
        task_weight,
    )


MESH_ID = pl.DeviceIdType.MESH
LANE = 128


GELU_A = 0.7978845608028654
GELU_B = 0.044715


def gelu_of(value):
    return 0.5 * value * (1.0 + jnp.tanh(GELU_A * (value + GELU_B * value * value * value)))


def gelu_slope(value):
    square = value * value
    bend = jnp.tanh(GELU_A * value * (1.0 + GELU_B * square))
    return 0.5 * (1.0 + bend) + 0.5 * value * (1.0 - bend * bend) * (
        GELU_A * (1.0 + 3.0 * GELU_B * square)
    )


def dot_nn(left_side, right_side):
    return jnp.dot(left_side, right_side, preferred_element_type=jnp.float32)


def dot_nt(left_side, right_side):
    return lax.dot_general(
        left_side, right_side, (((1,), (1,)), ((), ())), preferred_element_type=jnp.float32
    )


def shift_pixels(value, by, cols):
    if by == 0:
        return value
    rows = value.shape[0]
    column = lax.rem(lax.broadcasted_iota(jnp.int32, value.shape, 0), cols) + by
    rolled = pltpu.roll(value, (-by) % rows, 0)
    return jnp.where((column >= 0) & (column < cols), rolled, 0.0)


def row_mask(widths_ref, first_row, rows, cols):
    column = lax.broadcasted_iota(jnp.int32, (cols, LANE), 0)
    return jnp.concatenate(
        [
            jnp.where(column < widths_ref[first_row + number], 1.0, 0.0).astype(jnp.float32)
            for number in range(rows)
        ],
        axis=0,
    )


def count_pixels(widths_ref):
    total = widths_ref[0]
    for number in range(1, widths_ref.shape[0]):
        total = total + widths_ref[number]
    return jnp.full((1, LANE), total.astype(jnp.float32), jnp.float32)


class Post:
    def __init__(self, send_sem, recv_sem):
        self.send_sem, self.recv_sem = send_sem, recv_sem
        self.used = 0
        self.sent = []

    def copy(self, source, target, device):
        made = pltpu.make_async_remote_copy(
            source,
            target,
            self.send_sem.at[self.used],
            self.recv_sem.at[self.used],
            device_id=device,
            device_id_type=MESH_ID,
        )
        self.used += 1
        return made

    def push(self, source, target, device):
        made = self.copy(source, target, device)
        made.start()
        self.sent.append(made)
        return made

    def close(self):
        for made in self.sent:
            made.wait_send()


class Place:
    def __init__(self, tasks, bands):
        self.tasks, self.bands, self.chips = tasks, bands, bands // 2
        self.task = lax.axis_index("task")
        self.band = lax.axis_index("space")
        self.chip = self.band // 2
        self.core = lax.rem(self.band, 2)
        self.twin = {"space": self.chip * 2 + 1 - self.core}
        low, high = lax.rem(self.task, 2), self.task // 2
        self.other_tasks = [(1 - high) * 2 + 1 - low, high * 2 + 1 - low, (1 - high) * 2 + low]
        self.other_bands = [lax.rem(self.band + step, bands) for step in range(1, bands)]

    def greet(self):
        barrier = pltpu.get_barrier_semaphore()
        greeted = [{"task": task} for task in self.other_tasks]
        greeted += [{"space": band} for band in self.other_bands]
        for device in greeted:
            pl.semaphore_signal(barrier, inc=1, device_id=device, device_id_type=MESH_ID)

    def meet(self):
        barrier = pltpu.get_barrier_semaphore()
        pl.semaphore_wait(barrier, len(self.other_tasks) + len(self.other_bands))

    def sum_begin(self, post, axis, own_ref, land_ref):
        mine = self.task if axis == "task" else self.band
        others = self.other_tasks if axis == "task" else self.other_bands
        copies = [post.push(own_ref, land_ref.at[mine], {axis: other}) for other in others]
        land_ref[pl.ds(mine, 1)] = own_ref[...][None]
        return copies, land_ref

    def sum_end(self, begun):
        copies, land_ref = begun
        for made in copies:
            made.wait_recv()
        total = land_ref[0]
        for slot in range(1, len(copies) + 1):
            total = total + land_ref[slot]
        return total

    def sum_over(self, post, axis, own_ref, land_ref):
        return self.sum_end(self.sum_begin(post, axis, own_ref, land_ref))


def trunk_back_kernel(
    sizes,
    xg_hbm,
    h3_hbm,
    x_hbm,
    v3_hbm,
    h2_hbm,
    v2_hbm,
    h1_hbm,
    v1_hbm,
    act_hbm,
    a2_hbm,
    widths_ref,
    we_hbm,
    wd_hbm,
    wr_hbm,
    ps_hbm,
    tw_hbm,
    ig_hbm,
    rg_hbm,
    dg_hbm,
    eg_hbm,
    s3_hbm,
    s2_hbm,
    s1_hbm,
    pg_hbm,
    tw_out,
    ig_out,
    rg_out,
    dg_out,
    eg_out,
    s3_out,
    s2_out,
    s1_out,
    pg_out,
    we,
    wd,
    wr,
    xg,
    x_ref,
    v3_ref,
    v2_ref,
    v1_ref,
    act_ref,
    ps_ref,
    h3q,
    h2_ref,
    h1_ref,
    a2_ref,
    mask_ref,
    xq,
    gram_own,
    gram_land,
    gram_mid,
    gram_land_b,
    comb,
    comb_land,
    gate,
    scaled,
    gate_low,
    gate_band,
    st3,
    st3_land,
    st3_mid,
    st3_land_b,
    l3,
    l3x,
    st2,
    st2_land,
    st2_mid,
    st2_land_b,
    l2,
    l2_halo,
    ag1,
    st1,
    st1_land,
    l1,
    xt,
    a2t,
    e_term,
    e_twin,
    e_land,
    e_share,
    e_tasks,
    l2c,
    d_sum,
    d_share,
    d_tasks,
    r_term,
    r_twin,
    r_land,
    r_share,
    r_tasks,
    p_all,
    send_sem,
    recv_sem,
    local_sem,
    out_sem,
):
    tasks, bands, cols, quarter, mid, wide, piece = sizes
    low = jnp.bfloat16
    f32 = jnp.float32
    at = Place(tasks, bands)
    post = Post(send_sem, recv_sem)
    task, band = at.task, at.band
    my_rows = pl.ds(pl.multiple_of(task * quarter, quarter), quarter)
    arrays = {
        "xg": (xg_hbm, xg),
        "a2": (a2_hbm, a2_ref),
        "x": (x_hbm, x_ref),
        "xq": (x_hbm.at[my_rows], xq),
        "h3": (h3_hbm, h3q),
        "v3": (v3_hbm, v3_ref),
        "ps": (ps_hbm, ps_ref),
        "we": (we_hbm, we),
        "h2": (h2_hbm, h2_ref),
        "v2": (v2_hbm, v2_ref),
        "wd": (wd_hbm, wd),
        "h1": (h1_hbm, h1_ref),
        "v1": (v1_hbm, v1_ref),
        "act": (act_hbm, act_ref),
        "wr": (wr_hbm, wr),
    }
    loads = {
        name: pltpu.make_async_copy(source, target, local_sem.at[number])
        for number, (name, (source, target)) in enumerate(arrays.items())
    }

    writes = []

    def write(source, target):
        copy = pltpu.make_async_copy(source, target, out_sem.at[len(writes)])
        copy.start()
        writes.append(copy)

    def loaded(*names):
        for name in names:
            loads[name].wait()

    for load in loads.values():
        load.start()
    at.greet()
    band_rows = x_ref.shape[0] // cols
    mask_ref[...] = row_mask(widths_ref, band * band_rows, band_rows, cols)

    loaded("xg")
    pairs = [(a, b) for a in range(tasks) for b in range(a, tasks)]

    def gram_step(number, totals):
        grads = [xg[a, number].astype(f32) for a in range(tasks)]
        out = []
        for (a, b), total in zip(pairs, totals):
            product = grads[a] * grads[b]
            product = product.reshape(quarter // 8, 8, piece).sum(axis=0)
            for start in range(0, piece, LANE):
                total = total + product[:, start : start + LANE]
            out.append(total)
        return tuple(out)

    totals = lax.fori_loop(
        0, bands, gram_step, tuple(jnp.zeros((8, LANE), f32) for _ in pairs)
    )
    gram_own[...] = jnp.zeros_like(gram_own)
    for number, total in enumerate(totals):
        gram_own[number : number + 1] = jnp.sum(total, axis=0, keepdims=True)
    at.meet()
    begun = at.sum_begin(post, "task", gram_own, gram_land)
    loaded("a2")
    a2t[...] = a2_ref[...].T
    gram_mid[...] = at.sum_end(begun)
    begun = at.sum_begin(post, "space", gram_mid, gram_land_b)

    loaded("x")
    def turn_inputs(number, carry):
        lanes = pl.ds(pl.multiple_of(number * piece, piece), piece)
        xt[lanes, :] = x_ref[:, lanes].T
        return carry

    lax.fori_loop(0, wide // piece, turn_inputs, 0)
    gram_sum = at.sum_end(begun)
    gram_sum = jnp.broadcast_to(jnp.sum(gram_sum, axis=1, keepdims=True), gram_sum.shape)
    gram = [[None] * tasks for _ in range(tasks)]
    for number, (a, b) in enumerate(pairs):
        gram[a][b] = gram[b][a] = gram_sum[number : number + 1]
    norms = [jnp.sqrt(gram[a][a] + GRAM_EPS) for a in range(tasks)]
    cos = [[gram[a][b] / norms[b] for b in range(tasks)] for a in range(tasks)]
    rows_list = [
        [cos[0][0] - cos[0][l] - cos[k][0] + cos[k][l] for k in range(1, tasks)]
        for l in range(1, tasks)
    ]
    values = [cos[0][0] - cos[0][l] for l in range(1, tasks)]
    count = tasks - 1
    for pivot in range(count):
        for lower in range(pivot + 1, count):
            factor = rows_list[lower][pivot] / rows_list[pivot][pivot]
            rows_list[lower] = [
                under - factor * over for under, over in zip(rows_list[lower], rows_list[pivot])
            ]
            values[lower] = values[lower] - factor * values[pivot]
    answer = [None] * count
    for pivot in reversed(range(count)):
        running = values[pivot]
        for later in range(pivot + 1, count):
            running = running - rows_list[pivot][later] * answer[later]
        answer[pivot] = running / rows_list[pivot][pivot]
    rest = answer[0]
    for value in answer[1:]:
        rest = rest + value
    task_weight = [1.0 - rest] + answer
    for number in range(tasks):
        tw_out[number : number + 1] = task_weight[number]
    weights = [jnp.concatenate([value] * (piece // LANE), axis=1) for value in task_weight]

    def mixed(number):
        total = weights[0] * xg[0, number].astype(f32)
        for a in range(1, tasks):
            total = total + weights[a] * xg[a, number].astype(f32)
        return total.astype(low)

    comb_in = []
    for other in at.other_bands:
        comb[other] = mixed(other)
        comb_in.append(post.push(comb.at[other], comb_land.at[band], {"space": other}))
    comb_land[pl.ds(band, 1)] = mixed(band)[None]
    loaded("xq", "h3", "v3")
    for made in comb_in:
        made.wait_recv()

    mask_quarter = mask_ref[my_rows]
    mask_piece = jnp.concatenate([mask_quarter] * (piece // LANE), axis=1)
    inv_count = 1.0 / count_pixels(widths_ref)
    inv_piece = jnp.concatenate([inv_count] * (piece // LANE), axis=1)
    per_row = st3.shape[1] // piece
    half = st3.shape[0] // 2

    def gate_step(number, carry):
        lanes = pl.ds(pl.multiple_of(number * piece, piece), piece)
        hat = (h3q[:, lanes] - v3_ref[0:1, lanes]) * v3_ref[1:2, lanes]
        before = v3_ref[2:3, lanes] * hat + v3_ref[3:4, lanes] + xq[:, lanes].astype(f32)
        grad = gelu_slope(before) * comb_land[number].astype(f32) * mask_piece
        gate[number] = grad
        scaled[number] = hat
        gate_low[number] = grad.astype(low)
        row = number // per_row
        spot = pl.ds(pl.multiple_of(lax.rem(number, per_row) * piece, piece), piece)
        st3[pl.ds(row, 1), spot] = jnp.sum(grad, axis=0, keepdims=True)
        st3[pl.ds(half + row, 1), spot] = jnp.sum(grad * hat, axis=0, keepdims=True)
        return carry

    lax.fori_loop(0, bands, gate_step, 0)
    st3_mid[...] = at.sum_over(post, "task", st3, st3_land)
    s3_out[...] = at.sum_over(post, "space", st3_mid, st3_land_b)

    def third_step(number, carry):
        lanes = pl.ds(pl.multiple_of(number * piece, piece), piece)
        row = number // per_row
        spot = pl.ds(pl.multiple_of(lax.rem(number, per_row) * piece, piece), piece)
        shift_grad = s3_out[pl.ds(row, 1), spot] * inv_piece
        gain_grad = s3_out[pl.ds(half + row, 1), spot] * inv_piece
        l3[number] = (
            mask_piece
            * (v3_ref[2:3, lanes] * v3_ref[1:2, lanes])
            * (gate[number] - shift_grad - scaled[number] * gain_grad)
        ).astype(low)
        return carry

    lax.fori_loop(0, bands, third_step, 0)
    per_task = bands // tasks
    l3_in = []
    for other in at.other_tasks:
        l3_in.append(
            post.push(l3.at[pl.ds(other * per_task, per_task)], l3x.at[task], {"task": other})
        )
    l3x[pl.ds(task, 1)] = l3[pl.ds(task * per_task, per_task)][None]
    loaded("ps", "we")
    p_all[pl.ds(band, 1)] = ps_ref[...][None]
    p_block = p_all.at[band]
    p_near = post.push(p_block, p_block, at.twin)
    p_far = [
        post.push(
            p_block,
            p_block,
            {"space": lax.rem(at.chip + step, at.chips) * 2 + at.core},
        )
        for step in range(1, at.chips)
    ]

    def expand_step(number, total):
        lanes = pl.ds(pl.multiple_of(number * piece, piece), piece)
        return total + dot_nt(l3[number], we[:, lanes])

    ag2 = lax.fori_loop(0, bands, expand_step, jnp.zeros((quarter, mid), f32))

    mask_mid = jnp.concatenate([mask_quarter] * (mid // LANE), axis=1)
    inv_mid = jnp.concatenate([inv_count] * (mid // LANE), axis=1)
    loaded("h2", "v2")
    hat = (h2_ref[my_rows] - v2_ref[0:1]) * v2_ref[1:2]
    grad = gelu_slope(v2_ref[2:3] * hat + v2_ref[3:4]) * ag2 * mask_mid
    spread = mid // LANE

    def put_sums(target, first, second):
        for number in range(spread):
            lanes = slice(number * LANE, (number + 1) * LANE)
            target[number : number + 1] = first[:, lanes]
            target[spread + number : spread + number + 1] = second[:, lanes]

    def get_sums(total):
        return [
            jnp.concatenate([total[base + k : base + k + 1] for k in range(spread)], axis=1)
            for base in (0, spread)
        ]

    def to_twin(term, landing):
        return post.push(term.at[1 - at.core], landing, at.twin)

    def both_cores(pair, term, twin):
        pair.wait_recv()
        for step in range(1, at.chips):
            other = lax.rem(at.chip + step, at.chips)
            both = term[at.core, other].astype(f32) + twin[other].astype(f32)
            twin[other] = both.astype(low)

    def along(twin, landing):
        return [
            post.push(
                twin.at[other], landing.at[at.chip], {"space": other * 2 + at.core}
            )
            for other in [lax.rem(at.chip + step, at.chips) for step in range(1, at.chips)]
        ]

    def settle(arrivals, term, twin, landing):
        total = term[at.core, at.chip].astype(f32) + twin[at.chip].astype(f32)
        for made in arrivals:
            made.wait_recv()
        for step in range(1, at.chips):
            total = total + landing[lax.rem(at.chip + step, at.chips)].astype(f32)
        return total.astype(low)

    def to_tasks(share, landing):
        arrivals = [post.push(share, landing.at[task], {"task": other}) for other in at.other_tasks]
        landing[pl.ds(task, 1)] = share[...][None]
        return arrivals

    def expand_part(number):
        share = jnp.concatenate([l3x[a, number] for a in range(tasks)], axis=0)
        part = dot_nn(a2t[...], share).astype(low)
        per_band = part.shape[0] // bands
        for target in range(bands):
            e_term[target % 2, target // 2, :, number * piece : (number + 1) * piece] = part[
                target * per_band : (target + 1) * per_band
            ]

    narrow = mid // tasks
    my_lanes = pl.ds(pl.multiple_of(task * narrow, narrow), narrow)
    put_sums(
        st2, jnp.sum(grad, axis=0, keepdims=True), jnp.sum(grad * hat, axis=0, keepdims=True)
    )
    begun = at.sum_begin(post, "task", st2, st2_land)
    for made in l3_in:
        made.wait_recv()
    expand_part(0)
    st2_mid[...] = at.sum_end(begun)
    begun = at.sum_begin(post, "space", st2_mid, st2_land_b)
    for number in range(1, per_task):
        expand_part(number)
    e_pair = to_twin(e_term, e_twin)
    s2_out[...] = at.sum_end(begun)
    shift_grad, gain_grad = get_sums(s2_out[...])
    l2[my_rows] = (
        mask_mid
        * (v2_ref[2:3] * v2_ref[1:2])
        * (grad - shift_grad * inv_mid - hat * (gain_grad * inv_mid))
    ).astype(low)
    l2_in = [post.push(l2.at[my_rows], l2.at[my_rows], {"task": other}) for other in at.other_tasks]
    both_cores(e_pair, e_term, e_twin)
    e_in = along(e_twin, e_land)
    for made in l2_in:
        made.wait_recv()
    gate_in = [
        post.push(gate_low, gate_band.at[task], {"task": other}) for other in at.other_tasks
    ]
    gate_band[pl.ds(task, 1)] = gate_low[...][None]
    has_above, has_below = band > 0, band < bands - 1
    up = post.copy(l2, l2_halo.at[1], {"space": lax.rem(band + bands - 1, bands)})
    down = post.copy(l2, l2_halo.at[0], {"space": lax.rem(band + 1, bands)})

    @pl.when(has_above)
    def _():
        up.start()

    @pl.when(has_below)
    def _():
        down.start()

    @pl.when(jnp.logical_not(has_above))
    def _():
        l2_halo[0] = jnp.zeros_like(l2)

    @pl.when(jnp.logical_not(has_below))
    def _():
        l2_halo[1] = jnp.zeros_like(l2)

    p_passed = []
    for step, made in enumerate(p_far, start=1):
        made.wait_recv()
        block = p_all.at[lax.rem(at.chip + at.chips - step, at.chips) * 2 + at.core]
        p_passed.append(post.push(block, block, at.twin))
    loaded("wd")
    halves = [slice(start, start + piece) for start in range(0, mid, piece)]
    for lanes in halves:
        total = None
        for col_tap in range(3):
            part = shift_pixels(
                dot_nt(l2[...], wd[3 + col_tap, lanes, :]), -CONV_DILATION * (col_tap - 1), cols
            )
            total = part if total is None else total + part
        ag1[:, lanes] = total

    @pl.when(has_below)
    def _():
        up.wait_recv()

    @pl.when(has_above)
    def _():
        down.wait_recv()

    for lanes in halves:
        total = None
        for col_tap in range(3):
            part = dot_nt(l2_halo[1], wd[col_tap, lanes, :]) + dot_nt(
                l2_halo[0], wd[6 + col_tap, lanes, :]
            )
            part = shift_pixels(part, -CONV_DILATION * (col_tap - 1), cols)
            total = part if total is None else total + part
        ag1[:, lanes] += total

    loaded("h1", "v1")
    pixels = ag1.shape[0]
    chunk = pixels // 8

    def first_rows(number):
        return pl.ds(pl.multiple_of(number * chunk, chunk), chunk)

    def first_step(number, sums):
        rows = first_rows(number)
        hat = (h1_ref[rows] - v1_ref[0:1]) * v1_ref[1:2]
        keep = jnp.concatenate([mask_ref[rows]] * spread, axis=1)
        grad = gelu_slope(v1_ref[2:3] * hat + v1_ref[3:4]) * ag1[rows] * keep
        ag1[rows] = grad
        return (
            sums[0] + jnp.sum(grad, axis=0, keepdims=True),
            sums[1] + jnp.sum(grad * hat, axis=0, keepdims=True),
        )

    nothing = jnp.zeros((1, mid), f32)
    first, second = lax.fori_loop(0, 8, first_step, (nothing, nothing))
    put_sums(st1, first, second)
    begun = at.sum_begin(post, "space", st1, st1_land)
    l2c[pl.ds(band, 1)] = l2[:, my_lanes][None]
    l2_block = l2c.at[band]
    d_far = [
        post.push(
            l2_block,
            l2_block,
            {"space": lax.rem(at.chip + step, at.chips) * 2 + at.core},
        )
        for step in range(1, at.chips)
    ]
    d_near = [post.push(l2_block, l2_block, at.twin)]
    e_share[...] = settle(e_in, e_term, e_twin, e_land)
    s1_out[...] = at.sum_end(begun)
    shift_grad, gain_grad = get_sums(s1_out[...])
    shift_grad, gain_grad = shift_grad * inv_mid, gain_grad * inv_mid

    def first_finish(number, carry):
        rows = first_rows(number)
        hat = (h1_ref[rows] - v1_ref[0:1]) * v1_ref[1:2]
        keep = jnp.concatenate([mask_ref[rows]] * spread, axis=1)
        l1[rows] = (
            keep * (v1_ref[2:3] * v1_ref[1:2]) * (ag1[rows] - shift_grad - hat * gain_grad)
        ).astype(low)
        return carry

    lax.fori_loop(0, 8, first_finish, 0)

    share_r = l1[:, my_lanes]
    per_band_r = wide // bands

    def reduce_step(number, carry):
        rows = pl.ds(pl.multiple_of(number * per_band_r, per_band_r), per_band_r)
        r_term[lax.rem(number, 2), number // 2] = dot_nn(xt[rows, :], share_r).astype(low)
        return carry

    lax.fori_loop(0, bands, reduce_step, 0)
    r_pair = to_twin(r_term, r_twin)
    e_back = to_tasks(e_share, e_tasks)
    both_cores(r_pair, r_term, r_twin)
    r_in = along(r_twin, r_land)

    for step, made in enumerate(d_far, start=1):
        made.wait_recv()
        block = l2c.at[lax.rem(at.chip + at.chips - step, at.chips) * 2 + at.core]
        d_near.append(post.push(block, block, at.twin))

    loaded("wr", "act")
    for made in gate_in:
        made.wait_recv()

    def input_step(number, carry):
        lanes = pl.ds(pl.multiple_of(number * piece, piece), piece)
        gates = jnp.concatenate([gate_band[a, number] for a in range(tasks)], axis=0).astype(f32)
        ig_out[:, lanes] = (dot_nt(l1[...], wr[lanes, :]) + gates).astype(low)
        return carry

    lax.fori_loop(0, bands, input_step, 0)
    write(ig_out, ig_hbm)
    for source, target in ((tw_out, tw_hbm), (s3_out, s3_hbm), (s2_out, s2_hbm), (s1_out, s1_hbm)):
        write(source, target)
    for made in d_near:
        made.wait_recv()
    d_sum[...] = jnp.zeros_like(d_sum)

    def dilated_step(number, carry):
        left = jnp.concatenate([act_ref[number + row_tap] for row_tap in range(3)], axis=0)
        right = l2c[number].astype(f32)
        for col_tap in range(3):
            moved = shift_pixels(right, -CONV_DILATION * (col_tap - 1), cols).astype(low)
            d_sum[col_tap] += dot_nn(left, moved)
        return carry

    lax.fori_loop(0, bands, dilated_step, 0)
    part = d_share.shape[1]
    for row_tap in range(3):
        for col_tap in range(3):
            d_share[3 * row_tap + col_tap] = d_sum[
                col_tap, row_tap * part : (row_tap + 1) * part
            ].astype(low)
    d_back = to_tasks(d_share, d_tasks)
    r_share[...] = settle(r_in, r_term, r_twin, r_land)
    r_back = to_tasks(r_share, r_tasks)
    for made in [p_near] + p_passed:
        made.wait_recv()
    pg_out[...] = p_all[...]
    write(pg_out, pg_hbm)
    for made in e_back:
        made.wait_recv()
    broad = wide // tasks
    for a in range(tasks):
        eg_out[:, a * broad : (a + 1) * broad] = e_tasks[a].astype(f32)
    write(eg_out, eg_hbm)
    for made in d_back:
        made.wait_recv()
    for a in range(tasks):
        dg_out[:, :, a * narrow : (a + 1) * narrow] = d_tasks[a].astype(f32)
    write(dg_out, dg_hbm)
    for made in r_back:
        made.wait_recv()
    for a in range(tasks):
        rg_out[:, a * narrow : (a + 1) * narrow] = r_tasks[a].astype(f32)
    write(rg_out, rg_hbm)
    post.close()

    @pl.when(has_above)
    def _():
        up.wait_send()

    @pl.when(has_below)
    def _():
        down.wait_send()
    for copy in writes:
        copy.wait()


def trunk_back(
    tasks, bands, cols, collective, xg, h3, x, v3, h2, v2, h1, v1, act, a2, widths, we, wd, wr, ps
):
    low, f32 = jnp.bfloat16, jnp.float32
    pixels, wide = x.shape
    mid = a2.shape[1]
    quarter = pixels // tasks
    piece = wide // bands
    narrow, broad = mid // tasks, wide // tasks
    chips = bands // 2
    part = mid // bands
    anywhere = pl.BlockSpec(memory_space=pl.ANY)
    shape = jax.ShapeDtypeStruct

    def stats(rows, lanes):
        return [
            pltpu.VMEM((rows, lanes), f32),
            pltpu.VMEM((tasks, rows, lanes), f32),
            pltpu.VMEM((rows, lanes), f32),
            pltpu.VMEM((bands, rows, lanes), f32),
        ]

    def terms(*dims):
        return [
            pltpu.VMEM((2, chips) + dims, low),
            pltpu.VMEM((chips,) + dims, low),
            pltpu.VMEM((chips,) + dims, low),
            pltpu.VMEM(dims, low),
            pltpu.VMEM((tasks,) + dims, low),
        ]

    stat_wide = 2 * wide // 8
    scratch = (
        [
            pltpu.VMEM(we.shape, low),
            pltpu.VMEM(wd.shape, low),
            pltpu.VMEM(wr.shape, low),
            pltpu.VMEM(xg.shape, low),
            pltpu.VMEM(x.shape, low),
            pltpu.VMEM(v3.shape, f32),
            pltpu.VMEM(v2.shape, f32),
            pltpu.VMEM(v1.shape, f32),
            pltpu.VMEM(act.shape, low),
            pltpu.VMEM(ps.shape, low),
            pltpu.VMEM(h3.shape, f32),
            pltpu.VMEM(h2.shape, f32),
            pltpu.VMEM(h1.shape, f32),
            pltpu.VMEM(a2.shape, low),
            pltpu.VMEM((pixels, LANE), f32),
            pltpu.VMEM((quarter, wide), low),
        ]
        + stats(16, LANE)
        + [
            pltpu.VMEM((bands, quarter, piece), low),
            pltpu.VMEM((bands, quarter, piece), low),
            pltpu.VMEM((bands, quarter, piece), f32),
            pltpu.VMEM((bands, quarter, piece), f32),
            pltpu.VMEM((bands, quarter, piece), low),
            pltpu.VMEM((tasks, bands, quarter, piece), low),
        ]
        + stats(8, stat_wide)
        + [
            pltpu.VMEM((bands, quarter, piece), low),
            pltpu.VMEM((tasks, bands // tasks, quarter, piece), low),
        ]
        + stats(2 * mid // LANE, LANE)
        + [
            pltpu.VMEM((pixels, mid), low),
            pltpu.VMEM((2, pixels, mid), low),
            pltpu.VMEM((pixels, mid), f32),
            pltpu.VMEM((2 * mid // LANE, LANE), f32),
            pltpu.VMEM((bands, 2 * mid // LANE, LANE), f32),
            pltpu.VMEM((pixels, mid), low),
            pltpu.VMEM((wide, pixels), low),
            pltpu.VMEM((mid, pixels), low),
        ]
        + terms(part, broad)
        + [
            pltpu.VMEM((bands, pixels, narrow), low),
            pltpu.VMEM((3, 3 * part, narrow), f32),
            pltpu.VMEM((9, part, narrow), low),
            pltpu.VMEM((tasks, 9, part, narrow), low),
        ]
        + terms(piece, narrow)
        + [
            pltpu.VMEM((bands,) + ps.shape, low),
            pltpu.SemaphoreType.DMA((96,)),
            pltpu.SemaphoreType.DMA((96,)),
            pltpu.SemaphoreType.DMA((15,)),
            pltpu.SemaphoreType.DMA((9,)),
        ]
    )
    out_shapes = (
        shape((8, LANE), f32),
        shape((pixels, wide), low),
        shape((piece, mid), f32),
        shape((9, part, mid), f32),
        shape((part, wide), f32),
        shape((8, stat_wide), f32),
        shape((2 * mid // LANE, LANE), f32),
        shape((2 * mid // LANE, LANE), f32),
        shape((bands,) + ps.shape, low),
    )
    return pl.pallas_call(
        functools.partial(trunk_back_kernel, (tasks, bands, cols, quarter, mid, wide, piece)),
        name="trunk_back",
        out_shape=out_shapes,
        in_specs=[anywhere] * 10
        + [pl.BlockSpec(memory_space=pltpu.SMEM)]
        + [anywhere] * 4,
        out_specs=(anywhere,) * len(out_shapes),
        scratch_shapes=[pltpu.VMEM(out.shape, out.dtype) for out in out_shapes] + scratch,
        compiler_params=pltpu.CompilerParams(
            collective_id=collective, has_side_effects=True, vmem_limit_bytes=60 << 20
        ),
    )(xg, h3, x, v3, h2, v2, h1, v1, act, a2, widths, we, wd, wr, ps)


def head_phase(
    at,
    post,
    plan,
    rate_loads,
    sh_ref,
    widths_ref,
    gain_ref,
    shift_ref,
    cot_ref,
    bw_ref,
    pw_ref,
    head_out,
    xg_out,
    grads_out,
    proj_share,
    both_sums_out,
    proj_sums_out,
    rate,
    turned,
    extra,
    term,
    twin_land,
    right_land,
    left_land,
    pre,
    joined,
    upstream,
    st_both,
    st_both_sum,
    st_both_land,
    st_proj,
    st_proj_sum,
    st_proj_land,
    st_pback,
    st_pback_land,
    st_back,
    st_back_land,
    both_all,
    moved,
    grads,
    back,
    sg,
    proj_term,
    p_twin,
    p_land,
):
    tasks, bands, cols, pixels, width, taps, extras = plan
    low, f32 = jnp.bfloat16, jnp.float32
    send_sem, recv_sem = post.send_sem, post.recv_sem
    chips, chip, core, band = at.chips, at.chip, at.core, at.band
    last = chips - 1
    group = 2 * pixels
    number_of = {tap[:3]: number for number, tap in enumerate(taps)}
    for load in rate_loads:
        load.wait()

    def rows_of(ref, number):
        return jnp.concatenate([ref[2 * number], ref[2 * number + 1]], axis=0)

    def right_of(level, col_tap):
        return (col_tap - 1) * level * RATE

    def forward_taps(source, level, row_tap):
        total = None
        for col_tap in range(3):
            number = number_of.get((level, row_tap, col_tap))
            if number is None:
                continue
            part = shift_pixels(
                dot_nn(source, rate[number]), right_of(level, col_tap), cols
            )
            total = part if total is None else total + part
        return total

    extra[...] = jnp.zeros_like(extra)
    for level, target, source, row_tap in extras:
        extra[level - 1, target] += forward_taps(rows_of(sh_ref, source), level, row_tap)

    first_twin = post.used
    post.used += chips

    def twin_term(number):
        return pltpu.make_async_remote_copy(
            term.at[number, 1 - core],
            twin_land.at[number],
            send_sem.at[first_twin + number],
            recv_sem.at[first_twin + number],
            device_id=at.twin,
            device_id_type=MESH_ID,
        )


    side = chip // (chips // 2)

    def forward_group(step, carry):
        near = lax.rem(step, 2) * (step // 2) + (1 - lax.rem(step, 2)) * (last - step // 2)
        number = near * (1 - side) + (last - near) * side
        source = rows_of(sh_ref, number)

        def put(branch, value):
            value = value.astype(low)
            term[number, 0, branch] = value[:pixels]
            term[number, 1, branch] = value[pixels:]

        put(0, dot_nn(source, bw_ref[:, :width]))
        for level in (1, 2, 3):
            total = forward_taps(source, level, 1)
            if any(level == entry[0] for entry in extras):
                total = total + extra[level - 1, number]
            put(level, total)
        twin_term(number).start()
        return carry

    lax.fori_loop(0, 1, forward_group, 0)

    def hop(source, landing, device_chip, number):
        return pltpu.make_async_remote_copy(
            source,
            landing,
            send_sem.at[number],
            recv_sem.at[number],
            device_id={"space": device_chip * 2 + core},
            device_id_type=MESH_ID,
        )

    base_right, base_left = post.used, post.used + chips
    post.used += 2 * chips
    next_chip = lax.rem(chip + 1, chips)
    prev_chip = lax.rem(chip + last, chips)

    def go_right(number):
        return hop(twin_land.at[number], right_land.at[number], next_chip, base_right + number)

    def go_left(number):
        return hop(twin_land.at[number], left_land.at[number], prev_chip, base_left + number)

    def start_off(number, copy):
        twin_term(number).wait_recv()

        def add(branch, carry):
            twin_land[number, branch] = (
                term[number, core, branch].astype(f32) + twin_land[number, branch].astype(f32)
            ).astype(low)
            return carry

        lax.fori_loop(0, 4, add, 0)
        copy.start()

    def pass_on(number, copy, landing, has_incoming):

        @pl.when(jnp.logical_not(has_incoming))
        def _():
            start_off(number, copy)

        @pl.when(has_incoming)
        def _():
            twin_term(number).wait_recv()
            copy.wait_recv()

            def add(branch, carry):
                twin_land[number, branch] = (
                    term[number, core, branch].astype(f32)
                    + twin_land[number, branch].astype(f32)
                    + landing[number, branch].astype(f32)
                ).astype(low)
                return carry

            lax.fori_loop(0, 4, add, 0)
            copy.start()

    @pl.when(chip == 0)
    def _():
        start_off(last, go_right(last))

    @pl.when(chip == last)
    def _():
        start_off(0, go_left(0))

    lax.fori_loop(1, chips, forward_group, 0)

    def pass_right(number):
        there = (chip < number) if number < last else ((chip < number) & (chip > 0))

        @pl.when(there)
        def _():
            pass_on(number, go_right(number), right_land, chip > 0)

    def pass_left(number):
        there = (chip > number) if number > 0 else ((chip > number) & (chip < last))

        @pl.when(there)
        def _():
            pass_on(number, go_left(number), left_land, chip < last)

    def turn_group(number, carry):
        source = rows_of(sh_ref, number)
        turned[:, pl.ds(pl.multiple_of(number * group, group), group)] = source.T
        return carry + jnp.sum(source.astype(f32), axis=0, keepdims=True)

    pixel_sum = lax.fori_loop(0, chips, turn_group, jnp.zeros((1, width), f32))

    @pl.when(chip < chips // 2)
    def _():
        for number in range(last):
            pass_right(last - number)
            pass_left(number)

    @pl.when(chip >= chips // 2)
    def _():
        for number in range(last):
            pass_left(number)
            pass_right(last - number)

    band_rows = pixels // cols
    mask_own = row_mask(widths_ref, band * band_rows, band_rows, cols)
    mask_own = jnp.concatenate([mask_own] * (width // LANE), axis=1)
    inv_count = jnp.concatenate([1.0 / count_pixels(widths_ref)] * (width // LANE), axis=1)
    spread = width // LANE

    def put_rows(target, number, value):
        for part in range(spread):
            target[pl.ds(number * spread + part, 1), :] = value[:, part * LANE : (part + 1) * LANE]

    def get_rows(target, number):
        return jnp.concatenate(
            [target[pl.ds(number * spread + part, 1), :] for part in range(spread)], axis=1
        )

    def column_sum(value):
        return jnp.sum(value, axis=0, keepdims=True)

    twin_term(chip).wait_recv()

    @pl.when(chip > 0)
    def _():
        go_right(chip).wait_recv()

    @pl.when(chip < last)
    def _():
        go_left(chip).wait_recv()

    @pl.when(chip == 0)
    def _():
        right_land[0] = jnp.zeros(right_land.shape[1:], low)

    @pl.when(chip == last)
    def _():
        left_land[last] = jnp.zeros(left_land.shape[1:], low)

    st_both[...] = jnp.zeros_like(st_both)

    def settle(branch, carry):
        value = (
            term[chip, core, branch].astype(f32)
            + twin_land[chip, branch].astype(f32)
            + right_land[chip, branch].astype(f32)
            + left_land[chip, branch].astype(f32)
        )
        pre[branch] = value
        kept = value * mask_own
        put_rows(st_both, branch, column_sum(kept))
        put_rows(st_both, 4 + branch, column_sum(kept * value))
        return carry

    lax.fori_loop(0, 4, settle, 0)
    high = pixel_sum.astype(low)
    rest = pixel_sum - high.astype(f32)
    middle = rest.astype(low)
    tail = (rest - middle.astype(f32)).astype(low)
    pieces = jnp.concatenate(
        [high.astype(f32), middle.astype(f32), tail.astype(f32), jnp.zeros((13, width), f32)],
        axis=0,
    ).astype(low)
    put_rows(st_both, 8, column_sum(dot_nn(pieces, bw_ref[:, width:])))
    st_both_sum[...] = at.sum_over(post, "space", st_both, st_both_land)
    pooled = get_rows(st_both_sum, 8) * inv_count

    def lanes_of(number):
        return pl.ds(pl.multiple_of(number * width, width), width)

    def scale_of(target, first, second):
        mean_value = get_rows(target, first) * inv_count
        variance = get_rows(target, second) * inv_count - mean_value * mean_value
        return mean_value, lax.rsqrt(variance + NORM_EPS)

    def activate(branch, projected):
        mean_value, inv_std = scale_of(st_both_sum, branch, 4 + branch)
        hat = (pre[branch] - mean_value) * inv_std
        pre[branch] = hat
        normed = gain_ref[:, lanes_of(branch)] * hat + shift_ref[:, lanes_of(branch)]
        active = (gelu_of(normed) * mask_own).astype(low)
        joined[branch] = active
        return projected + dot_nn(active, pw_ref[lanes_of(branch), :])

    joined[4] = (gelu_of(pooled).astype(low).astype(f32) * mask_own).astype(low)
    projected = dot_nn(joined[4], pw_ref[4 * width : 5 * width, :])
    projected = lax.fori_loop(0, 4, activate, projected)
    kept = projected * mask_own
    st_proj[...] = jnp.zeros_like(st_proj)
    put_rows(st_proj, 0, column_sum(kept))
    put_rows(st_proj, 1, column_sum(kept * projected))
    st_proj_sum[...] = at.sum_over(post, "space", st_proj, st_proj_land)
    mean_value, inv_std = scale_of(st_proj_sum, 0, 1)
    hat = (projected - mean_value) * inv_std
    gain_proj = gain_ref[:, 4 * width : 5 * width]
    normed = gain_proj * hat + shift_ref[:, 4 * width : 5 * width]
    proj_up = gelu_slope(normed) * cot_ref[...].astype(f32) * mask_own
    st_pback[...] = jnp.zeros_like(st_pback)
    put_rows(st_pback, 0, column_sum(proj_up))
    put_rows(st_pback, 1, column_sum(proj_up * hat))
    proj_sums_out[...] = at.sum_over(post, "space", st_pback, st_pback_land)
    head_out[...] = (gelu_of(normed) * mask_own).astype(low)
    shift_grad, gain_grad = get_rows(proj_sums_out, 0), get_rows(proj_sums_out, 1)
    proj_low = (
        mask_own
        * (gain_proj * inv_std)
        * (proj_up - shift_grad * inv_count - hat * (gain_grad * inv_count))
    ).astype(low)
    st_back[...] = jnp.zeros_like(st_back)

    def back_step(branch, carry):
        joined_grad = dot_nt(proj_low, pw_ref[lanes_of(branch), :])
        hat = pre[branch]
        normed = gain_ref[:, lanes_of(branch)] * hat + shift_ref[:, lanes_of(branch)]
        up = gelu_slope(normed) * joined_grad * mask_own
        upstream[branch] = up
        put_rows(st_back, branch, column_sum(up))
        put_rows(st_back, 4 + branch, column_sum(up * hat))
        return carry

    lax.fori_loop(0, 4, back_step, 0)
    pool_total = column_sum(dot_nt(proj_low, pw_ref[4 * width : 5 * width, :]) * mask_own)
    put_rows(st_back, 8, pool_total)
    both_sums_out[...] = at.sum_over(post, "space", st_back, st_back_land)
    pool_grad = (gelu_slope(pooled) * get_rows(both_sums_out, 8)).astype(low)
    column = jnp.broadcast_to(pixel_sum, (8, width)).T[:, 0:1]
    grads_out[len(taps) + 1] = (
        column * (pool_grad.astype(f32) * inv_count)
    ).astype(low)

    def make_both(branch):
        _, inv_std = scale_of(st_both_sum, branch, 4 + branch)
        shift_grad = get_rows(both_sums_out, branch) * inv_count
        gain_grad = get_rows(both_sums_out, 4 + branch) * inv_count
        both_all[band, branch] = (
            mask_own
            * (gain_ref[:, lanes_of(branch)] * inv_std)
            * (upstream[branch] - shift_grad - pre[branch] * gain_grad)
        ).astype(low)

    moved_levels = sorted({entry[0] for entry in extras})
    slots = moved_levels + [branch for branch in range(4) if branch not in moved_levels]
    all_right = post.used
    all_left = all_right + 4 * chips
    all_twin = all_left + 4 * chips

    def block_of(number, slot):
        return both_all.at[number * 2 + core, slots[slot]]

    def send_right(step, slot):
        block = block_of(lax.rem(chip - step + 1 + chips, chips), slot)
        return hop(block, block, next_chip, all_right + 4 * step + slot)

    def send_left(step, slot):
        block = block_of(lax.rem(chip + step - 1, chips), slot)
        return hop(block, block, prev_chip, all_left + 4 * step + slot)

    def hand_over(number, slot):
        block = block_of(number, slot)
        return pltpu.make_async_remote_copy(
            block,
            block,
            send_sem.at[all_twin + 4 * number + slot],
            recv_sem.at[all_twin + 4 * number + slot],
            device_id=at.twin,
            device_id_type=MESH_ID,
        )

    def from_left(step, slot):
        block = block_of(lax.rem(chip - step + chips, chips), slot)
        return hop(block, block, next_chip, all_right + 4 * step + slot)

    def from_right(step, slot):
        block = block_of(lax.rem(chip + step, chips), slot)
        return hop(block, block, prev_chip, all_left + 4 * step + slot)

    for slot in range(4):
        make_both(slots[slot])

        @pl.when(chip < last)
        def _():
            send_right(1, slot).start()

        @pl.when(chip > 0)
        def _():
            send_left(1, slot).start()

        hand_over(chip, slot).start()

    def proj_step(branch, carry):
        proj_term[lanes_of(branch), :] = dot_nn(joined[branch].T, proj_low).astype(low)
        return carry

    lax.fori_loop(0, 5, proj_step, 0)
    rows_p = proj_share.shape[0]

    def proj_rows(number):
        return pl.ds(pl.multiple_of(number * rows_p, rows_p), rows_p)

    post.used = all_twin + 4 * chips
    p_pair = [
        post.push(proj_term.at[proj_rows(2 * number + 1 - core)], p_twin.at[number], at.twin)
        for number in range(chips)
    ]
    grads[...] = jnp.zeros_like(grads)
    pool_row = dot_nt(
        jnp.broadcast_to(pool_grad, (16, width)), bw_ref[:, width:]
    )[0:1] * inv_count
    quarter = pixels // tasks
    my_rows = pl.ds(pl.multiple_of(at.task * quarter, quarter), quarter)
    late = sorted({entry[2] for entry in extras})
    first_task = post.used
    post.used += chips * len(at.other_tasks)

    def to_task(number, turn):
        other = at.other_tasks[turn]
        theirs = pl.ds(pl.multiple_of(other * quarter, quarter), quarter)
        two = pl.ds(2 * number, 2)
        spot = first_task + number * len(at.other_tasks) + turn
        return pltpu.make_async_remote_copy(
            sg.at[two, theirs],
            xg_out.at[at.task, two],
            send_sem.at[spot],
            recv_sem.at[spot],
            device_id={"task": other},
            device_id_type=MESH_ID,
        )

    def finish_group(number, total):
        keep = row_mask(widths_ref, number * 2 * band_rows, 2 * band_rows, cols)
        keep = jnp.concatenate([keep] * spread, axis=1)
        value = (total + keep * pool_row).astype(low)
        sg[2 * number] = value[:pixels]
        sg[2 * number + 1] = value[pixels:]
        for turn in range(len(at.other_tasks)):
            to_task(number, turn).start()
        for half in range(2):
            xg_out[at.task, 2 * number + half] = sg[2 * number + half, my_rows]

    def back_slot(slot):
        branch = slots[slot]

        def step_of(step, carry):
            number = group_at(step)
            hand_over(number, slot).wait_recv()
            columns = turned[:, pl.ds(pl.multiple_of(number * group, group), group)]
            part = jnp.concatenate(
                [both_all[2 * number, branch], both_all[2 * number + 1, branch]], axis=0
            )
            if branch == 0:
                total = dot_nt(part, bw_ref[:, :width])
                grads[len(taps)] += dot_nn(columns, part)
            else:
                total = None
                image = part.astype(f32)
                for col_tap in range(3):
                    tap = number_of.get((branch, 1, col_tap))
                    if tap is None:
                        continue
                    part = shift_pixels(image, -right_of(branch, col_tap), cols).astype(low)
                    if branch in moved_levels:
                        moved[moved_levels.index(branch), number, col_tap] = part
                    term_now = dot_nt(part, rate[tap])
                    total = term_now if total is None else total + term_now
                    grads[tap] += dot_nn(columns, part)
            if slot == 0:
                back[number] = total
            else:
                back[number] += total
            if slot == 3:
                ready = number >= 0
                for entry in late:
                    ready = ready & (number != entry)

                @pl.when(ready)
                def _():
                    finish_group(number, back[number])

            return carry

        return step_of

    def far_taps():
        for level, target, source, row_tap in extras:
            columns = turned[:, source * group : (source + 1) * group]
            total = back[source]
            for col_tap in range(3):
                tap = number_of.get((level, row_tap, col_tap))
                if tap is None:
                    continue
                part = moved[moved_levels.index(level), target, col_tap]
                total = total + dot_nt(part, rate[tap])
                grads[tap] += dot_nn(columns, part)
            back[source] = total

    def finish_late(early):
        for number in late:
            near_enough = (chip - number < last) & (number - chip < last)

            @pl.when(near_enough if early else jnp.logical_not(near_enough))
            def _():
                finish_group(number, back[number])

    mirror = chip // 2
    near = chip * (1 - mirror) + (last - chip) * mirror

    def group_at(step):
        place = step + near * (1 - 2 * step) * ((last - step) // 2)
        return place * (1 - mirror) + (last - place) * mirror

    for slot in range(4):
        lax.fori_loop(0, 1, back_slot(slot), 0)
    done = 1
    for step in range(1, chips):
        upto = chips if step == last else step + 1 + near
        for slot in range(4):

            @pl.when(chip >= step)
            def _():
                from_left(step, slot).wait_recv()
                if step < last:

                    @pl.when(chip < last)
                    def _():
                        send_right(step + 1, slot).start()

                hand_over(lax.rem(chip - step + chips, chips), slot).start()

            @pl.when(chip + step <= last)
            def _():
                from_right(step, slot).wait_recv()
                if step < last:

                    @pl.when(chip > 0)
                    def _():
                        send_left(step + 1, slot).start()

                hand_over(lax.rem(chip + step, chips), slot).start()

            lax.fori_loop(done, upto, back_slot(slot), 0)
            if step == last and slot == len(moved_levels) - 1:
                far_taps()
                finish_late(True)
        done = upto

    for made in p_pair:
        made.wait_recv()
    p_in = []
    for step in range(1, chips):
        other = lax.rem(chip + step, chips)
        both = proj_term[proj_rows(2 * other + core)].astype(f32) + p_twin[other].astype(f32)
        p_twin[other] = both.astype(low)
        p_in.append(
            post.push(p_twin.at[other], p_land.at[chip], {"space": other * 2 + core})
        )

    finish_late(False)

    def finish_tap(number, carry):
        grads_out[number] = grads[number].astype(low)
        return carry

    lax.fori_loop(0, len(taps) + 1, finish_tap, 0)

    p_total = proj_term[proj_rows(band)].astype(f32) + p_twin[chip].astype(f32)
    for made in p_in:
        made.wait_recv()
    for step in range(1, chips):
        p_total = p_total + p_land[lax.rem(chip + step, chips)].astype(f32)
    proj_share[...] = p_total.astype(low)

    def tasks_in(number, carry):
        for turn in range(len(at.other_tasks)):
            to_task(number, turn).wait()
        return carry

    lax.fori_loop(0, chips, tasks_in, 0)

    post.close()

    def twin_left(number, carry):
        twin_term(number).wait_send()
        for slot in range(4):
            hand_over(number, slot).wait_send()
        return carry

    lax.fori_loop(0, chips, twin_left, 0)
    for number in range(last):
        to_right, to_left = last - number, number

        @pl.when(chip < to_right)
        def _():
            go_right(to_right).wait_send()

        @pl.when(chip > to_left)
        def _():
            go_left(to_left).wait_send()

    for step in range(1, chips):

        @pl.when((chip < last) & (chip - step + 1 >= 0))
        def _():
            for slot in range(4):
                send_right(step, slot).wait_send()

        @pl.when((chip > 0) & (chip + step - 1 <= last))
        def _():
            for slot in range(4):
                send_left(step, slot).wait_send()


def trunk_phase(
    at,
    post,
    sizes,
    when_loaded,
    x_hbm,
    widths_ref,
    gain_ref,
    shift_ref,
    wr_hbm,
    wd_hbm,
    we_hbm,
    sh_out,
    act,
    h1,
    h2,
    a2,
    h3q,
    v1,
    v2,
    v3,
    stats_out,
    x,
    wr,
    wd,
    we,
    rim,
    turned,
    h3,
    blocks,
    mask_own,
    st1,
    st1_land,
    st2,
    st2_land,
    st3,
    st3_land,
    local_sem,
):
    tasks, bands, cols, quarter, mid, wide, piece = sizes
    low, f32 = jnp.bfloat16, jnp.float32
    task, band = at.task, at.band
    my_rows = pl.ds(pl.multiple_of(task * quarter, quarter), quarter)
    loads = [
        pltpu.make_async_copy(source, target, local_sem.at[number])
        for number, (source, target) in enumerate(
            ((x_hbm, x), (wr_hbm, wr), (wd_hbm, wd), (we_hbm, we))
        )
    ]
    for load in loads[:2]:
        load.start()
    at.greet()
    pixels = x.shape[0]
    band_rows = pixels // cols
    mask = row_mask(widths_ref, band * band_rows, band_rows, cols)
    count = count_pixels(widths_ref)
    spread = mid // LANE

    def across(value, lanes):
        return jnp.concatenate([value] * (lanes // LANE), axis=1)

    def put_sums(target, value, keep):
        kept = value * keep
        first = jnp.sum(kept, axis=0, keepdims=True)
        second = jnp.sum(kept * value, axis=0, keepdims=True)
        for number in range(spread):
            lanes = slice(number * LANE, (number + 1) * LANE)
            target[number : number + 1] = first[:, lanes]
            target[spread + number : spread + number + 1] = second[:, lanes]

    def get_sums(total):
        return [
            jnp.concatenate([total[base + k : base + k + 1] for k in range(spread)], axis=1)
            for base in (0, spread)
        ]

    def put_norm(vectors, lanes, first, second, start):
        width = first.shape[1]
        inv = across(1.0 / count, width)
        mean_value = first * inv
        variance = second * inv - mean_value * mean_value
        vectors[0:1, lanes] = mean_value
        vectors[1:2, lanes] = lax.rsqrt(variance + NORM_EPS)
        vectors[2:3, lanes] = gain_ref[:, start : start + width]
        vectors[3:4, lanes] = shift_ref[:, start : start + width]
        stats_out[0:1, start : start + width] = mean_value
        stats_out[1:2, start : start + width] = variance * across(count / (count - 1.0), width)

    def activate(hidden, vectors, keep):
        normed = vectors[2:3] * ((hidden - vectors[0:1]) * vectors[1:2]) + vectors[3:4]
        return (gelu_of(normed) * keep).astype(low)

    mask_mid = across(mask, mid)
    for load in loads[:2]:
        load.wait()
    for load in loads[2:]:
        load.start()
    when_loaded()
    h1[...] = dot_nn(x[...], wr[...])
    at.meet()
    put_sums(st1, h1[...], mask_mid)
    first, second = get_sums(at.sum_over(post, "space", st1, st1_land))
    put_norm(v1, slice(0, mid), first, second, 0)
    rim[1] = activate(h1[...], v1, mask_mid)

    has_above, has_below = band > 0, band < bands - 1
    up = post.copy(rim.at[1], rim.at[2], {"space": lax.rem(band + bands - 1, bands)})
    down = post.copy(rim.at[1], rim.at[0], {"space": lax.rem(band + 1, bands)})

    @pl.when(has_above)
    def _():
        up.start()

    @pl.when(has_below)
    def _():
        down.start()

    @pl.when(jnp.logical_not(has_above))
    def _():
        rim[0] = jnp.zeros(rim.shape[1:], low)

    @pl.when(jnp.logical_not(has_below))
    def _():
        rim[2] = jnp.zeros(rim.shape[1:], low)

    loads[2].wait()
    halves = [slice(start, start + piece) for start in range(0, mid, piece)]

    def tap_sum(row_taps, lanes):
        total = None
        for col_tap in range(3):
            part = None
            for row_tap in row_taps:
                term = dot_nn(rim[row_tap], wd[3 * row_tap + col_tap, :, lanes])
                part = term if part is None else part + term
            part = shift_pixels(part, CONV_DILATION * (col_tap - 1), cols)
            total = part if total is None else total + part
        return total

    for lanes in halves:
        h2[:, lanes] = tap_sum((1,), lanes)

    turned[...] = rim[1].T

    @pl.when(has_below)
    def _():
        up.wait_recv()

    @pl.when(has_above)
    def _():
        down.wait_recv()

    for lanes in halves:
        h2[:, lanes] += tap_sum((0, 2), lanes)

    put_sums(st2, h2[...], mask_mid)
    first, second = get_sums(at.sum_over(post, "space", st2, st2_land))
    put_norm(v2, slice(0, mid), first, second, mid)
    a2[...] = activate(h2[...], v2, mask_mid)

    loads[3].wait()
    mask_piece = across(mask, piece)
    per_row = st3.shape[1] // piece
    half = st3.shape[0] // 2

    def expand_step(number, carry):
        lanes = pl.ds(pl.multiple_of(number * piece, piece), piece)
        value = dot_nn(a2[...], we[:, lanes])
        h3[:, lanes] = value
        kept = value * mask_piece
        row = number // per_row
        spot = pl.ds(pl.multiple_of(lax.rem(number, per_row) * piece, piece), piece)
        st3[pl.ds(row, 1), spot] = jnp.sum(kept, axis=0, keepdims=True)
        st3[pl.ds(half + row, 1), spot] = jnp.sum(kept * value, axis=0, keepdims=True)
        return carry

    lax.fori_loop(0, bands, expand_step, 0)
    begun = at.sum_begin(post, "space", st3, st3_land)
    h3q[...] = h3[my_rows]
    total = at.sum_end(begun)
    lanes_in = st3.shape[1]
    for row in range(half):
        put_norm(
            v3,
            slice(row * lanes_in, (row + 1) * lanes_in),
            total[row : row + 1],
            total[half + row : half + row + 1],
            2 * mid + row * lanes_in,
        )

    mask_own[...] = mask
    mask_quarter = across(mask_own[my_rows], piece)

    def shared_of(number):
        lanes = pl.ds(pl.multiple_of(number * piece, piece), piece)
        hat = (h3q[:, lanes] - v3[0:1, lanes]) * v3[1:2, lanes]
        before = v3[2:3, lanes] * hat + v3[3:4, lanes] + x[my_rows, lanes].astype(f32)
        return (gelu_of(before) * mask_quarter).astype(low)

    slices_in = []
    for other in at.other_bands:
        blocks[other] = shared_of(other)
        slices_in.append(
            post.push(blocks.at[other], sh_out.at[band, my_rows], {"space": other})
        )
    sh_out[band, my_rows] = shared_of(band)

    part = mid // bands

    def part_of(number):
        return turned.at[pl.ds(pl.multiple_of(number * part, part), part)]

    act[0] = jnp.zeros(act.shape[1:], low)
    act[bands + 1] = jnp.zeros(act.shape[1:], low)
    act[band + 1] = part_of(band)[...]
    parts_in = [
        post.push(part_of(other), act.at[band + 1], {"space": other}) for other in at.other_bands
    ]

    def to_tasks(number):
        block = sh_out.at[number, my_rows]
        return [post.push(block, block, {"task": other}) for other in at.other_tasks]

    quarters_in = to_tasks(band)
    for step, made in enumerate(slices_in, start=1):
        made.wait_recv()
        quarters_in += to_tasks(lax.rem(band + bands - step, bands))
    for made in quarters_in + parts_in:
        made.wait_recv()

    @pl.when(has_above)
    def _():
        up.wait_send()

    @pl.when(has_below)
    def _():
        down.wait_send()


def front_kernel(sizes, plan, counts, *refs):
    refs = list(refs)

    def take(count):
        taken = refs[:count]
        del refs[:count]
        return taken

    x_hbm, widths, gain, shift, wr_hbm, wd_hbm, we_hbm = take(7)
    head_gain, head_shift, cot, bw, pw, rate_hbm = take(6)
    trunk_hbm, head_hbm = take(9), take(6)
    trunk_outs, head_outs = take(9), take(6)
    (shared,), trunk_scratch, head_scratch = take(1), take(counts[0]), take(counts[1])
    send_sem, recv_sem, local_sem, rate_sem, out_sem = refs
    tasks, bands, width, taps = sizes[0], sizes[1], plan[4], plan[5]
    at = Place(tasks, bands)
    post = Post(send_sem, recv_sem)
    rate = head_scratch[0]
    rate_loads = []
    for number, (level, row_tap, col_tap, _, _) in enumerate(taps):
        start = (9 * (level - 1) + 3 * row_tap + col_tap) * width
        rate_loads.append(
            pltpu.make_async_copy(
                rate_hbm.at[:, start : start + width], rate.at[number], rate_sem.at[number]
            )
        )

    def when_loaded():
        for load in rate_loads:
            load.start()

    trunk_phase(
        at,
        post,
        sizes,
        when_loaded,
        x_hbm,
        widths,
        gain,
        shift,
        wr_hbm,
        wd_hbm,
        we_hbm,
        shared,
        *trunk_outs,
        *trunk_scratch,
        local_sem,
    )
    writes = []

    def write(sources, targets):
        for source, target in zip(sources, targets):
            copy = pltpu.make_async_copy(source, target, out_sem.at[len(writes)])
            copy.start()
            writes.append(copy)

    write(trunk_outs, trunk_hbm)
    head_phase(
        at,
        post,
        plan,
        rate_loads,
        shared,
        widths,
        head_gain,
        head_shift,
        cot,
        bw,
        pw,
        *head_outs,
        *head_scratch,
    )
    write(head_outs, head_hbm)
    for copy in writes:
        copy.wait()


def front(tasks, bands, cols, rows, collective, x, widths, gain, shift, wr, wd, we, *head_in):
    low, f32 = jnp.bfloat16, jnp.float32
    head_gain, head_shift, cot, bw, pw, rate = head_in
    pixels, wide = x.shape
    mid = wr.shape[1]
    quarter, piece = pixels // tasks, wide // bands
    width = pw.shape[1]
    chips = bands // 2
    group_rows = rows // chips
    taps = live_taps(rows, cols)
    extras = []
    for level in (1, 2, 3):
        for row_tap in (0, 2):
            if (level, row_tap, 1) in [tap[:3] for tap in taps]:
                away = (row_tap - 1) * level * RATE // group_rows
                extras += [
                    (level, target, target + away, row_tap)
                    for target in range(chips)
                    if 0 <= target + away < chips
                ]
    levels = max([entry[0] for entry in extras], default=1)
    in_vmem = pl.BlockSpec(memory_space=pltpu.VMEM)
    anywhere = pl.BlockSpec(memory_space=pl.ANY)
    shape = jax.ShapeDtypeStruct
    block = (pixels, width)
    both_rows, proj_rows = -(-9 * width // LANE // 8) * 8, 8

    def stats(count, lanes=LANE):
        return [pltpu.VMEM((count, lanes), f32), pltpu.VMEM((bands, count, lanes), f32)]

    trunk_scratch = (
        [
            pltpu.VMEM(x.shape, low),
            pltpu.VMEM(wr.shape, low),
            pltpu.VMEM(wd.shape, low),
            pltpu.VMEM(we.shape, low),
            pltpu.VMEM((3, pixels, mid), low),
            pltpu.VMEM((mid, pixels), low),
            pltpu.VMEM((pixels, wide), f32),
            pltpu.VMEM((bands, quarter, piece), low),
            pltpu.VMEM((pixels, LANE), f32),
        ]
        + stats(2 * mid // LANE)
        + stats(2 * mid // LANE)
        + stats(8, wide // 4)
    )
    head_scratch = (
        [
            pltpu.VMEM((len(taps), piece, width), low),
            pltpu.VMEM((piece, bands * pixels), low),
            pltpu.VMEM((levels, chips, 2 * pixels, width), f32),
            pltpu.VMEM((chips, 2, 4) + block, low),
            pltpu.VMEM((chips, 4) + block, low),
            pltpu.VMEM((chips, 4) + block, low),
            pltpu.VMEM((chips, 4) + block, low),
            pltpu.VMEM((4,) + block, f32),
            pltpu.VMEM((5,) + block, low),
            pltpu.VMEM((4,) + block, f32),
        ]
        + [pltpu.VMEM((both_rows, LANE), f32)]
        + stats(both_rows)
        + [pltpu.VMEM((proj_rows, LANE), f32)]
        + stats(proj_rows)
        + stats(proj_rows)
        + stats(both_rows)
        + [
            pltpu.VMEM((bands, 4) + block, low),
            pltpu.VMEM((levels, chips, 3, 2 * pixels, width), low),
            pltpu.VMEM((len(taps) + 1, piece, width), f32),
            pltpu.VMEM((chips, 2 * pixels, width), f32),
            pltpu.VMEM((bands, pixels, piece), low),
            pltpu.VMEM(pw.shape, low),
            pltpu.VMEM((chips, pw.shape[0] // bands, width), low),
            pltpu.VMEM((chips, pw.shape[0] // bands, width), low),
        ]
    )
    sizes = (tasks, bands, cols, quarter, mid, wide, piece)
    plan = (tasks, bands, cols, pixels, width, tuple(taps), tuple(extras))
    out_shapes = (
        shape((bands + 2, mid // bands, pixels), low),
        shape((pixels, mid), f32),
        shape((pixels, mid), f32),
        shape((pixels, mid), low),
        shape((quarter, wide), f32),
        shape((8, mid), f32),
        shape((8, mid), f32),
        shape((8, wide), f32),
        shape((2, 2 * mid + wide), f32),
        shape(block, low),
        shape((tasks, bands, quarter, piece), low),
        shape((len(taps) + 2, piece, width), low),
        shape((pw.shape[0] // bands, width), low),
        shape((both_rows, LANE), f32),
        shape((proj_rows, LANE), f32),
    )
    return taps, pl.pallas_call(
        functools.partial(front_kernel, sizes, plan, (len(trunk_scratch), len(head_scratch))),
        name="front",
        out_shape=out_shapes,
        in_specs=[anywhere, pl.BlockSpec(memory_space=pltpu.SMEM), in_vmem, in_vmem]
        + [anywhere] * 3
        + [in_vmem] * 5
        + [anywhere],
        out_specs=(anywhere,) * len(out_shapes),
        scratch_shapes=[pltpu.VMEM(out.shape, out.dtype) for out in out_shapes]
        + [pltpu.VMEM((bands, pixels, piece), low)]
        + trunk_scratch
        + head_scratch
        + [
            pltpu.SemaphoreType.DMA((192,)),
            pltpu.SemaphoreType.DMA((192,)),
            pltpu.SemaphoreType.DMA((4,)),
            pltpu.SemaphoreType.DMA((len(taps),)),
            pltpu.SemaphoreType.DMA((len(out_shapes),)),
        ],
        compiler_params=pltpu.CompilerParams(
            collective_id=collective, has_side_effects=True, vmem_limit_bytes=60 << 20
        ),
    )(x, widths, gain, shift, wr, wd, we, *head_in)


def finish_kernel(
    places,
    tap_hbm,
    ho_in,
    ig_in,
    rg_in,
    dg_in,
    eg_in,
    bs_in,
    tw_hbm,
    pg_hbm,
    s3_hbm,
    s2_hbm,
    s1_hbm,
    both_hbm,
    proj_hbm,
    ho_out,
    ig_out,
    rg_out,
    dg_out,
    eg_out,
    bs_out,
    branch_out,
    rate_out,
    pg_out,
    tg_out,
    ts_out,
    hg_out,
    hs_out,
    tw_out,
    tap_ref,
    tw_ref,
    pg_ref,
    s3_ref,
    s2_ref,
    s1_ref,
    both_ref,
    proj_ref,
    ho_buf,
    ig_buf,
    rg_buf,
    dg_buf,
    eg_buf,
    bs_buf,
    branch,
    rate,
    sems,
    load_sems,
):
    f32 = jnp.float32
    width = tap_ref.shape[2]
    loads = [
        pltpu.make_async_copy(source, target, load_sems.at[number])
        for number, (source, target) in enumerate(
            (
                (tap_hbm, tap_ref),
                (pg_hbm, pg_ref),
                (tw_hbm, tw_ref),
                (s3_hbm, s3_ref),
                (s2_hbm, s2_ref),
                (s1_hbm, s1_ref),
                (both_hbm, both_ref),
                (proj_hbm, proj_ref),
            )
        )
    ]
    for load in loads:
        load.start()
    passed = [
        (ho_in, ho_buf, ho_out),
        (ig_in, ig_buf, ig_out),
        (rg_in, rg_buf, rg_out),
        (dg_in, dg_buf, dg_out),
        (eg_in, eg_buf, eg_out),
        (bs_in, bs_buf, bs_out),
    ]
    passes = [
        (
            pltpu.make_async_copy(source, buffer, load_sems.at[len(loads) + number]),
            pltpu.make_async_copy(buffer, target, sems.at[number]),
        )
        for number, (source, buffer, target) in enumerate(passed)
    ]
    for copy, _ in passes:
        copy.start()
    copies = [copy for _, copy in passes]
    per_level = len(places) // 3
    loads[0].wait()
    for level in range(3):
        for number in range(level * per_level, (level + 1) * per_level):
            lanes = slice(number * width, (number + 1) * width)
            if places[number] is None:
                rate[:, lanes] = jnp.zeros((rate.shape[0], width), f32)
            else:
                rate[:, lanes] = tap_ref[places[number]].astype(f32)
        lanes = slice(level * per_level * width, (level + 1) * per_level * width)
        copy = pltpu.make_async_copy(
            rate.at[:, lanes], rate_out.at[:, lanes], sems.at[len(copies)]
        )
        copy.start()
        copies.append(copy)
    for arrival, copy in passes:
        arrival.wait()
        copy.start()
    count = tap_ref.shape[0]
    branch[:, :width] = tap_ref[count - 2].astype(f32)
    branch[:, width:] = tap_ref[count - 1].astype(f32)
    copy = pltpu.make_async_copy(branch, branch_out, sems.at[len(copies)])
    copy.start()
    copies.append(copy)
    for load in loads[1:]:
        load.wait()
    pg_out[...] = pg_ref[...].astype(f32)
    rows = s1_ref.shape[0] // 2
    ts_out[0:rows] = s1_ref[0:rows]
    tg_out[0:rows] = s1_ref[rows : 2 * rows]
    ts_out[rows : 2 * rows] = s2_ref[0:rows]
    tg_out[rows : 2 * rows] = s2_ref[rows : 2 * rows]
    half, lanes_in = s3_ref.shape[0] // 2, s3_ref.shape[1]
    for row in range(half):
        for part in range(lanes_in // LANE):
            target = 2 * rows + row * (lanes_in // LANE) + part
            lanes = slice(part * LANE, (part + 1) * LANE)
            ts_out[target : target + 1] = s3_ref[row : row + 1, lanes]
            tg_out[target : target + 1] = s3_ref[half + row : half + row + 1, lanes]
    spread = width // LANE
    for row in range(4 * spread):
        lanes = slice(row * LANE, (row + 1) * LANE)
        hs_out[:, lanes] = both_ref[row : row + 1]
        hg_out[:, lanes] = both_ref[4 * spread + row : 4 * spread + row + 1]
    for row in range(spread):
        lanes = slice((4 * spread + row) * LANE, (4 * spread + row + 1) * LANE)
        hs_out[:, lanes] = proj_ref[row : row + 1]
        hg_out[:, lanes] = proj_ref[spread + row : spread + row + 1]
    tasks = tw_out.shape[1]
    place = lax.broadcasted_iota(jnp.int32, (1, LANE), 1)
    weights = jnp.zeros((1, LANE), f32)
    for number in range(tasks):
        weights = jnp.where(place == number, tw_ref[number : number + 1], weights)
    tw_out[...] = weights[:, :tasks]
    for copy in copies:
        copy.wait()


def finish(places, tasks, taps, ho, ig, rg, dg, eg, bs, tw, pg, s3, s2, s1, both, proj):
    f32 = jnp.float32
    in_vmem = pl.BlockSpec(memory_space=pltpu.VMEM)
    anywhere = pl.BlockSpec(memory_space=pl.ANY)
    shape = jax.ShapeDtypeStruct
    depth, width = taps.shape[1:]
    rows = (s1.size + s2.size + s3.size) // 2 // LANE
    return pl.pallas_call(
        functools.partial(finish_kernel, places),
        name="finish",
        out_shape=(
            shape(ho.shape, ho.dtype),
            shape(ig.shape, ig.dtype),
            shape(rg.shape, rg.dtype),
            shape(dg.shape, dg.dtype),
            shape(eg.shape, eg.dtype),
            shape(bs.shape, bs.dtype),
            shape((depth, 2 * width), f32),
            shape((depth, len(places) * width), f32),
            shape(pg.shape, f32),
            shape((rows, LANE), f32),
            shape((rows, LANE), f32),
            shape((1, 5 * width), f32),
            shape((1, 5 * width), f32),
            shape((1, tasks), f32),
        ),
        in_specs=[anywhere] * 14,
        out_specs=(anywhere,) * 8 + (in_vmem,) * 6,
        scratch_shapes=[
            pltpu.VMEM(value.shape, value.dtype) for value in (taps, tw, pg, s3, s2, s1, both, proj, ho, ig, rg, dg, eg, bs)
        ]
        + [
            pltpu.VMEM((depth, 2 * width), f32),
            pltpu.VMEM((depth, len(places) * width), f32),
            pltpu.SemaphoreType.DMA((10,)),
            pltpu.SemaphoreType.DMA((14,)),
        ],
        compiler_params=pltpu.CompilerParams(vmem_limit_bytes=60 << 20),
    )(taps, ho, ig, rg, dg, eg, bs, tw, pg, s3, s2, s1, both, proj)


def live_taps(rows, cols):
    taps = []
    for level in (1, 2, 3):
        for row_tap in range(3):
            for col_tap in range(3):
                down, right = (row_tap - 1) * level * RATE, (col_tap - 1) * level * RATE
                if abs(down) < rows and abs(right) < cols:
                    taps.append((level, row_tap, col_tap, down, right))
    return taps


def per_device_slices(
    features,
    row_width,
    w_reduce,
    w_dilated,
    w_expand,
    trunk_gain,
    trunk_shift,
    branch_weight,
    rate_weight,
    proj_weight,
    head_gain,
    head_shift,
    head_cot,
):
    bands, tasks = lax.axis_size("space"), lax.axis_size("task")
    band_rows, cols, in_width = features.shape
    rows = band_rows * bands
    pixels = band_rows * cols
    head_width = proj_weight.shape[2]
    inputs = features.reshape(pixels, in_width)
    dilated = w_dilated.transpose(1, 0, 2)
    taps, (
        act,
        h1,
        h2,
        a2,
        h3q,
        v1,
        v2,
        v3,
        batch_stats,
        head_out,
        task_grads,
        tap_grads,
        proj_share,
        both_sums,
        proj_sums,
    ) = front(
        tasks,
        bands,
        cols,
        rows,
        0,
        inputs,
        row_width,
        trunk_gain.reshape(1, -1),
        trunk_shift.reshape(1, -1),
        w_reduce,
        dilated,
        w_expand,
        head_gain,
        head_shift,
        head_cot.reshape(pixels, head_width),
        branch_weight[0],
        proj_weight[0],
        rate_weight[0],
    )
    (
        weight_rows,
        input_grad,
        reduce_grad,
        dilated_grad,
        expand_grad,
        sums_three,
        sums_two,
        sums_one,
        proj_grad,
    ) = trunk_back(
        tasks,
        bands,
        cols,
        1,
        task_grads,
        h3q,
        inputs,
        v3,
        h2,
        v2,
        h1,
        v1,
        act,
        a2,
        row_width,
        w_expand,
        dilated,
        w_reduce,
        proj_share,
    )
    place_of = {tap[:3]: number for number, tap in enumerate(taps)}
    places = tuple(
        place_of.get((level, row_tap, col_tap))
        for level in (1, 2, 3)
        for row_tap in range(3)
        for col_tap in range(3)
    )
    (
        head_out,
        input_grad,
        reduce_grad,
        dilated_grad,
        expand_grad,
        batch_stats,
        branch_grad,
        rate_grad,
        proj_grad,
        trunk_gains,
        trunk_shifts,
        head_gains,
        head_shifts,
        task_weight,
    ) = finish(
        places,
        tasks,
        tap_grads,
        head_out,
        input_grad,
        reduce_grad,
        dilated_grad,
        expand_grad,
        batch_stats,
        weight_rows,
        proj_grad.reshape(-1, head_width),
        sums_three,
        sums_two,
        sums_one,
        both_sums,
        proj_sums,
    )
    return (
        head_out.reshape(1, band_rows, cols, head_width),
        input_grad.reshape(features.shape),
        reduce_grad,
        dilated_grad.transpose(1, 0, 2),
        expand_grad,
        trunk_gains.reshape(-1),
        trunk_shifts.reshape(-1),
        batch_stats,
        branch_grad[None],
        rate_grad[None],
        proj_grad[None],
        head_gains,
        head_shifts,
        task_weight.reshape(-1),
    )


def solution(mesh):
    body = per_device_slices if mesh.shape["space"] == 8 else per_device
    return jax.shard_map(
        body,
        mesh=mesh,
        in_specs=(
            P("space", None, None),
            P(),
            P(),
            P(),
            P(),
            P(),
            P(),
            P("task", "space", None),
            P("task", "space", None),
            P("task", None, None),
            P("task", None),
            P("task", None),
            P("task", "space", None, None),
        ),
        out_specs=(
            P("task", "space", None, None),
            P("space", None, None),
            P("space", None),
            P("space", None, None),
            P("space", None),
            P(),
            P(),
            P(),
            P("task", "space", None),
            P("task", "space", None),
            P("task", None, None),
            P("task", None),
            P("task", None),
            P(),
        ),
        check_vma=False,
    )
```

```python
import functools

import jax
import jax.numpy as jnp
from jax import lax
from jax.experimental import pallas as pl
from jax.experimental.pallas import tpu as pltpu
from jax.sharding import PartitionSpec as P

CONV_DILATION = 2
RATE = 12


NORM_EPS = 1e-05
GRAM_EPS = 1e-06
PRECISE = lax.Precision.HIGHEST


def with_halo(block, sides, width):
    for axis, dim in sides:
        count = lax.axis_size(axis)
        forward = [(i, i + 1) for i in range(count - 1)]
        backward = [(target, source) for source, target in forward]
        low = lax.ppermute(
            lax.slice_in_dim(block, block.shape[dim] - width, None, axis=dim), axis, forward
        )
        high = lax.ppermute(lax.slice_in_dim(block, 0, width, axis=dim), axis, backward)
        block = jnp.concatenate([low, block, high], axis=dim)
    return block


def from_behind(shard, axis, by):
    count = lax.axis_size(axis)
    pairs = [(i, i + by) for i in range(count) if 0 <= i + by < count]
    return lax.ppermute(shard, axis, pairs)


def small_solve(matrix, target):
    size_n = matrix.shape[0]
    rows_list = [matrix[number] for number in range(size_n)]
    values = [target[number] for number in range(size_n)]
    for pivot_row in range(size_n):
        for lower_row in range(pivot_row + 1, size_n):
            factor = rows_list[lower_row][pivot_row] / rows_list[pivot_row][pivot_row]
            rows_list[lower_row] = rows_list[lower_row] - factor * rows_list[pivot_row]
            values[lower_row] = values[lower_row] - factor * values[pivot_row]
    answer = [None] * size_n
    for pivot_row in reversed(range(size_n)):
        running = values[pivot_row]
        for later_row in range(pivot_row + 1, size_n):
            running = running - rows_list[pivot_row][later_row] * answer[later_row]
        answer[pivot_row] = running / rows_list[pivot_row][pivot_row]
    return jnp.stack(answer)


def imtl_weights(gram_matrix):
    grad_norms = jnp.sqrt(jnp.diagonal(gram_matrix) + GRAM_EPS)
    projections = gram_matrix / grad_norms[None, :]
    system = projections[0, 0] - projections[0:1, 1:] - projections[1:, 0:1] + projections[1:, 1:]
    target = projections[0, 0] - projections[0, 1:]
    other_weights = small_solve(jnp.transpose(system), target)
    return jnp.concatenate([(1.0 - jnp.sum(other_weights))[None], other_weights])


def gelu_back(value, upstream):
    return jax.vjp(jax.nn.gelu, value)[1](upstream)[0]


def channel_sums(members):
    return lax.psum(members, "space")


def norm_values(hidden, first_total, second_total, gain_vec, shift_vec, pixel_count):
    mean_value = first_total / pixel_count
    variance = second_total / pixel_count - mean_value * mean_value
    inv_std = lax.rsqrt(variance + NORM_EPS)
    scaled = (hidden - mean_value) * inv_std
    return (gain_vec * scaled + shift_vec, scaled, inv_std, mean_value, variance)


def norm_forward(hidden, gain_vec, shift_vec, valid_mask, pixel_count):
    totals = channel_sums(
        (jnp.sum(hidden * valid_mask, axis=0), jnp.sum(hidden * hidden * valid_mask, axis=0))
    )
    return norm_values(hidden, totals[0], totals[1], gain_vec, shift_vec, pixel_count)


def norm_finish(
    upstream, scaled, inv_std, gain_vec, gain_grad, shift_grad, valid_mask, pixel_count
):
    return (
        valid_mask
        * gain_vec
        * inv_std
        * (upstream - shift_grad / pixel_count - scaled * gain_grad / pixel_count)
    )


def norm_backward(upstream, scaled, inv_std, gain_vec, valid_mask, pixel_count):
    totals = channel_sums(
        (jnp.sum(upstream * valid_mask, axis=0), jnp.sum(upstream * scaled * valid_mask, axis=0))
    )
    hidden_grad = norm_finish(
        upstream, scaled, inv_std, gain_vec, totals[1], totals[0], valid_mask, pixel_count
    )
    return (hidden_grad, totals[1], totals[0])


def band_rim(strip_image):
    return with_halo(strip_image, (("space", 0),), CONV_DILATION)


def far_rows(strip_image, bands_away, upward):
    if bands_away >= lax.axis_size("space"):
        return jnp.zeros_like(strip_image)
    if upward:
        return from_behind(strip_image, "space", bands_away)
    return from_behind(strip_image, "space", -bands_away)


def trunk_taps(padded, reach_cells, rows_count, cols_count, flipped):
    col_padded = jnp.pad(padded, ((0, 0), (reach_cells, reach_cells), (0, 0)))
    pieces = []
    for row_tap in range(3):
        for col_tap in range(3):
            row_from = (2 - row_tap) * reach_cells if flipped else row_tap * reach_cells
            col_from = (2 - col_tap) * reach_cells if flipped else col_tap * reach_cells
            pieces.append(
                col_padded[
                    row_from : row_from + rows_count, col_from : col_from + cols_count
                ].reshape(rows_count * cols_count, -1)
            )
    return jnp.stack(pieces, axis=1)


def per_device(
    features,
    row_width,
    w_reduce,
    w_dilated,
    w_expand,
    trunk_gain,
    trunk_shift,
    branch_weight,
    rate_weight,
    proj_weight,
    head_gain,
    head_shift,
    head_cot,
):
    band_rows, cols_count, in_width = features.shape
    pixels = band_rows * cols_count
    middle_width = w_reduce.shape[1]
    head_width = proj_weight.shape[2]
    first_row = lax.axis_index("space") * band_rows
    widths = lax.dynamic_slice_in_dim(row_width, first_row, band_rows)
    valid_mask = (
        (jnp.arange(cols_count)[None, :] < widths[:, None]).astype(jnp.float32).reshape(pixels, 1)
    )
    pixel_count = jnp.sum(row_width).astype(jnp.float32)
    inputs = features.reshape(pixels, in_width)
    gain_one, shift_one = (trunk_gain[:middle_width], trunk_shift[:middle_width])
    gain_two, shift_two = (
        trunk_gain[middle_width : 2 * middle_width],
        trunk_shift[middle_width : 2 * middle_width],
    )
    gain_three, shift_three = (trunk_gain[2 * middle_width :], trunk_shift[2 * middle_width :])
    hidden_one = jnp.dot(inputs, w_reduce, preferred_element_type=jnp.float32)
    stats_one = norm_forward(hidden_one, gain_one, shift_one, valid_mask, pixel_count)
    first_active = (jax.nn.gelu(stats_one[0]) * valid_mask).astype(jnp.bfloat16)
    patches = trunk_taps(
        band_rim(first_active.reshape(band_rows, cols_count, middle_width)),
        CONV_DILATION,
        band_rows,
        cols_count,
        False,
    )
    hidden_two = jnp.einsum("pti,ito->po", patches, w_dilated, preferred_element_type=jnp.float32)
    stats_two = norm_forward(hidden_two, gain_two, shift_two, valid_mask, pixel_count)
    active_two = (jax.nn.gelu(stats_two[0]) * valid_mask).astype(jnp.bfloat16)
    hidden_three = jnp.dot(active_two, w_expand, preferred_element_type=jnp.float32)
    stats_three = norm_forward(hidden_three, gain_three, shift_three, valid_mask, pixel_count)
    before_act = stats_three[0] + inputs.astype(jnp.float32)
    shared = (jax.nn.gelu(before_act) * valid_mask).astype(jnp.bfloat16)
    proj_local = proj_weight[0]
    gain_local = head_gain[0]
    shift_local = head_shift[0]
    joined_weight = jnp.concatenate([branch_weight[0], rate_weight[0]], axis=1)
    pixel_sum = jnp.dot(
        valid_mask.reshape(1, pixels).astype(jnp.bfloat16),
        shared,
        preferred_element_type=jnp.float32,
    )[0]
    shared_image = shared.reshape(band_rows, cols_count, in_width)
    padded_sources = []
    for level in (1, 2, 3):
        reach = level * RATE
        bands_away = reach // band_rows
        triple = (
            far_rows(shared_image, bands_away, True),
            shared_image,
            far_rows(shared_image, bands_away, False),
        )
        padded_sources.append(
            [jnp.pad(source, ((0, 0), (reach, reach), (0, 0))) for source in triple]
        )
    zero_rows = jnp.zeros((pixels, head_width), jnp.float32)
    start_totals = (
        zero_rows,
        jnp.zeros((1, head_width), jnp.float32),
        zero_rows,
        zero_rows,
        zero_rows,
    )
    all_weights = lax.all_gather(joined_weight, "space", axis=0, tiled=True)
    width_now = all_weights.shape[0]
    one_acc = jnp.dot(shared, all_weights[:, :head_width], preferred_element_type=jnp.float32)
    pool_cols = pixel_sum[None]
    pool_acc = jnp.dot(
        pool_cols,
        all_weights[:, head_width : 2 * head_width].astype(jnp.float32),
        precision=PRECISE,
        preferred_element_type=jnp.float32,
    )
    rate_accs = []
    for fold_level_index in range(3):
        fold_reach = (fold_level_index + 1) * RATE
        running = start_totals[2 + fold_level_index]
        for fold_row_tap in range(3):
            fold_source = padded_sources[fold_level_index][fold_row_tap]
            for fold_col_tap in range(3):
                window = fold_source[
                    :, fold_col_tap * fold_reach : fold_col_tap * fold_reach + cols_count
                ].reshape(pixels, width_now)
                column = (2 + 9 * fold_level_index + 3 * fold_row_tap + fold_col_tap) * head_width
                running = running + jnp.dot(
                    window,
                    all_weights[:, column : column + head_width],
                    preferred_element_type=jnp.float32,
                )
        rate_accs.append(running)
    pre_both = jnp.concatenate([one_acc, rate_accs[0], rate_accs[1], rate_accs[2]], axis=1)
    gain_both, shift_both = (gain_local[: 4 * head_width], shift_local[: 4 * head_width])
    totals = channel_sums(
        (
            jnp.sum(pre_both * valid_mask, axis=0),
            jnp.sum(pre_both * pre_both * valid_mask, axis=0),
            pool_acc[0],
        )
    )
    stats_both = norm_values(pre_both, totals[0], totals[1], gain_both, shift_both, pixel_count)
    pooled = totals[2][None] / pixel_count
    active_both = (jax.nn.gelu(stats_both[0]) * valid_mask).astype(jnp.bfloat16)
    active_pool = jax.nn.gelu(pooled).astype(jnp.bfloat16)
    joined = jnp.concatenate(
        [active_both, (active_pool.astype(jnp.float32) * valid_mask).astype(jnp.bfloat16)], axis=1
    )
    projected = jnp.dot(joined, proj_local, preferred_element_type=jnp.float32)
    gain_proj = gain_local[4 * head_width :]
    stats_proj = norm_forward(
        projected, gain_proj, shift_local[4 * head_width :], valid_mask, pixel_count
    )
    head_result = (jax.nn.gelu(stats_proj[0]) * valid_mask).astype(jnp.bfloat16)
    cot_rows = head_cot[0].reshape(pixels, head_width).astype(jnp.float32)
    proj_upstream = gelu_back(stats_proj[0], cot_rows * valid_mask)
    proj_hidden, proj_gain_grad, proj_shift_grad = norm_backward(
        proj_upstream, stats_proj[1], stats_proj[2], gain_proj, valid_mask, pixel_count
    )
    proj_low = proj_hidden.astype(jnp.bfloat16)
    joined_grad = lax.dot_general(
        proj_low, proj_local, (((1,), (1,)), ((), ())), preferred_element_type=jnp.float32
    )
    proj_term = lax.dot_general(
        joined, proj_low, (((0,), (0,)), ((), ())), preferred_element_type=jnp.float32
    )
    both_upstream = gelu_back(stats_both[0], joined_grad[:, : 4 * head_width] * valid_mask)
    pool_total = jnp.sum(joined_grad[:, 4 * head_width :] * valid_mask, axis=0)
    back_totals = channel_sums(
        (
            proj_term,
            pool_total,
            jnp.sum(both_upstream * valid_mask, axis=0),
            jnp.sum(both_upstream * stats_both[1] * valid_mask, axis=0),
        )
    )
    pool_grad = gelu_back(pooled, back_totals[1][None]).astype(jnp.bfloat16)
    both_grad = norm_finish(
        both_upstream,
        stats_both[1],
        stats_both[2],
        gain_both,
        back_totals[3],
        back_totals[2],
        valid_mask,
        pixel_count,
    ).astype(jnp.bfloat16)
    tap_grads = []
    for level_index in range(3):
        reach = (level_index + 1) * RATE
        bands_away = reach // band_rows
        rate_image = both_grad[
            :, (1 + level_index) * head_width : (2 + level_index) * head_width
        ].reshape(band_rows, cols_count, head_width)
        back_sources = [
            jnp.pad(source, ((0, 0), (reach, reach), (0, 0)))
            for source in (
                far_rows(rate_image, bands_away, False),
                rate_image,
                far_rows(rate_image, bands_away, True),
            )
        ]
        for row_tap in range(3):
            for col_tap in range(3):
                tap_grads.append(
                    back_sources[row_tap][
                        :, (2 - col_tap) * reach : (2 - col_tap) * reach + cols_count
                    ].reshape(pixels, head_width)
                )
    right_side = jnp.concatenate([both_grad[:, :head_width]] + tap_grads, axis=1)
    used_rows = jnp.concatenate(
        [all_weights[:, :head_width], all_weights[:, 2 * head_width :]], axis=1
    )
    main_part = lax.dot_general(
        right_side, used_rows, (((1,), (1,)), ((), ())), preferred_element_type=jnp.float32
    )
    pool_part = lax.dot_general(
        pool_grad,
        all_weights[:, head_width : 2 * head_width],
        (((1,), (1,)), ((), ())),
        preferred_element_type=jnp.float32,
    )
    shared_grad = (main_part + valid_mask * pool_part / pixel_count).astype(jnp.bfloat16)
    head_term = lax.dot_general(
        shared, right_side, (((0,), (0,)), ((), ())), preferred_element_type=jnp.float32
    )
    pool_term = pixel_sum[:, None] * pool_grad.astype(jnp.float32) / pixel_count
    head_term = jnp.concatenate(
        [head_term[:, :head_width], pool_term, head_term[:, head_width:]], axis=1
    )
    all_grads = lax.all_gather(shared_grad[None], "task", axis=0, tiled=True)
    flat_grads = all_grads.reshape(all_grads.shape[0], -1)
    gram_matrix = lax.psum(
        lax.dot_general(
            flat_grads, flat_grads, (((1,), (1,)), ((), ())), preferred_element_type=jnp.float32
        ),
        "space",
    )
    task_weight = imtl_weights(gram_matrix)
    mixed_grad = task_weight[0] * all_grads[0].astype(jnp.float32)
    for task_index in range(1, all_grads.shape[0]):
        mixed_grad = mixed_grad + task_weight[task_index] * all_grads[task_index].astype(
            jnp.float32
        )
    combined = mixed_grad.astype(jnp.bfloat16)
    gate_grad = gelu_back(before_act, combined.astype(jnp.float32) * valid_mask)
    hidden_grad_three, gain_grad_three, shift_grad_three = norm_backward(
        gate_grad, stats_three[1], stats_three[2], gain_three, valid_mask, pixel_count
    )
    low_three = hidden_grad_three.astype(jnp.bfloat16)
    expand_term = lax.dot_general(
        active_two, low_three, (((0,), (0,)), ((), ())), preferred_element_type=jnp.float32
    )
    active_grad_two = lax.dot_general(
        low_three, w_expand, (((1,), (1,)), ((), ())), preferred_element_type=jnp.float32
    )
    upstream_two = gelu_back(stats_two[0], active_grad_two * valid_mask)
    hidden_grad_two, gain_grad_two, shift_grad_two = norm_backward(
        upstream_two, stats_two[1], stats_two[2], gain_two, valid_mask, pixel_count
    )
    low_two = hidden_grad_two.astype(jnp.bfloat16)
    dilated_term = jnp.einsum("pti,po->ito", patches, low_two, preferred_element_type=jnp.float32)
    back_patches = trunk_taps(
        band_rim(low_two.reshape(band_rows, cols_count, middle_width)),
        CONV_DILATION,
        band_rows,
        cols_count,
        True,
    )
    active_grad_one = jnp.einsum(
        "pto,ito->pi", back_patches, w_dilated, preferred_element_type=jnp.float32
    )
    upstream_one = gelu_back(stats_one[0], active_grad_one * valid_mask)
    hidden_grad_one, gain_grad_one, shift_grad_one = norm_backward(
        upstream_one, stats_one[1], stats_one[2], gain_one, valid_mask, pixel_count
    )
    low_one = hidden_grad_one.astype(jnp.bfloat16)
    reduce_term = lax.dot_general(
        inputs, low_one, (((0,), (0,)), ((), ())), preferred_element_type=jnp.float32
    )
    input_grad = (
        lax.dot_general(
            low_one, w_reduce, (((1,), (1,)), ((), ())), preferred_element_type=jnp.float32
        )
        + gate_grad
    )
    reduced = (
        lax.psum_scatter(head_term, "space", scatter_dimension=0, tiled=True),
        lax.psum_scatter(reduce_term, "space", scatter_dimension=0, tiled=True),
        lax.psum_scatter(dilated_term, "space", scatter_dimension=0, tiled=True),
        lax.psum_scatter(expand_term, "space", scatter_dimension=0, tiled=True),
    )
    means = jnp.concatenate([stats_one[3], stats_two[3], stats_three[3]])
    variances = (
        jnp.concatenate([stats_one[4], stats_two[4], stats_three[4]])
        * pixel_count
        / (pixel_count - 1.0)
    )
    batch_stats = jnp.stack([means, variances])
    head_gain_grad = jnp.concatenate([back_totals[3], proj_gain_grad])[None]
    head_shift_grad = jnp.concatenate([back_totals[2], proj_shift_grad])[None]
    return (
        head_result.reshape(1, band_rows, cols_count, head_width),
        input_grad.reshape(band_rows, cols_count, in_width).astype(jnp.bfloat16),
        reduced[1],
        reduced[2],
        reduced[3],
        jnp.concatenate([gain_grad_one, gain_grad_two, gain_grad_three]),
        jnp.concatenate([shift_grad_one, shift_grad_two, shift_grad_three]),
        batch_stats,
        reduced[0][:, : 2 * head_width][None],
        reduced[0][:, 2 * head_width :][None],
        back_totals[0][None],
        head_gain_grad,
        head_shift_grad,
        task_weight,
    )


MESH_ID = pl.DeviceIdType.MESH
LANE = 128


FAR_LAG = 3
GELU_A = 0.7978845608028654
GELU_B = 0.044715


def gelu_of(value):
    return 0.5 * value * (1.0 + jnp.tanh(GELU_A * (value + GELU_B * value * value * value)))


def gelu_slope(value):
    square = value * value
    bend = jnp.tanh(GELU_A * value * (1.0 + GELU_B * square))
    return 0.5 * (1.0 + bend) + 0.5 * value * (1.0 - bend * bend) * (
        GELU_A * (1.0 + 3.0 * GELU_B * square)
    )


def gelu_both(value):
    square = value * value
    bend = jnp.tanh(GELU_A * value * (1.0 + GELU_B * square))
    lift = 0.5 * (1.0 + bend)
    slope = lift + 0.5 * value * (1.0 - bend * bend) * (GELU_A * (1.0 + 3.0 * GELU_B * square))
    return value * lift, slope


def dot_nn(left_side, right_side):
    return jnp.dot(left_side, right_side, preferred_element_type=jnp.float32)


def dot_nt(left_side, right_side):
    return lax.dot_general(
        left_side, right_side, (((1,), (1,)), ((), ())), preferred_element_type=jnp.float32
    )


def shift_pixels(value, by, cols):
    if by == 0:
        return value
    rows = value.shape[0]
    column = lax.rem(lax.broadcasted_iota(jnp.int32, value.shape, 0), cols) + by
    rolled = pltpu.roll(value, (-by) % rows, 0)
    return jnp.where((column >= 0) & (column < cols), rolled, 0.0)


def row_mask(widths_ref, first_row, rows, cols):
    column = lax.broadcasted_iota(jnp.int32, (cols, LANE), 0)
    return jnp.concatenate(
        [
            jnp.where(column < widths_ref[first_row + number], 1.0, 0.0).astype(jnp.float32)
            for number in range(rows)
        ],
        axis=0,
    )


def count_pixels(widths_ref):
    total = widths_ref[0]
    for number in range(1, widths_ref.shape[0]):
        total = total + widths_ref[number]
    return jnp.full((1, LANE), total.astype(jnp.float32), jnp.float32)


class Post:
    def __init__(self, send_sem, recv_sem):
        self.send_sem, self.recv_sem = send_sem, recv_sem
        self.used = 0
        self.sent = []

    def copy(self, source, target, device):
        made = pltpu.make_async_remote_copy(
            source,
            target,
            self.send_sem.at[self.used],
            self.recv_sem.at[self.used],
            device_id=device,
            device_id_type=MESH_ID,
        )
        self.used += 1
        return made

    def push(self, source, target, device):
        made = self.copy(source, target, device)
        made.start()
        self.sent.append(made)
        return made

    def close(self):
        for made in self.sent:
            made.wait_send()
        self.sent = []


class Place:
    def __init__(self, tasks, bands):
        self.tasks, self.bands, self.chips = tasks, bands, bands // 2
        self.task = lax.axis_index("task")
        self.band = lax.axis_index("space")
        self.chip = self.band // 2
        self.core = lax.rem(self.band, 2)
        self.twin = {"space": self.chip * 2 + 1 - self.core}
        low, high = lax.rem(self.task, 2), self.task // 2
        self.other_tasks = [(1 - high) * 2 + 1 - low, high * 2 + 1 - low, (1 - high) * 2 + low]
        self.other_bands = [lax.rem(self.band + step, bands) for step in range(1, bands)]

    def greet(self):
        barrier = pltpu.get_barrier_semaphore()
        greeted = [{"task": task} for task in self.other_tasks]
        greeted += [{"space": band} for band in self.other_bands]
        for device in greeted:
            pl.semaphore_signal(barrier, inc=1, device_id=device, device_id_type=MESH_ID)

    def meet(self):
        barrier = pltpu.get_barrier_semaphore()
        pl.semaphore_wait(barrier, len(self.other_tasks) + len(self.other_bands))

    def sum_begin(self, post, axis, own_ref, land_ref):
        mine = self.task if axis == "task" else self.band
        others = self.other_tasks if axis == "task" else self.other_bands
        copies = [post.push(own_ref, land_ref.at[mine], {axis: other}) for other in others]
        land_ref[pl.ds(mine, 1)] = own_ref[...][None]
        return copies, land_ref

    def sum_end(self, begun):
        copies, land_ref = begun
        for made in copies:
            made.wait_recv()
        total = land_ref[0]
        for slot in range(1, len(copies) + 1):
            total = total + land_ref[slot]
        return total

    def sum_over(self, post, axis, own_ref, land_ref):
        return self.sum_end(self.sum_begin(post, axis, own_ref, land_ref))


def back_phase(
    at,
    post,
    sizes,
    local_sem,
    xg,
    h3q,
    v3_ref,
    h2_ref,
    v2_ref,
    h1_ref,
    v1_ref,
    act_ref,
    a2_ref,
    ps_ref,
    x_hbm,
    widths_ref,
    we_hbm,
    wd_hbm,
    wr_hbm,
    write,
    tw_hbm,
    ig_hbm,
    rg_hbm,
    dg_hbm,
    eg_hbm,
    s3_hbm,
    s2_hbm,
    s1_hbm,
    pg_hbm,
    tw_out,
    ig_out,
    rg_out,
    dg_out,
    eg_out,
    s3_out,
    s2_out,
    s1_out,
    pg_out,
    we,
    wd,
    wr,
    x_ref,
    mask_ref,
    gram_own,
    gram_land,
    gram_mid,
    gram_land_b,
    comb,
    comb_land,
    gate,
    scaled,
    gate_low,
    gate_band,
    st3,
    st3_land,
    st3_mid,
    st3_land_b,
    l3,
    l3x,
    st2,
    st2_land,
    st2_mid,
    st2_land_b,
    l2,
    l2_halo,
    ag1,
    st1,
    st1_land,
    l1,
    xt,
    a2t,
    e_term,
    e_twin,
    e_land,
    e_share,
    e_tasks,
    l2c,
    d_sum,
    d_share,
    d_tasks,
    r_term,
    r_twin,
    r_land,
    r_share,
    r_tasks,
    p_all,
):
    tasks, bands, cols, quarter, mid, wide, piece = sizes
    low = jnp.bfloat16
    f32 = jnp.float32
    task, band = at.task, at.band
    my_rows = pl.ds(pl.multiple_of(task * quarter, quarter), quarter)
    arrays = {
        "x": (x_hbm, x_ref),
        "we": (we_hbm, we),
        "wd": (wd_hbm, wd),
        "wr": (wr_hbm, wr),
    }
    loads = {
        name: pltpu.make_async_copy(source, target, local_sem.at[number])
        for number, (name, (source, target)) in enumerate(arrays.items())
    }

    def loaded(*names):
        for name in names:
            loads[name].wait()

    for load in loads.values():
        load.start()
    band_rows = x_ref.shape[0] // cols
    mask_ref[...] = row_mask(widths_ref, band * band_rows, band_rows, cols)

    pairs = [(a, b) for a in range(tasks) for b in range(a, tasks)]

    def gram_step(number, totals):
        grads = [xg[a, number].astype(f32) for a in range(tasks)]
        out = []
        for (a, b), total in zip(pairs, totals):
            product = grads[a] * grads[b]
            product = product.reshape(quarter // 8, 8, piece).sum(axis=0)
            for start in range(0, piece, LANE):
                total = total + product[:, start : start + LANE]
            out.append(total)
        return tuple(out)

    totals = lax.fori_loop(
        0, bands, gram_step, tuple(jnp.zeros((8, LANE), f32) for _ in pairs)
    )
    gram_own[...] = jnp.zeros_like(gram_own)
    for number, total in enumerate(totals):
        gram_own[number : number + 1] = jnp.sum(total, axis=0, keepdims=True)
    begun = at.sum_begin(post, "task", gram_own, gram_land)
    a2t[...] = a2_ref[...].T
    gram_mid[...] = at.sum_end(begun)
    begun = at.sum_begin(post, "space", gram_mid, gram_land_b)

    loaded("x")
    def turn_inputs(number, carry):
        lanes = pl.ds(pl.multiple_of(number * piece, piece), piece)
        xt[lanes, :] = x_ref[:, lanes].T
        return carry

    lax.fori_loop(0, wide // piece, turn_inputs, 0)
    gram_sum = at.sum_end(begun)
    gram_sum = jnp.broadcast_to(jnp.sum(gram_sum, axis=1, keepdims=True), gram_sum.shape)
    gram = [[None] * tasks for _ in range(tasks)]
    for number, (a, b) in enumerate(pairs):
        gram[a][b] = gram[b][a] = gram_sum[number : number + 1]
    norms = [jnp.sqrt(gram[a][a] + GRAM_EPS) for a in range(tasks)]
    cos = [[gram[a][b] / norms[b] for b in range(tasks)] for a in range(tasks)]
    rows_list = [
        [cos[0][0] - cos[0][l] - cos[k][0] + cos[k][l] for k in range(1, tasks)]
        for l in range(1, tasks)
    ]
    values = [cos[0][0] - cos[0][l] for l in range(1, tasks)]
    count = tasks - 1
    for pivot in range(count):
        for lower in range(pivot + 1, count):
            factor = rows_list[lower][pivot] / rows_list[pivot][pivot]
            rows_list[lower] = [
                under - factor * over for under, over in zip(rows_list[lower], rows_list[pivot])
            ]
            values[lower] = values[lower] - factor * values[pivot]
    answer = [None] * count
    for pivot in reversed(range(count)):
        running = values[pivot]
        for later in range(pivot + 1, count):
            running = running - rows_list[pivot][later] * answer[later]
        answer[pivot] = running / rows_list[pivot][pivot]
    rest = answer[0]
    for value in answer[1:]:
        rest = rest + value
    task_weight = [1.0 - rest] + answer
    for number in range(tasks):
        tw_out[number : number + 1] = task_weight[number]
    weights = [jnp.concatenate([value] * (piece // LANE), axis=1) for value in task_weight]

    def mixed(number):
        total = weights[0] * xg[0, number].astype(f32)
        for a in range(1, tasks):
            total = total + weights[a] * xg[a, number].astype(f32)
        return total.astype(low)

    comb_in = []
    for other in at.other_bands:
        comb[other] = mixed(other)
        comb_in.append(post.push(comb.at[other], comb_land.at[band], {"space": other}))
    comb_land[pl.ds(band, 1)] = mixed(band)[None]
    for made in comb_in:
        made.wait_recv()

    mask_quarter = mask_ref[my_rows]
    mask_piece = jnp.concatenate([mask_quarter] * (piece // LANE), axis=1)
    inv_count = 1.0 / count_pixels(widths_ref)
    inv_piece = jnp.concatenate([inv_count] * (piece // LANE), axis=1)
    per_row = st3.shape[1] // piece
    half = st3.shape[0] // 2

    def gate_step(number, carry):
        lanes = pl.ds(pl.multiple_of(number * piece, piece), piece)
        hat = (h3q[:, lanes] - v3_ref[0:1, lanes]) * v3_ref[1:2, lanes]
        before = v3_ref[2:3, lanes] * hat + v3_ref[3:4, lanes] + x_ref[my_rows, lanes].astype(f32)
        grad = gelu_slope(before) * comb_land[number].astype(f32) * mask_piece
        gate[number] = grad
        scaled[number] = hat
        gate_low[number] = grad.astype(low)
        row = number // per_row
        spot = pl.ds(pl.multiple_of(lax.rem(number, per_row) * piece, piece), piece)
        st3[pl.ds(row, 1), spot] = jnp.sum(grad, axis=0, keepdims=True)
        st3[pl.ds(half + row, 1), spot] = jnp.sum(grad * hat, axis=0, keepdims=True)
        return carry

    lax.fori_loop(0, bands, gate_step, 0)
    st3_mid[...] = at.sum_over(post, "task", st3, st3_land)
    s3_out[...] = at.sum_over(post, "space", st3_mid, st3_land_b)

    def third_step(number, carry):
        lanes = pl.ds(pl.multiple_of(number * piece, piece), piece)
        row = number // per_row
        spot = pl.ds(pl.multiple_of(lax.rem(number, per_row) * piece, piece), piece)
        shift_grad = s3_out[pl.ds(row, 1), spot] * inv_piece
        gain_grad = s3_out[pl.ds(half + row, 1), spot] * inv_piece
        l3[number] = (
            mask_piece
            * (v3_ref[2:3, lanes] * v3_ref[1:2, lanes])
            * (gate[number] - shift_grad - scaled[number] * gain_grad)
        ).astype(low)
        return carry

    lax.fori_loop(0, bands, third_step, 0)
    per_task = bands // tasks
    l3_in = []
    for other in at.other_tasks:
        l3_in.append(
            post.push(l3.at[pl.ds(other * per_task, per_task)], l3x.at[task], {"task": other})
        )
    l3x[pl.ds(task, 1)] = l3[pl.ds(task * per_task, per_task)][None]
    loaded("we")
    p_all[pl.ds(band, 1)] = ps_ref[...][None]
    p_block = p_all.at[band]
    p_near = post.push(p_block, p_block, at.twin)
    p_far = [
        post.push(
            p_block,
            p_block,
            {"space": lax.rem(at.chip + step, at.chips) * 2 + at.core},
        )
        for step in range(1, at.chips)
    ]

    def expand_step(number, total):
        lanes = pl.ds(pl.multiple_of(number * piece, piece), piece)
        return total + dot_nt(l3[number], we[:, lanes])

    ag2 = lax.fori_loop(0, bands, expand_step, jnp.zeros((quarter, mid), f32))

    mask_mid = jnp.concatenate([mask_quarter] * (mid // LANE), axis=1)
    inv_mid = jnp.concatenate([inv_count] * (mid // LANE), axis=1)
    hat = (h2_ref[my_rows] - v2_ref[0:1]) * v2_ref[1:2]
    grad = gelu_slope(v2_ref[2:3] * hat + v2_ref[3:4]) * ag2 * mask_mid
    spread = mid // LANE

    def put_sums(target, first, second):
        for number in range(spread):
            lanes = slice(number * LANE, (number + 1) * LANE)
            target[number : number + 1] = first[:, lanes]
            target[spread + number : spread + number + 1] = second[:, lanes]

    def get_sums(total):
        return [
            jnp.concatenate([total[base + k : base + k + 1] for k in range(spread)], axis=1)
            for base in (0, spread)
        ]

    def to_twin(term, landing):
        return post.push(term.at[1 - at.core], landing, at.twin)

    def both_cores(pair, term, twin):
        pair.wait_recv()
        for step in range(1, at.chips):
            other = lax.rem(at.chip + step, at.chips)
            both = term[at.core, other].astype(f32) + twin[other].astype(f32)
            twin[other] = both.astype(low)

    def along(twin, landing):
        return [
            post.push(
                twin.at[other], landing.at[at.chip], {"space": other * 2 + at.core}
            )
            for other in [lax.rem(at.chip + step, at.chips) for step in range(1, at.chips)]
        ]

    def settle(arrivals, term, twin, landing):
        total = term[at.core, at.chip].astype(f32) + twin[at.chip].astype(f32)
        for made in arrivals:
            made.wait_recv()
        for step in range(1, at.chips):
            total = total + landing[lax.rem(at.chip + step, at.chips)].astype(f32)
        return total.astype(low)

    def to_tasks(share, landing):
        arrivals = [post.push(share, landing.at[task], {"task": other}) for other in at.other_tasks]
        landing[pl.ds(task, 1)] = share[...][None]
        return arrivals

    def expand_part(number):
        share = jnp.concatenate([l3x[a, number] for a in range(tasks)], axis=0)
        part = dot_nn(a2t[...], share).astype(low)
        per_band = part.shape[0] // bands
        for target in range(bands):
            e_term[target % 2, target // 2, :, number * piece : (number + 1) * piece] = part[
                target * per_band : (target + 1) * per_band
            ]

    narrow = mid // tasks
    my_lanes = pl.ds(pl.multiple_of(task * narrow, narrow), narrow)
    put_sums(
        st2, jnp.sum(grad, axis=0, keepdims=True), jnp.sum(grad * hat, axis=0, keepdims=True)
    )
    begun = at.sum_begin(post, "task", st2, st2_land)
    for made in l3_in:
        made.wait_recv()
    expand_part(0)
    st2_mid[...] = at.sum_end(begun)
    begun = at.sum_begin(post, "space", st2_mid, st2_land_b)
    for number in range(1, per_task):
        expand_part(number)
    e_pair = to_twin(e_term, e_twin)
    s2_out[...] = at.sum_end(begun)
    shift_grad, gain_grad = get_sums(s2_out[...])
    l2[my_rows] = (
        mask_mid
        * (v2_ref[2:3] * v2_ref[1:2])
        * (grad - shift_grad * inv_mid - hat * (gain_grad * inv_mid))
    ).astype(low)
    l2_in = [post.push(l2.at[my_rows], l2.at[my_rows], {"task": other}) for other in at.other_tasks]
    both_cores(e_pair, e_term, e_twin)
    e_in = along(e_twin, e_land)
    for made in l2_in:
        made.wait_recv()
    gate_in = [
        post.push(gate_low, gate_band.at[task], {"task": other}) for other in at.other_tasks
    ]
    gate_band[pl.ds(task, 1)] = gate_low[...][None]
    has_above, has_below = band > 0, band < bands - 1
    up = post.copy(l2, l2_halo.at[1], {"space": lax.rem(band + bands - 1, bands)})
    down = post.copy(l2, l2_halo.at[0], {"space": lax.rem(band + 1, bands)})

    @pl.when(has_above)
    def _():
        up.start()

    @pl.when(has_below)
    def _():
        down.start()

    @pl.when(jnp.logical_not(has_above))
    def _():
        l2_halo[0] = jnp.zeros_like(l2)

    @pl.when(jnp.logical_not(has_below))
    def _():
        l2_halo[1] = jnp.zeros_like(l2)

    p_passed = []
    for step, made in enumerate(p_far, start=1):
        made.wait_recv()
        block = p_all.at[lax.rem(at.chip + at.chips - step, at.chips) * 2 + at.core]
        p_passed.append(post.push(block, block, at.twin))
    loaded("wd")
    halves = [slice(start, start + piece) for start in range(0, mid, piece)]
    for lanes in halves:
        total = None
        for col_tap in range(3):
            part = shift_pixels(
                dot_nt(l2[...], wd[3 + col_tap, lanes, :]), -CONV_DILATION * (col_tap - 1), cols
            )
            total = part if total is None else total + part
        ag1[:, lanes] = total

    @pl.when(has_below)
    def _():
        up.wait_recv()

    @pl.when(has_above)
    def _():
        down.wait_recv()

    for lanes in halves:
        total = None
        for col_tap in range(3):
            part = dot_nt(l2_halo[1], wd[col_tap, lanes, :]) + dot_nt(
                l2_halo[0], wd[6 + col_tap, lanes, :]
            )
            part = shift_pixels(part, -CONV_DILATION * (col_tap - 1), cols)
            total = part if total is None else total + part
        ag1[:, lanes] += total

    pixels = ag1.shape[0]
    chunk = pixels // 8

    def first_rows(number):
        return pl.ds(pl.multiple_of(number * chunk, chunk), chunk)

    def first_step(number, sums):
        rows = first_rows(number)
        hat = (h1_ref[rows] - v1_ref[0:1]) * v1_ref[1:2]
        keep = jnp.concatenate([mask_ref[rows]] * spread, axis=1)
        grad = gelu_slope(v1_ref[2:3] * hat + v1_ref[3:4]) * ag1[rows] * keep
        ag1[rows] = grad
        return (
            sums[0] + jnp.sum(grad, axis=0, keepdims=True),
            sums[1] + jnp.sum(grad * hat, axis=0, keepdims=True),
        )

    nothing = jnp.zeros((1, mid), f32)
    first, second = lax.fori_loop(0, 8, first_step, (nothing, nothing))
    put_sums(st1, first, second)
    begun = at.sum_begin(post, "space", st1, st1_land)
    l2c[pl.ds(band, 1)] = l2[:, my_lanes][None]
    l2_block = l2c.at[band]
    d_far = [
        post.push(
            l2_block,
            l2_block,
            {"space": lax.rem(at.chip + step, at.chips) * 2 + at.core},
        )
        for step in range(1, at.chips)
    ]
    d_near = [post.push(l2_block, l2_block, at.twin)]
    e_share[...] = settle(e_in, e_term, e_twin, e_land)
    s1_out[...] = at.sum_end(begun)
    shift_grad, gain_grad = get_sums(s1_out[...])
    shift_grad, gain_grad = shift_grad * inv_mid, gain_grad * inv_mid

    def first_finish(number, carry):
        rows = first_rows(number)
        hat = (h1_ref[rows] - v1_ref[0:1]) * v1_ref[1:2]
        keep = jnp.concatenate([mask_ref[rows]] * spread, axis=1)
        l1[rows] = (
            keep * (v1_ref[2:3] * v1_ref[1:2]) * (ag1[rows] - shift_grad - hat * gain_grad)
        ).astype(low)
        return carry

    lax.fori_loop(0, 8, first_finish, 0)

    share_r = l1[:, my_lanes]
    per_band_r = wide // bands

    def reduce_step(number, carry):
        rows = pl.ds(pl.multiple_of(number * per_band_r, per_band_r), per_band_r)
        r_term[lax.rem(number, 2), number // 2] = dot_nn(xt[rows, :], share_r).astype(low)
        return carry

    lax.fori_loop(0, bands, reduce_step, 0)
    r_pair = to_twin(r_term, r_twin)
    e_back = to_tasks(e_share, e_tasks)
    both_cores(r_pair, r_term, r_twin)
    r_in = along(r_twin, r_land)

    for step, made in enumerate(d_far, start=1):
        made.wait_recv()
        block = l2c.at[lax.rem(at.chip + at.chips - step, at.chips) * 2 + at.core]
        d_near.append(post.push(block, block, at.twin))

    loaded("wr")
    for made in gate_in:
        made.wait_recv()

    def input_step(number, carry):
        lanes = pl.ds(pl.multiple_of(number * piece, piece), piece)
        gates = jnp.concatenate([gate_band[a, number] for a in range(tasks)], axis=0).astype(f32)
        ig_out[:, lanes] = (dot_nt(l1[...], wr[lanes, :]) + gates).astype(low)
        return carry

    lax.fori_loop(0, bands, input_step, 0)
    write(ig_out, ig_hbm)
    for source, target in ((tw_out, tw_hbm), (s3_out, s3_hbm), (s2_out, s2_hbm), (s1_out, s1_hbm)):
        write(source, target)
    for made in d_near:
        made.wait_recv()
    d_sum[...] = jnp.zeros_like(d_sum)

    def dilated_step(number, carry):
        left = jnp.concatenate([act_ref[number + row_tap] for row_tap in range(3)], axis=0)
        right = l2c[number].astype(f32)
        for col_tap in range(3):
            moved = shift_pixels(right, -CONV_DILATION * (col_tap - 1), cols).astype(low)
            d_sum[col_tap] += dot_nn(left, moved)
        return carry

    lax.fori_loop(0, bands, dilated_step, 0)
    part = d_share.shape[1]
    for row_tap in range(3):
        for col_tap in range(3):
            d_share[3 * row_tap + col_tap] = d_sum[
                col_tap, row_tap * part : (row_tap + 1) * part
            ].astype(low)
    d_back = to_tasks(d_share, d_tasks)
    r_share[...] = settle(r_in, r_term, r_twin, r_land)
    r_back = to_tasks(r_share, r_tasks)
    for made in [p_near] + p_passed:
        made.wait_recv()
    pg_out[...] = p_all[...]
    write(pg_out, pg_hbm)
    for made in e_back:
        made.wait_recv()
    broad = wide // tasks
    for a in range(tasks):
        eg_out[:, a * broad : (a + 1) * broad] = e_tasks[a].astype(f32)
    write(eg_out, eg_hbm)
    for made in d_back:
        made.wait_recv()
    for a in range(tasks):
        dg_out[:, :, a * narrow : (a + 1) * narrow] = d_tasks[a].astype(f32)
    write(dg_out, dg_hbm)
    for made in r_back:
        made.wait_recv()
    for a in range(tasks):
        rg_out[:, a * narrow : (a + 1) * narrow] = r_tasks[a].astype(f32)
    write(rg_out, rg_hbm)
    post.close()

    @pl.when(has_above)
    def _():
        up.wait_send()

    @pl.when(has_below)
    def _():
        down.wait_send()


def head_phase(
    at,
    post,
    plan,
    rate_loads,
    sh_ref,
    widths_ref,
    gain_ref,
    shift_ref,
    cot_ref,
    bw_ref,
    pw_ref,
    head_out,
    xg_out,
    grads_out,
    proj_share,
    both_sums_out,
    proj_sums_out,
    rate,
    turned,
    extra,
    term,
    twin_land,
    right_land,
    left_land,
    pre,
    joined,
    upstream,
    cot,
    out_rows,
    masks,
    projected,
    proj_up,
    proj_low,
    pixel_sum,
    st_both,
    st_both_sum,
    st_both_land,
    st_proj,
    st_proj_sum,
    st_proj_land,
    st_pback,
    st_pback_land,
    st_back,
    st_back_land,
    both_all,
    moved,
    grads,
    back,
    sg,
    proj_term,
    p_twin,
    p_land,
):
    tasks, bands, cols, pixels, width, taps, extras = plan
    low, f32 = jnp.bfloat16, jnp.float32
    send_sem, recv_sem = post.send_sem, post.recv_sem
    chips, chip, core, band = at.chips, at.chip, at.core, at.band
    last, half = chips - 1, chips // 2
    group = 2 * pixels
    band_rows = pixels // cols
    spread = width // LANE
    number_of = {tap[:3]: number for number, tap in enumerate(taps)}
    moved_levels = sorted({entry[0] for entry in extras})
    late = sorted({entry[2] for entry in extras})
    slots = moved_levels + [branch for branch in range(4) if branch not in moved_levels]
    side = chip // half
    is_end = (chip == 0) | (chip == last)
    next_chip = lax.rem(chip + 1, chips)
    prev_chip = lax.rem(chip + last, chips)
    own = side * (half - 1)

    def reserve(count):
        first = post.used
        post.used += count
        return first

    def hop(source, landing, device_chip, number):
        return pltpu.make_async_remote_copy(
            source,
            landing,
            send_sem.at[number],
            recv_sem.at[number],
            device_id={"space": device_chip * 2 + core},
            device_id_type=MESH_ID,
        )

    def to_twin(source, landing, number):
        return pltpu.make_async_remote_copy(
            source,
            landing,
            send_sem.at[number],
            recv_sem.at[number],
            device_id=at.twin,
            device_id_type=MESH_ID,
        )

    first_cot = reserve(half)

    def send_cot(number):
        return hop(cot_ref, cot.at[number], side * last, first_cot + number)

    cot[pl.ds(own, 1)] = cot_ref[...][None]

    @pl.when(jnp.logical_not(is_end))
    def _():
        send_cot(chip - side * half).start()

    for load in rate_loads:
        load.wait()

    def rows_of(ref, number):
        return jnp.concatenate([ref[2 * number], ref[2 * number + 1]], axis=0)

    def right_of(level, col_tap):
        return (col_tap - 1) * level * RATE

    def forward_taps(source, level, row_tap):
        total = None
        for col_tap in range(3):
            number = number_of.get((level, row_tap, col_tap))
            if number is None:
                continue
            part = shift_pixels(
                dot_nn(source, rate[number]), right_of(level, col_tap), cols
            )
            total = part if total is None else total + part
        return total

    extra[...] = jnp.zeros_like(extra)
    for level, target, source, row_tap in extras:
        extra[moved_levels.index(level), target // last] += forward_taps(
            rows_of(sh_ref, source), level, row_tap
        )

    first_twin = reserve(4 * chips)

    def twin_term(number, branch):
        return to_twin(
            term.at[number, 1 - core, branch],
            twin_land.at[number, branch],
            first_twin + 4 * number + branch,
        )

    def forward_group(step, carry):
        number = lax.rem(step + half * (1 - side), chips)
        at_rim = jnp.where(lax.rem(number, last) == 0, 1.0, 0.0)
        source = rows_of(sh_ref, number)
        for branch in slots:
            if branch == 0:
                value = dot_nn(source, bw_ref[:, :width])
            else:
                value = forward_taps(source, branch, 1)
                if branch in moved_levels:
                    value = value + at_rim * extra[moved_levels.index(branch), number // last]
            value = value.astype(low)
            term[number, 0, branch] = value[:pixels]
            term[number, 1, branch] = value[pixels:]
            twin_term(number, branch).start()
        return carry

    first_right, first_left = reserve(8 * half), reserve(8 * half)
    portion = pixels // 2

    def rows_at(part):
        return pl.ds(part * portion, portion)

    def go_right(number, branch, part):
        return hop(
            twin_land.at[half + number, branch, rows_at(part)],
            right_land.at[number, branch, rows_at(part)],
            next_chip,
            first_right + 8 * number + 2 * branch + part,
        )

    def go_left(number, branch, part):
        return hop(
            twin_land.at[number, branch, rows_at(part)],
            left_land.at[number, branch, rows_at(part)],
            prev_chip,
            first_left + 8 * number + 2 * branch + part,
        )

    def both_cores(number, branch):
        twin_term(number, branch).wait_recv()
        return term[number, core, branch].astype(f32) + twin_land[number, branch].astype(f32)

    def start_off(number, copy_of):
        for branch in slots:
            twin_land[number, branch] = both_cores(number, branch).astype(low)
            for part in range(2):
                copy_of(branch, part).start()

    for number in range(half):
        lax.fori_loop(number, number + 1, forward_group, 0)

        @pl.when(chip == 0)
        def _():
            start_off(half + number, functools.partial(go_right, number))

        @pl.when(chip == last)
        def _():
            start_off(number, functools.partial(go_left, number))

    lax.fori_loop(half, chips, forward_group, 0)

    def pass_on(number, branch, part, copy, landing):
        if part == 0:
            twin_term(number, branch).wait_recv()
        copy.wait_recv()
        rows = rows_at(part)
        twin_land[number, branch, rows] = (
            term[number, core, branch, rows].astype(f32)
            + twin_land[number, branch, rows].astype(f32)
            + landing[rows].astype(f32)
        ).astype(low)
        copy.start()

    def pass_right(number, branch, part):
        landing = right_land.at[number, branch]
        pass_on(half + number, branch, part, go_right(number, branch, part), landing)

    def pass_left(number, branch, part):
        landing = left_land.at[number, branch]
        pass_on(number, branch, part, go_left(number, branch, part), landing)

    order = [
        (number, branch, part) for number in range(half) for branch in slots for part in range(2)
    ]

    def pass_both(near, far):
        for step in range(len(order) + FAR_LAG):
            if step < len(order):
                near(*order[step])
            if step >= FAR_LAG:
                far(*order[step - FAR_LAG])

    @pl.when(jnp.logical_not(is_end) & (side == 0))
    def _():
        pass_both(pass_right, pass_left)

    @pl.when(jnp.logical_not(is_end) & (side == 1))
    def _():
        pass_both(pass_left, pass_right)

    pixel_sum[...] = jnp.zeros_like(pixel_sum)

    def turn_group(number, carry):
        source = rows_of(sh_ref, number)
        turned[:, pl.ds(pl.multiple_of(number * group, group), group)] = source.T
        pixel_sum[0:1] += jnp.sum(source.astype(f32), axis=0, keepdims=True)
        return carry

    lax.fori_loop(0, chips, turn_group, 0)
    inv_count = jnp.concatenate([1.0 / count_pixels(widths_ref)] * spread, axis=1)

    def put_rows(target, number, value):
        for part in range(spread):
            target[pl.ds(number * spread + part, 1), :] = value[:, part * LANE : (part + 1) * LANE]

    def add_rows(target, number, value):
        for part in range(spread):
            target[pl.ds(number * spread + part, 1), :] += value[
                :, part * LANE : (part + 1) * LANE
            ]

    def get_rows(target, number):
        return jnp.concatenate(
            [target[pl.ds(number * spread + part, 1), :] for part in range(spread)], axis=1
        )

    def column_sum(value):
        return jnp.sum(value, axis=0, keepdims=True)

    def mask_of(number):
        return jnp.concatenate([masks[number]] * spread, axis=1)

    for target in (st_both, st_proj, st_pback, st_back):
        target[...] = jnp.zeros_like(target)
    for number in range(half):
        masks[number] = row_mask(
            widths_ref, (2 * (side * half + number) + core) * band_rows, band_rows, cols
        )

    def settle(copy_of, landing):
        def step_of(step, carry):
            number, branch = step // 4, lax.rem(step, 4)
            total = both_cores(side * half + number, branch)
            for part in range(2):
                copy_of(number, branch, part).wait_recv()
            value = total + landing[number, branch].astype(f32)
            pre[number, branch] = value
            kept = value * mask_of(number)
            add_rows(st_both, branch, column_sum(kept))
            add_rows(st_both, 4 + branch, column_sum(kept * value))
            return carry

        lax.fori_loop(0, 4 * half, step_of, 0)

    @pl.when(chip == 0)
    def _():
        settle(go_left, left_land)

    @pl.when(chip == last)
    def _():
        settle(go_right, right_land)

    sums_now = pixel_sum[0:1]
    high = sums_now.astype(low)
    rest = sums_now - high.astype(f32)
    middle = rest.astype(low)
    tail = (rest - middle.astype(f32)).astype(low)
    pieces = jnp.concatenate(
        [high.astype(f32), middle.astype(f32), tail.astype(f32), jnp.zeros((13, width), f32)],
        axis=0,
    ).astype(low)
    put_rows(st_both, 8, column_sum(dot_nn(pieces, bw_ref[:, width:])))
    st_both_sum[...] = at.sum_over(post, "space", st_both, st_both_land)
    pooled = get_rows(st_both_sum, 8) * inv_count

    def lanes_of(number):
        return pl.ds(pl.multiple_of(number * width, width), width)

    def scale_of(target, first, second):
        mean_value = get_rows(target, first) * inv_count
        variance = get_rows(target, second) * inv_count - mean_value * mean_value
        return mean_value, lax.rsqrt(variance + NORM_EPS)

    def at_ends(body, count):
        @pl.when(is_end)
        def _():
            lax.fori_loop(0, count, body, 0)

    pool_lanes = slice(4 * width, 5 * width)

    def pool_step(number, carry):
        joined[number, 4] = (
            gelu_of(pooled).astype(low).astype(f32) * mask_of(number)
        ).astype(low)
        projected[number] = dot_nn(joined[number, 4], pw_ref[pool_lanes, :])
        return carry

    at_ends(pool_step, half)

    def activate(step, carry):
        number, branch = step // 4, lax.rem(step, 4)
        mean_value, inv_std = scale_of(st_both_sum, branch, 4 + branch)
        hat = (pre[number, branch] - mean_value) * inv_std
        pre[number, branch] = hat
        normed = gain_ref[:, lanes_of(branch)] * hat + shift_ref[:, lanes_of(branch)]
        active, slope = gelu_both(normed)
        keep = mask_of(number)
        active = (active * keep).astype(low)
        upstream[number, branch] = slope * keep
        joined[number, branch] = active
        projected[number] += dot_nn(active, pw_ref[lanes_of(branch), :])
        return carry

    at_ends(activate, 4 * half)

    def project_sums(number, carry):
        value = projected[number]
        kept = value * mask_of(number)
        add_rows(st_proj, 0, column_sum(kept))
        add_rows(st_proj, 1, column_sum(kept * value))
        return carry

    at_ends(project_sums, half)
    st_proj_sum[...] = at.sum_over(post, "space", st_proj, st_proj_land)
    proj_mean, proj_inv = scale_of(st_proj_sum, 0, 1)
    gain_proj = gain_ref[:, pool_lanes]

    def proj_back(number, carry):
        hat = (projected[number] - proj_mean) * proj_inv
        projected[number] = hat
        normed = gain_proj * hat + shift_ref[:, pool_lanes]
        keep = mask_of(number)
        active, slope = gelu_both(normed)
        up = slope * cot[number].astype(f32) * keep
        proj_up[number] = up
        add_rows(st_pback, 0, column_sum(up))
        add_rows(st_pback, 1, column_sum(up * hat))
        out_rows[number] = (active * keep).astype(low)
        return carry

    @pl.when(is_end)
    def _():
        for number in range(half):

            @pl.when(own != number)
            def _():
                send_cot(number).wait_recv()

    at_ends(proj_back, half)
    proj_sums_out[...] = at.sum_over(post, "space", st_pback, st_pback_land)
    shift_proj, gain_grad_proj = get_rows(proj_sums_out, 0), get_rows(proj_sums_out, 1)

    def proj_finish(number, carry):
        keep = mask_of(number)
        proj_low[number] = (
            keep
            * (gain_proj * proj_inv)
            * (
                proj_up[number]
                - shift_proj * inv_count
                - projected[number] * (gain_grad_proj * inv_count)
            )
        ).astype(low)
        add_rows(
            st_back, 8, column_sum(dot_nt(proj_low[number], pw_ref[pool_lanes, :]) * keep)
        )
        return carry

    at_ends(proj_finish, half)

    def back_step(step, carry):
        number, branch = step // 4, lax.rem(step, 4)
        joined_grad = dot_nt(proj_low[number], pw_ref[lanes_of(branch), :])
        hat = pre[number, branch]
        up = upstream[number, branch] * joined_grad
        upstream[number, branch] = up
        add_rows(st_back, branch, column_sum(up))
        add_rows(st_back, 4 + branch, column_sum(up * hat))
        return carry

    at_ends(back_step, 4 * half)
    both_sums_out[...] = at.sum_over(post, "space", st_back, st_back_land)
    pool_grad = (gelu_slope(pooled) * get_rows(both_sums_out, 8)).astype(low)

    order = [(number, branch) for branch in moved_levels for number in range(half)]
    order += [
        (number, branch)
        for number in range(half)
        for branch in slots
        if branch not in moved_levels
    ]
    first_right_all, first_left_all = reserve(8 * half), reserve(8 * half)
    first_twin_all, first_out = reserve(8 * chips), reserve(half)

    def block_of(number, branch, part):
        return both_all.at[number * 2 + core, branch, rows_at(part)]

    def along_right(number, branch, part):
        block = block_of(number, branch, part)
        return hop(block, block, next_chip, first_right_all + 8 * number + 2 * branch + part)

    def along_left(number, branch, part):
        block = block_of(half + number, branch, part)
        return hop(block, block, prev_chip, first_left_all + 8 * number + 2 * branch + part)

    def hand_over(number, branch, part):
        block = block_of(number, branch, part)
        return to_twin(block, block, first_twin_all + 8 * number + 2 * branch + part)

    def make_both(number, branch):
        _, inv_std = scale_of(st_both_sum, branch, 4 + branch)
        shift_grad = get_rows(both_sums_out, branch) * inv_count
        gain_grad = get_rows(both_sums_out, 4 + branch) * inv_count
        mine = side * half + number
        both_all[2 * mine + core, branch] = (
            mask_of(number)
            * (gain_ref[:, lanes_of(branch)] * inv_std)
            * (upstream[number, branch] - shift_grad - pre[number, branch] * gain_grad)
        ).astype(low)

        for part in range(2):

            @pl.when(chip == 0)
            def _():
                along_right(number, branch, part).start()

            @pl.when(chip == last)
            def _():
                along_left(number, branch, part).start()

            hand_over(mine, branch, part).start()

    def send_out(number):
        return hop(out_rows.at[number], head_out, side * half + number, first_out + number)

    @pl.when(is_end)
    def _():
        for number, branch in order:
            make_both(number, branch)
        for number in range(half):

            @pl.when(own != number)
            def _():
                send_out(number).start()

        head_out[...] = out_rows[own]

    def proj_step(branch, carry):
        total = dot_nn(joined[0, branch].T, proj_low[0])
        for number in range(1, half):
            total = total + dot_nn(joined[number, branch].T, proj_low[number])
        proj_term[lanes_of(branch), :] = total.astype(low)
        return carry

    at_ends(proj_step, 5)

    rows_p = proj_share.shape[0]

    def proj_rows(number):
        return pl.ds(pl.multiple_of(number * rows_p, rows_p), rows_p)

    first_pair, first_p = reserve(chips), reserve(2 * chips)

    def p_pair(number):
        return to_twin(
            proj_term.at[proj_rows(2 * number + 1 - core)], p_twin.at[number], first_pair + number
        )

    def p_hop(end, number):
        return hop(p_twin.at[number], p_land.at[end], number, first_p + end * chips + number)

    @pl.when(is_end)
    def _():
        for number in range(chips):
            p_pair(number).start()

    def send_projection():
        for number in range(chips):
            p_pair(number).wait_recv()
            both = proj_term[proj_rows(2 * number + core)].astype(f32)
            p_twin[number] = (both + p_twin[number].astype(f32)).astype(low)

            @pl.when(chip != number)
            def _():
                p_hop(side, number).start()

    grads[...] = jnp.zeros_like(grads)
    pool_row = dot_nt(
        jnp.broadcast_to(pool_grad, (16, width)), bw_ref[:, width:]
    )[0:1] * inv_count
    quarter = pixels // tasks
    my_rows = pl.ds(pl.multiple_of(at.task * quarter, quarter), quarter)
    first_task = reserve(chips * len(at.other_tasks))

    def to_task(number, turn):
        other = at.other_tasks[turn]
        theirs = pl.ds(pl.multiple_of(other * quarter, quarter), quarter)
        two = pl.ds(2 * number, 2)
        spot = first_task + number * len(at.other_tasks) + turn
        return pltpu.make_async_remote_copy(
            sg.at[two, theirs],
            xg_out.at[at.task, two],
            send_sem.at[spot],
            recv_sem.at[spot],
            device_id={"task": other},
            device_id_type=MESH_ID,
        )

    def finish_group(number):
        keep = row_mask(widths_ref, number * 2 * band_rows, 2 * band_rows, cols)
        keep = jnp.concatenate([keep] * spread, axis=1)
        value = (back[number] + keep * pool_row).astype(low)
        sg[2 * number] = value[:pixels]
        sg[2 * number + 1] = value[pixels:]
        for turn in range(len(at.other_tasks)):
            to_task(number, turn).start()
        for part in range(2):
            xg_out[at.task, 2 * number + part] = sg[2 * number + part, my_rows]

    def back_part(number, branch):
        for part in range(2):
            hand_over(number, branch, part).wait_recv()
        columns = turned[:, number * group : (number + 1) * group]
        part = jnp.concatenate(
            [both_all[2 * number, branch], both_all[2 * number + 1, branch]], axis=0
        )
        if branch == 0:
            total = dot_nt(part, bw_ref[:, :width])
            grads[len(taps)] += dot_nn(columns, part)
        else:
            total = None
            image = part.astype(f32)
            for col_tap in range(3):
                tap = number_of.get((branch, 1, col_tap))
                if tap is None:
                    continue
                part = shift_pixels(image, -right_of(branch, col_tap), cols).astype(low)
                if branch in moved_levels and number in late:
                    moved[moved_levels.index(branch), number // last, col_tap] = part
                now = dot_nt(part, rate[tap])
                total = now if total is None else total + now
                grads[tap] += dot_nn(columns, part)
        if branch == slots[0]:
            back[number] = total
        else:
            back[number] += total

    def far_taps():
        for level, target, source, row_tap in extras:
            columns = turned[:, source * group : (source + 1) * group]
            total = back[source]
            for col_tap in range(3):
                tap = number_of.get((level, row_tap, col_tap))
                if tap is None:
                    continue
                part = moved[moved_levels.index(level), target // last, col_tap]
                total = total + dot_nt(part, rate[tap])
                grads[tap] += dot_nn(columns, part)
            back[source] = total

    def take_right(number, branch, part):
        along_right(number, branch, part).wait_recv()

        @pl.when(chip < last)
        def _():
            along_right(number, branch, part).start()

        hand_over(number, branch, part).start()

    def take_left(number, branch, part):
        along_left(number, branch, part).wait_recv()

        @pl.when(chip > 0)
        def _():
            along_left(number, branch, part).start()

        hand_over(half + number, branch, part).start()

    parts = [entry + (part,) for entry in order for part in range(2)]
    for step in range(len(parts) + FAR_LAG + 1):
        if step < len(parts):

            @pl.when(jnp.logical_not(is_end) & (side == 0))
            def _():
                take_right(*parts[step])

            @pl.when(jnp.logical_not(is_end) & (side == 1))
            def _():
                take_left(*parts[step])

        if FAR_LAG <= step < len(parts) + FAR_LAG:

            @pl.when(side == 0)
            def _():
                take_left(*parts[step - FAR_LAG])

            @pl.when(side == 1)
            def _():
                take_right(*parts[step - FAR_LAG])

        if step == len(parts) + FAR_LAG:

            @pl.when(is_end)
            def _():
                send_projection()

        done = step - FAR_LAG - 2
        if done >= 0 and done % 2 == 0:
            number, branch = order[done // 2]
            back_part(number, branch)
            back_part(half + number, branch)
            if done // 2 + 1 == half * len(moved_levels):
                far_taps()
            if branch == slots[3]:
                finish_group(number)
                finish_group(half + number)
    column = jnp.broadcast_to(pixel_sum[0:1], (8, width)).T[:, 0:1]
    grads_out[len(taps) + 1] = (column * (pool_grad.astype(f32) * inv_count)).astype(low)

    def finish_tap(number, carry):
        grads_out[number] = grads[number].astype(low)
        return carry

    lax.fori_loop(0, len(taps) + 1, finish_tap, 0)
    for end in range(2):

        @pl.when(chip == end * last)
        def _():
            p_land[end] = p_twin[end * last]

        @pl.when(chip != end * last)
        def _():
            p_hop(end, chip).wait_recv()

    proj_share[...] = (p_land[0].astype(f32) + p_land[1].astype(f32)).astype(low)

    def tasks_in(number, carry):
        for turn in range(len(at.other_tasks)):
            to_task(number, turn).wait()
        return carry

    lax.fori_loop(0, chips, tasks_in, 0)

    @pl.when(jnp.logical_not(is_end))
    def _():
        send_out(chip - side * half).wait_recv()
        send_cot(chip - side * half).wait_send()

    post.close()

    def twin_left(number, carry):
        for branch in range(4):
            twin_term(number, branch).wait_send()
            for part in range(2):
                hand_over(number, branch, part).wait_send()
        return carry

    lax.fori_loop(0, chips, twin_left, 0)

    def line_left(number, carry):
        for branch in range(4):
            for part in range(2):

                @pl.when(chip < last)
                def _():
                    go_right(number, branch, part).wait_send()
                    along_right(number, branch, part).wait_send()

                @pl.when(chip > 0)
                def _():
                    go_left(number, branch, part).wait_send()
                    along_left(number, branch, part).wait_send()

        return carry

    lax.fori_loop(0, half, line_left, 0)

    @pl.when(is_end)
    def _():
        for number in range(half):

            @pl.when(own != number)
            def _():
                send_out(number).wait_send()

        for number in range(chips):
            p_pair(number).wait_send()

            @pl.when(chip != number)
            def _():
                p_hop(side, number).wait_send()


def trunk_phase(
    at,
    post,
    sizes,
    when_loaded,
    x_hbm,
    widths_ref,
    gain_ref,
    shift_ref,
    wr_hbm,
    wd_hbm,
    we_hbm,
    sh_out,
    act,
    h1,
    h2,
    a2,
    h3q,
    v1,
    v2,
    v3,
    stats_out,
    x,
    wr,
    wd,
    we,
    rim,
    turned,
    h3,
    blocks,
    mask_own,
    st1,
    st1_land,
    st2,
    st2_land,
    st3,
    st3_land,
    local_sem,
):
    tasks, bands, cols, quarter, mid, wide, piece = sizes
    low, f32 = jnp.bfloat16, jnp.float32
    task, band = at.task, at.band
    my_rows = pl.ds(pl.multiple_of(task * quarter, quarter), quarter)
    loads = [
        pltpu.make_async_copy(source, target, local_sem.at[number])
        for number, (source, target) in enumerate(
            ((x_hbm, x), (wr_hbm, wr), (wd_hbm, wd), (we_hbm, we))
        )
    ]
    for load in loads[:2]:
        load.start()
    at.greet()
    pixels = x.shape[0]
    band_rows = pixels // cols
    mask = row_mask(widths_ref, band * band_rows, band_rows, cols)
    count = count_pixels(widths_ref)
    spread = mid // LANE

    def across(value, lanes):
        return jnp.concatenate([value] * (lanes // LANE), axis=1)

    def put_sums(target, value, keep):
        kept = value * keep
        first = jnp.sum(kept, axis=0, keepdims=True)
        second = jnp.sum(kept * value, axis=0, keepdims=True)
        for number in range(spread):
            lanes = slice(number * LANE, (number + 1) * LANE)
            target[number : number + 1] = first[:, lanes]
            target[spread + number : spread + number + 1] = second[:, lanes]

    def get_sums(total):
        return [
            jnp.concatenate([total[base + k : base + k + 1] for k in range(spread)], axis=1)
            for base in (0, spread)
        ]

    def put_norm(vectors, lanes, first, second, start):
        width = first.shape[1]
        inv = across(1.0 / count, width)
        mean_value = first * inv
        variance = second * inv - mean_value * mean_value
        vectors[0:1, lanes] = mean_value
        vectors[1:2, lanes] = lax.rsqrt(variance + NORM_EPS)
        vectors[2:3, lanes] = gain_ref[:, start : start + width]
        vectors[3:4, lanes] = shift_ref[:, start : start + width]
        stats_out[0:1, start : start + width] = mean_value
        stats_out[1:2, start : start + width] = variance * across(count / (count - 1.0), width)

    def activate(hidden, vectors, keep):
        normed = vectors[2:3] * ((hidden - vectors[0:1]) * vectors[1:2]) + vectors[3:4]
        return (gelu_of(normed) * keep).astype(low)

    mask_mid = across(mask, mid)
    for load in loads[:2]:
        load.wait()
    for load in loads[2:]:
        load.start()
    when_loaded()
    h1[...] = dot_nn(x[...], wr[...])
    at.meet()
    put_sums(st1, h1[...], mask_mid)
    first, second = get_sums(at.sum_over(post, "space", st1, st1_land))
    put_norm(v1, slice(0, mid), first, second, 0)
    rim[1] = activate(h1[...], v1, mask_mid)

    has_above, has_below = band > 0, band < bands - 1
    up = post.copy(rim.at[1], rim.at[2], {"space": lax.rem(band + bands - 1, bands)})
    down = post.copy(rim.at[1], rim.at[0], {"space": lax.rem(band + 1, bands)})

    @pl.when(has_above)
    def _():
        up.start()

    @pl.when(has_below)
    def _():
        down.start()

    @pl.when(jnp.logical_not(has_above))
    def _():
        rim[0] = jnp.zeros(rim.shape[1:], low)

    @pl.when(jnp.logical_not(has_below))
    def _():
        rim[2] = jnp.zeros(rim.shape[1:], low)

    loads[2].wait()
    halves = [slice(start, start + piece) for start in range(0, mid, piece)]

    def tap_sum(row_taps, lanes):
        total = None
        for col_tap in range(3):
            part = None
            for row_tap in row_taps:
                term = dot_nn(rim[row_tap], wd[3 * row_tap + col_tap, :, lanes])
                part = term if part is None else part + term
            part = shift_pixels(part, CONV_DILATION * (col_tap - 1), cols)
            total = part if total is None else total + part
        return total

    for lanes in halves:
        h2[:, lanes] = tap_sum((1,), lanes)

    turned[...] = rim[1].T

    @pl.when(has_below)
    def _():
        up.wait_recv()

    @pl.when(has_above)
    def _():
        down.wait_recv()

    for lanes in halves:
        h2[:, lanes] += tap_sum((0, 2), lanes)

    put_sums(st2, h2[...], mask_mid)
    first, second = get_sums(at.sum_over(post, "space", st2, st2_land))
    put_norm(v2, slice(0, mid), first, second, mid)
    a2[...] = activate(h2[...], v2, mask_mid)

    loads[3].wait()
    mask_piece = across(mask, piece)
    per_row = st3.shape[1] // piece
    half = st3.shape[0] // 2

    def expand_step(number, carry):
        lanes = pl.ds(pl.multiple_of(number * piece, piece), piece)
        value = dot_nn(a2[...], we[:, lanes])
        h3[:, lanes] = value
        kept = value * mask_piece
        row = number // per_row
        spot = pl.ds(pl.multiple_of(lax.rem(number, per_row) * piece, piece), piece)
        st3[pl.ds(row, 1), spot] = jnp.sum(kept, axis=0, keepdims=True)
        st3[pl.ds(half + row, 1), spot] = jnp.sum(kept * value, axis=0, keepdims=True)
        return carry

    lax.fori_loop(0, bands, expand_step, 0)
    begun = at.sum_begin(post, "space", st3, st3_land)
    h3q[...] = h3[my_rows]
    total = at.sum_end(begun)
    lanes_in = st3.shape[1]
    for row in range(half):
        put_norm(
            v3,
            slice(row * lanes_in, (row + 1) * lanes_in),
            total[row : row + 1],
            total[half + row : half + row + 1],
            2 * mid + row * lanes_in,
        )

    mask_own[...] = mask
    mask_quarter = across(mask_own[my_rows], piece)

    def shared_of(number):
        lanes = pl.ds(pl.multiple_of(number * piece, piece), piece)
        hat = (h3q[:, lanes] - v3[0:1, lanes]) * v3[1:2, lanes]
        before = v3[2:3, lanes] * hat + v3[3:4, lanes] + x[my_rows, lanes].astype(f32)
        return (gelu_of(before) * mask_quarter).astype(low)

    slices_in = []
    for other in at.other_bands:
        blocks[other] = shared_of(other)
        slices_in.append(
            post.push(blocks.at[other], sh_out.at[band, my_rows], {"space": other})
        )
    sh_out[band, my_rows] = shared_of(band)

    part = mid // bands

    def part_of(number):
        return turned.at[pl.ds(pl.multiple_of(number * part, part), part)]

    act[0] = jnp.zeros(act.shape[1:], low)
    act[bands + 1] = jnp.zeros(act.shape[1:], low)
    act[band + 1] = part_of(band)[...]
    parts_in = [
        post.push(part_of(other), act.at[band + 1], {"space": other}) for other in at.other_bands
    ]

    def to_tasks(number):
        block = sh_out.at[number, my_rows]
        return [post.push(block, block, {"task": other}) for other in at.other_tasks]

    quarters_in = to_tasks(band)
    for step, made in enumerate(slices_in, start=1):
        made.wait_recv()
        quarters_in += to_tasks(lax.rem(band + bands - step, bands))
    for made in quarters_in + parts_in:
        made.wait_recv()
    post.close()

    @pl.when(has_above)
    def _():
        up.wait_send()

    @pl.when(has_below)
    def _():
        down.wait_send()


class Held:
    def __init__(self, shape, dtype, passing=False):
        self.memory = pltpu.VMEM(shape, dtype)
        self.passing = passing


def with_phase(entries, refs, body):
    def run(*passing):
        passing, kept = list(passing), list(refs)
        body([(passing if entry.passing else kept).pop(0) for entry in entries])

    pl.run_scoped(run, *[entry.memory for entry in entries if entry.passing])


def whole_kernel(sizes, plan, phases, counts, *refs):
    refs = list(refs)

    def take(count):
        taken = refs[:count]
        del refs[:count]
        return taken

    x_hbm, widths, gain, shift, wr_hbm, wd_hbm, we_hbm = take(7)
    head_gain, head_shift, cot, bw, pw, rate_hbm = take(6)
    stats_hbm, head_hbm, grads_hbm, both_hbm, proj_hbm = take(5)
    back_hbm = take(counts[2])
    trunk_outs, head_outs = take(counts[0]), take(counts[1])
    (shared,) = take(1)
    kept = [take(sum(not entry.passing for entry in entries)) for entries in phases]
    send_sem, recv_sem, local_sem, rate_sem, out_sem = refs
    tasks, bands, width, taps = sizes[0], sizes[1], plan[4], plan[5]
    at = Place(tasks, bands)
    post = Post(send_sem, recv_sem)
    writes = []

    def write(source, target):
        copy = pltpu.make_async_copy(source, target, out_sem.at[len(writes)])
        copy.start()
        writes.append(copy)

    rate = kept[1][0]
    rate_loads = []
    for number, (level, row_tap, col_tap, _, _) in enumerate(taps):
        start = (9 * (level - 1) + 3 * row_tap + col_tap) * width
        rate_loads.append(
            pltpu.make_async_copy(
                rate_hbm.at[:, start : start + width], rate.at[number], rate_sem.at[number]
            )
        )

    def when_loaded():
        for load in rate_loads:
            load.start()

    def run_trunk(scratch):
        trunk_phase(
            at,
            post,
            sizes,
            when_loaded,
            x_hbm,
            widths,
            gain,
            shift,
            wr_hbm,
            wd_hbm,
            we_hbm,
            shared,
            *trunk_outs,
            *scratch,
            local_sem,
        )

    def run_head(scratch):
        head_phase(
            at,
            post,
            plan,
            rate_loads,
            shared,
            widths,
            head_gain,
            head_shift,
            cot,
            bw,
            pw,
            *head_outs,
            *scratch,
        )

    with_phase(phases[0], kept[0], run_trunk)
    act, h1, h2, a2, h3q, v1, v2, v3, stats = trunk_outs
    write(stats, stats_hbm)
    with_phase(phases[1], kept[1], run_head)
    head_out, xg, grads_out, proj_share, both_sums, proj_sums = head_outs
    for source, target in (
        (head_out, head_hbm),
        (grads_out, grads_hbm),
        (both_sums, both_hbm),
        (proj_sums, proj_hbm),
    ):
        write(source, target)

    def run_back(scratch):
        back_phase(
            at,
            post,
            sizes,
            local_sem,
            xg,
            h3q,
            v3,
            h2,
            v2,
            h1,
            v1,
            act,
            a2,
            proj_share,
            x_hbm,
            widths,
            we_hbm,
            wd_hbm,
            wr_hbm,
            write,
            *back_hbm,
            *scratch,
        )
        while len(writes) > before:
            writes.pop().wait()

    before = len(writes)
    with_phase(phases[2], kept[2], run_back)
    for copy in writes:
        copy.wait()


def whole(tasks, bands, cols, rows, collective, x, widths, gain, shift, wr, wd, we, *head_in):
    low, f32 = jnp.bfloat16, jnp.float32
    head_gain, head_shift, cot, bw, pw, rate = head_in
    pixels, wide = x.shape
    mid = wr.shape[1]
    quarter, piece = pixels // tasks, wide // bands
    width = pw.shape[1]
    chips = bands // 2
    group_rows = rows // chips
    taps = live_taps(rows, cols)
    extras = []
    for level in (1, 2, 3):
        for row_tap in (0, 2):
            if (level, row_tap, 1) in [tap[:3] for tap in taps]:
                away = (row_tap - 1) * level * RATE // group_rows
                extras += [
                    (level, target, target + away, row_tap)
                    for target in range(chips)
                    if 0 <= target + away < chips
                ]
    levels = max(len({entry[0] for entry in extras}), 1)
    in_vmem = pl.BlockSpec(memory_space=pltpu.VMEM)
    anywhere = pl.BlockSpec(memory_space=pl.ANY)
    shape = jax.ShapeDtypeStruct
    block = (pixels, width)
    both_rows, proj_rows = -(-9 * width // LANE // 8) * 8, 8

    part, narrow, broad = mid // bands, mid // tasks, wide // tasks
    half = chips // 2
    pool_rows = pw.shape[0] // bands
    mid_rows, stat_wide = 2 * mid // LANE, wide // 4

    def kept(dims, dtype=low):
        return Held(tuple(dims), dtype)

    def passing(dims, dtype=low):
        return Held(tuple(dims), dtype, True)

    def over_bands(count, lanes=LANE):
        return [kept((count, lanes), f32), kept((bands, count, lanes), f32)]

    def over_all(count, lanes=LANE):
        return [kept((count, lanes), f32), kept((tasks, count, lanes), f32)] + over_bands(
            count, lanes
        )

    def terms(*dims):
        return [
            kept((2, chips) + dims),
            kept((chips,) + dims),
            kept((chips,) + dims),
            kept(dims),
            kept((tasks,) + dims),
        ]

    trunk_scratch = (
        [
            passing(x.shape),
            passing(wr.shape),
            passing(wd.shape),
            passing(we.shape),
            kept((3, pixels, mid)),
            kept((mid, pixels)),
            passing((pixels, wide), f32),
            kept((bands, quarter, piece)),
            passing((pixels, LANE), f32),
        ]
        + over_bands(mid_rows)
        + over_bands(mid_rows)
        + over_bands(8, stat_wide)
    )
    head_scratch = (
        [
            kept((len(taps), piece, width)),
            passing((piece, bands * pixels)),
            passing((levels, 2, 2 * pixels, width), f32),
            passing((chips, 2, 4) + block),
            kept((chips, 4) + block),
            kept((half, 4) + block),
            kept((half, 4) + block),
            passing((half, 4) + block, f32),
            passing((half, 5) + block),
            passing((half, 4) + block, f32),
            kept((half,) + block),
            passing((half,) + block),
            passing((half, pixels, LANE), f32),
            passing((half,) + block, f32),
            passing((half,) + block, f32),
            passing((half,) + block),
            passing((8, piece), f32),
            kept((both_rows, LANE), f32),
        ]
        + over_bands(both_rows)
        + [kept((proj_rows, LANE), f32)]
        + over_bands(proj_rows)
        + over_bands(proj_rows)
        + over_bands(both_rows)
        + [
            kept((bands, 4) + block),
            passing((levels, 2, 3, 2 * pixels, width)),
            passing((len(taps) + 1, piece, width), f32),
            passing((chips, 2 * pixels, width), f32),
            passing((bands, pixels, piece)),
            passing(pw.shape),
            kept((chips, pool_rows, width)),
            kept((2, pool_rows, width)),
        ]
    )
    back_outs = (
        shape((8, LANE), f32),
        shape((pixels, wide), low),
        shape((piece, mid), f32),
        shape((9, part, mid), f32),
        shape((part, wide), f32),
        shape((8, stat_wide), f32),
        shape((mid_rows, LANE), f32),
        shape((mid_rows, LANE), f32),
        shape((bands, pool_rows, width), low),
    )
    back_scratch = (
        [kept(out.shape, out.dtype) for out in back_outs]
        + [
            passing(we.shape),
            passing(wd.shape),
            passing(wr.shape),
            passing(x.shape),
            passing((pixels, LANE), f32),
        ]
        + over_all(16)
        + [
            kept((bands, quarter, piece)),
            kept((bands, quarter, piece)),
            passing((bands, quarter, piece), f32),
            passing((bands, quarter, piece), f32),
            kept((bands, quarter, piece)),
            kept((tasks, bands, quarter, piece)),
        ]
        + over_all(8, stat_wide)
        + [
            kept((bands, quarter, piece)),
            kept((tasks, bands // tasks, quarter, piece)),
        ]
        + over_all(mid_rows)
        + [
            kept((pixels, mid)),
            kept((2, pixels, mid)),
            passing((pixels, mid), f32),
        ]
        + over_bands(mid_rows)
        + [
            passing((pixels, mid)),
            passing((wide, pixels)),
            passing((mid, pixels)),
        ]
        + terms(part, broad)
        + [
            kept((bands, pixels, narrow)),
            passing((3, 3 * part, narrow), f32),
            kept((9, part, narrow)),
            kept((tasks, 9, part, narrow)),
        ]
        + terms(piece, narrow)
        + [kept((bands, pool_rows, width))]
    )
    sizes = (tasks, bands, cols, quarter, mid, wide, piece)
    plan = (tasks, bands, cols, pixels, width, tuple(taps), tuple(extras))
    trunk_outs = (
        shape((bands + 2, part, pixels), low),
        shape((pixels, mid), f32),
        shape((pixels, mid), f32),
        shape((pixels, mid), low),
        shape((quarter, wide), f32),
        shape((8, mid), f32),
        shape((8, mid), f32),
        shape((8, wide), f32),
        shape((2, 2 * mid + wide), f32),
    )
    head_outs = (
        shape(block, low),
        shape((tasks, bands, quarter, piece), low),
        shape((len(taps) + 2, piece, width), low),
        shape((pool_rows, width), low),
        shape((both_rows, LANE), f32),
        shape((proj_rows, LANE), f32),
    )
    out_shapes = (trunk_outs[8], head_outs[0], head_outs[2], head_outs[4], head_outs[5])
    out_shapes += back_outs
    phases = (trunk_scratch, head_scratch, back_scratch)
    return taps, pl.pallas_call(
        functools.partial(
            whole_kernel, sizes, plan, phases, (len(trunk_outs), len(head_outs), len(back_outs))
        ),
        name="whole",
        out_shape=out_shapes,
        in_specs=[anywhere, pl.BlockSpec(memory_space=pltpu.SMEM), in_vmem, in_vmem]
        + [anywhere] * 3
        + [in_vmem] * 5
        + [anywhere],
        out_specs=(anywhere,) * len(out_shapes),
        scratch_shapes=[pltpu.VMEM(out.shape, out.dtype) for out in trunk_outs + head_outs]
        + [pltpu.VMEM((bands, pixels, piece), low)]
        + [entry.memory for entries in phases for entry in entries if not entry.passing]
        + [
            pltpu.SemaphoreType.DMA((352,)),
            pltpu.SemaphoreType.DMA((352,)),
            pltpu.SemaphoreType.DMA((4,)),
            pltpu.SemaphoreType.DMA((len(taps),)),
            pltpu.SemaphoreType.DMA((len(out_shapes),)),
        ],
        compiler_params=pltpu.CompilerParams(
            collective_id=collective, has_side_effects=True, vmem_limit_bytes=60 << 20
        ),
    )(x, widths, gain, shift, wr, wd, we, *head_in)


def finish_kernel(
    places,
    tap_hbm,
    ho_in,
    ig_in,
    rg_in,
    dg_in,
    eg_in,
    bs_in,
    tw_hbm,
    pg_hbm,
    s3_hbm,
    s2_hbm,
    s1_hbm,
    both_hbm,
    proj_hbm,
    ho_out,
    ig_out,
    rg_out,
    dg_out,
    eg_out,
    bs_out,
    branch_out,
    rate_out,
    pg_out,
    tg_out,
    ts_out,
    hg_out,
    hs_out,
    tw_out,
    tap_ref,
    tw_ref,
    pg_ref,
    s3_ref,
    s2_ref,
    s1_ref,
    both_ref,
    proj_ref,
    ho_buf,
    ig_buf,
    rg_buf,
    dg_buf,
    eg_buf,
    bs_buf,
    branch,
    rate,
    sems,
    load_sems,
):
    f32 = jnp.float32
    width = tap_ref.shape[2]
    loads = [
        pltpu.make_async_copy(source, target, load_sems.at[number])
        for number, (source, target) in enumerate(
            (
                (tap_hbm, tap_ref),
                (pg_hbm, pg_ref),
                (tw_hbm, tw_ref),
                (s3_hbm, s3_ref),
                (s2_hbm, s2_ref),
                (s1_hbm, s1_ref),
                (both_hbm, both_ref),
                (proj_hbm, proj_ref),
            )
        )
    ]
    for load in loads:
        load.start()
    passed = [
        (ho_in, ho_buf, ho_out),
        (ig_in, ig_buf, ig_out),
        (rg_in, rg_buf, rg_out),
        (dg_in, dg_buf, dg_out),
        (eg_in, eg_buf, eg_out),
        (bs_in, bs_buf, bs_out),
    ]
    passes = [
        (
            pltpu.make_async_copy(source, buffer, load_sems.at[len(loads) + number]),
            pltpu.make_async_copy(buffer, target, sems.at[number]),
        )
        for number, (source, buffer, target) in enumerate(passed)
    ]
    for copy, _ in passes:
        copy.start()
    copies = [copy for _, copy in passes]
    per_level = len(places) // 3
    loads[0].wait()
    for level in range(3):
        for number in range(level * per_level, (level + 1) * per_level):
            lanes = slice(number * width, (number + 1) * width)
            if places[number] is None:
                rate[:, lanes] = jnp.zeros((rate.shape[0], width), f32)
            else:
                rate[:, lanes] = tap_ref[places[number]].astype(f32)
        lanes = slice(level * per_level * width, (level + 1) * per_level * width)
        copy = pltpu.make_async_copy(
            rate.at[:, lanes], rate_out.at[:, lanes], sems.at[len(copies)]
        )
        copy.start()
        copies.append(copy)
    for arrival, copy in passes:
        arrival.wait()
        copy.start()
    count = tap_ref.shape[0]
    branch[:, :width] = tap_ref[count - 2].astype(f32)
    branch[:, width:] = tap_ref[count - 1].astype(f32)
    copy = pltpu.make_async_copy(branch, branch_out, sems.at[len(copies)])
    copy.start()
    copies.append(copy)
    for load in loads[1:]:
        load.wait()
    pg_out[...] = pg_ref[...].astype(f32)
    rows = s1_ref.shape[0] // 2
    ts_out[0:rows] = s1_ref[0:rows]
    tg_out[0:rows] = s1_ref[rows : 2 * rows]
    ts_out[rows : 2 * rows] = s2_ref[0:rows]
    tg_out[rows : 2 * rows] = s2_ref[rows : 2 * rows]
    half, lanes_in = s3_ref.shape[0] // 2, s3_ref.shape[1]
    for row in range(half):
        for part in range(lanes_in // LANE):
            target = 2 * rows + row * (lanes_in // LANE) + part
            lanes = slice(part * LANE, (part + 1) * LANE)
            ts_out[target : target + 1] = s3_ref[row : row + 1, lanes]
            tg_out[target : target + 1] = s3_ref[half + row : half + row + 1, lanes]
    spread = width // LANE
    for row in range(4 * spread):
        lanes = slice(row * LANE, (row + 1) * LANE)
        hs_out[:, lanes] = both_ref[row : row + 1]
        hg_out[:, lanes] = both_ref[4 * spread + row : 4 * spread + row + 1]
    for row in range(spread):
        lanes = slice((4 * spread + row) * LANE, (4 * spread + row + 1) * LANE)
        hs_out[:, lanes] = proj_ref[row : row + 1]
        hg_out[:, lanes] = proj_ref[spread + row : spread + row + 1]
    tasks = tw_out.shape[1]
    place = lax.broadcasted_iota(jnp.int32, (1, LANE), 1)
    weights = jnp.zeros((1, LANE), f32)
    for number in range(tasks):
        weights = jnp.where(place == number, tw_ref[number : number + 1], weights)
    tw_out[...] = weights[:, :tasks]
    for copy in copies:
        copy.wait()


def finish(places, tasks, taps, ho, ig, rg, dg, eg, bs, tw, pg, s3, s2, s1, both, proj):
    f32 = jnp.float32
    in_vmem = pl.BlockSpec(memory_space=pltpu.VMEM)
    anywhere = pl.BlockSpec(memory_space=pl.ANY)
    shape = jax.ShapeDtypeStruct
    depth, width = taps.shape[1:]
    rows = (s1.size + s2.size + s3.size) // 2 // LANE
    return pl.pallas_call(
        functools.partial(finish_kernel, places),
        name="finish",
        out_shape=(
            shape(ho.shape, ho.dtype),
            shape(ig.shape, ig.dtype),
            shape(rg.shape, rg.dtype),
            shape(dg.shape, dg.dtype),
            shape(eg.shape, eg.dtype),
            shape(bs.shape, bs.dtype),
            shape((depth, 2 * width), f32),
            shape((depth, len(places) * width), f32),
            shape(pg.shape, f32),
            shape((rows, LANE), f32),
            shape((rows, LANE), f32),
            shape((1, 5 * width), f32),
            shape((1, 5 * width), f32),
            shape((1, tasks), f32),
        ),
        in_specs=[anywhere] * 14,
        out_specs=(anywhere,) * 8 + (in_vmem,) * 6,
        scratch_shapes=[
            pltpu.VMEM(value.shape, value.dtype) for value in (taps, tw, pg, s3, s2, s1, both, proj, ho, ig, rg, dg, eg, bs)
        ]
        + [
            pltpu.VMEM((depth, 2 * width), f32),
            pltpu.VMEM((depth, len(places) * width), f32),
            pltpu.SemaphoreType.DMA((10,)),
            pltpu.SemaphoreType.DMA((14,)),
        ],
        compiler_params=pltpu.CompilerParams(vmem_limit_bytes=60 << 20),
    )(taps, ho, ig, rg, dg, eg, bs, tw, pg, s3, s2, s1, both, proj)


def live_taps(rows, cols):
    taps = []
    for level in (1, 2, 3):
        for row_tap in range(3):
            for col_tap in range(3):
                down, right = (row_tap - 1) * level * RATE, (col_tap - 1) * level * RATE
                if abs(down) < rows and abs(right) < cols:
                    taps.append((level, row_tap, col_tap, down, right))
    return taps


def per_device_slices(
    features,
    row_width,
    w_reduce,
    w_dilated,
    w_expand,
    trunk_gain,
    trunk_shift,
    branch_weight,
    rate_weight,
    proj_weight,
    head_gain,
    head_shift,
    head_cot,
):
    bands, tasks = lax.axis_size("space"), lax.axis_size("task")
    band_rows, cols, in_width = features.shape
    rows = band_rows * bands
    pixels = band_rows * cols
    head_width = proj_weight.shape[2]
    inputs = features.reshape(pixels, in_width)
    dilated = w_dilated.transpose(1, 0, 2)
    taps, (
        batch_stats,
        head_out,
        tap_grads,
        both_sums,
        proj_sums,
        weight_rows,
        input_grad,
        reduce_grad,
        dilated_grad,
        expand_grad,
        sums_three,
        sums_two,
        sums_one,
        proj_grad,
    ) = whole(
        tasks,
        bands,
        cols,
        rows,
        0,
        inputs,
        row_width,
        trunk_gain.reshape(1, -1),
        trunk_shift.reshape(1, -1),
        w_reduce,
        dilated,
        w_expand,
        head_gain,
        head_shift,
        head_cot.reshape(pixels, head_width),
        branch_weight[0],
        proj_weight[0],
        rate_weight[0],
    )
    place_of = {tap[:3]: number for number, tap in enumerate(taps)}
    places = tuple(
        place_of.get((level, row_tap, col_tap))
        for level in (1, 2, 3)
        for row_tap in range(3)
        for col_tap in range(3)
    )
    (
        head_out,
        input_grad,
        reduce_grad,
        dilated_grad,
        expand_grad,
        batch_stats,
        branch_grad,
        rate_grad,
        proj_grad,
        trunk_gains,
        trunk_shifts,
        head_gains,
        head_shifts,
        task_weight,
    ) = finish(
        places,
        tasks,
        tap_grads,
        head_out,
        input_grad,
        reduce_grad,
        dilated_grad,
        expand_grad,
        batch_stats,
        weight_rows,
        proj_grad.reshape(-1, head_width),
        sums_three,
        sums_two,
        sums_one,
        both_sums,
        proj_sums,
    )
    return (
        head_out.reshape(1, band_rows, cols, head_width),
        input_grad.reshape(features.shape),
        reduce_grad,
        dilated_grad.transpose(1, 0, 2),
        expand_grad,
        trunk_gains.reshape(-1),
        trunk_shifts.reshape(-1),
        batch_stats,
        branch_grad[None],
        rate_grad[None],
        proj_grad[None],
        head_gains,
        head_shifts,
        task_weight.reshape(-1),
    )


def solution(mesh):
    body = per_device_slices if mesh.shape["space"] == 8 else per_device
    return jax.shard_map(
        body,
        mesh=mesh,
        in_specs=(
            P("space", None, None),
            P(),
            P(),
            P(),
            P(),
            P(),
            P(),
            P("task", "space", None),
            P("task", "space", None),
            P("task", None, None),
            P("task", None),
            P("task", None),
            P("task", "space", None, None),
        ),
        out_specs=(
            P("task", "space", None, None),
            P("space", None, None),
            P("space", None),
            P("space", None, None),
            P("space", None),
            P(),
            P(),
            P(),
            P("task", "space", None),
            P("task", "space", None),
            P("task", None, None),
            P("task", None),
            P("task", None),
            P(),
        ),
        check_vma=False,
    )
```

```python
import functools

import jax
import jax.numpy as jnp
from jax import lax
from jax.experimental import pallas as pl
from jax.experimental.pallas import tpu as pltpu
from jax.sharding import PartitionSpec as P

CONV_DILATION = 2
RATE = 12


NORM_EPS = 1e-05
GRAM_EPS = 1e-06
PRECISE = lax.Precision.HIGHEST


def with_halo(block, sides, width):
    for axis, dim in sides:
        count = lax.axis_size(axis)
        forward = [(i, i + 1) for i in range(count - 1)]
        backward = [(target, source) for source, target in forward]
        low = lax.ppermute(
            lax.slice_in_dim(block, block.shape[dim] - width, None, axis=dim), axis, forward
        )
        high = lax.ppermute(lax.slice_in_dim(block, 0, width, axis=dim), axis, backward)
        block = jnp.concatenate([low, block, high], axis=dim)
    return block


def from_behind(shard, axis, by):
    count = lax.axis_size(axis)
    pairs = [(i, i + by) for i in range(count) if 0 <= i + by < count]
    return lax.ppermute(shard, axis, pairs)


def small_solve(matrix, target):
    size_n = matrix.shape[0]
    rows_list = [matrix[number] for number in range(size_n)]
    values = [target[number] for number in range(size_n)]
    for pivot_row in range(size_n):
        for lower_row in range(pivot_row + 1, size_n):
            factor = rows_list[lower_row][pivot_row] / rows_list[pivot_row][pivot_row]
            rows_list[lower_row] = rows_list[lower_row] - factor * rows_list[pivot_row]
            values[lower_row] = values[lower_row] - factor * values[pivot_row]
    answer = [None] * size_n
    for pivot_row in reversed(range(size_n)):
        running = values[pivot_row]
        for later_row in range(pivot_row + 1, size_n):
            running = running - rows_list[pivot_row][later_row] * answer[later_row]
        answer[pivot_row] = running / rows_list[pivot_row][pivot_row]
    return jnp.stack(answer)


def imtl_weights(gram_matrix):
    grad_norms = jnp.sqrt(jnp.diagonal(gram_matrix) + GRAM_EPS)
    projections = gram_matrix / grad_norms[None, :]
    system = projections[0, 0] - projections[0:1, 1:] - projections[1:, 0:1] + projections[1:, 1:]
    target = projections[0, 0] - projections[0, 1:]
    other_weights = small_solve(jnp.transpose(system), target)
    return jnp.concatenate([(1.0 - jnp.sum(other_weights))[None], other_weights])


def gelu_back(value, upstream):
    return jax.vjp(jax.nn.gelu, value)[1](upstream)[0]


def channel_sums(members):
    return lax.psum(members, "space")


def norm_values(hidden, first_total, second_total, gain_vec, shift_vec, pixel_count):
    mean_value = first_total / pixel_count
    variance = second_total / pixel_count - mean_value * mean_value
    inv_std = lax.rsqrt(variance + NORM_EPS)
    scaled = (hidden - mean_value) * inv_std
    return (gain_vec * scaled + shift_vec, scaled, inv_std, mean_value, variance)


def norm_forward(hidden, gain_vec, shift_vec, valid_mask, pixel_count):
    totals = channel_sums(
        (jnp.sum(hidden * valid_mask, axis=0), jnp.sum(hidden * hidden * valid_mask, axis=0))
    )
    return norm_values(hidden, totals[0], totals[1], gain_vec, shift_vec, pixel_count)


def norm_finish(
    upstream, scaled, inv_std, gain_vec, gain_grad, shift_grad, valid_mask, pixel_count
):
    return (
        valid_mask
        * gain_vec
        * inv_std
        * (upstream - shift_grad / pixel_count - scaled * gain_grad / pixel_count)
    )


def norm_backward(upstream, scaled, inv_std, gain_vec, valid_mask, pixel_count):
    totals = channel_sums(
        (jnp.sum(upstream * valid_mask, axis=0), jnp.sum(upstream * scaled * valid_mask, axis=0))
    )
    hidden_grad = norm_finish(
        upstream, scaled, inv_std, gain_vec, totals[1], totals[0], valid_mask, pixel_count
    )
    return (hidden_grad, totals[1], totals[0])


def band_rim(strip_image):
    return with_halo(strip_image, (("space", 0),), CONV_DILATION)


def far_rows(strip_image, bands_away, upward):
    if bands_away >= lax.axis_size("space"):
        return jnp.zeros_like(strip_image)
    if upward:
        return from_behind(strip_image, "space", bands_away)
    return from_behind(strip_image, "space", -bands_away)


def trunk_taps(padded, reach_cells, rows_count, cols_count, flipped):
    col_padded = jnp.pad(padded, ((0, 0), (reach_cells, reach_cells), (0, 0)))
    pieces = []
    for row_tap in range(3):
        for col_tap in range(3):
            row_from = (2 - row_tap) * reach_cells if flipped else row_tap * reach_cells
            col_from = (2 - col_tap) * reach_cells if flipped else col_tap * reach_cells
            pieces.append(
                col_padded[
                    row_from : row_from + rows_count, col_from : col_from + cols_count
                ].reshape(rows_count * cols_count, -1)
            )
    return jnp.stack(pieces, axis=1)


def per_device(
    features,
    row_width,
    w_reduce,
    w_dilated,
    w_expand,
    trunk_gain,
    trunk_shift,
    branch_weight,
    rate_weight,
    proj_weight,
    head_gain,
    head_shift,
    head_cot,
):
    band_rows, cols_count, in_width = features.shape
    pixels = band_rows * cols_count
    middle_width = w_reduce.shape[1]
    head_width = proj_weight.shape[2]
    first_row = lax.axis_index("space") * band_rows
    widths = lax.dynamic_slice_in_dim(row_width, first_row, band_rows)
    valid_mask = (
        (jnp.arange(cols_count)[None, :] < widths[:, None]).astype(jnp.float32).reshape(pixels, 1)
    )
    pixel_count = jnp.sum(row_width).astype(jnp.float32)
    inputs = features.reshape(pixels, in_width)
    gain_one, shift_one = (trunk_gain[:middle_width], trunk_shift[:middle_width])
    gain_two, shift_two = (
        trunk_gain[middle_width : 2 * middle_width],
        trunk_shift[middle_width : 2 * middle_width],
    )
    gain_three, shift_three = (trunk_gain[2 * middle_width :], trunk_shift[2 * middle_width :])
    hidden_one = jnp.dot(inputs, w_reduce, preferred_element_type=jnp.float32)
    stats_one = norm_forward(hidden_one, gain_one, shift_one, valid_mask, pixel_count)
    first_active = (jax.nn.gelu(stats_one[0]) * valid_mask).astype(jnp.bfloat16)
    patches = trunk_taps(
        band_rim(first_active.reshape(band_rows, cols_count, middle_width)),
        CONV_DILATION,
        band_rows,
        cols_count,
        False,
    )
    hidden_two = jnp.einsum("pti,ito->po", patches, w_dilated, preferred_element_type=jnp.float32)
    stats_two = norm_forward(hidden_two, gain_two, shift_two, valid_mask, pixel_count)
    active_two = (jax.nn.gelu(stats_two[0]) * valid_mask).astype(jnp.bfloat16)
    hidden_three = jnp.dot(active_two, w_expand, preferred_element_type=jnp.float32)
    stats_three = norm_forward(hidden_three, gain_three, shift_three, valid_mask, pixel_count)
    before_act = stats_three[0] + inputs.astype(jnp.float32)
    shared = (jax.nn.gelu(before_act) * valid_mask).astype(jnp.bfloat16)
    proj_local = proj_weight[0]
    gain_local = head_gain[0]
    shift_local = head_shift[0]
    joined_weight = jnp.concatenate([branch_weight[0], rate_weight[0]], axis=1)
    pixel_sum = jnp.dot(
        valid_mask.reshape(1, pixels).astype(jnp.bfloat16),
        shared,
        preferred_element_type=jnp.float32,
    )[0]
    shared_image = shared.reshape(band_rows, cols_count, in_width)
    padded_sources = []
    for level in (1, 2, 3):
        reach = level * RATE
        bands_away = reach // band_rows
        triple = (
            far_rows(shared_image, bands_away, True),
            shared_image,
            far_rows(shared_image, bands_away, False),
        )
        padded_sources.append(
            [jnp.pad(source, ((0, 0), (reach, reach), (0, 0))) for source in triple]
        )
    zero_rows = jnp.zeros((pixels, head_width), jnp.float32)
    start_totals = (
        zero_rows,
        jnp.zeros((1, head_width), jnp.float32),
        zero_rows,
        zero_rows,
        zero_rows,
    )
    all_weights = lax.all_gather(joined_weight, "space", axis=0, tiled=True)
    width_now = all_weights.shape[0]
    one_acc = jnp.dot(shared, all_weights[:, :head_width], preferred_element_type=jnp.float32)
    pool_cols = pixel_sum[None]
    pool_acc = jnp.dot(
        pool_cols,
        all_weights[:, head_width : 2 * head_width].astype(jnp.float32),
        precision=PRECISE,
        preferred_element_type=jnp.float32,
    )
    rate_accs = []
    for fold_level_index in range(3):
        fold_reach = (fold_level_index + 1) * RATE
        running = start_totals[2 + fold_level_index]
        for fold_row_tap in range(3):
            fold_source = padded_sources[fold_level_index][fold_row_tap]
            for fold_col_tap in range(3):
                window = fold_source[
                    :, fold_col_tap * fold_reach : fold_col_tap * fold_reach + cols_count
                ].reshape(pixels, width_now)
                column = (2 + 9 * fold_level_index + 3 * fold_row_tap + fold_col_tap) * head_width
                running = running + jnp.dot(
                    window,
                    all_weights[:, column : column + head_width],
                    preferred_element_type=jnp.float32,
                )
        rate_accs.append(running)
    pre_both = jnp.concatenate([one_acc, rate_accs[0], rate_accs[1], rate_accs[2]], axis=1)
    gain_both, shift_both = (gain_local[: 4 * head_width], shift_local[: 4 * head_width])
    totals = channel_sums(
        (
            jnp.sum(pre_both * valid_mask, axis=0),
            jnp.sum(pre_both * pre_both * valid_mask, axis=0),
            pool_acc[0],
        )
    )
    stats_both = norm_values(pre_both, totals[0], totals[1], gain_both, shift_both, pixel_count)
    pooled = totals[2][None] / pixel_count
    active_both = (jax.nn.gelu(stats_both[0]) * valid_mask).astype(jnp.bfloat16)
    active_pool = jax.nn.gelu(pooled).astype(jnp.bfloat16)
    joined = jnp.concatenate(
        [active_both, (active_pool.astype(jnp.float32) * valid_mask).astype(jnp.bfloat16)], axis=1
    )
    projected = jnp.dot(joined, proj_local, preferred_element_type=jnp.float32)
    gain_proj = gain_local[4 * head_width :]
    stats_proj = norm_forward(
        projected, gain_proj, shift_local[4 * head_width :], valid_mask, pixel_count
    )
    head_result = (jax.nn.gelu(stats_proj[0]) * valid_mask).astype(jnp.bfloat16)
    cot_rows = head_cot[0].reshape(pixels, head_width).astype(jnp.float32)
    proj_upstream = gelu_back(stats_proj[0], cot_rows * valid_mask)
    proj_hidden, proj_gain_grad, proj_shift_grad = norm_backward(
        proj_upstream, stats_proj[1], stats_proj[2], gain_proj, valid_mask, pixel_count
    )
    proj_low = proj_hidden.astype(jnp.bfloat16)
    joined_grad = lax.dot_general(
        proj_low, proj_local, (((1,), (1,)), ((), ())), preferred_element_type=jnp.float32
    )
    proj_term = lax.dot_general(
        joined, proj_low, (((0,), (0,)), ((), ())), preferred_element_type=jnp.float32
    )
    both_upstream = gelu_back(stats_both[0], joined_grad[:, : 4 * head_width] * valid_mask)
    pool_total = jnp.sum(joined_grad[:, 4 * head_width :] * valid_mask, axis=0)
    back_totals = channel_sums(
        (
            proj_term,
            pool_total,
            jnp.sum(both_upstream * valid_mask, axis=0),
            jnp.sum(both_upstream * stats_both[1] * valid_mask, axis=0),
        )
    )
    pool_grad = gelu_back(pooled, back_totals[1][None]).astype(jnp.bfloat16)
    both_grad = norm_finish(
        both_upstream,
        stats_both[1],
        stats_both[2],
        gain_both,
        back_totals[3],
        back_totals[2],
        valid_mask,
        pixel_count,
    ).astype(jnp.bfloat16)
    tap_grads = []
    for level_index in range(3):
        reach = (level_index + 1) * RATE
        bands_away = reach // band_rows
        rate_image = both_grad[
            :, (1 + level_index) * head_width : (2 + level_index) * head_width
        ].reshape(band_rows, cols_count, head_width)
        back_sources = [
            jnp.pad(source, ((0, 0), (reach, reach), (0, 0)))
            for source in (
                far_rows(rate_image, bands_away, False),
                rate_image,
                far_rows(rate_image, bands_away, True),
            )
        ]
        for row_tap in range(3):
            for col_tap in range(3):
                tap_grads.append(
                    back_sources[row_tap][
                        :, (2 - col_tap) * reach : (2 - col_tap) * reach + cols_count
                    ].reshape(pixels, head_width)
                )
    right_side = jnp.concatenate([both_grad[:, :head_width]] + tap_grads, axis=1)
    used_rows = jnp.concatenate(
        [all_weights[:, :head_width], all_weights[:, 2 * head_width :]], axis=1
    )
    main_part = lax.dot_general(
        right_side, used_rows, (((1,), (1,)), ((), ())), preferred_element_type=jnp.float32
    )
    pool_part = lax.dot_general(
        pool_grad,
        all_weights[:, head_width : 2 * head_width],
        (((1,), (1,)), ((), ())),
        preferred_element_type=jnp.float32,
    )
    shared_grad = (main_part + valid_mask * pool_part / pixel_count).astype(jnp.bfloat16)
    head_term = lax.dot_general(
        shared, right_side, (((0,), (0,)), ((), ())), preferred_element_type=jnp.float32
    )
    pool_term = pixel_sum[:, None] * pool_grad.astype(jnp.float32) / pixel_count
    head_term = jnp.concatenate(
        [head_term[:, :head_width], pool_term, head_term[:, head_width:]], axis=1
    )
    all_grads = lax.all_gather(shared_grad[None], "task", axis=0, tiled=True)
    flat_grads = all_grads.reshape(all_grads.shape[0], -1)
    gram_matrix = lax.psum(
        lax.dot_general(
            flat_grads, flat_grads, (((1,), (1,)), ((), ())), preferred_element_type=jnp.float32
        ),
        "space",
    )
    task_weight = imtl_weights(gram_matrix)
    mixed_grad = task_weight[0] * all_grads[0].astype(jnp.float32)
    for task_index in range(1, all_grads.shape[0]):
        mixed_grad = mixed_grad + task_weight[task_index] * all_grads[task_index].astype(
            jnp.float32
        )
    combined = mixed_grad.astype(jnp.bfloat16)
    gate_grad = gelu_back(before_act, combined.astype(jnp.float32) * valid_mask)
    hidden_grad_three, gain_grad_three, shift_grad_three = norm_backward(
        gate_grad, stats_three[1], stats_three[2], gain_three, valid_mask, pixel_count
    )
    low_three = hidden_grad_three.astype(jnp.bfloat16)
    expand_term = lax.dot_general(
        active_two, low_three, (((0,), (0,)), ((), ())), preferred_element_type=jnp.float32
    )
    active_grad_two = lax.dot_general(
        low_three, w_expand, (((1,), (1,)), ((), ())), preferred_element_type=jnp.float32
    )
    upstream_two = gelu_back(stats_two[0], active_grad_two * valid_mask)
    hidden_grad_two, gain_grad_two, shift_grad_two = norm_backward(
        upstream_two, stats_two[1], stats_two[2], gain_two, valid_mask, pixel_count
    )
    low_two = hidden_grad_two.astype(jnp.bfloat16)
    dilated_term = jnp.einsum("pti,po->ito", patches, low_two, preferred_element_type=jnp.float32)
    back_patches = trunk_taps(
        band_rim(low_two.reshape(band_rows, cols_count, middle_width)),
        CONV_DILATION,
        band_rows,
        cols_count,
        True,
    )
    active_grad_one = jnp.einsum(
        "pto,ito->pi", back_patches, w_dilated, preferred_element_type=jnp.float32
    )
    upstream_one = gelu_back(stats_one[0], active_grad_one * valid_mask)
    hidden_grad_one, gain_grad_one, shift_grad_one = norm_backward(
        upstream_one, stats_one[1], stats_one[2], gain_one, valid_mask, pixel_count
    )
    low_one = hidden_grad_one.astype(jnp.bfloat16)
    reduce_term = lax.dot_general(
        inputs, low_one, (((0,), (0,)), ((), ())), preferred_element_type=jnp.float32
    )
    input_grad = (
        lax.dot_general(
            low_one, w_reduce, (((1,), (1,)), ((), ())), preferred_element_type=jnp.float32
        )
        + gate_grad
    )
    reduced = (
        lax.psum_scatter(head_term, "space", scatter_dimension=0, tiled=True),
        lax.psum_scatter(reduce_term, "space", scatter_dimension=0, tiled=True),
        lax.psum_scatter(dilated_term, "space", scatter_dimension=0, tiled=True),
        lax.psum_scatter(expand_term, "space", scatter_dimension=0, tiled=True),
    )
    means = jnp.concatenate([stats_one[3], stats_two[3], stats_three[3]])
    variances = (
        jnp.concatenate([stats_one[4], stats_two[4], stats_three[4]])
        * pixel_count
        / (pixel_count - 1.0)
    )
    batch_stats = jnp.stack([means, variances])
    head_gain_grad = jnp.concatenate([back_totals[3], proj_gain_grad])[None]
    head_shift_grad = jnp.concatenate([back_totals[2], proj_shift_grad])[None]
    return (
        head_result.reshape(1, band_rows, cols_count, head_width),
        input_grad.reshape(band_rows, cols_count, in_width).astype(jnp.bfloat16),
        reduced[1],
        reduced[2],
        reduced[3],
        jnp.concatenate([gain_grad_one, gain_grad_two, gain_grad_three]),
        jnp.concatenate([shift_grad_one, shift_grad_two, shift_grad_three]),
        batch_stats,
        reduced[0][:, : 2 * head_width][None],
        reduced[0][:, 2 * head_width :][None],
        back_totals[0][None],
        head_gain_grad,
        head_shift_grad,
        task_weight,
    )


MESH_ID = pl.DeviceIdType.MESH
LANE = 128


FAR_LAG = 2
SEND_LAG = 0
GELU_A = 0.7978845608028654
GELU_B = 0.044715


def gelu_of(value):
    return 0.5 * value * (1.0 + jnp.tanh(GELU_A * (value + GELU_B * value * value * value)))


def gelu_slope(value):
    square = value * value
    bend = jnp.tanh(GELU_A * value * (1.0 + GELU_B * square))
    return 0.5 * (1.0 + bend) + 0.5 * value * (1.0 - bend * bend) * (
        GELU_A * (1.0 + 3.0 * GELU_B * square)
    )


def gelu_both(value):
    square = value * value
    bend = jnp.tanh(GELU_A * value * (1.0 + GELU_B * square))
    lift = 0.5 * (1.0 + bend)
    slope = lift + 0.5 * value * (1.0 - bend * bend) * (GELU_A * (1.0 + 3.0 * GELU_B * square))
    return value * lift, slope


def dot_nn(left_side, right_side):
    return jnp.dot(left_side, right_side, preferred_element_type=jnp.float32)


def dot_nt(left_side, right_side):
    return lax.dot_general(
        left_side, right_side, (((1,), (1,)), ((), ())), preferred_element_type=jnp.float32
    )


def shift_pixels(value, by, cols):
    if by == 0:
        return value
    rows = value.shape[0]
    column = lax.rem(lax.broadcasted_iota(jnp.int32, value.shape, 0), cols) + by
    rolled = pltpu.roll(value, (-by) % rows, 0)
    return jnp.where((column >= 0) & (column < cols), rolled, 0.0)


def row_mask(widths_ref, first_row, rows, cols):
    column = lax.broadcasted_iota(jnp.int32, (cols, LANE), 0)
    return jnp.concatenate(
        [
            jnp.where(column < widths_ref[first_row + number], 1.0, 0.0).astype(jnp.float32)
            for number in range(rows)
        ],
        axis=0,
    )


def count_pixels(widths_ref):
    total = widths_ref[0]
    for number in range(1, widths_ref.shape[0]):
        total = total + widths_ref[number]
    return jnp.full((1, LANE), total.astype(jnp.float32), jnp.float32)


class Post:
    def __init__(self, send_sem, recv_sem):
        self.send_sem, self.recv_sem = send_sem, recv_sem
        self.used = 0
        self.sent = []

    def copy(self, source, target, device):
        made = pltpu.make_async_remote_copy(
            source,
            target,
            self.send_sem.at[self.used],
            self.recv_sem.at[self.used],
            device_id=device,
            device_id_type=MESH_ID,
        )
        self.used += 1
        return made

    def push(self, source, target, device):
        made = self.copy(source, target, device)
        made.start()
        self.sent.append(made)
        return made

    def close(self):
        for made in self.sent:
            made.wait_send()
        self.sent = []


class Place:
    def __init__(self, tasks, bands):
        self.tasks, self.bands, self.chips = tasks, bands, bands // 2
        self.task = lax.axis_index("task")
        self.band = lax.axis_index("space")
        self.chip = self.band // 2
        self.core = lax.rem(self.band, 2)
        self.twin = {"space": self.chip * 2 + 1 - self.core}
        low, high = lax.rem(self.task, 2), self.task // 2
        self.other_tasks = [(1 - high) * 2 + 1 - low, high * 2 + 1 - low, (1 - high) * 2 + low]
        self.other_bands = [lax.rem(self.band + step, bands) for step in range(1, bands)]

    def greet(self):
        barrier = pltpu.get_barrier_semaphore()
        greeted = [{"task": task} for task in self.other_tasks]
        greeted += [{"space": band} for band in self.other_bands]
        for device in greeted:
            pl.semaphore_signal(barrier, inc=1, device_id=device, device_id_type=MESH_ID)

    def meet(self):
        barrier = pltpu.get_barrier_semaphore()
        pl.semaphore_wait(barrier, len(self.other_tasks) + len(self.other_bands))

    def sum_begin(self, post, axis, own_ref, land_ref):
        mine = self.task if axis == "task" else self.band
        others = self.other_tasks if axis == "task" else self.other_bands
        copies = [post.push(own_ref, land_ref.at[mine], {axis: other}) for other in others]
        land_ref[pl.ds(mine, 1)] = own_ref[...][None]
        return copies, land_ref

    def sum_end(self, begun):
        copies, land_ref = begun
        for made in copies:
            made.wait_recv()
        total = land_ref[0]
        for slot in range(1, len(copies) + 1):
            total = total + land_ref[slot]
        return total

    def sum_over(self, post, axis, own_ref, land_ref):
        return self.sum_end(self.sum_begin(post, axis, own_ref, land_ref))


def back_phase(
    at,
    post,
    sizes,
    local_sem,
    xg,
    h3q,
    v3_ref,
    h2_ref,
    v2_ref,
    h1_ref,
    v1_ref,
    act_ref,
    a2_ref,
    ps_ref,
    x_hbm,
    widths_ref,
    we_hbm,
    wd_hbm,
    wr_hbm,
    write,
    tw_hbm,
    ig_hbm,
    rg_hbm,
    dg_hbm,
    eg_hbm,
    s3_hbm,
    s2_hbm,
    s1_hbm,
    pg_hbm,
    tw_out,
    ig_out,
    rg_out,
    dg_out,
    eg_out,
    s3_out,
    s2_out,
    s1_out,
    pg_out,
    we,
    wd,
    wr,
    x_ref,
    mask_ref,
    gram_own,
    gram_land,
    gram_mid,
    gram_land_b,
    comb,
    comb_land,
    gate,
    scaled,
    gate_low,
    gate_band,
    st3,
    st3_land,
    st3_mid,
    st3_land_b,
    l3,
    l3x,
    st2,
    st2_land,
    st2_mid,
    st2_land_b,
    l2,
    l2_halo,
    ag1,
    st1,
    st1_land,
    l1,
    xt,
    a2t,
    e_term,
    e_twin,
    e_land,
    e_share,
    e_tasks,
    l2c,
    d_sum,
    d_share,
    d_tasks,
    r_term,
    r_twin,
    r_land,
    r_share,
    r_tasks,
    p_all,
):
    tasks, bands, cols, quarter, mid, wide, piece = sizes
    low = jnp.bfloat16
    f32 = jnp.float32
    task, band = at.task, at.band
    my_rows = pl.ds(pl.multiple_of(task * quarter, quarter), quarter)
    arrays = {
        "x": (x_hbm, x_ref),
        "we": (we_hbm, we),
        "wd": (wd_hbm, wd),
        "wr": (wr_hbm, wr),
    }
    loads = {
        name: pltpu.make_async_copy(source, target, local_sem.at[number])
        for number, (name, (source, target)) in enumerate(arrays.items())
    }

    def loaded(*names):
        for name in names:
            loads[name].wait()

    for load in loads.values():
        load.start()
    band_rows = x_ref.shape[0] // cols
    mask_ref[...] = row_mask(widths_ref, band * band_rows, band_rows, cols)

    pairs = [(a, b) for a in range(tasks) for b in range(a, tasks)]

    def gram_step(number, totals):
        grads = [xg[a, number].astype(f32) for a in range(tasks)]
        out = []
        for (a, b), total in zip(pairs, totals):
            product = grads[a] * grads[b]
            product = product.reshape(quarter // 8, 8, piece).sum(axis=0)
            for start in range(0, piece, LANE):
                total = total + product[:, start : start + LANE]
            out.append(total)
        return tuple(out)

    totals = lax.fori_loop(
        0, bands, gram_step, tuple(jnp.zeros((8, LANE), f32) for _ in pairs)
    )
    gram_own[...] = jnp.zeros_like(gram_own)
    for number, total in enumerate(totals):
        gram_own[number : number + 1] = jnp.sum(total, axis=0, keepdims=True)
    begun = at.sum_begin(post, "task", gram_own, gram_land)
    a2t[...] = a2_ref[...].T
    gram_mid[...] = at.sum_end(begun)
    begun = at.sum_begin(post, "space", gram_mid, gram_land_b)

    loaded("x")
    def turn_inputs(number, carry):
        lanes = pl.ds(pl.multiple_of(number * piece, piece), piece)
        xt[lanes, :] = x_ref[:, lanes].T
        return carry

    lax.fori_loop(0, wide // piece, turn_inputs, 0)
    gram_sum = at.sum_end(begun)
    gram_sum = jnp.broadcast_to(jnp.sum(gram_sum, axis=1, keepdims=True), gram_sum.shape)
    gram = [[None] * tasks for _ in range(tasks)]
    for number, (a, b) in enumerate(pairs):
        gram[a][b] = gram[b][a] = gram_sum[number : number + 1]
    norms = [jnp.sqrt(gram[a][a] + GRAM_EPS) for a in range(tasks)]
    cos = [[gram[a][b] / norms[b] for b in range(tasks)] for a in range(tasks)]
    rows_list = [
        [cos[0][0] - cos[0][l] - cos[k][0] + cos[k][l] for k in range(1, tasks)]
        for l in range(1, tasks)
    ]
    values = [cos[0][0] - cos[0][l] for l in range(1, tasks)]
    count = tasks - 1
    for pivot in range(count):
        for lower in range(pivot + 1, count):
            factor = rows_list[lower][pivot] / rows_list[pivot][pivot]
            rows_list[lower] = [
                under - factor * over for under, over in zip(rows_list[lower], rows_list[pivot])
            ]
            values[lower] = values[lower] - factor * values[pivot]
    answer = [None] * count
    for pivot in reversed(range(count)):
        running = values[pivot]
        for later in range(pivot + 1, count):
            running = running - rows_list[pivot][later] * answer[later]
        answer[pivot] = running / rows_list[pivot][pivot]
    rest = answer[0]
    for value in answer[1:]:
        rest = rest + value
    task_weight = [1.0 - rest] + answer
    for number in range(tasks):
        tw_out[number : number + 1] = task_weight[number]
    weights = [jnp.concatenate([value] * (piece // LANE), axis=1) for value in task_weight]

    def mixed(number):
        total = weights[0] * xg[0, number].astype(f32)
        for a in range(1, tasks):
            total = total + weights[a] * xg[a, number].astype(f32)
        return total.astype(low)

    comb_in = []
    for other in at.other_bands:
        comb[other] = mixed(other)
        comb_in.append(post.push(comb.at[other], comb_land.at[band], {"space": other}))
    comb_land[pl.ds(band, 1)] = mixed(band)[None]
    for made in comb_in:
        made.wait_recv()

    mask_quarter = mask_ref[my_rows]
    mask_piece = jnp.concatenate([mask_quarter] * (piece // LANE), axis=1)
    inv_count = 1.0 / count_pixels(widths_ref)
    inv_piece = jnp.concatenate([inv_count] * (piece // LANE), axis=1)
    per_row = st3.shape[1] // piece
    half = st3.shape[0] // 2

    def gate_step(number, carry):
        lanes = pl.ds(pl.multiple_of(number * piece, piece), piece)
        hat = (h3q[:, lanes] - v3_ref[0:1, lanes]) * v3_ref[1:2, lanes]
        before = v3_ref[2:3, lanes] * hat + v3_ref[3:4, lanes] + x_ref[my_rows, lanes].astype(f32)
        grad = gelu_slope(before) * comb_land[number].astype(f32) * mask_piece
        gate[number] = grad
        scaled[number] = hat
        gate_low[number] = grad.astype(low)
        row = number // per_row
        spot = pl.ds(pl.multiple_of(lax.rem(number, per_row) * piece, piece), piece)
        st3[pl.ds(row, 1), spot] = jnp.sum(grad, axis=0, keepdims=True)
        st3[pl.ds(half + row, 1), spot] = jnp.sum(grad * hat, axis=0, keepdims=True)
        return carry

    lax.fori_loop(0, bands, gate_step, 0)
    st3_mid[...] = at.sum_over(post, "task", st3, st3_land)
    s3_out[...] = at.sum_over(post, "space", st3_mid, st3_land_b)

    def third_step(number, carry):
        lanes = pl.ds(pl.multiple_of(number * piece, piece), piece)
        row = number // per_row
        spot = pl.ds(pl.multiple_of(lax.rem(number, per_row) * piece, piece), piece)
        shift_grad = s3_out[pl.ds(row, 1), spot] * inv_piece
        gain_grad = s3_out[pl.ds(half + row, 1), spot] * inv_piece
        l3[number] = (
            mask_piece
            * (v3_ref[2:3, lanes] * v3_ref[1:2, lanes])
            * (gate[number] - shift_grad - scaled[number] * gain_grad)
        ).astype(low)
        return carry

    lax.fori_loop(0, bands, third_step, 0)
    per_task = bands // tasks
    l3_in = []
    for other in at.other_tasks:
        l3_in.append(
            post.push(l3.at[pl.ds(other * per_task, per_task)], l3x.at[task], {"task": other})
        )
    l3x[pl.ds(task, 1)] = l3[pl.ds(task * per_task, per_task)][None]
    loaded("we")
    p_all[pl.ds(band, 1)] = ps_ref[...][None]
    p_block = p_all.at[band]
    p_near = post.push(p_block, p_block, at.twin)
    p_far = [
        post.push(
            p_block,
            p_block,
            {"space": lax.rem(at.chip + step, at.chips) * 2 + at.core},
        )
        for step in range(1, at.chips)
    ]

    def expand_step(number, total):
        lanes = pl.ds(pl.multiple_of(number * piece, piece), piece)
        return total + dot_nt(l3[number], we[:, lanes])

    ag2 = lax.fori_loop(0, bands, expand_step, jnp.zeros((quarter, mid), f32))

    mask_mid = jnp.concatenate([mask_quarter] * (mid // LANE), axis=1)
    inv_mid = jnp.concatenate([inv_count] * (mid // LANE), axis=1)
    hat = (h2_ref[my_rows] - v2_ref[0:1]) * v2_ref[1:2]
    grad = gelu_slope(v2_ref[2:3] * hat + v2_ref[3:4]) * ag2 * mask_mid
    spread = mid // LANE

    def put_sums(target, first, second):
        for number in range(spread):
            lanes = slice(number * LANE, (number + 1) * LANE)
            target[number : number + 1] = first[:, lanes]
            target[spread + number : spread + number + 1] = second[:, lanes]

    def get_sums(total):
        return [
            jnp.concatenate([total[base + k : base + k + 1] for k in range(spread)], axis=1)
            for base in (0, spread)
        ]

    def to_twin(term, landing):
        return post.push(term.at[1 - at.core], landing, at.twin)

    def both_cores(pair, term, twin):
        pair.wait_recv()
        for step in range(1, at.chips):
            other = lax.rem(at.chip + step, at.chips)
            both = term[at.core, other].astype(f32) + twin[other].astype(f32)
            twin[other] = both.astype(low)

    def along(twin, landing):
        return [
            post.push(
                twin.at[other], landing.at[at.chip], {"space": other * 2 + at.core}
            )
            for other in [lax.rem(at.chip + step, at.chips) for step in range(1, at.chips)]
        ]

    def settle(arrivals, term, twin, landing):
        total = term[at.core, at.chip].astype(f32) + twin[at.chip].astype(f32)
        for made in arrivals:
            made.wait_recv()
        for step in range(1, at.chips):
            total = total + landing[lax.rem(at.chip + step, at.chips)].astype(f32)
        return total.astype(low)

    def to_tasks(share, landing):
        arrivals = [post.push(share, landing.at[task], {"task": other}) for other in at.other_tasks]
        landing[pl.ds(task, 1)] = share[...][None]
        return arrivals

    def expand_part(number):
        share = jnp.concatenate([l3x[a, number] for a in range(tasks)], axis=0)
        part = dot_nn(a2t[...], share).astype(low)
        per_band = part.shape[0] // bands
        for target in range(bands):
            e_term[target % 2, target // 2, :, number * piece : (number + 1) * piece] = part[
                target * per_band : (target + 1) * per_band
            ]

    narrow = mid // tasks
    my_lanes = pl.ds(pl.multiple_of(task * narrow, narrow), narrow)
    put_sums(
        st2, jnp.sum(grad, axis=0, keepdims=True), jnp.sum(grad * hat, axis=0, keepdims=True)
    )
    begun = at.sum_begin(post, "task", st2, st2_land)
    for made in l3_in:
        made.wait_recv()
    expand_part(0)
    st2_mid[...] = at.sum_end(begun)
    begun = at.sum_begin(post, "space", st2_mid, st2_land_b)
    for number in range(1, per_task):
        expand_part(number)
    e_pair = to_twin(e_term, e_twin)
    s2_out[...] = at.sum_end(begun)
    shift_grad, gain_grad = get_sums(s2_out[...])
    l2[my_rows] = (
        mask_mid
        * (v2_ref[2:3] * v2_ref[1:2])
        * (grad - shift_grad * inv_mid - hat * (gain_grad * inv_mid))
    ).astype(low)
    l2_in = [post.push(l2.at[my_rows], l2.at[my_rows], {"task": other}) for other in at.other_tasks]
    both_cores(e_pair, e_term, e_twin)
    e_in = along(e_twin, e_land)
    for made in l2_in:
        made.wait_recv()
    gate_in = [
        post.push(gate_low, gate_band.at[task], {"task": other}) for other in at.other_tasks
    ]
    gate_band[pl.ds(task, 1)] = gate_low[...][None]
    has_above, has_below = band > 0, band < bands - 1
    up = post.copy(l2, l2_halo.at[1], {"space": lax.rem(band + bands - 1, bands)})
    down = post.copy(l2, l2_halo.at[0], {"space": lax.rem(band + 1, bands)})

    @pl.when(has_above)
    def _():
        up.start()

    @pl.when(has_below)
    def _():
        down.start()

    @pl.when(jnp.logical_not(has_above))
    def _():
        l2_halo[0] = jnp.zeros_like(l2)

    @pl.when(jnp.logical_not(has_below))
    def _():
        l2_halo[1] = jnp.zeros_like(l2)

    p_passed = []
    for step, made in enumerate(p_far, start=1):
        made.wait_recv()
        block = p_all.at[lax.rem(at.chip + at.chips - step, at.chips) * 2 + at.core]
        p_passed.append(post.push(block, block, at.twin))
    loaded("wd")
    halves = [slice(start, start + piece) for start in range(0, mid, piece)]
    for lanes in halves:
        total = None
        for col_tap in range(3):
            part = shift_pixels(
                dot_nt(l2[...], wd[3 + col_tap, lanes, :]), -CONV_DILATION * (col_tap - 1), cols
            )
            total = part if total is None else total + part
        ag1[:, lanes] = total

    @pl.when(has_below)
    def _():
        up.wait_recv()

    @pl.when(has_above)
    def _():
        down.wait_recv()

    for lanes in halves:
        total = None
        for col_tap in range(3):
            part = dot_nt(l2_halo[1], wd[col_tap, lanes, :]) + dot_nt(
                l2_halo[0], wd[6 + col_tap, lanes, :]
            )
            part = shift_pixels(part, -CONV_DILATION * (col_tap - 1), cols)
            total = part if total is None else total + part
        ag1[:, lanes] += total

    pixels = ag1.shape[0]
    chunk = pixels // 8

    def first_rows(number):
        return pl.ds(pl.multiple_of(number * chunk, chunk), chunk)

    def first_step(number, sums):
        rows = first_rows(number)
        hat = (h1_ref[rows] - v1_ref[0:1]) * v1_ref[1:2]
        keep = jnp.concatenate([mask_ref[rows]] * spread, axis=1)
        grad = gelu_slope(v1_ref[2:3] * hat + v1_ref[3:4]) * ag1[rows] * keep
        ag1[rows] = grad
        return (
            sums[0] + jnp.sum(grad, axis=0, keepdims=True),
            sums[1] + jnp.sum(grad * hat, axis=0, keepdims=True),
        )

    nothing = jnp.zeros((1, mid), f32)
    first, second = lax.fori_loop(0, 8, first_step, (nothing, nothing))
    put_sums(st1, first, second)
    begun = at.sum_begin(post, "space", st1, st1_land)
    l2c[pl.ds(band, 1)] = l2[:, my_lanes][None]
    l2_block = l2c.at[band]
    d_far = [
        post.push(
            l2_block,
            l2_block,
            {"space": lax.rem(at.chip + step, at.chips) * 2 + at.core},
        )
        for step in range(1, at.chips)
    ]
    d_near = [post.push(l2_block, l2_block, at.twin)]
    e_share[...] = settle(e_in, e_term, e_twin, e_land)
    s1_out[...] = at.sum_end(begun)
    shift_grad, gain_grad = get_sums(s1_out[...])
    shift_grad, gain_grad = shift_grad * inv_mid, gain_grad * inv_mid

    def first_finish(number, carry):
        rows = first_rows(number)
        hat = (h1_ref[rows] - v1_ref[0:1]) * v1_ref[1:2]
        keep = jnp.concatenate([mask_ref[rows]] * spread, axis=1)
        l1[rows] = (
            keep * (v1_ref[2:3] * v1_ref[1:2]) * (ag1[rows] - shift_grad - hat * gain_grad)
        ).astype(low)
        return carry

    lax.fori_loop(0, 8, first_finish, 0)

    share_r = l1[:, my_lanes]
    per_band_r = wide // bands

    def reduce_step(number, carry):
        rows = pl.ds(pl.multiple_of(number * per_band_r, per_band_r), per_band_r)
        r_term[lax.rem(number, 2), number // 2] = dot_nn(xt[rows, :], share_r).astype(low)
        return carry

    lax.fori_loop(0, bands, reduce_step, 0)
    r_pair = to_twin(r_term, r_twin)
    e_back = to_tasks(e_share, e_tasks)
    both_cores(r_pair, r_term, r_twin)
    r_in = along(r_twin, r_land)

    for step, made in enumerate(d_far, start=1):
        made.wait_recv()
        block = l2c.at[lax.rem(at.chip + at.chips - step, at.chips) * 2 + at.core]
        d_near.append(post.push(block, block, at.twin))

    loaded("wr")
    for made in gate_in:
        made.wait_recv()

    def input_step(number, carry):
        lanes = pl.ds(pl.multiple_of(number * piece, piece), piece)
        gates = jnp.concatenate([gate_band[a, number] for a in range(tasks)], axis=0).astype(f32)
        ig_out[:, lanes] = (dot_nt(l1[...], wr[lanes, :]) + gates).astype(low)
        return carry

    lax.fori_loop(0, bands, input_step, 0)
    write(ig_out, ig_hbm)
    for source, target in ((tw_out, tw_hbm), (s3_out, s3_hbm), (s2_out, s2_hbm), (s1_out, s1_hbm)):
        write(source, target)
    for made in d_near:
        made.wait_recv()
    d_sum[...] = jnp.zeros_like(d_sum)

    def dilated_step(number, carry):
        left = jnp.concatenate([act_ref[number + row_tap] for row_tap in range(3)], axis=0)
        right = l2c[number].astype(f32)
        for col_tap in range(3):
            moved = shift_pixels(right, -CONV_DILATION * (col_tap - 1), cols).astype(low)
            d_sum[col_tap] += dot_nn(left, moved)
        return carry

    lax.fori_loop(0, bands, dilated_step, 0)
    part = d_share.shape[1]
    for row_tap in range(3):
        for col_tap in range(3):
            d_share[3 * row_tap + col_tap] = d_sum[
                col_tap, row_tap * part : (row_tap + 1) * part
            ].astype(low)
    d_back = to_tasks(d_share, d_tasks)
    r_share[...] = settle(r_in, r_term, r_twin, r_land)
    r_back = to_tasks(r_share, r_tasks)
    for made in [p_near] + p_passed:
        made.wait_recv()
    pg_out[...] = p_all[...]
    write(pg_out, pg_hbm)
    for made in e_back:
        made.wait_recv()
    broad = wide // tasks
    for a in range(tasks):
        eg_out[:, a * broad : (a + 1) * broad] = e_tasks[a].astype(f32)
    write(eg_out, eg_hbm)
    for made in d_back:
        made.wait_recv()
    for a in range(tasks):
        dg_out[:, :, a * narrow : (a + 1) * narrow] = d_tasks[a].astype(f32)
    write(dg_out, dg_hbm)
    for made in r_back:
        made.wait_recv()
    for a in range(tasks):
        rg_out[:, a * narrow : (a + 1) * narrow] = r_tasks[a].astype(f32)
    write(rg_out, rg_hbm)
    post.close()

    @pl.when(has_above)
    def _():
        up.wait_send()

    @pl.when(has_below)
    def _():
        down.wait_send()


def head_phase(
    at,
    post,
    plan,
    rate_loads,
    sh_ref,
    widths_ref,
    gain_ref,
    shift_ref,
    cot_ref,
    bw_ref,
    pw_ref,
    head_out,
    xg_out,
    grads_out,
    proj_share,
    both_sums_out,
    proj_sums_out,
    rate,
    turned,
    extra,
    term,
    twin_land,
    right_land,
    left_land,
    pre,
    joined,
    upstream,
    cot,
    out_rows,
    masks,
    projected,
    proj_up,
    proj_low,
    pixel_sum,
    st_both,
    st_both_sum,
    st_both_land,
    st_proj,
    st_proj_sum,
    st_proj_land,
    st_pback,
    st_pback_land,
    st_back,
    st_back_land,
    st_rim_sum,
    st_rim,
    st_rim_land,
    both_all,
    moved,
    grads,
    back,
    sg,
    proj_term,
    p_twin,
    p_land,
):
    tasks, bands, cols, pixels, width, taps, extras = plan
    low, f32 = jnp.bfloat16, jnp.float32
    send_sem, recv_sem = post.send_sem, post.recv_sem
    chips, chip, core, band = at.chips, at.chip, at.core, at.band
    last, half = chips - 1, chips // 2
    group = 2 * pixels
    band_rows = pixels // cols
    spread = width // LANE
    number_of = {tap[:3]: number for number, tap in enumerate(taps)}
    moved_levels = sorted({entry[0] for entry in extras})
    late = sorted({entry[2] for entry in extras})
    slots = moved_levels + [branch for branch in range(4) if branch not in moved_levels]
    side = chip // half
    is_end = (chip == 0) | (chip == last)
    next_chip = lax.rem(chip + 1, chips)
    prev_chip = lax.rem(chip + last, chips)
    own = side * (half - 1)

    def reserve(count):
        first = post.used
        post.used += count
        return first

    def hop(source, landing, device_chip, number):
        return pltpu.make_async_remote_copy(
            source,
            landing,
            send_sem.at[number],
            recv_sem.at[number],
            device_id={"space": device_chip * 2 + core},
            device_id_type=MESH_ID,
        )

    def to_twin(source, landing, number):
        return pltpu.make_async_remote_copy(
            source,
            landing,
            send_sem.at[number],
            recv_sem.at[number],
            device_id=at.twin,
            device_id_type=MESH_ID,
        )

    first_cot = reserve(half)

    def send_cot(number):
        return hop(cot_ref, cot.at[number], side * last, first_cot + number)

    for load in rate_loads:
        load.wait()
    cot[pl.ds(own, 1)] = cot_ref[...][None]

    @pl.when(jnp.logical_not(is_end))
    def _():
        send_cot(chip - side * half).start()

    def rows_of(ref, number):
        return jnp.concatenate([ref[2 * number], ref[2 * number + 1]], axis=0)

    def right_of(level, col_tap):
        return (col_tap - 1) * level * RATE

    def forward_taps(source, level, row_tap):
        total = None
        for col_tap in range(3):
            number = number_of.get((level, row_tap, col_tap))
            if number is None:
                continue
            part = shift_pixels(
                dot_nn(source, rate[number]), right_of(level, col_tap), cols
            )
            total = part if total is None else total + part
        return total

    extra[...] = jnp.zeros_like(extra)
    for level, target, source, row_tap in extras:
        extra[moved_levels.index(level), target // last] += forward_taps(
            rows_of(sh_ref, source), level, row_tap
        )

    first_twin = reserve(4 * chips)

    def twin_term(number, branch):
        return to_twin(
            term.at[number, 1 - core, branch],
            twin_land.at[number, branch],
            first_twin + 4 * number + branch,
        )

    def forward_group(step, carry):
        number = lax.rem(step + half * (1 - side), chips)
        at_rim = jnp.where(lax.rem(number, last) == 0, 1.0, 0.0)
        source = rows_of(sh_ref, number)
        for branch in slots:
            if branch == 0:
                value = dot_nn(source, bw_ref[:, :width])
            else:
                value = forward_taps(source, branch, 1)
                if branch in moved_levels:
                    value = value + at_rim * extra[moved_levels.index(branch), number // last]
            value = value.astype(low)
            term[number, 0, branch] = value[:pixels]
            term[number, 1, branch] = value[pixels:]
            twin_term(number, branch).start()
        return carry

    first_right, first_left = reserve(8 * half), reserve(8 * half)
    portion = pixels // 2

    def rows_at(part):
        return pl.ds(part * portion, portion)

    def go_right(number, branch, part):
        return hop(
            twin_land.at[half + number, branch, rows_at(part)],
            right_land.at[number, branch, rows_at(part)],
            next_chip,
            first_right + 8 * number + 2 * branch + part,
        )

    def go_left(number, branch, part):
        return hop(
            twin_land.at[number, branch, rows_at(part)],
            left_land.at[number, branch, rows_at(part)],
            prev_chip,
            first_left + 8 * number + 2 * branch + part,
        )

    def both_cores(number, branch):
        twin_term(number, branch).wait_recv()
        return term[number, core, branch].astype(f32) + twin_land[number, branch].astype(f32)

    def start_off(number, copy_of):
        for branch in slots:
            twin_land[number, branch] = both_cores(number, branch).astype(low)
            for part in range(2):
                copy_of(branch, part).start()

    for number in range(half):
        lax.fori_loop(number, number + 1, forward_group, 0)

        @pl.when(chip == 0)
        def _():
            start_off(half + number, functools.partial(go_right, number))

        @pl.when(chip == last)
        def _():
            start_off(number, functools.partial(go_left, number))

    lax.fori_loop(half, chips, forward_group, 0)

    def pass_on(number, branch, part, copy, landing):
        if part == 0:
            twin_term(number, branch).wait_recv()
        copy.wait_recv()
        rows = rows_at(part)
        twin_land[number, branch, rows] = (
            term[number, core, branch, rows].astype(f32)
            + twin_land[number, branch, rows].astype(f32)
            + landing[rows].astype(f32)
        ).astype(low)
        copy.start()

    def pass_right(number, branch, part):
        landing = right_land.at[number, branch]
        pass_on(half + number, branch, part, go_right(number, branch, part), landing)

    def pass_left(number, branch, part):
        landing = left_land.at[number, branch]
        pass_on(number, branch, part, go_left(number, branch, part), landing)

    order = [
        (number, branch, part) for number in range(half) for branch in slots for part in range(2)
    ]

    def pass_both(near, far):
        for step in range(len(order) + FAR_LAG):
            if step < len(order):
                near(*order[step])
            if step >= FAR_LAG:
                far(*order[step - FAR_LAG])

    @pl.when(jnp.logical_not(is_end) & (side == 0))
    def _():
        pass_both(pass_right, pass_left)

    @pl.when(jnp.logical_not(is_end) & (side == 1))
    def _():
        pass_both(pass_left, pass_right)

    pixel_sum[...] = jnp.zeros_like(pixel_sum)

    def turn_group(number, carry):
        source = rows_of(sh_ref, number)
        turned[:, pl.ds(pl.multiple_of(number * group, group), group)] = source.T
        pixel_sum[0:1] += jnp.sum(source.astype(f32), axis=0, keepdims=True)
        return carry

    lax.fori_loop(0, chips, turn_group, 0)
    inv_count = jnp.concatenate([1.0 / count_pixels(widths_ref)] * spread, axis=1)

    def put_rows(target, number, value):
        for part in range(spread):
            target[pl.ds(number * spread + part, 1), :] = value[:, part * LANE : (part + 1) * LANE]

    def add_rows(target, number, value):
        for part in range(spread):
            target[pl.ds(number * spread + part, 1), :] += value[
                :, part * LANE : (part + 1) * LANE
            ]

    def get_rows(target, number):
        return jnp.concatenate(
            [target[pl.ds(number * spread + part, 1), :] for part in range(spread)], axis=1
        )

    def column_sum(value):
        return jnp.sum(value, axis=0, keepdims=True)

    def mask_of(number):
        return jnp.concatenate([masks[number]] * spread, axis=1)

    for target in (st_both, st_proj, st_pback, st_back, st_rim):
        target[...] = jnp.zeros_like(target)
    for number in range(half):
        masks[number] = row_mask(
            widths_ref, (2 * (side * half + number) + core) * band_rows, band_rows, cols
        )

    def settle(copy_of, landing):
        def step_of(step, carry):
            number, branch = step // 4, lax.rem(step, 4)
            total = both_cores(side * half + number, branch)
            for part in range(2):
                copy_of(number, branch, part).wait_recv()
            value = total + landing[number, branch].astype(f32)
            pre[number, branch] = value
            kept = value * mask_of(number)
            add_rows(st_both, branch, column_sum(kept))
            add_rows(st_both, 4 + branch, column_sum(kept * value))
            return carry

        lax.fori_loop(0, 4 * half, step_of, 0)

    @pl.when(chip == 0)
    def _():
        settle(go_left, left_land)

    @pl.when(chip == last)
    def _():
        settle(go_right, right_land)

    sums_now = pixel_sum[0:1]
    high = sums_now.astype(low)
    rest = sums_now - high.astype(f32)
    middle = rest.astype(low)
    tail = (rest - middle.astype(f32)).astype(low)
    pieces = jnp.concatenate(
        [high.astype(f32), middle.astype(f32), tail.astype(f32), jnp.zeros((13, width), f32)],
        axis=0,
    ).astype(low)
    put_rows(st_both, 8, column_sum(dot_nn(pieces, bw_ref[:, width:])))
    st_both_sum[...] = at.sum_over(post, "space", st_both, st_both_land)
    pooled = get_rows(st_both_sum, 8) * inv_count

    def lanes_of(number):
        return pl.ds(pl.multiple_of(number * width, width), width)

    def scale_of(target, first, second):
        mean_value = get_rows(target, first) * inv_count
        variance = get_rows(target, second) * inv_count - mean_value * mean_value
        return mean_value, lax.rsqrt(variance + NORM_EPS)

    def at_ends(body, count):
        @pl.when(is_end)
        def _():
            lax.fori_loop(0, count, body, 0)

    pool_lanes = slice(4 * width, 5 * width)

    def pool_step(number, carry):
        joined[number, 4] = (
            gelu_of(pooled).astype(low).astype(f32) * mask_of(number)
        ).astype(low)
        projected[number] = dot_nn(joined[number, 4], pw_ref[pool_lanes, :])
        return carry

    at_ends(pool_step, half)

    def activate(step, carry):
        number, branch = step // 4, lax.rem(step, 4)
        mean_value, inv_std = scale_of(st_both_sum, branch, 4 + branch)
        hat = (pre[number, branch] - mean_value) * inv_std
        pre[number, branch] = hat
        normed = gain_ref[:, lanes_of(branch)] * hat + shift_ref[:, lanes_of(branch)]
        active, slope = gelu_both(normed)
        keep = mask_of(number)
        active = (active * keep).astype(low)
        upstream[number, branch] = slope * keep
        joined[number, branch] = active
        projected[number] += dot_nn(active, pw_ref[lanes_of(branch), :])
        return carry

    at_ends(activate, 4 * half)

    def project_sums(number, carry):
        value = projected[number]
        kept = value * mask_of(number)
        add_rows(st_proj, 0, column_sum(kept))
        add_rows(st_proj, 1, column_sum(kept * value))
        return carry

    at_ends(project_sums, half)
    st_proj_sum[...] = at.sum_over(post, "space", st_proj, st_proj_land)
    proj_mean, proj_inv = scale_of(st_proj_sum, 0, 1)
    gain_proj = gain_ref[:, pool_lanes]

    def proj_back(number, carry):
        hat = (projected[number] - proj_mean) * proj_inv
        projected[number] = hat
        normed = gain_proj * hat + shift_ref[:, pool_lanes]
        keep = mask_of(number)
        active, slope = gelu_both(normed)
        up = slope * cot[number].astype(f32) * keep
        proj_up[number] = up
        add_rows(st_pback, 0, column_sum(up))
        add_rows(st_pback, 1, column_sum(up * hat))
        out_rows[number] = (active * keep).astype(low)
        return carry

    @pl.when(is_end)
    def _():
        for number in range(half):

            @pl.when(own != number)
            def _():
                send_cot(number).wait_recv()

    at_ends(proj_back, half)
    proj_sums_out[...] = at.sum_over(post, "space", st_pback, st_pback_land)
    shift_proj, gain_grad_proj = get_rows(proj_sums_out, 0), get_rows(proj_sums_out, 1)

    def proj_finish(number, carry):
        keep = mask_of(number)
        proj_low[number] = (
            keep
            * (gain_proj * proj_inv)
            * (
                proj_up[number]
                - shift_proj * inv_count
                - projected[number] * (gain_grad_proj * inv_count)
            )
        ).astype(low)
        return carry

    def pool_back(number, carry):
        joined_grad = dot_nt(proj_low[number], pw_ref[pool_lanes, :])
        add_rows(st_back, 8, column_sum(joined_grad * mask_of(number)))
        return carry

    def back_step(branch):
        def step_of(number, carry):
            joined_grad = dot_nt(proj_low[number], pw_ref[lanes_of(branch), :])
            hat = pre[number, branch]
            up = upstream[number, branch] * joined_grad
            upstream[number, branch] = up
            shift_sum, gain_sum = column_sum(up), column_sum(up * hat)
            add_rows(st_back, branch, shift_sum)
            add_rows(st_back, 4 + branch, gain_sum)
            if branch == slots[0]:
                add_rows(st_rim, 0, shift_sum)
                add_rows(st_rim, 1, gain_sum)
            return carry

        return step_of

    at_ends(proj_finish, half)
    at_ends(back_step(slots[0]), half)
    begun_rim = at.sum_begin(post, "space", st_rim, st_rim_land)
    at_ends(pool_back, half)
    for branch in slots[1:]:
        at_ends(back_step(branch), half)
    begun_back = at.sum_begin(post, "space", st_back, st_back_land)
    st_rim_sum[...] = at.sum_end(begun_rim)

    order = [(number, branch) for branch in moved_levels for number in range(half)]
    order += [
        (number, branch)
        for number in range(half)
        for branch in slots
        if branch not in moved_levels
    ]
    first_right_all, first_left_all = reserve(8 * half), reserve(8 * half)
    first_twin_all, first_out = reserve(8 * chips), reserve(half)

    def block_of(number, branch, part):
        return both_all.at[number * 2 + core, branch, rows_at(part)]

    def along_right(number, branch, part):
        block = block_of(number, branch, part)
        return hop(block, block, next_chip, first_right_all + 8 * number + 2 * branch + part)

    def along_left(number, branch, part):
        block = block_of(half + number, branch, part)
        return hop(block, block, prev_chip, first_left_all + 8 * number + 2 * branch + part)

    def hand_over(number, branch, part):
        block = block_of(number, branch, part)
        return to_twin(block, block, first_twin_all + 8 * number + 2 * branch + part)

    def make_both(number, branch):
        _, inv_std = scale_of(st_both_sum, branch, 4 + branch)
        if branch == slots[0]:
            sums = get_rows(st_rim_sum, 0), get_rows(st_rim_sum, 1)
        else:
            sums = get_rows(both_sums_out, branch), get_rows(both_sums_out, 4 + branch)
        shift_grad, gain_grad = sums[0] * inv_count, sums[1] * inv_count
        both_all[2 * (side * half + number) + core, branch] = (
            mask_of(number)
            * (gain_ref[:, lanes_of(branch)] * inv_std)
            * (upstream[number, branch] - shift_grad - pre[number, branch] * gain_grad)
        ).astype(low)

    parts = [(number, branch, part) for number, branch in order for part in range(2)]
    by_halves = [entry for entry in order[half:] if entry[0] == half - 1]
    parts = parts[: -2 * len(by_halves)]
    parts += [entry + (part,) for part in range(2) for entry in by_halves]

    def send_out(number):
        return hop(out_rows.at[number], head_out, side * half + number, first_out + number)

    def send_parts(some):
        made = set()
        for number, branch, part in some:
            if (number, branch) not in made:
                make_both(number, branch)
                made.add((number, branch))

            @pl.when(chip == 0)
            def _():
                along_right(number, branch, part).start()
                hand_over(number, branch, part).start()

            @pl.when(chip == last)
            def _():
                along_left(number, branch, 1 - part).start()
                hand_over(half + number, branch, 1 - part).start()

    @pl.when(is_end)
    def _():
        send_parts([entry for entry in parts if entry[1] == slots[0]])

    both_sums_out[...] = at.sum_end(begun_back)
    pool_grad = (gelu_slope(pooled) * get_rows(both_sums_out, 8)).astype(low)

    @pl.when(is_end)
    def _():
        send_parts([entry for entry in parts if entry[1] != slots[0]])
        for number in range(half):

            @pl.when(own != number)
            def _():
                send_out(number).start()

        head_out[...] = out_rows[own]

    def proj_step(branch, carry):
        total = dot_nn(joined[0, branch].T, proj_low[0])
        for number in range(1, half):
            total = total + dot_nn(joined[number, branch].T, proj_low[number])
        proj_term[lanes_of(branch), :] = total.astype(low)
        return carry

    at_ends(proj_step, 5)

    rows_p = proj_share.shape[0]

    def proj_rows(number):
        return pl.ds(pl.multiple_of(number * rows_p, rows_p), rows_p)

    first_pair, first_p = reserve(chips), reserve(2 * chips)

    def p_pair(number):
        return to_twin(
            proj_term.at[proj_rows(2 * number + 1 - core)], p_twin.at[number], first_pair + number
        )

    def p_hop(end, number):
        return hop(p_twin.at[number], p_land.at[end], number, first_p + end * chips + number)

    @pl.when(is_end)
    def _():
        for number in range(chips):
            p_pair(number).start()

    def send_projection():
        for number in range(chips):
            p_pair(number).wait_recv()
            both = proj_term[proj_rows(2 * number + core)].astype(f32)
            p_twin[number] = (both + p_twin[number].astype(f32)).astype(low)

            @pl.when(chip != number)
            def _():
                p_hop(side, number).start()

    grads[...] = jnp.zeros_like(grads)
    pool_row = dot_nt(
        jnp.broadcast_to(pool_grad, (16, width)), bw_ref[:, width:]
    )[0:1] * inv_count
    quarter = pixels // tasks
    my_rows = pl.ds(pl.multiple_of(at.task * quarter, quarter), quarter)
    first_task = reserve(chips * len(at.other_tasks))

    def to_task(number, turn):
        other = at.other_tasks[turn]
        theirs = pl.ds(pl.multiple_of(other * quarter, quarter), quarter)
        two = pl.ds(2 * number, 2)
        spot = first_task + number * len(at.other_tasks) + turn
        return pltpu.make_async_remote_copy(
            sg.at[two, theirs],
            xg_out.at[at.task, two],
            send_sem.at[spot],
            recv_sem.at[spot],
            device_id={"task": other},
            device_id_type=MESH_ID,
        )

    def finish_group(number, part=None):
        some = band_rows if part is None else band_rows // 2
        for place in range(2):
            first = (2 * number + place) * band_rows + (0 if part is None else part * some)
            keep = row_mask(widths_ref, first, some, cols)
            keep = jnp.concatenate([keep] * spread, axis=1)
            start = 0 if part is None else part * portion
            rows = slice(start, start + some * cols)
            value = back[number, place * pixels + start : place * pixels + start + some * cols]
            sg[2 * number + place, rows] = (value + keep * pool_row).astype(low)

        def there(task):
            return task >= 0 if part is None else task // (tasks // 2) == part

        for turn, other in enumerate(at.other_tasks):

            @pl.when(there(other))
            def _():
                to_task(number, turn).start()

        @pl.when(there(at.task))
        def _():
            for place in range(2):
                xg_out[at.task, 2 * number + place] = sg[2 * number + place, my_rows]

    def back_part(number, branch, part=None):
        for piece in range(2) if part is None else (part,):
            hand_over(number, branch, piece).wait_recv()
        rows = slice(0, pixels) if part is None else slice(part * portion, (part + 1) * portion)
        count = rows.stop - rows.start
        starts = [(2 * number + place) * pixels + rows.start for place in range(2)]
        columns = jnp.concatenate([turned[:, start : start + count] for start in starts], axis=1)
        image = jnp.concatenate(
            [both_all[2 * number, branch, rows], both_all[2 * number + 1, branch, rows]], axis=0
        )
        if branch == 0:
            total = dot_nt(image, bw_ref[:, :width])
            grads[len(taps)] += dot_nn(columns, image)
        else:
            total = None
            image = image.astype(f32)
            for col_tap in range(3):
                tap = number_of.get((branch, 1, col_tap))
                if tap is None:
                    continue
                moved_now = shift_pixels(image, -right_of(branch, col_tap), cols).astype(low)
                if branch in moved_levels and number in late:
                    moved[moved_levels.index(branch), number // last, col_tap] = moved_now
                now = dot_nt(moved_now, rate[tap])
                total = now if total is None else total + now
                grads[tap] += dot_nn(columns, moved_now)
        for place in range(2):
            target = slice(place * pixels + rows.start, place * pixels + rows.stop)
            share = total[place * count : (place + 1) * count]
            if branch == slots[0]:
                back[number, target] = share
            else:
                back[number, target] += share

    def far_taps():
        for level, target, source, row_tap in extras:
            columns = turned[:, source * group : (source + 1) * group]
            total = back[source]
            for col_tap in range(3):
                tap = number_of.get((level, row_tap, col_tap))
                if tap is None:
                    continue
                part = moved[moved_levels.index(level), target // last, col_tap]
                total = total + dot_nt(part, rate[tap])
                grads[tap] += dot_nn(columns, part)
            back[source] = total

    def take_right(number, branch, part):
        along_right(number, branch, part).wait_recv()

        @pl.when(chip < last)
        def _():
            along_right(number, branch, part).start()

        hand_over(number, branch, part).start()

    def take_left(number, branch, part):
        along_left(number, branch, part).wait_recv()

        @pl.when(chip > 0)
        def _():
            along_left(number, branch, part).start()

        hand_over(half + number, branch, part).start()

    for step in range(len(parts) + FAR_LAG + 1):
        if step < len(parts):
            number, branch, part = parts[step]

            @pl.when(jnp.logical_not(is_end) & (side == 0))
            def _():
                take_right(number, branch, part)

            @pl.when(jnp.logical_not(is_end) & (side == 1))
            def _():
                take_left(number, branch, 1 - part)

        if FAR_LAG <= step < len(parts) + FAR_LAG:
            number, branch, part = parts[step - FAR_LAG]

            @pl.when(side == 0)
            def _():
                take_left(number, branch, 1 - part)

            @pl.when(side == 1)
            def _():
                take_right(number, branch, part)

        if step == len(parts) + SEND_LAG:

            @pl.when(is_end)
            def _():
                send_projection()

        done = step - FAR_LAG - 1
        if done < 0:
            continue
        number, branch, part = parts[done]
        if (number, branch) in by_halves:
            back_part(number, branch, part)
            back_part(half + number, branch, 1 - part)
            if (number, branch) == by_halves[-1]:
                finish_group(number, part)
                finish_group(half + number, 1 - part)
        elif part == 1:
            back_part(number, branch)
            back_part(half + number, branch)
            if (number, branch) == order[half - 1]:
                far_taps()
            if branch == slots[3]:
                finish_group(number)
                finish_group(half + number)

    column = jnp.broadcast_to(pixel_sum[0:1], (8, width)).T[:, 0:1]
    grads_out[len(taps) + 1] = (column * (pool_grad.astype(f32) * inv_count)).astype(low)

    def finish_tap(number, carry):
        grads_out[number] = grads[number].astype(low)
        return carry

    lax.fori_loop(0, len(taps) + 1, finish_tap, 0)
    for end in range(2):

        @pl.when(chip == end * last)
        def _():
            p_land[end] = p_twin[end * last]

        @pl.when(chip != end * last)
        def _():
            p_hop(end, chip).wait_recv()

    proj_share[...] = (p_land[0].astype(f32) + p_land[1].astype(f32)).astype(low)

    def tasks_in(number, carry):
        for turn in range(len(at.other_tasks)):
            to_task(number, turn).wait()
        return carry

    lax.fori_loop(0, chips, tasks_in, 0)

    @pl.when(jnp.logical_not(is_end))
    def _():
        send_out(chip - side * half).wait_recv()
        send_cot(chip - side * half).wait_send()

    post.close()

    def twin_left(number, carry):
        for branch in range(4):
            twin_term(number, branch).wait_send()
            for part in range(2):
                hand_over(number, branch, part).wait_send()
        return carry

    lax.fori_loop(0, chips, twin_left, 0)

    def line_left(number, carry):
        for branch in range(4):
            for part in range(2):

                @pl.when(chip < last)
                def _():
                    go_right(number, branch, part).wait_send()
                    along_right(number, branch, part).wait_send()

                @pl.when(chip > 0)
                def _():
                    go_left(number, branch, part).wait_send()
                    along_left(number, branch, part).wait_send()

        return carry

    lax.fori_loop(0, half, line_left, 0)

    @pl.when(is_end)
    def _():
        for number in range(half):

            @pl.when(own != number)
            def _():
                send_out(number).wait_send()

        for number in range(chips):
            p_pair(number).wait_send()

            @pl.when(chip != number)
            def _():
                p_hop(side, number).wait_send()


def trunk_phase(
    at,
    post,
    sizes,
    when_loaded,
    norm_loads,
    x_hbm,
    widths_ref,
    gain_ref,
    shift_ref,
    wr_hbm,
    wd_hbm,
    we_hbm,
    sh_out,
    act,
    h1,
    h2,
    a2,
    h3q,
    v1,
    v2,
    v3,
    stats_out,
    x,
    wr,
    wd,
    we,
    rim,
    turned,
    h3,
    blocks,
    mask_own,
    st1,
    st1_land,
    st2,
    st2_land,
    st3,
    st3_land,
    local_sem,
):
    tasks, bands, cols, quarter, mid, wide, piece = sizes
    low, f32 = jnp.bfloat16, jnp.float32
    task, band = at.task, at.band
    my_rows = pl.ds(pl.multiple_of(task * quarter, quarter), quarter)
    loads = [
        pltpu.make_async_copy(source, target, local_sem.at[number])
        for number, (source, target) in enumerate(
            ((x_hbm, x), (wr_hbm, wr), (wd_hbm, wd), (we_hbm, we))
        )
    ]
    for load in loads[:2]:
        load.start()
    at.greet()
    pixels = x.shape[0]
    band_rows = pixels // cols
    mask = row_mask(widths_ref, band * band_rows, band_rows, cols)
    count = count_pixels(widths_ref)
    spread = mid // LANE

    def across(value, lanes):
        return jnp.concatenate([value] * (lanes // LANE), axis=1)

    def put_sums(target, value, keep):
        kept = value * keep
        first = jnp.sum(kept, axis=0, keepdims=True)
        second = jnp.sum(kept * value, axis=0, keepdims=True)
        for number in range(spread):
            lanes = slice(number * LANE, (number + 1) * LANE)
            target[number : number + 1] = first[:, lanes]
            target[spread + number : spread + number + 1] = second[:, lanes]

    def get_sums(total):
        return [
            jnp.concatenate([total[base + k : base + k + 1] for k in range(spread)], axis=1)
            for base in (0, spread)
        ]

    def put_norm(vectors, lanes, first, second, start):
        width = first.shape[1]
        inv = across(1.0 / count, width)
        mean_value = first * inv
        variance = second * inv - mean_value * mean_value
        vectors[0:1, lanes] = mean_value
        vectors[1:2, lanes] = lax.rsqrt(variance + NORM_EPS)
        vectors[2:3, lanes] = gain_ref[:, start : start + width]
        vectors[3:4, lanes] = shift_ref[:, start : start + width]
        stats_out[0:1, start : start + width] = mean_value
        stats_out[1:2, start : start + width] = variance * across(count / (count - 1.0), width)

    def activate(hidden, vectors, keep):
        normed = vectors[2:3] * ((hidden - vectors[0:1]) * vectors[1:2]) + vectors[3:4]
        return (gelu_of(normed) * keep).astype(low)

    mask_mid = across(mask, mid)
    for load in loads[:2]:
        load.wait()
    for load in loads[2:]:
        load.start()
    h1[...] = dot_nn(x[...], wr[...])
    at.meet()
    put_sums(st1, h1[...], mask_mid)
    begun = at.sum_begin(post, "space", st1, st1_land)
    for load in norm_loads:
        load.wait()
    first, second = get_sums(at.sum_end(begun))
    when_loaded()
    put_norm(v1, slice(0, mid), first, second, 0)
    rim[1] = activate(h1[...], v1, mask_mid)

    has_above, has_below = band > 0, band < bands - 1
    up = post.copy(rim.at[1], rim.at[2], {"space": lax.rem(band + bands - 1, bands)})
    down = post.copy(rim.at[1], rim.at[0], {"space": lax.rem(band + 1, bands)})

    @pl.when(has_above)
    def _():
        up.start()

    @pl.when(has_below)
    def _():
        down.start()

    @pl.when(jnp.logical_not(has_above))
    def _():
        rim[0] = jnp.zeros(rim.shape[1:], low)

    @pl.when(jnp.logical_not(has_below))
    def _():
        rim[2] = jnp.zeros(rim.shape[1:], low)

    loads[2].wait()
    halves = [slice(start, start + piece) for start in range(0, mid, piece)]

    def tap_sum(row_taps, lanes):
        total = None
        for col_tap in range(3):
            part = None
            for row_tap in row_taps:
                term = dot_nn(rim[row_tap], wd[3 * row_tap + col_tap, :, lanes])
                part = term if part is None else part + term
            part = shift_pixels(part, CONV_DILATION * (col_tap - 1), cols)
            total = part if total is None else total + part
        return total

    for lanes in halves:
        h2[:, lanes] = tap_sum((1,), lanes)

    turned[...] = rim[1].T

    @pl.when(has_below)
    def _():
        up.wait_recv()

    @pl.when(has_above)
    def _():
        down.wait_recv()

    for lanes in halves:
        h2[:, lanes] += tap_sum((0, 2), lanes)

    put_sums(st2, h2[...], mask_mid)
    first, second = get_sums(at.sum_over(post, "space", st2, st2_land))
    put_norm(v2, slice(0, mid), first, second, mid)
    a2[...] = activate(h2[...], v2, mask_mid)

    loads[3].wait()
    mask_piece = across(mask, piece)
    per_row = st3.shape[1] // piece
    half = st3.shape[0] // 2

    def expand_step(number, carry):
        lanes = pl.ds(pl.multiple_of(number * piece, piece), piece)
        value = dot_nn(a2[...], we[:, lanes])
        h3[:, lanes] = value
        kept = value * mask_piece
        row = number // per_row
        spot = pl.ds(pl.multiple_of(lax.rem(number, per_row) * piece, piece), piece)
        st3[pl.ds(row, 1), spot] = jnp.sum(kept, axis=0, keepdims=True)
        st3[pl.ds(half + row, 1), spot] = jnp.sum(kept * value, axis=0, keepdims=True)
        return carry

    lax.fori_loop(0, bands, expand_step, 0)
    begun = at.sum_begin(post, "space", st3, st3_land)
    h3q[...] = h3[my_rows]
    total = at.sum_end(begun)
    lanes_in = st3.shape[1]
    for row in range(half):
        put_norm(
            v3,
            slice(row * lanes_in, (row + 1) * lanes_in),
            total[row : row + 1],
            total[half + row : half + row + 1],
            2 * mid + row * lanes_in,
        )

    mask_own[...] = mask
    mask_quarter = across(mask_own[my_rows], piece)

    def shared_of(number):
        lanes = pl.ds(pl.multiple_of(number * piece, piece), piece)
        hat = (h3q[:, lanes] - v3[0:1, lanes]) * v3[1:2, lanes]
        before = v3[2:3, lanes] * hat + v3[3:4, lanes] + x[my_rows, lanes].astype(f32)
        return (gelu_of(before) * mask_quarter).astype(low)

    slices_in = []
    for other in at.other_bands:
        blocks[other] = shared_of(other)
        slices_in.append(
            post.push(blocks.at[other], sh_out.at[band, my_rows], {"space": other})
        )
    sh_out[band, my_rows] = shared_of(band)

    part = mid // bands

    def part_of(number):
        return turned.at[pl.ds(pl.multiple_of(number * part, part), part)]

    act[0] = jnp.zeros(act.shape[1:], low)
    act[bands + 1] = jnp.zeros(act.shape[1:], low)
    act[band + 1] = part_of(band)[...]
    parts_in = [
        post.push(part_of(other), act.at[band + 1], {"space": other}) for other in at.other_bands
    ]

    def to_tasks(number):
        block = sh_out.at[number, my_rows]
        return [post.push(block, block, {"task": other}) for other in at.other_tasks]

    quarters_in = to_tasks(band)
    for step, made in enumerate(slices_in, start=1):
        made.wait_recv()
        quarters_in += to_tasks(lax.rem(band + bands - step, bands))
    for made in quarters_in + parts_in:
        made.wait_recv()
    post.close()

    @pl.when(has_above)
    def _():
        up.wait_send()

    @pl.when(has_below)
    def _():
        down.wait_send()


class Held:
    def __init__(self, shape, dtype, passing=False):
        self.memory = pltpu.VMEM(shape, dtype)
        self.passing = passing


def with_phase(entries, refs, body):
    def run(*passing):
        passing, kept = list(passing), list(refs)
        body([(passing if entry.passing else kept).pop(0) for entry in entries])

    pl.run_scoped(run, *[entry.memory for entry in entries if entry.passing])


def whole_kernel(sizes, plan, phases, counts, *refs):
    refs = list(refs)

    def take(count):
        taken = refs[:count]
        del refs[:count]
        return taken

    x_hbm, widths, gain_hbm, shift_hbm, wr_hbm, wd_hbm, we_hbm = take(7)
    head_hbm_in = take(5)
    (rate_hbm,) = take(1)
    stats_hbm, head_hbm, grads_hbm, both_hbm, proj_hbm = take(5)
    back_hbm = take(counts[2])
    trunk_outs, head_outs = take(counts[0]), take(counts[1])
    gain, shift, *head_in = take(7)
    head_gain, head_shift, cot, bw, pw = head_in
    (shared,) = take(1)
    kept = [take(sum(not entry.passing for entry in entries)) for entries in phases]
    send_sem, recv_sem, local_sem, rate_sem, out_sem, in_sem = refs
    tasks, bands, width, taps = sizes[0], sizes[1], plan[4], plan[5]
    at = Place(tasks, bands)
    post = Post(send_sem, recv_sem)
    writes = []

    def write(source, target):
        copy = pltpu.make_async_copy(source, target, out_sem.at[len(writes)])
        copy.start()
        writes.append(copy)

    rate = kept[1][0]
    rate_loads = []
    for number, (level, row_tap, col_tap, _, _) in enumerate(taps):
        start = (9 * (level - 1) + 3 * row_tap + col_tap) * width
        rate_loads.append(
            pltpu.make_async_copy(
                rate_hbm.at[:, start : start + width], rate.at[number], rate_sem.at[number]
            )
        )

    norm_loads = [
        pltpu.make_async_copy(source, target, in_sem.at[number])
        for number, (source, target) in enumerate(((gain_hbm, gain), (shift_hbm, shift)))
    ]
    for load in norm_loads:
        load.start()
    rate_loads += [
        pltpu.make_async_copy(source, target, in_sem.at[2 + number])
        for number, (source, target) in enumerate(zip(head_hbm_in, head_in))
    ]

    def when_loaded():
        for load in rate_loads:
            load.start()

    def run_trunk(scratch):
        trunk_phase(
            at,
            post,
            sizes,
            when_loaded,
            norm_loads,
            x_hbm,
            widths,
            gain,
            shift,
            wr_hbm,
            wd_hbm,
            we_hbm,
            shared,
            *trunk_outs,
            *scratch,
            local_sem,
        )

    def run_head(scratch):
        head_phase(
            at,
            post,
            plan,
            rate_loads,
            shared,
            widths,
            head_gain,
            head_shift,
            cot,
            bw,
            pw,
            *head_outs,
            *scratch,
        )

    with_phase(phases[0], kept[0], run_trunk)
    act, h1, h2, a2, h3q, v1, v2, v3, stats = trunk_outs
    write(stats, stats_hbm)
    with_phase(phases[1], kept[1], run_head)
    head_out, xg, grads_out, proj_share, both_sums, proj_sums = head_outs
    for source, target in (
        (head_out, head_hbm),
        (grads_out, grads_hbm),
        (both_sums, both_hbm),
        (proj_sums, proj_hbm),
    ):
        write(source, target)

    def run_back(scratch):
        back_phase(
            at,
            post,
            sizes,
            local_sem,
            xg,
            h3q,
            v3,
            h2,
            v2,
            h1,
            v1,
            act,
            a2,
            proj_share,
            x_hbm,
            widths,
            we_hbm,
            wd_hbm,
            wr_hbm,
            write,
            *back_hbm,
            *scratch,
        )
        while len(writes) > before:
            writes.pop().wait()

    before = len(writes)
    with_phase(phases[2], kept[2], run_back)
    for copy in writes:
        copy.wait()


def whole(tasks, bands, cols, rows, collective, x, widths, gain, shift, wr, wd, we, *head_in):
    low, f32 = jnp.bfloat16, jnp.float32
    head_gain, head_shift, cot, bw, pw, rate = head_in
    pixels, wide = x.shape
    mid = wr.shape[1]
    quarter, piece = pixels // tasks, wide // bands
    width = pw.shape[1]
    chips = bands // 2
    group_rows = rows // chips
    taps = live_taps(rows, cols)
    extras = []
    for level in (1, 2, 3):
        for row_tap in (0, 2):
            if (level, row_tap, 1) in [tap[:3] for tap in taps]:
                away = (row_tap - 1) * level * RATE // group_rows
                extras += [
                    (level, target, target + away, row_tap)
                    for target in range(chips)
                    if 0 <= target + away < chips
                ]
    levels = max(len({entry[0] for entry in extras}), 1)
    anywhere = pl.BlockSpec(memory_space=pl.ANY)
    shape = jax.ShapeDtypeStruct
    block = (pixels, width)
    both_rows, proj_rows = -(-9 * width // LANE // 8) * 8, 8

    part, narrow, broad = mid // bands, mid // tasks, wide // tasks
    half = chips // 2
    pool_rows = pw.shape[0] // bands
    mid_rows, stat_wide = 2 * mid // LANE, wide // 4

    def kept(dims, dtype=low):
        return Held(tuple(dims), dtype)

    def passing(dims, dtype=low):
        return Held(tuple(dims), dtype, True)

    def over_bands(count, lanes=LANE):
        return [kept((count, lanes), f32), kept((bands, count, lanes), f32)]

    def over_all(count, lanes=LANE):
        return [kept((count, lanes), f32), kept((tasks, count, lanes), f32)] + over_bands(
            count, lanes
        )

    def terms(*dims):
        return [
            kept((2, chips) + dims),
            kept((chips,) + dims),
            kept((chips,) + dims),
            kept(dims),
            kept((tasks,) + dims),
        ]

    trunk_scratch = (
        [
            passing(x.shape),
            passing(wr.shape),
            passing(wd.shape),
            passing(we.shape),
            kept((3, pixels, mid)),
            kept((mid, pixels)),
            passing((pixels, wide), f32),
            kept((bands, quarter, piece)),
            passing((pixels, LANE), f32),
        ]
        + over_bands(mid_rows)
        + over_bands(mid_rows)
        + over_bands(8, stat_wide)
    )
    head_scratch = (
        [
            kept((len(taps), piece, width)),
            passing((piece, bands * pixels)),
            passing((levels, 2, 2 * pixels, width), f32),
            passing((chips, 2, 4) + block),
            kept((chips, 4) + block),
            kept((half, 4) + block),
            kept((half, 4) + block),
            passing((half, 4) + block, f32),
            passing((half, 5) + block),
            passing((half, 4) + block, f32),
            kept((half,) + block),
            passing((half,) + block),
            passing((half, pixels, LANE), f32),
            passing((half,) + block, f32),
            passing((half,) + block, f32),
            passing((half,) + block),
            passing((8, piece), f32),
            kept((both_rows, LANE), f32),
        ]
        + over_bands(both_rows)
        + [kept((proj_rows, LANE), f32)]
        + over_bands(proj_rows)
        + over_bands(proj_rows)
        + over_bands(both_rows)
        + [kept((proj_rows, LANE), f32)]
        + over_bands(proj_rows)
        + [
            kept((bands, 4) + block),
            passing((levels, 2, 3, 2 * pixels, width)),
            passing((len(taps) + 1, piece, width), f32),
            passing((chips, 2 * pixels, width), f32),
            passing((bands, pixels, piece)),
            passing(pw.shape),
            kept((chips, pool_rows, width)),
            kept((2, pool_rows, width)),
        ]
    )
    back_outs = (
        shape((8, LANE), f32),
        shape((pixels, wide), low),
        shape((piece, mid), f32),
        shape((9, part, mid), f32),
        shape((part, wide), f32),
        shape((8, stat_wide), f32),
        shape((mid_rows, LANE), f32),
        shape((mid_rows, LANE), f32),
        shape((bands, pool_rows, width), low),
    )
    back_scratch = (
        [kept(out.shape, out.dtype) for out in back_outs]
        + [
            passing(we.shape),
            passing(wd.shape),
            passing(wr.shape),
            passing(x.shape),
            passing((pixels, LANE), f32),
        ]
        + over_all(16)
        + [
            kept((bands, quarter, piece)),
            kept((bands, quarter, piece)),
            passing((bands, quarter, piece), f32),
            passing((bands, quarter, piece), f32),
            kept((bands, quarter, piece)),
            kept((tasks, bands, quarter, piece)),
        ]
        + over_all(8, stat_wide)
        + [
            kept((bands, quarter, piece)),
            kept((tasks, bands // tasks, quarter, piece)),
        ]
        + over_all(mid_rows)
        + [
            kept((pixels, mid)),
            kept((2, pixels, mid)),
            passing((pixels, mid), f32),
        ]
        + over_bands(mid_rows)
        + [
            passing((pixels, mid)),
            passing((wide, pixels)),
            passing((mid, pixels)),
        ]
        + terms(part, broad)
        + [
            kept((bands, pixels, narrow)),
            passing((3, 3 * part, narrow), f32),
            kept((9, part, narrow)),
            kept((tasks, 9, part, narrow)),
        ]
        + terms(piece, narrow)
        + [kept((bands, pool_rows, width))]
    )
    sizes = (tasks, bands, cols, quarter, mid, wide, piece)
    plan = (tasks, bands, cols, pixels, width, tuple(taps), tuple(extras))
    trunk_outs = (
        shape((bands + 2, part, pixels), low),
        shape((pixels, mid), f32),
        shape((pixels, mid), f32),
        shape((pixels, mid), low),
        shape((quarter, wide), f32),
        shape((8, mid), f32),
        shape((8, mid), f32),
        shape((8, wide), f32),
        shape((2, 2 * mid + wide), f32),
    )
    head_outs = (
        shape(block, low),
        shape((tasks, bands, quarter, piece), low),
        shape((len(taps) + 2, piece, width), low),
        shape((pool_rows, width), low),
        shape((both_rows, LANE), f32),
        shape((proj_rows, LANE), f32),
    )
    out_shapes = (trunk_outs[8], head_outs[0], head_outs[2], head_outs[4], head_outs[5])
    out_shapes += back_outs
    phases = (trunk_scratch, head_scratch, back_scratch)
    return taps, pl.pallas_call(
        functools.partial(
            whole_kernel, sizes, plan, phases, (len(trunk_outs), len(head_outs), len(back_outs))
        ),
        name="whole",
        out_shape=out_shapes,
        in_specs=[anywhere, pl.BlockSpec(memory_space=pltpu.SMEM)] + [anywhere] * 11,
        out_specs=(anywhere,) * len(out_shapes),
        scratch_shapes=[pltpu.VMEM(out.shape, out.dtype) for out in trunk_outs + head_outs]
        + [
            pltpu.VMEM(value.shape, value.dtype)
            for value in (gain, shift, head_gain, head_shift, cot, bw, pw)
        ]
        + [pltpu.VMEM((bands, pixels, piece), low)]
        + [entry.memory for entries in phases for entry in entries if not entry.passing]
        + [
            pltpu.SemaphoreType.DMA((352,)),
            pltpu.SemaphoreType.DMA((352,)),
            pltpu.SemaphoreType.DMA((4,)),
            pltpu.SemaphoreType.DMA((len(taps),)),
            pltpu.SemaphoreType.DMA((len(out_shapes),)),
            pltpu.SemaphoreType.DMA((7,)),
        ],
        compiler_params=pltpu.CompilerParams(
            collective_id=collective, has_side_effects=True, vmem_limit_bytes=60 << 20
        ),
    )(x, widths, gain, shift, wr, wd, we, *head_in)


def finish_kernel(
    places,
    tap_hbm,
    ho_in,
    ig_in,
    rg_in,
    dg_in,
    eg_in,
    bs_in,
    tw_hbm,
    pg_hbm,
    s3_hbm,
    s2_hbm,
    s1_hbm,
    both_hbm,
    proj_hbm,
    ho_out,
    ig_out,
    rg_out,
    dg_out,
    eg_out,
    bs_out,
    branch_out,
    rate_out,
    pg_out,
    tg_out,
    ts_out,
    hg_out,
    hs_out,
    tw_out,
    tap_ref,
    tw_ref,
    pg_ref,
    s3_ref,
    s2_ref,
    s1_ref,
    both_ref,
    proj_ref,
    ho_buf,
    ig_buf,
    rg_buf,
    dg_buf,
    eg_buf,
    bs_buf,
    branch,
    rate,
    sems,
    load_sems,
):
    f32 = jnp.float32
    width = tap_ref.shape[2]
    loads = [
        pltpu.make_async_copy(source, target, load_sems.at[number])
        for number, (source, target) in enumerate(
            (
                (tap_hbm, tap_ref),
                (pg_hbm, pg_ref),
                (tw_hbm, tw_ref),
                (s3_hbm, s3_ref),
                (s2_hbm, s2_ref),
                (s1_hbm, s1_ref),
                (both_hbm, both_ref),
                (proj_hbm, proj_ref),
            )
        )
    ]
    for load in loads:
        load.start()
    passed = [
        (ho_in, ho_buf, ho_out),
        (ig_in, ig_buf, ig_out),
        (rg_in, rg_buf, rg_out),
        (dg_in, dg_buf, dg_out),
        (eg_in, eg_buf, eg_out),
        (bs_in, bs_buf, bs_out),
    ]
    passes = [
        (
            pltpu.make_async_copy(source, buffer, load_sems.at[len(loads) + number]),
            pltpu.make_async_copy(buffer, target, sems.at[number]),
        )
        for number, (source, buffer, target) in enumerate(passed)
    ]
    for copy, _ in passes:
        copy.start()
    copies = [copy for _, copy in passes]
    per_level = len(places) // 3
    loads[0].wait()
    for level in range(3):
        for number in range(level * per_level, (level + 1) * per_level):
            lanes = slice(number * width, (number + 1) * width)
            if places[number] is None:
                rate[:, lanes] = jnp.zeros((rate.shape[0], width), f32)
            else:
                rate[:, lanes] = tap_ref[places[number]].astype(f32)
        lanes = slice(level * per_level * width, (level + 1) * per_level * width)
        copy = pltpu.make_async_copy(
            rate.at[:, lanes], rate_out.at[:, lanes], sems.at[len(copies)]
        )
        copy.start()
        copies.append(copy)
    for arrival, copy in passes:
        arrival.wait()
        copy.start()
    count = tap_ref.shape[0]
    branch[:, :width] = tap_ref[count - 2].astype(f32)
    branch[:, width:] = tap_ref[count - 1].astype(f32)
    copy = pltpu.make_async_copy(branch, branch_out, sems.at[len(copies)])
    copy.start()
    copies.append(copy)
    for load in loads[1:]:
        load.wait()
    pg_out[...] = pg_ref[...].astype(f32)
    rows = s1_ref.shape[0] // 2
    ts_out[0:rows] = s1_ref[0:rows]
    tg_out[0:rows] = s1_ref[rows : 2 * rows]
    ts_out[rows : 2 * rows] = s2_ref[0:rows]
    tg_out[rows : 2 * rows] = s2_ref[rows : 2 * rows]
    half, lanes_in = s3_ref.shape[0] // 2, s3_ref.shape[1]
    for row in range(half):
        for part in range(lanes_in // LANE):
            target = 2 * rows + row * (lanes_in // LANE) + part
            lanes = slice(part * LANE, (part + 1) * LANE)
            ts_out[target : target + 1] = s3_ref[row : row + 1, lanes]
            tg_out[target : target + 1] = s3_ref[half + row : half + row + 1, lanes]
    spread = width // LANE
    for row in range(4 * spread):
        lanes = slice(row * LANE, (row + 1) * LANE)
        hs_out[:, lanes] = both_ref[row : row + 1]
        hg_out[:, lanes] = both_ref[4 * spread + row : 4 * spread + row + 1]
    for row in range(spread):
        lanes = slice((4 * spread + row) * LANE, (4 * spread + row + 1) * LANE)
        hs_out[:, lanes] = proj_ref[row : row + 1]
        hg_out[:, lanes] = proj_ref[spread + row : spread + row + 1]
    tasks = tw_out.shape[1]
    place = lax.broadcasted_iota(jnp.int32, (1, LANE), 1)
    weights = jnp.zeros((1, LANE), f32)
    for number in range(tasks):
        weights = jnp.where(place == number, tw_ref[number : number + 1], weights)
    tw_out[...] = weights[:, :tasks]
    for copy in copies:
        copy.wait()


def finish(places, tasks, taps, ho, ig, rg, dg, eg, bs, tw, pg, s3, s2, s1, both, proj):
    f32 = jnp.float32
    in_vmem = pl.BlockSpec(memory_space=pltpu.VMEM)
    anywhere = pl.BlockSpec(memory_space=pl.ANY)
    shape = jax.ShapeDtypeStruct
    depth, width = taps.shape[1:]
    rows = (s1.size + s2.size + s3.size) // 2 // LANE
    return pl.pallas_call(
        functools.partial(finish_kernel, places),
        name="finish",
        out_shape=(
            shape(ho.shape, ho.dtype),
            shape(ig.shape, ig.dtype),
            shape(rg.shape, rg.dtype),
            shape(dg.shape, dg.dtype),
            shape(eg.shape, eg.dtype),
            shape(bs.shape, bs.dtype),
            shape((depth, 2 * width), f32),
            shape((depth, len(places) * width), f32),
            shape(pg.shape, f32),
            shape((rows, LANE), f32),
            shape((rows, LANE), f32),
            shape((1, 5 * width), f32),
            shape((1, 5 * width), f32),
            shape((1, tasks), f32),
        ),
        in_specs=[anywhere] * 14,
        out_specs=(anywhere,) * 8 + (in_vmem,) * 6,
        scratch_shapes=[
            pltpu.VMEM(value.shape, value.dtype) for value in (taps, tw, pg, s3, s2, s1, both, proj, ho, ig, rg, dg, eg, bs)
        ]
        + [
            pltpu.VMEM((depth, 2 * width), f32),
            pltpu.VMEM((depth, len(places) * width), f32),
            pltpu.SemaphoreType.DMA((10,)),
            pltpu.SemaphoreType.DMA((14,)),
        ],
        compiler_params=pltpu.CompilerParams(vmem_limit_bytes=60 << 20),
    )(taps, ho, ig, rg, dg, eg, bs, tw, pg, s3, s2, s1, both, proj)


def live_taps(rows, cols):
    taps = []
    for level in (1, 2, 3):
        for row_tap in range(3):
            for col_tap in range(3):
                down, right = (row_tap - 1) * level * RATE, (col_tap - 1) * level * RATE
                if abs(down) < rows and abs(right) < cols:
                    taps.append((level, row_tap, col_tap, down, right))
    return taps


def per_device_slices(
    features,
    row_width,
    w_reduce,
    w_dilated,
    w_expand,
    trunk_gain,
    trunk_shift,
    branch_weight,
    rate_weight,
    proj_weight,
    head_gain,
    head_shift,
    head_cot,
):
    bands, tasks = lax.axis_size("space"), lax.axis_size("task")
    band_rows, cols, in_width = features.shape
    rows = band_rows * bands
    pixels = band_rows * cols
    head_width = proj_weight.shape[2]
    inputs = features.reshape(pixels, in_width)
    dilated = w_dilated.transpose(1, 0, 2)
    taps, (
        batch_stats,
        head_out,
        tap_grads,
        both_sums,
        proj_sums,
        weight_rows,
        input_grad,
        reduce_grad,
        dilated_grad,
        expand_grad,
        sums_three,
        sums_two,
        sums_one,
        proj_grad,
    ) = whole(
        tasks,
        bands,
        cols,
        rows,
        0,
        inputs,
        row_width,
        trunk_gain.reshape(1, -1),
        trunk_shift.reshape(1, -1),
        w_reduce,
        dilated,
        w_expand,
        head_gain,
        head_shift,
        head_cot.reshape(pixels, head_width),
        branch_weight[0],
        proj_weight[0],
        rate_weight[0],
    )
    place_of = {tap[:3]: number for number, tap in enumerate(taps)}
    places = tuple(
        place_of.get((level, row_tap, col_tap))
        for level in (1, 2, 3)
        for row_tap in range(3)
        for col_tap in range(3)
    )
    (
        head_out,
        input_grad,
        reduce_grad,
        dilated_grad,
        expand_grad,
        batch_stats,
        branch_grad,
        rate_grad,
        proj_grad,
        trunk_gains,
        trunk_shifts,
        head_gains,
        head_shifts,
        task_weight,
    ) = finish(
        places,
        tasks,
        tap_grads,
        head_out,
        input_grad,
        reduce_grad,
        dilated_grad,
        expand_grad,
        batch_stats,
        weight_rows,
        proj_grad.reshape(-1, head_width),
        sums_three,
        sums_two,
        sums_one,
        both_sums,
        proj_sums,
    )
    return (
        head_out.reshape(1, band_rows, cols, head_width),
        input_grad.reshape(features.shape),
        reduce_grad,
        dilated_grad.transpose(1, 0, 2),
        expand_grad,
        trunk_gains.reshape(-1),
        trunk_shifts.reshape(-1),
        batch_stats,
        branch_grad[None],
        rate_grad[None],
        proj_grad[None],
        head_gains,
        head_shifts,
        task_weight.reshape(-1),
    )


def solution(mesh):
    body = per_device_slices if mesh.shape["space"] == 8 else per_device
    return jax.shard_map(
        body,
        mesh=mesh,
        in_specs=(
            P("space", None, None),
            P(),
            P(),
            P(),
            P(),
            P(),
            P(),
            P("task", "space", None),
            P("task", "space", None),
            P("task", None, None),
            P("task", None),
            P("task", None),
            P("task", "space", None, None),
        ),
        out_specs=(
            P("task", "space", None, None),
            P("space", None, None),
            P("space", None),
            P("space", None, None),
            P("space", None),
            P(),
            P(),
            P(),
            P("task", "space", None),
            P("task", "space", None),
            P("task", None, None),
            P("task", None),
            P("task", None),
            P(),
        ),
        check_vma=False,
    )
```

```python
import functools

import jax
import jax.numpy as jnp
from jax import lax
from jax.experimental import pallas as pl
from jax.experimental.pallas import tpu as pltpu
from jax.sharding import PartitionSpec as P

CONV_DILATION = 2
RATE = 12


NORM_EPS = 1e-05
GRAM_EPS = 1e-06
PRECISE = lax.Precision.HIGHEST


def with_halo(block, sides, width):
    for axis, dim in sides:
        count = lax.axis_size(axis)
        forward = [(i, i + 1) for i in range(count - 1)]
        backward = [(target, source) for source, target in forward]
        low = lax.ppermute(
            lax.slice_in_dim(block, block.shape[dim] - width, None, axis=dim), axis, forward
        )
        high = lax.ppermute(lax.slice_in_dim(block, 0, width, axis=dim), axis, backward)
        block = jnp.concatenate([low, block, high], axis=dim)
    return block


def from_behind(shard, axis, by):
    count = lax.axis_size(axis)
    pairs = [(i, i + by) for i in range(count) if 0 <= i + by < count]
    return lax.ppermute(shard, axis, pairs)


def small_solve(matrix, target):
    size_n = matrix.shape[0]
    rows_list = [matrix[number] for number in range(size_n)]
    values = [target[number] for number in range(size_n)]
    for pivot_row in range(size_n):
        for lower_row in range(pivot_row + 1, size_n):
            factor = rows_list[lower_row][pivot_row] / rows_list[pivot_row][pivot_row]
            rows_list[lower_row] = rows_list[lower_row] - factor * rows_list[pivot_row]
            values[lower_row] = values[lower_row] - factor * values[pivot_row]
    answer = [None] * size_n
    for pivot_row in reversed(range(size_n)):
        running = values[pivot_row]
        for later_row in range(pivot_row + 1, size_n):
            running = running - rows_list[pivot_row][later_row] * answer[later_row]
        answer[pivot_row] = running / rows_list[pivot_row][pivot_row]
    return jnp.stack(answer)


def imtl_weights(gram_matrix):
    grad_norms = jnp.sqrt(jnp.diagonal(gram_matrix) + GRAM_EPS)
    projections = gram_matrix / grad_norms[None, :]
    system = projections[0, 0] - projections[0:1, 1:] - projections[1:, 0:1] + projections[1:, 1:]
    target = projections[0, 0] - projections[0, 1:]
    other_weights = small_solve(jnp.transpose(system), target)
    return jnp.concatenate([(1.0 - jnp.sum(other_weights))[None], other_weights])


def gelu_back(value, upstream):
    return jax.vjp(jax.nn.gelu, value)[1](upstream)[0]


def channel_sums(members):
    return lax.psum(members, "space")


def norm_values(hidden, first_total, second_total, gain_vec, shift_vec, pixel_count):
    mean_value = first_total / pixel_count
    variance = second_total / pixel_count - mean_value * mean_value
    inv_std = lax.rsqrt(variance + NORM_EPS)
    scaled = (hidden - mean_value) * inv_std
    return (gain_vec * scaled + shift_vec, scaled, inv_std, mean_value, variance)


def norm_forward(hidden, gain_vec, shift_vec, valid_mask, pixel_count):
    totals = channel_sums(
        (jnp.sum(hidden * valid_mask, axis=0), jnp.sum(hidden * hidden * valid_mask, axis=0))
    )
    return norm_values(hidden, totals[0], totals[1], gain_vec, shift_vec, pixel_count)


def norm_finish(
    upstream, scaled, inv_std, gain_vec, gain_grad, shift_grad, valid_mask, pixel_count
):
    return (
        valid_mask
        * gain_vec
        * inv_std
        * (upstream - shift_grad / pixel_count - scaled * gain_grad / pixel_count)
    )


def norm_backward(upstream, scaled, inv_std, gain_vec, valid_mask, pixel_count):
    totals = channel_sums(
        (jnp.sum(upstream * valid_mask, axis=0), jnp.sum(upstream * scaled * valid_mask, axis=0))
    )
    hidden_grad = norm_finish(
        upstream, scaled, inv_std, gain_vec, totals[1], totals[0], valid_mask, pixel_count
    )
    return (hidden_grad, totals[1], totals[0])


def band_rim(strip_image):
    return with_halo(strip_image, (("space", 0),), CONV_DILATION)


def far_rows(strip_image, bands_away, upward):
    if bands_away >= lax.axis_size("space"):
        return jnp.zeros_like(strip_image)
    if upward:
        return from_behind(strip_image, "space", bands_away)
    return from_behind(strip_image, "space", -bands_away)


def trunk_taps(padded, reach_cells, rows_count, cols_count, flipped):
    col_padded = jnp.pad(padded, ((0, 0), (reach_cells, reach_cells), (0, 0)))
    pieces = []
    for row_tap in range(3):
        for col_tap in range(3):
            row_from = (2 - row_tap) * reach_cells if flipped else row_tap * reach_cells
            col_from = (2 - col_tap) * reach_cells if flipped else col_tap * reach_cells
            pieces.append(
                col_padded[
                    row_from : row_from + rows_count, col_from : col_from + cols_count
                ].reshape(rows_count * cols_count, -1)
            )
    return jnp.stack(pieces, axis=1)


def per_device(
    features,
    row_width,
    w_reduce,
    w_dilated,
    w_expand,
    trunk_gain,
    trunk_shift,
    branch_weight,
    rate_weight,
    proj_weight,
    head_gain,
    head_shift,
    head_cot,
):
    band_rows, cols_count, in_width = features.shape
    pixels = band_rows * cols_count
    middle_width = w_reduce.shape[1]
    head_width = proj_weight.shape[2]
    first_row = lax.axis_index("space") * band_rows
    widths = lax.dynamic_slice_in_dim(row_width, first_row, band_rows)
    valid_mask = (
        (jnp.arange(cols_count)[None, :] < widths[:, None]).astype(jnp.float32).reshape(pixels, 1)
    )
    pixel_count = jnp.sum(row_width).astype(jnp.float32)
    inputs = features.reshape(pixels, in_width)
    gain_one, shift_one = (trunk_gain[:middle_width], trunk_shift[:middle_width])
    gain_two, shift_two = (
        trunk_gain[middle_width : 2 * middle_width],
        trunk_shift[middle_width : 2 * middle_width],
    )
    gain_three, shift_three = (trunk_gain[2 * middle_width :], trunk_shift[2 * middle_width :])
    hidden_one = jnp.dot(inputs, w_reduce, preferred_element_type=jnp.float32)
    stats_one = norm_forward(hidden_one, gain_one, shift_one, valid_mask, pixel_count)
    first_active = (jax.nn.gelu(stats_one[0]) * valid_mask).astype(jnp.bfloat16)
    patches = trunk_taps(
        band_rim(first_active.reshape(band_rows, cols_count, middle_width)),
        CONV_DILATION,
        band_rows,
        cols_count,
        False,
    )
    hidden_two = jnp.einsum("pti,ito->po", patches, w_dilated, preferred_element_type=jnp.float32)
    stats_two = norm_forward(hidden_two, gain_two, shift_two, valid_mask, pixel_count)
    active_two = (jax.nn.gelu(stats_two[0]) * valid_mask).astype(jnp.bfloat16)
    hidden_three = jnp.dot(active_two, w_expand, preferred_element_type=jnp.float32)
    stats_three = norm_forward(hidden_three, gain_three, shift_three, valid_mask, pixel_count)
    before_act = stats_three[0] + inputs.astype(jnp.float32)
    shared = (jax.nn.gelu(before_act) * valid_mask).astype(jnp.bfloat16)
    proj_local = proj_weight[0]
    gain_local = head_gain[0]
    shift_local = head_shift[0]
    joined_weight = jnp.concatenate([branch_weight[0], rate_weight[0]], axis=1)
    pixel_sum = jnp.dot(
        valid_mask.reshape(1, pixels).astype(jnp.bfloat16),
        shared,
        preferred_element_type=jnp.float32,
    )[0]
    shared_image = shared.reshape(band_rows, cols_count, in_width)
    padded_sources = []
    for level in (1, 2, 3):
        reach = level * RATE
        bands_away = reach // band_rows
        triple = (
            far_rows(shared_image, bands_away, True),
            shared_image,
            far_rows(shared_image, bands_away, False),
        )
        padded_sources.append(
            [jnp.pad(source, ((0, 0), (reach, reach), (0, 0))) for source in triple]
        )
    zero_rows = jnp.zeros((pixels, head_width), jnp.float32)
    start_totals = (
        zero_rows,
        jnp.zeros((1, head_width), jnp.float32),
        zero_rows,
        zero_rows,
        zero_rows,
    )
    all_weights = lax.all_gather(joined_weight, "space", axis=0, tiled=True)
    width_now = all_weights.shape[0]
    one_acc = jnp.dot(shared, all_weights[:, :head_width], preferred_element_type=jnp.float32)
    pool_cols = pixel_sum[None]
    pool_acc = jnp.dot(
        pool_cols,
        all_weights[:, head_width : 2 * head_width].astype(jnp.float32),
        precision=PRECISE,
        preferred_element_type=jnp.float32,
    )
    rate_accs = []
    for fold_level_index in range(3):
        fold_reach = (fold_level_index + 1) * RATE
        running = start_totals[2 + fold_level_index]
        for fold_row_tap in range(3):
            fold_source = padded_sources[fold_level_index][fold_row_tap]
            for fold_col_tap in range(3):
                window = fold_source[
                    :, fold_col_tap * fold_reach : fold_col_tap * fold_reach + cols_count
                ].reshape(pixels, width_now)
                column = (2 + 9 * fold_level_index + 3 * fold_row_tap + fold_col_tap) * head_width
                running = running + jnp.dot(
                    window,
                    all_weights[:, column : column + head_width],
                    preferred_element_type=jnp.float32,
                )
        rate_accs.append(running)
    pre_both = jnp.concatenate([one_acc, rate_accs[0], rate_accs[1], rate_accs[2]], axis=1)
    gain_both, shift_both = (gain_local[: 4 * head_width], shift_local[: 4 * head_width])
    totals = channel_sums(
        (
            jnp.sum(pre_both * valid_mask, axis=0),
            jnp.sum(pre_both * pre_both * valid_mask, axis=0),
            pool_acc[0],
        )
    )
    stats_both = norm_values(pre_both, totals[0], totals[1], gain_both, shift_both, pixel_count)
    pooled = totals[2][None] / pixel_count
    active_both = (jax.nn.gelu(stats_both[0]) * valid_mask).astype(jnp.bfloat16)
    active_pool = jax.nn.gelu(pooled).astype(jnp.bfloat16)
    joined = jnp.concatenate(
        [active_both, (active_pool.astype(jnp.float32) * valid_mask).astype(jnp.bfloat16)], axis=1
    )
    projected = jnp.dot(joined, proj_local, preferred_element_type=jnp.float32)
    gain_proj = gain_local[4 * head_width :]
    stats_proj = norm_forward(
        projected, gain_proj, shift_local[4 * head_width :], valid_mask, pixel_count
    )
    head_result = (jax.nn.gelu(stats_proj[0]) * valid_mask).astype(jnp.bfloat16)
    cot_rows = head_cot[0].reshape(pixels, head_width).astype(jnp.float32)
    proj_upstream = gelu_back(stats_proj[0], cot_rows * valid_mask)
    proj_hidden, proj_gain_grad, proj_shift_grad = norm_backward(
        proj_upstream, stats_proj[1], stats_proj[2], gain_proj, valid_mask, pixel_count
    )
    proj_low = proj_hidden.astype(jnp.bfloat16)
    joined_grad = lax.dot_general(
        proj_low, proj_local, (((1,), (1,)), ((), ())), preferred_element_type=jnp.float32
    )
    proj_term = lax.dot_general(
        joined, proj_low, (((0,), (0,)), ((), ())), preferred_element_type=jnp.float32
    )
    both_upstream = gelu_back(stats_both[0], joined_grad[:, : 4 * head_width] * valid_mask)
    pool_total = jnp.sum(joined_grad[:, 4 * head_width :] * valid_mask, axis=0)
    back_totals = channel_sums(
        (
            proj_term,
            pool_total,
            jnp.sum(both_upstream * valid_mask, axis=0),
            jnp.sum(both_upstream * stats_both[1] * valid_mask, axis=0),
        )
    )
    pool_grad = gelu_back(pooled, back_totals[1][None]).astype(jnp.bfloat16)
    both_grad = norm_finish(
        both_upstream,
        stats_both[1],
        stats_both[2],
        gain_both,
        back_totals[3],
        back_totals[2],
        valid_mask,
        pixel_count,
    ).astype(jnp.bfloat16)
    tap_grads = []
    for level_index in range(3):
        reach = (level_index + 1) * RATE
        bands_away = reach // band_rows
        rate_image = both_grad[
            :, (1 + level_index) * head_width : (2 + level_index) * head_width
        ].reshape(band_rows, cols_count, head_width)
        back_sources = [
            jnp.pad(source, ((0, 0), (reach, reach), (0, 0)))
            for source in (
                far_rows(rate_image, bands_away, False),
                rate_image,
                far_rows(rate_image, bands_away, True),
            )
        ]
        for row_tap in range(3):
            for col_tap in range(3):
                tap_grads.append(
                    back_sources[row_tap][
                        :, (2 - col_tap) * reach : (2 - col_tap) * reach + cols_count
                    ].reshape(pixels, head_width)
                )
    right_side = jnp.concatenate([both_grad[:, :head_width]] + tap_grads, axis=1)
    used_rows = jnp.concatenate(
        [all_weights[:, :head_width], all_weights[:, 2 * head_width :]], axis=1
    )
    main_part = lax.dot_general(
        right_side, used_rows, (((1,), (1,)), ((), ())), preferred_element_type=jnp.float32
    )
    pool_part = lax.dot_general(
        pool_grad,
        all_weights[:, head_width : 2 * head_width],
        (((1,), (1,)), ((), ())),
        preferred_element_type=jnp.float32,
    )
    shared_grad = (main_part + valid_mask * pool_part / pixel_count).astype(jnp.bfloat16)
    head_term = lax.dot_general(
        shared, right_side, (((0,), (0,)), ((), ())), preferred_element_type=jnp.float32
    )
    pool_term = pixel_sum[:, None] * pool_grad.astype(jnp.float32) / pixel_count
    head_term = jnp.concatenate(
        [head_term[:, :head_width], pool_term, head_term[:, head_width:]], axis=1
    )
    all_grads = lax.all_gather(shared_grad[None], "task", axis=0, tiled=True)
    flat_grads = all_grads.reshape(all_grads.shape[0], -1)
    gram_matrix = lax.psum(
        lax.dot_general(
            flat_grads, flat_grads, (((1,), (1,)), ((), ())), preferred_element_type=jnp.float32
        ),
        "space",
    )
    task_weight = imtl_weights(gram_matrix)
    mixed_grad = task_weight[0] * all_grads[0].astype(jnp.float32)
    for task_index in range(1, all_grads.shape[0]):
        mixed_grad = mixed_grad + task_weight[task_index] * all_grads[task_index].astype(
            jnp.float32
        )
    combined = mixed_grad.astype(jnp.bfloat16)
    gate_grad = gelu_back(before_act, combined.astype(jnp.float32) * valid_mask)
    hidden_grad_three, gain_grad_three, shift_grad_three = norm_backward(
        gate_grad, stats_three[1], stats_three[2], gain_three, valid_mask, pixel_count
    )
    low_three = hidden_grad_three.astype(jnp.bfloat16)
    expand_term = lax.dot_general(
        active_two, low_three, (((0,), (0,)), ((), ())), preferred_element_type=jnp.float32
    )
    active_grad_two = lax.dot_general(
        low_three, w_expand, (((1,), (1,)), ((), ())), preferred_element_type=jnp.float32
    )
    upstream_two = gelu_back(stats_two[0], active_grad_two * valid_mask)
    hidden_grad_two, gain_grad_two, shift_grad_two = norm_backward(
        upstream_two, stats_two[1], stats_two[2], gain_two, valid_mask, pixel_count
    )
    low_two = hidden_grad_two.astype(jnp.bfloat16)
    dilated_term = jnp.einsum("pti,po->ito", patches, low_two, preferred_element_type=jnp.float32)
    back_patches = trunk_taps(
        band_rim(low_two.reshape(band_rows, cols_count, middle_width)),
        CONV_DILATION,
        band_rows,
        cols_count,
        True,
    )
    active_grad_one = jnp.einsum(
        "pto,ito->pi", back_patches, w_dilated, preferred_element_type=jnp.float32
    )
    upstream_one = gelu_back(stats_one[0], active_grad_one * valid_mask)
    hidden_grad_one, gain_grad_one, shift_grad_one = norm_backward(
        upstream_one, stats_one[1], stats_one[2], gain_one, valid_mask, pixel_count
    )
    low_one = hidden_grad_one.astype(jnp.bfloat16)
    reduce_term = lax.dot_general(
        inputs, low_one, (((0,), (0,)), ((), ())), preferred_element_type=jnp.float32
    )
    input_grad = (
        lax.dot_general(
            low_one, w_reduce, (((1,), (1,)), ((), ())), preferred_element_type=jnp.float32
        )
        + gate_grad
    )
    reduced = (
        lax.psum_scatter(head_term, "space", scatter_dimension=0, tiled=True),
        lax.psum_scatter(reduce_term, "space", scatter_dimension=0, tiled=True),
        lax.psum_scatter(dilated_term, "space", scatter_dimension=0, tiled=True),
        lax.psum_scatter(expand_term, "space", scatter_dimension=0, tiled=True),
    )
    means = jnp.concatenate([stats_one[3], stats_two[3], stats_three[3]])
    variances = (
        jnp.concatenate([stats_one[4], stats_two[4], stats_three[4]])
        * pixel_count
        / (pixel_count - 1.0)
    )
    batch_stats = jnp.stack([means, variances])
    head_gain_grad = jnp.concatenate([back_totals[3], proj_gain_grad])[None]
    head_shift_grad = jnp.concatenate([back_totals[2], proj_shift_grad])[None]
    return (
        head_result.reshape(1, band_rows, cols_count, head_width),
        input_grad.reshape(band_rows, cols_count, in_width).astype(jnp.bfloat16),
        reduced[1],
        reduced[2],
        reduced[3],
        jnp.concatenate([gain_grad_one, gain_grad_two, gain_grad_three]),
        jnp.concatenate([shift_grad_one, shift_grad_two, shift_grad_three]),
        batch_stats,
        reduced[0][:, : 2 * head_width][None],
        reduced[0][:, 2 * head_width :][None],
        back_totals[0][None],
        head_gain_grad,
        head_shift_grad,
        task_weight,
    )


MESH_ID = pl.DeviceIdType.MESH
LANE = 128


FAR_LAG = 2
SEND_LAG = 0
GELU_A = 0.7978845608028654
GELU_B = 0.044715


def gelu_of(value):
    return 0.5 * value * (1.0 + jnp.tanh(GELU_A * (value + GELU_B * value * value * value)))


def gelu_slope(value):
    square = value * value
    bend = jnp.tanh(GELU_A * value * (1.0 + GELU_B * square))
    return 0.5 * (1.0 + bend) + 0.5 * value * (1.0 - bend * bend) * (
        GELU_A * (1.0 + 3.0 * GELU_B * square)
    )


def gelu_both(value):
    square = value * value
    bend = jnp.tanh(GELU_A * value * (1.0 + GELU_B * square))
    lift = 0.5 * (1.0 + bend)
    slope = lift + 0.5 * value * (1.0 - bend * bend) * (GELU_A * (1.0 + 3.0 * GELU_B * square))
    return value * lift, slope


def dot_nn(left_side, right_side):
    return jnp.dot(left_side, right_side, preferred_element_type=jnp.float32)


def dot_nt(left_side, right_side):
    return lax.dot_general(
        left_side, right_side, (((1,), (1,)), ((), ())), preferred_element_type=jnp.float32
    )


def shift_pixels(value, by, cols):
    if by == 0:
        return value
    rows = value.shape[0]
    column = lax.rem(lax.broadcasted_iota(jnp.int32, value.shape, 0), cols) + by
    rolled = pltpu.roll(value, (-by) % rows, 0)
    return jnp.where((column >= 0) & (column < cols), rolled, 0.0)


def row_mask(widths_ref, first_row, rows, cols):
    column = lax.broadcasted_iota(jnp.int32, (cols, LANE), 0)
    return jnp.concatenate(
        [
            jnp.where(column < widths_ref[first_row + number], 1.0, 0.0).astype(jnp.float32)
            for number in range(rows)
        ],
        axis=0,
    )


def count_pixels(widths_ref):
    total = widths_ref[0]
    for number in range(1, widths_ref.shape[0]):
        total = total + widths_ref[number]
    return jnp.full((1, LANE), total.astype(jnp.float32), jnp.float32)


class Post:
    def __init__(self, send_sem, recv_sem):
        self.send_sem, self.recv_sem = send_sem, recv_sem
        self.used = 0
        self.sent = []

    def copy(self, source, target, device):
        made = pltpu.make_async_remote_copy(
            source,
            target,
            self.send_sem.at[self.used],
            self.recv_sem.at[self.used],
            device_id=device,
            device_id_type=MESH_ID,
        )
        self.used += 1
        return made

    def push(self, source, target, device):
        made = self.copy(source, target, device)
        made.start()
        self.sent.append(made)
        return made

    def close(self):
        for made in self.sent:
            made.wait_send()
        self.sent = []


class Place:
    def __init__(self, tasks, bands):
        self.tasks, self.bands, self.chips = tasks, bands, bands // 2
        self.task = lax.axis_index("task")
        self.band = lax.axis_index("space")
        self.chip = self.band // 2
        self.core = lax.rem(self.band, 2)
        self.twin = {"space": self.chip * 2 + 1 - self.core}
        low, high = lax.rem(self.task, 2), self.task // 2
        self.other_tasks = [(1 - high) * 2 + 1 - low, high * 2 + 1 - low, (1 - high) * 2 + low]
        self.other_bands = [lax.rem(self.band + step, bands) for step in range(1, bands)]

    def greet(self):
        barrier = pltpu.get_barrier_semaphore()
        greeted = [{"task": task} for task in self.other_tasks]
        greeted += [{"space": band} for band in self.other_bands]
        for device in greeted:
            pl.semaphore_signal(barrier, inc=1, device_id=device, device_id_type=MESH_ID)

    def meet(self):
        barrier = pltpu.get_barrier_semaphore()
        pl.semaphore_wait(barrier, len(self.other_tasks) + len(self.other_bands))

    def sum_begin(self, post, axis, own_ref, land_ref):
        mine = self.task if axis == "task" else self.band
        others = self.other_tasks if axis == "task" else self.other_bands
        copies = [post.push(own_ref, land_ref.at[mine], {axis: other}) for other in others]
        land_ref[pl.ds(mine, 1)] = own_ref[...][None]
        return copies, land_ref

    def sum_end(self, begun):
        copies, land_ref = begun
        for made in copies:
            made.wait_recv()
        total = land_ref[0]
        for slot in range(1, len(copies) + 1):
            total = total + land_ref[slot]
        return total

    def sum_over(self, post, axis, own_ref, land_ref):
        return self.sum_end(self.sum_begin(post, axis, own_ref, land_ref))


def back_phase(
    at,
    post,
    sizes,
    local_sem,
    xg,
    h3q,
    v3_ref,
    h2_ref,
    v2_ref,
    h1_ref,
    v1_ref,
    act_ref,
    a2_ref,
    ps_ref,
    x_hbm,
    widths_ref,
    we_hbm,
    wd_hbm,
    wr_hbm,
    write,
    tw_hbm,
    ig_hbm,
    rg_hbm,
    dg_hbm,
    eg_hbm,
    s3_hbm,
    s2_hbm,
    s1_hbm,
    pg_hbm,
    tw_out,
    ig_out,
    rg_out,
    dg_out,
    eg_out,
    s3_out,
    s2_out,
    s1_out,
    pg_out,
    we,
    wd,
    wr,
    x_ref,
    mask_ref,
    gram_own,
    gram_land,
    gram_mid,
    gram_land_b,
    comb,
    comb_land,
    gate,
    scaled,
    gate_low,
    gate_band,
    st3,
    st3_land,
    st3_mid,
    st3_land_b,
    l3,
    l3x,
    st2,
    st2_land,
    st2_mid,
    st2_land_b,
    l2,
    l2_halo,
    ag1,
    st1,
    st1_land,
    l1,
    xt,
    a2t,
    e_term,
    e_twin,
    e_land,
    e_share,
    e_tasks,
    l2c,
    d_sum,
    d_share,
    d_tasks,
    r_term,
    r_twin,
    r_land,
    r_share,
    r_tasks,
    p_all,
):
    tasks, bands, cols, quarter, mid, wide, piece = sizes
    low = jnp.bfloat16
    f32 = jnp.float32
    task, band = at.task, at.band
    my_rows = pl.ds(pl.multiple_of(task * quarter, quarter), quarter)
    arrays = {
        "x": (x_hbm, x_ref),
        "we": (we_hbm, we),
        "wd": (wd_hbm, wd),
        "wr": (wr_hbm, wr),
    }
    loads = {
        name: pltpu.make_async_copy(source, target, local_sem.at[number])
        for number, (name, (source, target)) in enumerate(arrays.items())
    }

    def loaded(*names):
        for name in names:
            loads[name].wait()

    for load in loads.values():
        load.start()
    band_rows = x_ref.shape[0] // cols
    mask_ref[...] = row_mask(widths_ref, band * band_rows, band_rows, cols)

    pairs = [(a, b) for a in range(tasks) for b in range(a, tasks)]

    def gram_step(number, totals):
        grads = [xg[a, number].astype(f32) for a in range(tasks)]
        out = []
        for (a, b), total in zip(pairs, totals):
            product = grads[a] * grads[b]
            product = product.reshape(quarter // 8, 8, piece).sum(axis=0)
            for start in range(0, piece, LANE):
                total = total + product[:, start : start + LANE]
            out.append(total)
        return tuple(out)

    totals = lax.fori_loop(
        0, bands, gram_step, tuple(jnp.zeros((8, LANE), f32) for _ in pairs)
    )
    gram_own[...] = jnp.zeros_like(gram_own)
    for number, total in enumerate(totals):
        gram_own[number : number + 1] = jnp.sum(total, axis=0, keepdims=True)
    begun = at.sum_begin(post, "task", gram_own, gram_land)
    a2t[...] = a2_ref[...].T
    gram_mid[...] = at.sum_end(begun)
    begun = at.sum_begin(post, "space", gram_mid, gram_land_b)

    loaded("x")
    def turn_inputs(number, carry):
        lanes = pl.ds(pl.multiple_of(number * piece, piece), piece)
        xt[lanes, :] = x_ref[:, lanes].T
        return carry

    lax.fori_loop(0, wide // piece, turn_inputs, 0)
    gram_sum = at.sum_end(begun)
    gram_sum = jnp.broadcast_to(jnp.sum(gram_sum, axis=1, keepdims=True), gram_sum.shape)
    gram = [[None] * tasks for _ in range(tasks)]
    for number, (a, b) in enumerate(pairs):
        gram[a][b] = gram[b][a] = gram_sum[number : number + 1]
    norms = [jnp.sqrt(gram[a][a] + GRAM_EPS) for a in range(tasks)]
    cos = [[gram[a][b] / norms[b] for b in range(tasks)] for a in range(tasks)]
    rows_list = [
        [cos[0][0] - cos[0][l] - cos[k][0] + cos[k][l] for k in range(1, tasks)]
        for l in range(1, tasks)
    ]
    values = [cos[0][0] - cos[0][l] for l in range(1, tasks)]
    count = tasks - 1
    for pivot in range(count):
        for lower in range(pivot + 1, count):
            factor = rows_list[lower][pivot] / rows_list[pivot][pivot]
            rows_list[lower] = [
                under - factor * over for under, over in zip(rows_list[lower], rows_list[pivot])
            ]
            values[lower] = values[lower] - factor * values[pivot]
    answer = [None] * count
    for pivot in reversed(range(count)):
        running = values[pivot]
        for later in range(pivot + 1, count):
            running = running - rows_list[pivot][later] * answer[later]
        answer[pivot] = running / rows_list[pivot][pivot]
    rest = answer[0]
    for value in answer[1:]:
        rest = rest + value
    task_weight = [1.0 - rest] + answer
    for number in range(tasks):
        tw_out[number : number + 1] = task_weight[number]
    weights = [jnp.concatenate([value] * (piece // LANE), axis=1) for value in task_weight]

    def mixed(number):
        total = weights[0] * xg[0, number].astype(f32)
        for a in range(1, tasks):
            total = total + weights[a] * xg[a, number].astype(f32)
        return total.astype(low)

    comb_in = []
    for other in at.other_bands:
        comb[other] = mixed(other)
        comb_in.append(post.push(comb.at[other], comb_land.at[band], {"space": other}))
    comb_land[pl.ds(band, 1)] = mixed(band)[None]
    for made in comb_in:
        made.wait_recv()

    mask_quarter = mask_ref[my_rows]
    mask_piece = jnp.concatenate([mask_quarter] * (piece // LANE), axis=1)
    inv_count = 1.0 / count_pixels(widths_ref)
    inv_piece = jnp.concatenate([inv_count] * (piece // LANE), axis=1)
    per_row = st3.shape[1] // piece
    half = st3.shape[0] // 2

    def gate_step(number, carry):
        lanes = pl.ds(pl.multiple_of(number * piece, piece), piece)
        hat = (h3q[:, lanes] - v3_ref[0:1, lanes]) * v3_ref[1:2, lanes]
        before = v3_ref[2:3, lanes] * hat + v3_ref[3:4, lanes] + x_ref[my_rows, lanes].astype(f32)
        grad = gelu_slope(before) * comb_land[number].astype(f32) * mask_piece
        gate[number] = grad
        scaled[number] = hat
        gate_low[number] = grad.astype(low)
        row = number // per_row
        spot = pl.ds(pl.multiple_of(lax.rem(number, per_row) * piece, piece), piece)
        st3[pl.ds(row, 1), spot] = jnp.sum(grad, axis=0, keepdims=True)
        st3[pl.ds(half + row, 1), spot] = jnp.sum(grad * hat, axis=0, keepdims=True)
        return carry

    lax.fori_loop(0, bands, gate_step, 0)
    st3_mid[...] = at.sum_over(post, "task", st3, st3_land)
    s3_out[...] = at.sum_over(post, "space", st3_mid, st3_land_b)

    def third_step(number, carry):
        lanes = pl.ds(pl.multiple_of(number * piece, piece), piece)
        row = number // per_row
        spot = pl.ds(pl.multiple_of(lax.rem(number, per_row) * piece, piece), piece)
        shift_grad = s3_out[pl.ds(row, 1), spot] * inv_piece
        gain_grad = s3_out[pl.ds(half + row, 1), spot] * inv_piece
        l3[number] = (
            mask_piece
            * (v3_ref[2:3, lanes] * v3_ref[1:2, lanes])
            * (gate[number] - shift_grad - scaled[number] * gain_grad)
        ).astype(low)
        return carry

    lax.fori_loop(0, bands, third_step, 0)
    per_task = bands // tasks
    l3_in = []
    for other in at.other_tasks:
        l3_in.append(
            post.push(l3.at[pl.ds(other * per_task, per_task)], l3x.at[task], {"task": other})
        )
    l3x[pl.ds(task, 1)] = l3[pl.ds(task * per_task, per_task)][None]
    loaded("we")
    p_all[pl.ds(band, 1)] = ps_ref[...][None]
    p_block = p_all.at[band]
    p_near = post.push(p_block, p_block, at.twin)
    p_far = [
        post.push(
            p_block,
            p_block,
            {"space": lax.rem(at.chip + step, at.chips) * 2 + at.core},
        )
        for step in range(1, at.chips)
    ]

    def expand_step(number, total):
        lanes = pl.ds(pl.multiple_of(number * piece, piece), piece)
        return total + dot_nt(l3[number], we[:, lanes])

    ag2 = lax.fori_loop(0, bands, expand_step, jnp.zeros((quarter, mid), f32))

    mask_mid = jnp.concatenate([mask_quarter] * (mid // LANE), axis=1)
    inv_mid = jnp.concatenate([inv_count] * (mid // LANE), axis=1)
    hat = (h2_ref[my_rows] - v2_ref[0:1]) * v2_ref[1:2]
    grad = gelu_slope(v2_ref[2:3] * hat + v2_ref[3:4]) * ag2 * mask_mid
    spread = mid // LANE

    def put_sums(target, first, second):
        for number in range(spread):
            lanes = slice(number * LANE, (number + 1) * LANE)
            target[number : number + 1] = first[:, lanes]
            target[spread + number : spread + number + 1] = second[:, lanes]

    def get_sums(total):
        return [
            jnp.concatenate([total[base + k : base + k + 1] for k in range(spread)], axis=1)
            for base in (0, spread)
        ]

    def to_twin(term, landing):
        return post.push(term.at[1 - at.core], landing, at.twin)

    def both_cores(pair, term, twin):
        pair.wait_recv()
        for step in range(1, at.chips):
            other = lax.rem(at.chip + step, at.chips)
            both = term[at.core, other].astype(f32) + twin[other].astype(f32)
            twin[other] = both.astype(low)

    def along(twin, landing):
        return [
            post.push(
                twin.at[other], landing.at[at.chip], {"space": other * 2 + at.core}
            )
            for other in [lax.rem(at.chip + step, at.chips) for step in range(1, at.chips)]
        ]

    def settle(arrivals, term, twin, landing):
        total = term[at.core, at.chip].astype(f32) + twin[at.chip].astype(f32)
        for made in arrivals:
            made.wait_recv()
        for step in range(1, at.chips):
            total = total + landing[lax.rem(at.chip + step, at.chips)].astype(f32)
        return total.astype(low)

    def to_tasks(share, landing):
        arrivals = [post.push(share, landing.at[task], {"task": other}) for other in at.other_tasks]
        landing[pl.ds(task, 1)] = share[...][None]
        return arrivals

    def expand_part(number):
        share = jnp.concatenate([l3x[a, number] for a in range(tasks)], axis=0)
        part = dot_nn(a2t[...], share).astype(low)
        per_band = part.shape[0] // bands
        for target in range(bands):
            e_term[target % 2, target // 2, :, number * piece : (number + 1) * piece] = part[
                target * per_band : (target + 1) * per_band
            ]

    narrow = mid // tasks
    my_lanes = pl.ds(pl.multiple_of(task * narrow, narrow), narrow)
    put_sums(
        st2, jnp.sum(grad, axis=0, keepdims=True), jnp.sum(grad * hat, axis=0, keepdims=True)
    )
    begun = at.sum_begin(post, "task", st2, st2_land)
    for made in l3_in:
        made.wait_recv()
    expand_part(0)
    st2_mid[...] = at.sum_end(begun)
    begun = at.sum_begin(post, "space", st2_mid, st2_land_b)
    for number in range(1, per_task):
        expand_part(number)
    e_pair = to_twin(e_term, e_twin)
    s2_out[...] = at.sum_end(begun)
    shift_grad, gain_grad = get_sums(s2_out[...])
    l2[my_rows] = (
        mask_mid
        * (v2_ref[2:3] * v2_ref[1:2])
        * (grad - shift_grad * inv_mid - hat * (gain_grad * inv_mid))
    ).astype(low)
    l2_in = [post.push(l2.at[my_rows], l2.at[my_rows], {"task": other}) for other in at.other_tasks]
    both_cores(e_pair, e_term, e_twin)
    e_in = along(e_twin, e_land)
    for made in l2_in:
        made.wait_recv()
    gate_in = [
        post.push(gate_low, gate_band.at[task], {"task": other}) for other in at.other_tasks
    ]
    gate_band[pl.ds(task, 1)] = gate_low[...][None]
    has_above, has_below = band > 0, band < bands - 1
    up = post.copy(l2, l2_halo.at[1], {"space": lax.rem(band + bands - 1, bands)})
    down = post.copy(l2, l2_halo.at[0], {"space": lax.rem(band + 1, bands)})

    @pl.when(has_above)
    def _():
        up.start()

    @pl.when(has_below)
    def _():
        down.start()

    @pl.when(jnp.logical_not(has_above))
    def _():
        l2_halo[0] = jnp.zeros_like(l2)

    @pl.when(jnp.logical_not(has_below))
    def _():
        l2_halo[1] = jnp.zeros_like(l2)

    p_passed = []
    for step, made in enumerate(p_far, start=1):
        made.wait_recv()
        block = p_all.at[lax.rem(at.chip + at.chips - step, at.chips) * 2 + at.core]
        p_passed.append(post.push(block, block, at.twin))
    loaded("wd")
    halves = [slice(start, start + piece) for start in range(0, mid, piece)]
    for lanes in halves:
        total = None
        for col_tap in range(3):
            part = shift_pixels(
                dot_nt(l2[...], wd[3 + col_tap, lanes, :]), -CONV_DILATION * (col_tap - 1), cols
            )
            total = part if total is None else total + part
        ag1[:, lanes] = total

    @pl.when(has_below)
    def _():
        up.wait_recv()

    @pl.when(has_above)
    def _():
        down.wait_recv()

    for lanes in halves:
        total = None
        for col_tap in range(3):
            part = dot_nt(l2_halo[1], wd[col_tap, lanes, :]) + dot_nt(
                l2_halo[0], wd[6 + col_tap, lanes, :]
            )
            part = shift_pixels(part, -CONV_DILATION * (col_tap - 1), cols)
            total = part if total is None else total + part
        ag1[:, lanes] += total

    pixels = ag1.shape[0]
    chunk = pixels // 8

    def first_rows(number):
        return pl.ds(pl.multiple_of(number * chunk, chunk), chunk)

    def first_step(number, sums):
        rows = first_rows(number)
        hat = (h1_ref[rows] - v1_ref[0:1]) * v1_ref[1:2]
        keep = jnp.concatenate([mask_ref[rows]] * spread, axis=1)
        grad = gelu_slope(v1_ref[2:3] * hat + v1_ref[3:4]) * ag1[rows] * keep
        ag1[rows] = grad
        return (
            sums[0] + jnp.sum(grad, axis=0, keepdims=True),
            sums[1] + jnp.sum(grad * hat, axis=0, keepdims=True),
        )

    nothing = jnp.zeros((1, mid), f32)
    first, second = lax.fori_loop(0, 8, first_step, (nothing, nothing))
    put_sums(st1, first, second)
    begun = at.sum_begin(post, "space", st1, st1_land)
    l2c[pl.ds(band, 1)] = l2[:, my_lanes][None]
    l2_block = l2c.at[band]
    d_far = [
        post.push(
            l2_block,
            l2_block,
            {"space": lax.rem(at.chip + step, at.chips) * 2 + at.core},
        )
        for step in range(1, at.chips)
    ]
    d_near = [post.push(l2_block, l2_block, at.twin)]
    e_share[...] = settle(e_in, e_term, e_twin, e_land)
    s1_out[...] = at.sum_end(begun)
    shift_grad, gain_grad = get_sums(s1_out[...])
    shift_grad, gain_grad = shift_grad * inv_mid, gain_grad * inv_mid

    def first_finish(number, carry):
        rows = first_rows(number)
        hat = (h1_ref[rows] - v1_ref[0:1]) * v1_ref[1:2]
        keep = jnp.concatenate([mask_ref[rows]] * spread, axis=1)
        l1[rows] = (
            keep * (v1_ref[2:3] * v1_ref[1:2]) * (ag1[rows] - shift_grad - hat * gain_grad)
        ).astype(low)
        return carry

    lax.fori_loop(0, 8, first_finish, 0)

    share_r = l1[:, my_lanes]
    per_band_r = wide // bands

    def reduce_step(number, carry):
        rows = pl.ds(pl.multiple_of(number * per_band_r, per_band_r), per_band_r)
        r_term[lax.rem(number, 2), number // 2] = dot_nn(xt[rows, :], share_r).astype(low)
        return carry

    lax.fori_loop(0, bands, reduce_step, 0)
    r_pair = to_twin(r_term, r_twin)
    e_back = to_tasks(e_share, e_tasks)
    both_cores(r_pair, r_term, r_twin)
    r_in = along(r_twin, r_land)

    for step, made in enumerate(d_far, start=1):
        made.wait_recv()
        block = l2c.at[lax.rem(at.chip + at.chips - step, at.chips) * 2 + at.core]
        d_near.append(post.push(block, block, at.twin))

    loaded("wr")
    for made in gate_in:
        made.wait_recv()

    def input_step(number, carry):
        lanes = pl.ds(pl.multiple_of(number * piece, piece), piece)
        gates = jnp.concatenate([gate_band[a, number] for a in range(tasks)], axis=0).astype(f32)
        ig_out[:, lanes] = (dot_nt(l1[...], wr[lanes, :]) + gates).astype(low)
        return carry

    lax.fori_loop(0, bands, input_step, 0)
    write(ig_out, ig_hbm)
    for source, target in ((tw_out, tw_hbm), (s3_out, s3_hbm), (s2_out, s2_hbm), (s1_out, s1_hbm)):
        write(source, target)
    for made in d_near:
        made.wait_recv()
    d_sum[...] = jnp.zeros_like(d_sum)

    def dilated_step(number, carry):
        left = jnp.concatenate([act_ref[number + row_tap] for row_tap in range(3)], axis=0)
        right = l2c[number].astype(f32)
        for col_tap in range(3):
            moved = shift_pixels(right, -CONV_DILATION * (col_tap - 1), cols).astype(low)
            d_sum[col_tap] += dot_nn(left, moved)
        return carry

    lax.fori_loop(0, bands, dilated_step, 0)
    part = d_share.shape[1]
    for row_tap in range(3):
        for col_tap in range(3):
            d_share[3 * row_tap + col_tap] = d_sum[
                col_tap, row_tap * part : (row_tap + 1) * part
            ].astype(low)
    d_back = to_tasks(d_share, d_tasks)
    r_share[...] = settle(r_in, r_term, r_twin, r_land)
    r_back = to_tasks(r_share, r_tasks)
    for made in [p_near] + p_passed:
        made.wait_recv()
    pg_out[...] = p_all[...]
    write(pg_out, pg_hbm)
    for made in e_back:
        made.wait_recv()
    broad = wide // tasks
    for a in range(tasks):
        eg_out[:, a * broad : (a + 1) * broad] = e_tasks[a].astype(f32)
    write(eg_out, eg_hbm)
    for made in d_back:
        made.wait_recv()
    for a in range(tasks):
        dg_out[:, :, a * narrow : (a + 1) * narrow] = d_tasks[a].astype(f32)
    write(dg_out, dg_hbm)
    for made in r_back:
        made.wait_recv()
    for a in range(tasks):
        rg_out[:, a * narrow : (a + 1) * narrow] = r_tasks[a].astype(f32)
    write(rg_out, rg_hbm)
    post.close()

    @pl.when(has_above)
    def _():
        up.wait_send()

    @pl.when(has_below)
    def _():
        down.wait_send()


def head_phase(
    at,
    post,
    plan,
    rate_loads,
    sh_ref,
    widths_ref,
    gain_ref,
    shift_ref,
    cot_ref,
    bw_ref,
    pw_ref,
    head_out,
    xg_out,
    grads_out,
    proj_share,
    both_sums_out,
    proj_sums_out,
    rate,
    turned,
    extra,
    term,
    twin_land,
    right_land,
    left_land,
    pre,
    joined,
    upstream,
    cot,
    out_rows,
    masks,
    projected,
    proj_up,
    proj_low,
    pixel_sum,
    st_both,
    st_both_sum,
    st_both_land,
    st_proj,
    st_proj_sum,
    st_proj_land,
    st_pback,
    st_pback_land,
    st_back,
    st_back_land,
    st_rim_sum,
    st_rim,
    st_rim_land,
    both_all,
    moved,
    grads,
    back,
    sg,
    proj_term,
    p_twin,
    p_land,
):
    tasks, bands, cols, pixels, width, taps, extras = plan
    low, f32 = jnp.bfloat16, jnp.float32
    send_sem, recv_sem = post.send_sem, post.recv_sem
    chips, chip, core, band = at.chips, at.chip, at.core, at.band
    last, half = chips - 1, chips // 2
    group = 2 * pixels
    band_rows = pixels // cols
    spread = width // LANE
    number_of = {tap[:3]: number for number, tap in enumerate(taps)}
    moved_levels = sorted({entry[0] for entry in extras})
    late = sorted({entry[2] for entry in extras})
    slots = moved_levels + [branch for branch in range(4) if branch not in moved_levels]
    side = chip // half
    is_end = (chip == 0) | (chip == last)
    next_chip = lax.rem(chip + 1, chips)
    prev_chip = lax.rem(chip + last, chips)
    own = side * (half - 1)

    def reserve(count):
        first = post.used
        post.used += count
        return first

    def hop(source, landing, device_chip, number):
        return pltpu.make_async_remote_copy(
            source,
            landing,
            send_sem.at[number],
            recv_sem.at[number],
            device_id={"space": device_chip * 2 + core},
            device_id_type=MESH_ID,
        )

    def to_twin(source, landing, number):
        return pltpu.make_async_remote_copy(
            source,
            landing,
            send_sem.at[number],
            recv_sem.at[number],
            device_id=at.twin,
            device_id_type=MESH_ID,
        )

    first_cot = reserve(half)

    def send_cot(number):
        return hop(cot_ref, cot.at[number], side * last, first_cot + number)

    for load in rate_loads:
        load.wait()
    cot[pl.ds(own, 1)] = cot_ref[...][None]

    @pl.when(jnp.logical_not(is_end))
    def _():
        send_cot(chip - side * half).start()

    def rows_of(ref, number):
        return jnp.concatenate([ref[2 * number], ref[2 * number + 1]], axis=0)

    def right_of(level, col_tap):
        return (col_tap - 1) * level * RATE

    def forward_taps(source, level, row_tap):
        total = None
        for col_tap in range(3):
            number = number_of.get((level, row_tap, col_tap))
            if number is None:
                continue
            part = shift_pixels(
                dot_nn(source, rate[number]), right_of(level, col_tap), cols
            )
            total = part if total is None else total + part
        return total

    extra[...] = jnp.zeros_like(extra)
    for level, target, source, row_tap in extras:
        extra[moved_levels.index(level), target // last] += forward_taps(
            rows_of(sh_ref, source), level, row_tap
        )

    first_twin = reserve(4 * chips)

    def twin_term(number, branch):
        return to_twin(
            term.at[number, 1 - core, branch],
            twin_land.at[number, branch],
            first_twin + 4 * number + branch,
        )

    def forward_group(step, carry):
        number = lax.rem(step + half * (1 - side), chips)
        at_rim = jnp.where(lax.rem(number, last) == 0, 1.0, 0.0)
        source = rows_of(sh_ref, number)
        for branch in slots:
            if branch == 0:
                value = dot_nn(source, bw_ref[:, :width])
            else:
                value = forward_taps(source, branch, 1)
                if branch in moved_levels:
                    value = value + at_rim * extra[moved_levels.index(branch), number // last]
            value = value.astype(low)
            term[number, 0, branch] = value[:pixels]
            term[number, 1, branch] = value[pixels:]
            twin_term(number, branch).start()
        return carry

    first_right, first_left = reserve(8 * half), reserve(8 * half)
    portion = pixels // 2

    def rows_at(part):
        return pl.ds(part * portion, portion)

    def go_right(number, branch, part):
        return hop(
            twin_land.at[half + number, branch, rows_at(part)],
            right_land.at[number, branch, rows_at(part)],
            next_chip,
            first_right + 8 * number + 2 * branch + part,
        )

    def go_left(number, branch, part):
        return hop(
            twin_land.at[number, branch, rows_at(part)],
            left_land.at[number, branch, rows_at(part)],
            prev_chip,
            first_left + 8 * number + 2 * branch + part,
        )

    def both_cores(number, branch):
        twin_term(number, branch).wait_recv()
        return term[number, core, branch].astype(f32) + twin_land[number, branch].astype(f32)

    def start_off(number, copy_of):
        for branch in slots:
            twin_land[number, branch] = both_cores(number, branch).astype(low)
            for part in range(2):
                copy_of(branch, part).start()

    for number in range(half):
        lax.fori_loop(number, number + 1, forward_group, 0)

        @pl.when(chip == 0)
        def _():
            start_off(half + number, functools.partial(go_right, number))

        @pl.when(chip == last)
        def _():
            start_off(number, functools.partial(go_left, number))

    lax.fori_loop(half, chips, forward_group, 0)

    def pass_on(number, branch, part, copy, landing):
        if part == 0:
            twin_term(number, branch).wait_recv()
        copy.wait_recv()
        rows = rows_at(part)
        twin_land[number, branch, rows] = (
            term[number, core, branch, rows].astype(f32)
            + twin_land[number, branch, rows].astype(f32)
            + landing[rows].astype(f32)
        ).astype(low)
        copy.start()

    def pass_right(number, branch, part):
        landing = right_land.at[number, branch]
        pass_on(half + number, branch, part, go_right(number, branch, part), landing)

    def pass_left(number, branch, part):
        landing = left_land.at[number, branch]
        pass_on(number, branch, part, go_left(number, branch, part), landing)

    order = [
        (number, branch, part) for number in range(half) for branch in slots for part in range(2)
    ]

    def pass_both(near, far):
        for step in range(len(order) + FAR_LAG):
            if step < len(order):
                near(*order[step])
            if step >= FAR_LAG:
                far(*order[step - FAR_LAG])

    @pl.when(jnp.logical_not(is_end) & (side == 0))
    def _():
        pass_both(pass_right, pass_left)

    @pl.when(jnp.logical_not(is_end) & (side == 1))
    def _():
        pass_both(pass_left, pass_right)

    pixel_sum[...] = jnp.zeros_like(pixel_sum)

    def turn_group(number, carry):
        source = rows_of(sh_ref, number)
        turned[:, pl.ds(pl.multiple_of(number * group, group), group)] = source.T
        pixel_sum[0:1] += jnp.sum(source.astype(f32), axis=0, keepdims=True)
        return carry

    lax.fori_loop(0, chips, turn_group, 0)
    inv_count = jnp.concatenate([1.0 / count_pixels(widths_ref)] * spread, axis=1)

    def put_rows(target, number, value):
        for part in range(spread):
            target[pl.ds(number * spread + part, 1), :] = value[:, part * LANE : (part + 1) * LANE]

    def add_rows(target, number, value):
        for part in range(spread):
            target[pl.ds(number * spread + part, 1), :] += value[
                :, part * LANE : (part + 1) * LANE
            ]

    def get_rows(target, number):
        return jnp.concatenate(
            [target[pl.ds(number * spread + part, 1), :] for part in range(spread)], axis=1
        )

    def column_sum(value):
        return jnp.sum(value, axis=0, keepdims=True)

    def mask_of(number):
        return jnp.concatenate([masks[number]] * spread, axis=1)

    for target in (st_both, st_proj, st_pback, st_back, st_rim):
        target[...] = jnp.zeros_like(target)
    for number in range(half):
        masks[number] = row_mask(
            widths_ref, (2 * (side * half + number) + core) * band_rows, band_rows, cols
        )

    def settle(copy_of, landing):
        def step_of(step, carry):
            number, branch = step // 4, lax.rem(step, 4)
            total = both_cores(side * half + number, branch)
            for part in range(2):
                copy_of(number, branch, part).wait_recv()
            value = total + landing[number, branch].astype(f32)
            pre[number, branch] = value
            kept = value * mask_of(number)
            add_rows(st_both, branch, column_sum(kept))
            add_rows(st_both, 4 + branch, column_sum(kept * value))
            return carry

        lax.fori_loop(0, 4 * half, step_of, 0)

    @pl.when(chip == 0)
    def _():
        settle(go_left, left_land)

    @pl.when(chip == last)
    def _():
        settle(go_right, right_land)

    sums_now = pixel_sum[0:1]
    high = sums_now.astype(low)
    rest = sums_now - high.astype(f32)
    middle = rest.astype(low)
    tail = (rest - middle.astype(f32)).astype(low)
    pieces = jnp.concatenate(
        [high.astype(f32), middle.astype(f32), tail.astype(f32), jnp.zeros((13, width), f32)],
        axis=0,
    ).astype(low)
    put_rows(st_both, 8, column_sum(dot_nn(pieces, bw_ref[:, width:])))
    st_both_sum[...] = at.sum_over(post, "space", st_both, st_both_land)
    pooled = get_rows(st_both_sum, 8) * inv_count

    def lanes_of(number):
        return pl.ds(pl.multiple_of(number * width, width), width)

    def scale_of(target, first, second):
        mean_value = get_rows(target, first) * inv_count
        variance = get_rows(target, second) * inv_count - mean_value * mean_value
        return mean_value, lax.rsqrt(variance + NORM_EPS)

    def at_ends(body, count):
        @pl.when(is_end)
        def _():
            lax.fori_loop(0, count, body, 0)

    pool_lanes = slice(4 * width, 5 * width)

    def pool_step(number, carry):
        joined[number, 4] = (
            gelu_of(pooled).astype(low).astype(f32) * mask_of(number)
        ).astype(low)
        projected[number] = dot_nn(joined[number, 4], pw_ref[pool_lanes, :])
        return carry

    at_ends(pool_step, half)

    def activate(step, carry):
        number, branch = step // 4, lax.rem(step, 4)
        mean_value, inv_std = scale_of(st_both_sum, branch, 4 + branch)
        hat = (pre[number, branch] - mean_value) * inv_std
        pre[number, branch] = hat
        normed = gain_ref[:, lanes_of(branch)] * hat + shift_ref[:, lanes_of(branch)]
        active, slope = gelu_both(normed)
        keep = mask_of(number)
        active = (active * keep).astype(low)
        upstream[number, branch] = slope * keep
        joined[number, branch] = active
        projected[number] += dot_nn(active, pw_ref[lanes_of(branch), :])
        return carry

    at_ends(activate, 4 * half)

    def project_sums(number, carry):
        value = projected[number]
        kept = value * mask_of(number)
        add_rows(st_proj, 0, column_sum(kept))
        add_rows(st_proj, 1, column_sum(kept * value))
        return carry

    at_ends(project_sums, half)
    st_proj_sum[...] = at.sum_over(post, "space", st_proj, st_proj_land)
    proj_mean, proj_inv = scale_of(st_proj_sum, 0, 1)
    gain_proj = gain_ref[:, pool_lanes]

    def proj_back(number, carry):
        hat = (projected[number] - proj_mean) * proj_inv
        projected[number] = hat
        normed = gain_proj * hat + shift_ref[:, pool_lanes]
        keep = mask_of(number)
        active, slope = gelu_both(normed)
        up = slope * cot[number].astype(f32) * keep
        proj_up[number] = up
        add_rows(st_pback, 0, column_sum(up))
        add_rows(st_pback, 1, column_sum(up * hat))
        out_rows[number] = (active * keep).astype(low)
        return carry

    @pl.when(is_end)
    def _():
        for number in range(half):

            @pl.when(own != number)
            def _():
                send_cot(number).wait_recv()

    at_ends(proj_back, half)
    proj_sums_out[...] = at.sum_over(post, "space", st_pback, st_pback_land)
    shift_proj, gain_grad_proj = get_rows(proj_sums_out, 0), get_rows(proj_sums_out, 1)

    def proj_finish(number, carry):
        keep = mask_of(number)
        proj_low[number] = (
            keep
            * (gain_proj * proj_inv)
            * (
                proj_up[number]
                - shift_proj * inv_count
                - projected[number] * (gain_grad_proj * inv_count)
            )
        ).astype(low)
        return carry

    def pool_back(number, carry):
        joined_grad = dot_nt(proj_low[number], pw_ref[pool_lanes, :])
        add_rows(st_back, 8, column_sum(joined_grad * mask_of(number)))
        return carry

    def back_step(branch):
        def step_of(number, carry):
            joined_grad = dot_nt(proj_low[number], pw_ref[lanes_of(branch), :])
            hat = pre[number, branch]
            up = upstream[number, branch] * joined_grad
            upstream[number, branch] = up
            shift_sum, gain_sum = column_sum(up), column_sum(up * hat)
            add_rows(st_back, branch, shift_sum)
            add_rows(st_back, 4 + branch, gain_sum)
            if branch == slots[0]:
                add_rows(st_rim, 0, shift_sum)
                add_rows(st_rim, 1, gain_sum)
            return carry

        return step_of

    at_ends(proj_finish, half)
    at_ends(back_step(slots[0]), half)
    begun_rim = at.sum_begin(post, "space", st_rim, st_rim_land)
    at_ends(pool_back, half)
    for branch in slots[1:]:
        at_ends(back_step(branch), half)
    begun_back = at.sum_begin(post, "space", st_back, st_back_land)
    st_rim_sum[...] = at.sum_end(begun_rim)

    order = [(number, branch) for branch in moved_levels for number in range(half)]
    order += [
        (number, branch)
        for number in range(half)
        for branch in slots
        if branch not in moved_levels
    ]
    first_right_all, first_left_all = reserve(8 * half), reserve(8 * half)
    first_twin_all, first_out = reserve(8 * chips), reserve(half)

    def block_of(number, branch, part):
        return both_all.at[number * 2 + core, branch, rows_at(part)]

    def along_right(number, branch, part):
        block = block_of(number, branch, part)
        return hop(block, block, next_chip, first_right_all + 8 * number + 2 * branch + part)

    def along_left(number, branch, part):
        block = block_of(half + number, branch, part)
        return hop(block, block, prev_chip, first_left_all + 8 * number + 2 * branch + part)

    def hand_over(number, branch, part):
        block = block_of(number, branch, part)
        return to_twin(block, block, first_twin_all + 8 * number + 2 * branch + part)

    def make_both(number, branch):
        _, inv_std = scale_of(st_both_sum, branch, 4 + branch)
        if branch == slots[0]:
            sums = get_rows(st_rim_sum, 0), get_rows(st_rim_sum, 1)
        else:
            sums = get_rows(both_sums_out, branch), get_rows(both_sums_out, 4 + branch)
        shift_grad, gain_grad = sums[0] * inv_count, sums[1] * inv_count
        both_all[2 * (side * half + number) + core, branch] = (
            mask_of(number)
            * (gain_ref[:, lanes_of(branch)] * inv_std)
            * (upstream[number, branch] - shift_grad - pre[number, branch] * gain_grad)
        ).astype(low)

    parts = [(number, branch, part) for number, branch in order for part in range(2)]
    by_halves = [entry for entry in order[half:] if entry[0] == half - 1]
    parts = parts[: -2 * len(by_halves)]
    parts += [entry + (part,) for part in range(2) for entry in by_halves]

    def send_out(number):
        return hop(out_rows.at[number], head_out, side * half + number, first_out + number)

    def send_parts(some):
        made = set()
        for number, branch, part in some:
            if (number, branch) not in made:
                make_both(number, branch)
                made.add((number, branch))

            @pl.when(chip == 0)
            def _():
                along_right(number, branch, part).start()
                hand_over(number, branch, part).start()

            @pl.when(chip == last)
            def _():
                along_left(number, branch, 1 - part).start()
                hand_over(half + number, branch, 1 - part).start()

    @pl.when(is_end)
    def _():
        send_parts([entry for entry in parts if entry[1] == slots[0]])

    both_sums_out[...] = at.sum_end(begun_back)
    pool_grad = (gelu_slope(pooled) * get_rows(both_sums_out, 8)).astype(low)

    @pl.when(is_end)
    def _():
        send_parts([entry for entry in parts if entry[1] != slots[0]])
        for number in range(half):

            @pl.when(own != number)
            def _():
                send_out(number).start()

        head_out[...] = out_rows[own]

    def proj_step(branch, carry):
        total = dot_nn(joined[0, branch].T, proj_low[0])
        for number in range(1, half):
            total = total + dot_nn(joined[number, branch].T, proj_low[number])
        proj_term[lanes_of(branch), :] = total.astype(low)
        return carry

    at_ends(proj_step, 5)

    rows_p = proj_share.shape[0]

    def proj_rows(number):
        return pl.ds(pl.multiple_of(number * rows_p, rows_p), rows_p)

    first_pair, first_p = reserve(chips), reserve(2 * chips)

    def p_pair(number):
        return to_twin(
            proj_term.at[proj_rows(2 * number + 1 - core)], p_twin.at[number], first_pair + number
        )

    def p_hop(end, number):
        return hop(p_twin.at[number], p_land.at[end], number, first_p + end * chips + number)

    @pl.when(is_end)
    def _():
        for number in range(chips):
            p_pair(number).start()

    def send_projection():
        for number in range(chips):
            p_pair(number).wait_recv()
            both = proj_term[proj_rows(2 * number + core)].astype(f32)
            p_twin[number] = (both + p_twin[number].astype(f32)).astype(low)

            @pl.when(chip != number)
            def _():
                p_hop(side, number).start()

    grads[...] = jnp.zeros_like(grads)
    pool_row = dot_nt(
        jnp.broadcast_to(pool_grad, (16, width)), bw_ref[:, width:]
    )[0:1] * inv_count
    quarter = pixels // tasks
    my_rows = pl.ds(pl.multiple_of(at.task * quarter, quarter), quarter)
    first_task = reserve(chips * len(at.other_tasks))

    def to_task(number, turn):
        other = at.other_tasks[turn]
        theirs = pl.ds(pl.multiple_of(other * quarter, quarter), quarter)
        two = pl.ds(2 * number, 2)
        spot = first_task + number * len(at.other_tasks) + turn
        return pltpu.make_async_remote_copy(
            sg.at[two, theirs],
            xg_out.at[at.task, two],
            send_sem.at[spot],
            recv_sem.at[spot],
            device_id={"task": other},
            device_id_type=MESH_ID,
        )

    def finish_group(number, part=None):
        some = band_rows if part is None else band_rows // 2
        for place in range(2):
            first = (2 * number + place) * band_rows + (0 if part is None else part * some)
            keep = row_mask(widths_ref, first, some, cols)
            keep = jnp.concatenate([keep] * spread, axis=1)
            start = 0 if part is None else part * portion
            rows = slice(start, start + some * cols)
            value = back[number, place * pixels + start : place * pixels + start + some * cols]
            sg[2 * number + place, rows] = (value + keep * pool_row).astype(low)

        def there(task):
            return task >= 0 if part is None else task // (tasks // 2) == part

        for turn, other in enumerate(at.other_tasks):

            @pl.when(there(other))
            def _():
                to_task(number, turn).start()

        @pl.when(there(at.task))
        def _():
            for place in range(2):
                xg_out[at.task, 2 * number + place] = sg[2 * number + place, my_rows]

    def back_part(number, branch, part=None):
        for piece in range(2) if part is None else (part,):
            hand_over(number, branch, piece).wait_recv()
        rows = slice(0, pixels) if part is None else slice(part * portion, (part + 1) * portion)
        count = rows.stop - rows.start
        starts = [(2 * number + place) * pixels + rows.start for place in range(2)]
        columns = jnp.concatenate([turned[:, start : start + count] for start in starts], axis=1)
        image = jnp.concatenate(
            [both_all[2 * number, branch, rows], both_all[2 * number + 1, branch, rows]], axis=0
        )
        if branch == 0:
            total = dot_nt(image, bw_ref[:, :width])
            grads[len(taps)] += dot_nn(columns, image)
        else:
            total = None
            image = image.astype(f32)
            for col_tap in range(3):
                tap = number_of.get((branch, 1, col_tap))
                if tap is None:
                    continue
                moved_now = shift_pixels(image, -right_of(branch, col_tap), cols).astype(low)
                if branch in moved_levels and number in late:
                    moved[moved_levels.index(branch), number // last, col_tap] = moved_now
                now = dot_nt(moved_now, rate[tap])
                total = now if total is None else total + now
                grads[tap] += dot_nn(columns, moved_now)
        for place in range(2):
            target = slice(place * pixels + rows.start, place * pixels + rows.stop)
            share = total[place * count : (place + 1) * count]
            if branch == slots[0]:
                back[number, target] = share
            else:
                back[number, target] += share

    def far_taps():
        for level, target, source, row_tap in extras:
            columns = turned[:, source * group : (source + 1) * group]
            total = back[source]
            for col_tap in range(3):
                tap = number_of.get((level, row_tap, col_tap))
                if tap is None:
                    continue
                part = moved[moved_levels.index(level), target // last, col_tap]
                total = total + dot_nt(part, rate[tap])
                grads[tap] += dot_nn(columns, part)
            back[source] = total

    def take_right(number, branch, part):
        along_right(number, branch, part).wait_recv()

        @pl.when(chip < last)
        def _():
            along_right(number, branch, part).start()

        hand_over(number, branch, part).start()

    def take_left(number, branch, part):
        along_left(number, branch, part).wait_recv()

        @pl.when(chip > 0)
        def _():
            along_left(number, branch, part).start()

        hand_over(half + number, branch, part).start()

    for step in range(len(parts) + FAR_LAG + 1):
        if step < len(parts):
            number, branch, part = parts[step]

            @pl.when(jnp.logical_not(is_end) & (side == 0))
            def _():
                take_right(number, branch, part)

            @pl.when(jnp.logical_not(is_end) & (side == 1))
            def _():
                take_left(number, branch, 1 - part)

        if FAR_LAG <= step < len(parts) + FAR_LAG:
            number, branch, part = parts[step - FAR_LAG]

            @pl.when(side == 0)
            def _():
                take_left(number, branch, 1 - part)

            @pl.when(side == 1)
            def _():
                take_right(number, branch, part)

        if step == len(parts) + SEND_LAG:

            @pl.when(is_end)
            def _():
                send_projection()

        done = step - FAR_LAG - 1
        if done < 0:
            continue
        number, branch, part = parts[done]
        if (number, branch) in by_halves:
            back_part(number, branch, part)
            back_part(half + number, branch, 1 - part)
            if (number, branch) == by_halves[-1]:
                finish_group(number, part)
                finish_group(half + number, 1 - part)
        elif part == 1:
            back_part(number, branch)
            back_part(half + number, branch)
            if (number, branch) == order[half - 1]:
                far_taps()
            if branch == slots[3]:
                finish_group(number)
                finish_group(half + number)

    column = jnp.broadcast_to(pixel_sum[0:1], (8, width)).T[:, 0:1]
    grads_out[len(taps) + 1] = (column * (pool_grad.astype(f32) * inv_count)).astype(low)

    def finish_tap(number, carry):
        grads_out[number] = grads[number].astype(low)
        return carry

    lax.fori_loop(0, len(taps) + 1, finish_tap, 0)
    for end in range(2):

        @pl.when(chip == end * last)
        def _():
            p_land[end] = p_twin[end * last]

        @pl.when(chip != end * last)
        def _():
            p_hop(end, chip).wait_recv()

    proj_share[...] = (p_land[0].astype(f32) + p_land[1].astype(f32)).astype(low)

    def tasks_in(number, carry):
        for turn in range(len(at.other_tasks)):
            to_task(number, turn).wait()
        return carry

    lax.fori_loop(0, chips, tasks_in, 0)

    @pl.when(jnp.logical_not(is_end))
    def _():
        send_out(chip - side * half).wait_recv()
        send_cot(chip - side * half).wait_send()

    post.close()

    def twin_left(number, carry):
        for branch in range(4):
            twin_term(number, branch).wait_send()
            for part in range(2):
                hand_over(number, branch, part).wait_send()
        return carry

    lax.fori_loop(0, chips, twin_left, 0)

    def line_left(number, carry):
        for branch in range(4):
            for part in range(2):

                @pl.when(chip < last)
                def _():
                    go_right(number, branch, part).wait_send()
                    along_right(number, branch, part).wait_send()

                @pl.when(chip > 0)
                def _():
                    go_left(number, branch, part).wait_send()
                    along_left(number, branch, part).wait_send()

        return carry

    lax.fori_loop(0, half, line_left, 0)

    @pl.when(is_end)
    def _():
        for number in range(half):

            @pl.when(own != number)
            def _():
                send_out(number).wait_send()

        for number in range(chips):
            p_pair(number).wait_send()

            @pl.when(chip != number)
            def _():
                p_hop(side, number).wait_send()


def trunk_phase(
    at,
    post,
    sizes,
    when_loaded,
    norm_loads,
    x_hbm,
    widths_ref,
    gain_ref,
    shift_ref,
    wr_hbm,
    wd_hbm,
    we_hbm,
    sh_out,
    act,
    h1,
    h2,
    a2,
    h3q,
    v1,
    v2,
    v3,
    stats_out,
    x,
    wr,
    wd,
    we,
    rim,
    turned,
    h3,
    blocks,
    mask_own,
    st1,
    st1_land,
    st2,
    st2_land,
    st3,
    st3_land,
    local_sem,
):
    tasks, bands, cols, quarter, mid, wide, piece = sizes
    low, f32 = jnp.bfloat16, jnp.float32
    task, band = at.task, at.band
    my_rows = pl.ds(pl.multiple_of(task * quarter, quarter), quarter)
    depth = x.shape[1] // 4
    pieces = []
    for number in range(4):
        some = slice(number * depth, (number + 1) * depth)
        pieces.append(
            (
                some,
                pltpu.make_async_copy(x_hbm.at[:, some], x.at[:, some], local_sem.at[2 * number]),
                pltpu.make_async_copy(wr_hbm.at[some], wr.at[some], local_sem.at[2 * number + 1]),
            )
        )
    for _, of_x, of_weight in pieces:
        of_x.start()
        of_weight.start()
    loads = [
        pltpu.make_async_copy(wd_hbm, wd, local_sem.at[8]),
        pltpu.make_async_copy(we_hbm, we, local_sem.at[9]),
    ]
    at.greet()
    pixels = x.shape[0]
    band_rows = pixels // cols
    mask = row_mask(widths_ref, band * band_rows, band_rows, cols)
    count = count_pixels(widths_ref)
    spread = mid // LANE

    def across(value, lanes):
        return jnp.concatenate([value] * (lanes // LANE), axis=1)

    def put_sums(target, value, keep):
        kept = value * keep
        first = jnp.sum(kept, axis=0, keepdims=True)
        second = jnp.sum(kept * value, axis=0, keepdims=True)
        for number in range(spread):
            lanes = slice(number * LANE, (number + 1) * LANE)
            target[number : number + 1] = first[:, lanes]
            target[spread + number : spread + number + 1] = second[:, lanes]

    def get_sums(total):
        return [
            jnp.concatenate([total[base + k : base + k + 1] for k in range(spread)], axis=1)
            for base in (0, spread)
        ]

    def put_norm(vectors, lanes, first, second, start):
        width = first.shape[1]
        inv = across(1.0 / count, width)
        mean_value = first * inv
        variance = second * inv - mean_value * mean_value
        vectors[0:1, lanes] = mean_value
        vectors[1:2, lanes] = lax.rsqrt(variance + NORM_EPS)
        vectors[2:3, lanes] = gain_ref[:, start : start + width]
        vectors[3:4, lanes] = shift_ref[:, start : start + width]
        stats_out[0:1, start : start + width] = mean_value
        stats_out[1:2, start : start + width] = variance * across(count / (count - 1.0), width)

    def activate(hidden, vectors, keep):
        normed = vectors[2:3] * ((hidden - vectors[0:1]) * vectors[1:2]) + vectors[3:4]
        return (gelu_of(normed) * keep).astype(low)

    mask_mid = across(mask, mid)
    for number, (some, of_x, of_weight) in enumerate(pieces):
        of_x.wait()
        of_weight.wait()
        term = dot_nn(x[:, some], wr[some])
        if number == 0:
            h1[...] = term
        else:
            h1[...] += term
    for load in loads:
        load.start()
    at.meet()
    put_sums(st1, h1[...], mask_mid)
    begun = at.sum_begin(post, "space", st1, st1_land)
    for load in norm_loads:
        load.wait()
    first, second = get_sums(at.sum_end(begun))
    when_loaded()
    put_norm(v1, slice(0, mid), first, second, 0)
    rim[1] = activate(h1[...], v1, mask_mid)

    has_above, has_below = band > 0, band < bands - 1
    up = post.copy(rim.at[1], rim.at[2], {"space": lax.rem(band + bands - 1, bands)})
    down = post.copy(rim.at[1], rim.at[0], {"space": lax.rem(band + 1, bands)})

    @pl.when(has_above)
    def _():
        up.start()

    @pl.when(has_below)
    def _():
        down.start()

    @pl.when(jnp.logical_not(has_above))
    def _():
        rim[0] = jnp.zeros(rim.shape[1:], low)

    @pl.when(jnp.logical_not(has_below))
    def _():
        rim[2] = jnp.zeros(rim.shape[1:], low)

    loads[0].wait()
    halves = [slice(start, start + piece) for start in range(0, mid, piece)]

    def tap_sum(row_taps, lanes):
        total = None
        for col_tap in range(3):
            part = None
            for row_tap in row_taps:
                term = dot_nn(rim[row_tap], wd[3 * row_tap + col_tap, :, lanes])
                part = term if part is None else part + term
            part = shift_pixels(part, CONV_DILATION * (col_tap - 1), cols)
            total = part if total is None else total + part
        return total

    for lanes in halves:
        h2[:, lanes] = tap_sum((1,), lanes)

    turned[...] = rim[1].T

    @pl.when(has_below)
    def _():
        up.wait_recv()

    @pl.when(has_above)
    def _():
        down.wait_recv()

    for lanes in halves:
        h2[:, lanes] += tap_sum((0, 2), lanes)

    put_sums(st2, h2[...], mask_mid)
    first, second = get_sums(at.sum_over(post, "space", st2, st2_land))
    put_norm(v2, slice(0, mid), first, second, mid)
    a2[...] = activate(h2[...], v2, mask_mid)

    loads[1].wait()
    mask_piece = across(mask, piece)
    per_row = st3.shape[1] // piece
    half = st3.shape[0] // 2

    def expand_step(number, carry):
        lanes = pl.ds(pl.multiple_of(number * piece, piece), piece)
        value = dot_nn(a2[...], we[:, lanes])
        h3[:, lanes] = value
        kept = value * mask_piece
        row = number // per_row
        spot = pl.ds(pl.multiple_of(lax.rem(number, per_row) * piece, piece), piece)
        st3[pl.ds(row, 1), spot] = jnp.sum(kept, axis=0, keepdims=True)
        st3[pl.ds(half + row, 1), spot] = jnp.sum(kept * value, axis=0, keepdims=True)
        return carry

    lax.fori_loop(0, bands, expand_step, 0)
    begun = at.sum_begin(post, "space", st3, st3_land)
    h3q[...] = h3[my_rows]
    total = at.sum_end(begun)
    lanes_in = st3.shape[1]
    for row in range(half):
        put_norm(
            v3,
            slice(row * lanes_in, (row + 1) * lanes_in),
            total[row : row + 1],
            total[half + row : half + row + 1],
            2 * mid + row * lanes_in,
        )

    mask_own[...] = mask
    mask_quarter = across(mask_own[my_rows], piece)

    def shared_of(number):
        lanes = pl.ds(pl.multiple_of(number * piece, piece), piece)
        hat = (h3q[:, lanes] - v3[0:1, lanes]) * v3[1:2, lanes]
        before = v3[2:3, lanes] * hat + v3[3:4, lanes] + x[my_rows, lanes].astype(f32)
        return (gelu_of(before) * mask_quarter).astype(low)

    slices_in = []
    for other in at.other_bands:
        blocks[other] = shared_of(other)
        slices_in.append(
            post.push(blocks.at[other], sh_out.at[band, my_rows], {"space": other})
        )
    sh_out[band, my_rows] = shared_of(band)

    part = mid // bands

    def part_of(number):
        return turned.at[pl.ds(pl.multiple_of(number * part, part), part)]

    act[0] = jnp.zeros(act.shape[1:], low)
    act[bands + 1] = jnp.zeros(act.shape[1:], low)
    act[band + 1] = part_of(band)[...]
    parts_in = [
        post.push(part_of(other), act.at[band + 1], {"space": other}) for other in at.other_bands
    ]

    def to_tasks(number):
        block = sh_out.at[number, my_rows]
        return [post.push(block, block, {"task": other}) for other in at.other_tasks]

    quarters_in = to_tasks(band)
    for step, made in enumerate(slices_in, start=1):
        made.wait_recv()
        quarters_in += to_tasks(lax.rem(band + bands - step, bands))
    for made in quarters_in + parts_in:
        made.wait_recv()
    post.close()

    @pl.when(has_above)
    def _():
        up.wait_send()

    @pl.when(has_below)
    def _():
        down.wait_send()


class Held:
    def __init__(self, shape, dtype, passing=False):
        self.memory = pltpu.VMEM(shape, dtype)
        self.passing = passing


def with_phase(entries, refs, body):
    def run(*passing):
        passing, kept = list(passing), list(refs)
        body([(passing if entry.passing else kept).pop(0) for entry in entries])

    pl.run_scoped(run, *[entry.memory for entry in entries if entry.passing])


def whole_kernel(sizes, plan, phases, counts, *refs):
    refs = list(refs)

    def take(count):
        taken = refs[:count]
        del refs[:count]
        return taken

    x_hbm, widths, gain_hbm, shift_hbm, wr_hbm, wd_hbm, we_hbm = take(7)
    head_hbm_in = take(5)
    (rate_hbm,) = take(1)
    stats_hbm, head_hbm, grads_hbm, both_hbm, proj_hbm = take(5)
    back_hbm = take(counts[2])
    trunk_outs, head_outs = take(counts[0]), take(counts[1])
    gain, shift, *head_in = take(7)
    head_gain, head_shift, cot, bw, pw = head_in
    (shared,) = take(1)
    kept = [take(sum(not entry.passing for entry in entries)) for entries in phases]
    send_sem, recv_sem, local_sem, rate_sem, out_sem, in_sem = refs
    tasks, bands, width, taps = sizes[0], sizes[1], plan[4], plan[5]
    at = Place(tasks, bands)
    post = Post(send_sem, recv_sem)
    writes = []

    def write(source, target):
        copy = pltpu.make_async_copy(source, target, out_sem.at[len(writes)])
        copy.start()
        writes.append(copy)

    rate = kept[1][0]
    rate_loads = []
    for number, (level, row_tap, col_tap, _, _) in enumerate(taps):
        start = (9 * (level - 1) + 3 * row_tap + col_tap) * width
        rate_loads.append(
            pltpu.make_async_copy(
                rate_hbm.at[:, start : start + width], rate.at[number], rate_sem.at[number]
            )
        )

    norm_loads = [
        pltpu.make_async_copy(source, target, in_sem.at[number])
        for number, (source, target) in enumerate(((gain_hbm, gain), (shift_hbm, shift)))
    ]
    for load in norm_loads:
        load.start()
    rate_loads += [
        pltpu.make_async_copy(source, target, in_sem.at[2 + number])
        for number, (source, target) in enumerate(zip(head_hbm_in, head_in))
    ]

    def when_loaded():
        for load in rate_loads:
            load.start()

    def run_trunk(scratch):
        trunk_phase(
            at,
            post,
            sizes,
            when_loaded,
            norm_loads,
            x_hbm,
            widths,
            gain,
            shift,
            wr_hbm,
            wd_hbm,
            we_hbm,
            shared,
            *trunk_outs,
            *scratch,
            local_sem,
        )

    def run_head(scratch):
        head_phase(
            at,
            post,
            plan,
            rate_loads,
            shared,
            widths,
            head_gain,
            head_shift,
            cot,
            bw,
            pw,
            *head_outs,
            *scratch,
        )

    with_phase(phases[0], kept[0], run_trunk)
    act, h1, h2, a2, h3q, v1, v2, v3, stats = trunk_outs
    write(stats, stats_hbm)
    with_phase(phases[1], kept[1], run_head)
    head_out, xg, grads_out, proj_share, both_sums, proj_sums = head_outs
    for source, target in (
        (head_out, head_hbm),
        (grads_out, grads_hbm),
        (both_sums, both_hbm),
        (proj_sums, proj_hbm),
    ):
        write(source, target)

    def run_back(scratch):
        back_phase(
            at,
            post,
            sizes,
            local_sem,
            xg,
            h3q,
            v3,
            h2,
            v2,
            h1,
            v1,
            act,
            a2,
            proj_share,
            x_hbm,
            widths,
            we_hbm,
            wd_hbm,
            wr_hbm,
            write,
            *back_hbm,
            *scratch,
        )
        while len(writes) > before:
            writes.pop().wait()

    before = len(writes)
    with_phase(phases[2], kept[2], run_back)
    for copy in writes:
        copy.wait()


def whole(tasks, bands, cols, rows, collective, x, widths, gain, shift, wr, wd, we, *head_in):
    low, f32 = jnp.bfloat16, jnp.float32
    head_gain, head_shift, cot, bw, pw, rate = head_in
    pixels, wide = x.shape
    mid = wr.shape[1]
    quarter, piece = pixels // tasks, wide // bands
    width = pw.shape[1]
    chips = bands // 2
    group_rows = rows // chips
    taps = live_taps(rows, cols)
    extras = []
    for level in (1, 2, 3):
        for row_tap in (0, 2):
            if (level, row_tap, 1) in [tap[:3] for tap in taps]:
                away = (row_tap - 1) * level * RATE // group_rows
                extras += [
                    (level, target, target + away, row_tap)
                    for target in range(chips)
                    if 0 <= target + away < chips
                ]
    levels = max(len({entry[0] for entry in extras}), 1)
    anywhere = pl.BlockSpec(memory_space=pl.ANY)
    shape = jax.ShapeDtypeStruct
    block = (pixels, width)
    both_rows, proj_rows = -(-9 * width // LANE // 8) * 8, 8

    part, narrow, broad = mid // bands, mid // tasks, wide // tasks
    half = chips // 2
    pool_rows = pw.shape[0] // bands
    mid_rows, stat_wide = 2 * mid // LANE, wide // 4

    def kept(dims, dtype=low):
        return Held(tuple(dims), dtype)

    def passing(dims, dtype=low):
        return Held(tuple(dims), dtype, True)

    def over_bands(count, lanes=LANE):
        return [kept((count, lanes), f32), kept((bands, count, lanes), f32)]

    def over_all(count, lanes=LANE):
        return [kept((count, lanes), f32), kept((tasks, count, lanes), f32)] + over_bands(
            count, lanes
        )

    def terms(*dims):
        return [
            kept((2, chips) + dims),
            kept((chips,) + dims),
            kept((chips,) + dims),
            kept(dims),
            kept((tasks,) + dims),
        ]

    trunk_scratch = (
        [
            passing(x.shape),
            passing(wr.shape),
            passing(wd.shape),
            passing(we.shape),
            kept((3, pixels, mid)),
            kept((mid, pixels)),
            passing((pixels, wide), f32),
            kept((bands, quarter, piece)),
            passing((pixels, LANE), f32),
        ]
        + over_bands(mid_rows)
        + over_bands(mid_rows)
        + over_bands(8, stat_wide)
    )
    head_scratch = (
        [
            kept((len(taps), piece, width)),
            passing((piece, bands * pixels)),
            passing((levels, 2, 2 * pixels, width), f32),
            passing((chips, 2, 4) + block),
            kept((chips, 4) + block),
            kept((half, 4) + block),
            kept((half, 4) + block),
            passing((half, 4) + block, f32),
            passing((half, 5) + block),
            passing((half, 4) + block, f32),
            kept((half,) + block),
            passing((half,) + block),
            passing((half, pixels, LANE), f32),
            passing((half,) + block, f32),
            passing((half,) + block, f32),
            passing((half,) + block),
            passing((8, piece), f32),
            kept((both_rows, LANE), f32),
        ]
        + over_bands(both_rows)
        + [kept((proj_rows, LANE), f32)]
        + over_bands(proj_rows)
        + over_bands(proj_rows)
        + over_bands(both_rows)
        + [kept((proj_rows, LANE), f32)]
        + over_bands(proj_rows)
        + [
            kept((bands, 4) + block),
            passing((levels, 2, 3, 2 * pixels, width)),
            passing((len(taps) + 1, piece, width), f32),
            passing((chips, 2 * pixels, width), f32),
            passing((bands, pixels, piece)),
            passing(pw.shape),
            kept((chips, pool_rows, width)),
            kept((2, pool_rows, width)),
        ]
    )
    back_outs = (
        shape((8, LANE), f32),
        shape((pixels, wide), low),
        shape((piece, mid), f32),
        shape((9, part, mid), f32),
        shape((part, wide), f32),
        shape((8, stat_wide), f32),
        shape((mid_rows, LANE), f32),
        shape((mid_rows, LANE), f32),
        shape((bands, pool_rows, width), low),
    )
    back_scratch = (
        [kept(out.shape, out.dtype) for out in back_outs]
        + [
            passing(we.shape),
            passing(wd.shape),
            passing(wr.shape),
            passing(x.shape),
            passing((pixels, LANE), f32),
        ]
        + over_all(16)
        + [
            kept((bands, quarter, piece)),
            kept((bands, quarter, piece)),
            passing((bands, quarter, piece), f32),
            passing((bands, quarter, piece), f32),
            kept((bands, quarter, piece)),
            kept((tasks, bands, quarter, piece)),
        ]
        + over_all(8, stat_wide)
        + [
            kept((bands, quarter, piece)),
            kept((tasks, bands // tasks, quarter, piece)),
        ]
        + over_all(mid_rows)
        + [
            kept((pixels, mid)),
            kept((2, pixels, mid)),
            passing((pixels, mid), f32),
        ]
        + over_bands(mid_rows)
        + [
            passing((pixels, mid)),
            passing((wide, pixels)),
            passing((mid, pixels)),
        ]
        + terms(part, broad)
        + [
            kept((bands, pixels, narrow)),
            passing((3, 3 * part, narrow), f32),
            kept((9, part, narrow)),
            kept((tasks, 9, part, narrow)),
        ]
        + terms(piece, narrow)
        + [kept((bands, pool_rows, width))]
    )
    sizes = (tasks, bands, cols, quarter, mid, wide, piece)
    plan = (tasks, bands, cols, pixels, width, tuple(taps), tuple(extras))
    trunk_outs = (
        shape((bands + 2, part, pixels), low),
        shape((pixels, mid), f32),
        shape((pixels, mid), f32),
        shape((pixels, mid), low),
        shape((quarter, wide), f32),
        shape((8, mid), f32),
        shape((8, mid), f32),
        shape((8, wide), f32),
        shape((2, 2 * mid + wide), f32),
    )
    head_outs = (
        shape(block, low),
        shape((tasks, bands, quarter, piece), low),
        shape((len(taps) + 2, piece, width), low),
        shape((pool_rows, width), low),
        shape((both_rows, LANE), f32),
        shape((proj_rows, LANE), f32),
    )
    out_shapes = (trunk_outs[8], head_outs[0], head_outs[2], head_outs[4], head_outs[5])
    out_shapes += back_outs
    phases = (trunk_scratch, head_scratch, back_scratch)
    return taps, pl.pallas_call(
        functools.partial(
            whole_kernel, sizes, plan, phases, (len(trunk_outs), len(head_outs), len(back_outs))
        ),
        name="whole",
        out_shape=out_shapes,
        in_specs=[anywhere, pl.BlockSpec(memory_space=pltpu.SMEM)] + [anywhere] * 11,
        out_specs=(anywhere,) * len(out_shapes),
        scratch_shapes=[pltpu.VMEM(out.shape, out.dtype) for out in trunk_outs + head_outs]
        + [
            pltpu.VMEM(value.shape, value.dtype)
            for value in (gain, shift, head_gain, head_shift, cot, bw, pw)
        ]
        + [pltpu.VMEM((bands, pixels, piece), low)]
        + [entry.memory for entries in phases for entry in entries if not entry.passing]
        + [
            pltpu.SemaphoreType.DMA((352,)),
            pltpu.SemaphoreType.DMA((352,)),
            pltpu.SemaphoreType.DMA((10,)),
            pltpu.SemaphoreType.DMA((len(taps),)),
            pltpu.SemaphoreType.DMA((len(out_shapes),)),
            pltpu.SemaphoreType.DMA((7,)),
        ],
        compiler_params=pltpu.CompilerParams(
            collective_id=collective, has_side_effects=True, vmem_limit_bytes=60 << 20
        ),
    )(x, widths, gain, shift, wr, wd, we, *head_in)


def finish_kernel(
    places,
    tap_hbm,
    ho_in,
    ig_in,
    rg_in,
    dg_in,
    eg_in,
    bs_in,
    tw_hbm,
    pg_hbm,
    s3_hbm,
    s2_hbm,
    s1_hbm,
    both_hbm,
    proj_hbm,
    ho_out,
    ig_out,
    rg_out,
    dg_out,
    eg_out,
    bs_out,
    branch_out,
    rate_out,
    pg_hbm_out,
    tg_hbm_out,
    ts_hbm_out,
    hg_hbm_out,
    hs_hbm_out,
    tw_hbm_out,
    tap_ref,
    tw_ref,
    pg_ref,
    s3_ref,
    s2_ref,
    s1_ref,
    both_ref,
    proj_ref,
    ho_buf,
    ig_buf,
    rg_buf,
    dg_buf,
    eg_buf,
    bs_buf,
    branch,
    rate,
    pg_out,
    tg_out,
    ts_out,
    hg_out,
    hs_out,
    tw_out,
    sems,
    load_sems,
):
    f32 = jnp.float32
    width = tap_ref.shape[2]
    loads = [
        pltpu.make_async_copy(source, target, load_sems.at[number])
        for number, (source, target) in enumerate(
            (
                (tap_hbm, tap_ref),
                (pg_hbm, pg_ref),
                (tw_hbm, tw_ref),
                (s3_hbm, s3_ref),
                (s2_hbm, s2_ref),
                (s1_hbm, s1_ref),
                (both_hbm, both_ref),
                (proj_hbm, proj_ref),
            )
        )
    ]
    for load in loads:
        load.start()
    passed = [
        (ho_in, ho_buf, ho_out),
        (ig_in, ig_buf, ig_out),
        (rg_in, rg_buf, rg_out),
        (dg_in, dg_buf, dg_out),
        (eg_in, eg_buf, eg_out),
        (bs_in, bs_buf, bs_out),
    ]
    passes = [
        (
            pltpu.make_async_copy(source, buffer, load_sems.at[len(loads) + number]),
            pltpu.make_async_copy(buffer, target, sems.at[number]),
        )
        for number, (source, buffer, target) in enumerate(passed)
    ]
    for copy, _ in passes:
        copy.start()
    copies = [copy for _, copy in passes]
    per_level = len(places) // 3
    for number, place in enumerate(places):
        if place is None:
            rate[:, number * width : (number + 1) * width] = jnp.zeros(
                (rate.shape[0], width), f32
            )
    loads[0].wait()
    for level in range(3):
        for number in range(level * per_level, (level + 1) * per_level):
            lanes = slice(number * width, (number + 1) * width)
            if places[number] is not None:
                rate[:, lanes] = tap_ref[places[number]].astype(f32)
        lanes = slice(level * per_level * width, (level + 1) * per_level * width)
        copy = pltpu.make_async_copy(
            rate.at[:, lanes], rate_out.at[:, lanes], sems.at[len(copies)]
        )
        copy.start()
        copies.append(copy)
    for arrival, copy in passes:
        arrival.wait()
        copy.start()
    count = tap_ref.shape[0]
    branch[:, :width] = tap_ref[count - 2].astype(f32)
    branch[:, width:] = tap_ref[count - 1].astype(f32)
    copy = pltpu.make_async_copy(branch, branch_out, sems.at[len(copies)])
    copy.start()
    copies.append(copy)
    loads[1].wait()
    pg_out[...] = pg_ref[...].astype(f32)
    copy = pltpu.make_async_copy(pg_out, pg_hbm_out, sems.at[len(copies)])
    copy.start()
    copies.append(copy)
    for load in loads[2:]:
        load.wait()
    rows = s1_ref.shape[0] // 2
    ts_out[0:rows] = s1_ref[0:rows]
    tg_out[0:rows] = s1_ref[rows : 2 * rows]
    ts_out[rows : 2 * rows] = s2_ref[0:rows]
    tg_out[rows : 2 * rows] = s2_ref[rows : 2 * rows]
    half, lanes_in = s3_ref.shape[0] // 2, s3_ref.shape[1]
    for row in range(half):
        for part in range(lanes_in // LANE):
            target = 2 * rows + row * (lanes_in // LANE) + part
            lanes = slice(part * LANE, (part + 1) * LANE)
            ts_out[target : target + 1] = s3_ref[row : row + 1, lanes]
            tg_out[target : target + 1] = s3_ref[half + row : half + row + 1, lanes]
    spread = width // LANE
    for row in range(4 * spread):
        lanes = slice(row * LANE, (row + 1) * LANE)
        hs_out[:, lanes] = both_ref[row : row + 1]
        hg_out[:, lanes] = both_ref[4 * spread + row : 4 * spread + row + 1]
    for row in range(spread):
        lanes = slice((4 * spread + row) * LANE, (4 * spread + row + 1) * LANE)
        hs_out[:, lanes] = proj_ref[row : row + 1]
        hg_out[:, lanes] = proj_ref[spread + row : spread + row + 1]
    tasks = tw_out.shape[1]
    place = lax.broadcasted_iota(jnp.int32, (1, LANE), 1)
    weights = jnp.zeros((1, LANE), f32)
    for number in range(tasks):
        weights = jnp.where(place == number, tw_ref[number : number + 1], weights)
    tw_out[...] = weights[:, :tasks]
    for source, target in (
        (tg_out, tg_hbm_out),
        (ts_out, ts_hbm_out),
        (hg_out, hg_hbm_out),
        (hs_out, hs_hbm_out),
        (tw_out, tw_hbm_out),
    ):
        copy = pltpu.make_async_copy(source, target, sems.at[len(copies)])
        copy.start()
        copies.append(copy)
    for copy in copies:
        copy.wait()


def finish(places, tasks, taps, ho, ig, rg, dg, eg, bs, tw, pg, s3, s2, s1, both, proj):
    f32 = jnp.float32
    anywhere = pl.BlockSpec(memory_space=pl.ANY)
    shape = jax.ShapeDtypeStruct
    depth, width = taps.shape[1:]
    rows = (s1.size + s2.size + s3.size) // 2 // LANE
    out_shapes = (
        shape(ho.shape, ho.dtype),
        shape(ig.shape, ig.dtype),
        shape(rg.shape, rg.dtype),
        shape(dg.shape, dg.dtype),
        shape(eg.shape, eg.dtype),
        shape(bs.shape, bs.dtype),
        shape((depth, 2 * width), f32),
        shape((depth, len(places) * width), f32),
        shape(pg.shape, f32),
        shape((rows, LANE), f32),
        shape((rows, LANE), f32),
        shape((1, 5 * width), f32),
        shape((1, 5 * width), f32),
        shape((1, tasks), f32),
        )
    small = out_shapes[8:]
    return pl.pallas_call(
        functools.partial(finish_kernel, places),
        name="finish",
        out_shape=out_shapes,
        in_specs=[anywhere] * 14,
        out_specs=(anywhere,) * 14,
        scratch_shapes=[
            pltpu.VMEM(value.shape, value.dtype) for value in (taps, tw, pg, s3, s2, s1, both, proj, ho, ig, rg, dg, eg, bs)
        ]
        + [
            pltpu.VMEM((depth, 2 * width), f32),
            pltpu.VMEM((depth, len(places) * width), f32),
        ]
        + [pltpu.VMEM(out.shape, out.dtype) for out in small]
        + [
            pltpu.SemaphoreType.DMA((16,)),
            pltpu.SemaphoreType.DMA((14,)),
        ],
        compiler_params=pltpu.CompilerParams(vmem_limit_bytes=60 << 20),
    )(taps, ho, ig, rg, dg, eg, bs, tw, pg, s3, s2, s1, both, proj)


def live_taps(rows, cols):
    taps = []
    for level in (1, 2, 3):
        for row_tap in range(3):
            for col_tap in range(3):
                down, right = (row_tap - 1) * level * RATE, (col_tap - 1) * level * RATE
                if abs(down) < rows and abs(right) < cols:
                    taps.append((level, row_tap, col_tap, down, right))
    return taps


def per_device_slices(
    features,
    row_width,
    w_reduce,
    w_dilated,
    w_expand,
    trunk_gain,
    trunk_shift,
    branch_weight,
    rate_weight,
    proj_weight,
    head_gain,
    head_shift,
    head_cot,
):
    bands, tasks = lax.axis_size("space"), lax.axis_size("task")
    band_rows, cols, in_width = features.shape
    rows = band_rows * bands
    pixels = band_rows * cols
    head_width = proj_weight.shape[2]
    inputs = features.reshape(pixels, in_width)
    dilated = w_dilated.transpose(1, 0, 2)
    taps, (
        batch_stats,
        head_out,
        tap_grads,
        both_sums,
        proj_sums,
        weight_rows,
        input_grad,
        reduce_grad,
        dilated_grad,
        expand_grad,
        sums_three,
        sums_two,
        sums_one,
        proj_grad,
    ) = whole(
        tasks,
        bands,
        cols,
        rows,
        0,
        inputs,
        row_width,
        trunk_gain.reshape(1, -1),
        trunk_shift.reshape(1, -1),
        w_reduce,
        dilated,
        w_expand,
        head_gain,
        head_shift,
        head_cot.reshape(pixels, head_width),
        branch_weight[0],
        proj_weight[0],
        rate_weight[0],
    )
    place_of = {tap[:3]: number for number, tap in enumerate(taps)}
    places = tuple(
        place_of.get((level, row_tap, col_tap))
        for level in (1, 2, 3)
        for row_tap in range(3)
        for col_tap in range(3)
    )
    (
        head_out,
        input_grad,
        reduce_grad,
        dilated_grad,
        expand_grad,
        batch_stats,
        branch_grad,
        rate_grad,
        proj_grad,
        trunk_gains,
        trunk_shifts,
        head_gains,
        head_shifts,
        task_weight,
    ) = finish(
        places,
        tasks,
        tap_grads,
        head_out,
        input_grad,
        reduce_grad,
        dilated_grad,
        expand_grad,
        batch_stats,
        weight_rows,
        proj_grad.reshape(-1, head_width),
        sums_three,
        sums_two,
        sums_one,
        both_sums,
        proj_sums,
    )
    return (
        head_out.reshape(1, band_rows, cols, head_width),
        input_grad.reshape(features.shape),
        reduce_grad,
        dilated_grad.transpose(1, 0, 2),
        expand_grad,
        trunk_gains.reshape(-1),
        trunk_shifts.reshape(-1),
        batch_stats,
        branch_grad[None],
        rate_grad[None],
        proj_grad[None],
        head_gains,
        head_shifts,
        task_weight.reshape(-1),
    )


def solution(mesh):
    def body(features, *others):
        small = mesh.shape["space"] == 8 and mesh.shape["task"] == 4
        if small and features.shape[:2] == (2, 128):
            return per_device_slices(features, *others)
        return per_device(features, *others)

    return jax.shard_map(
        body,
        mesh=mesh,
        in_specs=(
            P("space", None, None),
            P(),
            P(),
            P(),
            P(),
            P(),
            P(),
            P("task", "space", None),
            P("task", "space", None),
            P("task", None, None),
            P("task", None),
            P("task", None),
            P("task", "space", None, None),
        ),
        out_specs=(
            P("task", "space", None, None),
            P("space", None, None),
            P("space", None),
            P("space", None, None),
            P("space", None),
            P(),
            P(),
            P(),
            P("task", "space", None),
            P("task", "space", None),
            P("task", None, None),
            P("task", None),
            P("task", None),
            P(),
        ),
        check_vma=False,
    )
```

```python
import functools

import jax
import jax.numpy as jnp
from jax import lax
from jax.experimental import pallas as pl
from jax.experimental.pallas import tpu as pltpu
from jax.sharding import PartitionSpec as P

CONV_DILATION = 2
RATE = 12


NORM_EPS = 1e-05
GRAM_EPS = 1e-06
PRECISE = lax.Precision.HIGHEST


def with_halo(block, sides, width):
    for axis, dim in sides:
        count = lax.axis_size(axis)
        forward = [(i, i + 1) for i in range(count - 1)]
        backward = [(target, source) for source, target in forward]
        low = lax.ppermute(
            lax.slice_in_dim(block, block.shape[dim] - width, None, axis=dim), axis, forward
        )
        high = lax.ppermute(lax.slice_in_dim(block, 0, width, axis=dim), axis, backward)
        block = jnp.concatenate([low, block, high], axis=dim)
    return block


def from_behind(shard, axis, by):
    count = lax.axis_size(axis)
    pairs = [(i, i + by) for i in range(count) if 0 <= i + by < count]
    return lax.ppermute(shard, axis, pairs)


def small_solve(matrix, target):
    size_n = matrix.shape[0]
    rows_list = [matrix[number] for number in range(size_n)]
    values = [target[number] for number in range(size_n)]
    for pivot_row in range(size_n):
        for lower_row in range(pivot_row + 1, size_n):
            factor = rows_list[lower_row][pivot_row] / rows_list[pivot_row][pivot_row]
            rows_list[lower_row] = rows_list[lower_row] - factor * rows_list[pivot_row]
            values[lower_row] = values[lower_row] - factor * values[pivot_row]
    answer = [None] * size_n
    for pivot_row in reversed(range(size_n)):
        running = values[pivot_row]
        for later_row in range(pivot_row + 1, size_n):
            running = running - rows_list[pivot_row][later_row] * answer[later_row]
        answer[pivot_row] = running / rows_list[pivot_row][pivot_row]
    return jnp.stack(answer)


def imtl_weights(gram_matrix):
    grad_norms = jnp.sqrt(jnp.diagonal(gram_matrix) + GRAM_EPS)
    projections = gram_matrix / grad_norms[None, :]
    system = projections[0, 0] - projections[0:1, 1:] - projections[1:, 0:1] + projections[1:, 1:]
    target = projections[0, 0] - projections[0, 1:]
    other_weights = small_solve(jnp.transpose(system), target)
    return jnp.concatenate([(1.0 - jnp.sum(other_weights))[None], other_weights])


def gelu_back(value, upstream):
    return jax.vjp(jax.nn.gelu, value)[1](upstream)[0]


def channel_sums(members):
    return lax.psum(members, "space")


def norm_values(hidden, first_total, second_total, gain_vec, shift_vec, pixel_count):
    mean_value = first_total / pixel_count
    variance = second_total / pixel_count - mean_value * mean_value
    inv_std = lax.rsqrt(variance + NORM_EPS)
    scaled = (hidden - mean_value) * inv_std
    return (gain_vec * scaled + shift_vec, scaled, inv_std, mean_value, variance)


def norm_forward(hidden, gain_vec, shift_vec, valid_mask, pixel_count):
    totals = channel_sums(
        (jnp.sum(hidden * valid_mask, axis=0), jnp.sum(hidden * hidden * valid_mask, axis=0))
    )
    return norm_values(hidden, totals[0], totals[1], gain_vec, shift_vec, pixel_count)


def norm_finish(
    upstream, scaled, inv_std, gain_vec, gain_grad, shift_grad, valid_mask, pixel_count
):
    return (
        valid_mask
        * gain_vec
        * inv_std
        * (upstream - shift_grad / pixel_count - scaled * gain_grad / pixel_count)
    )


def norm_backward(upstream, scaled, inv_std, gain_vec, valid_mask, pixel_count):
    totals = channel_sums(
        (jnp.sum(upstream * valid_mask, axis=0), jnp.sum(upstream * scaled * valid_mask, axis=0))
    )
    hidden_grad = norm_finish(
        upstream, scaled, inv_std, gain_vec, totals[1], totals[0], valid_mask, pixel_count
    )
    return (hidden_grad, totals[1], totals[0])


def band_rim(strip_image):
    return with_halo(strip_image, (("space", 0),), CONV_DILATION)


def far_rows(strip_image, bands_away, upward):
    if bands_away >= lax.axis_size("space"):
        return jnp.zeros_like(strip_image)
    if upward:
        return from_behind(strip_image, "space", bands_away)
    return from_behind(strip_image, "space", -bands_away)


def trunk_taps(padded, reach_cells, rows_count, cols_count, flipped):
    col_padded = jnp.pad(padded, ((0, 0), (reach_cells, reach_cells), (0, 0)))
    pieces = []
    for row_tap in range(3):
        for col_tap in range(3):
            row_from = (2 - row_tap) * reach_cells if flipped else row_tap * reach_cells
            col_from = (2 - col_tap) * reach_cells if flipped else col_tap * reach_cells
            pieces.append(
                col_padded[
                    row_from : row_from + rows_count, col_from : col_from + cols_count
                ].reshape(rows_count * cols_count, -1)
            )
    return jnp.stack(pieces, axis=1)


def per_device(
    features,
    row_width,
    w_reduce,
    w_dilated,
    w_expand,
    trunk_gain,
    trunk_shift,
    branch_weight,
    rate_weight,
    proj_weight,
    head_gain,
    head_shift,
    head_cot,
):
    band_rows, cols_count, in_width = features.shape
    pixels = band_rows * cols_count
    middle_width = w_reduce.shape[1]
    head_width = proj_weight.shape[2]
    first_row = lax.axis_index("space") * band_rows
    widths = lax.dynamic_slice_in_dim(row_width, first_row, band_rows)
    valid_mask = (
        (jnp.arange(cols_count)[None, :] < widths[:, None]).astype(jnp.float32).reshape(pixels, 1)
    )
    pixel_count = jnp.sum(row_width).astype(jnp.float32)
    inputs = features.reshape(pixels, in_width)
    gain_one, shift_one = (trunk_gain[:middle_width], trunk_shift[:middle_width])
    gain_two, shift_two = (
        trunk_gain[middle_width : 2 * middle_width],
        trunk_shift[middle_width : 2 * middle_width],
    )
    gain_three, shift_three = (trunk_gain[2 * middle_width :], trunk_shift[2 * middle_width :])
    hidden_one = jnp.dot(inputs, w_reduce, preferred_element_type=jnp.float32)
    stats_one = norm_forward(hidden_one, gain_one, shift_one, valid_mask, pixel_count)
    first_active = (jax.nn.gelu(stats_one[0]) * valid_mask).astype(jnp.bfloat16)
    patches = trunk_taps(
        band_rim(first_active.reshape(band_rows, cols_count, middle_width)),
        CONV_DILATION,
        band_rows,
        cols_count,
        False,
    )
    hidden_two = jnp.einsum("pti,ito->po", patches, w_dilated, preferred_element_type=jnp.float32)
    stats_two = norm_forward(hidden_two, gain_two, shift_two, valid_mask, pixel_count)
    active_two = (jax.nn.gelu(stats_two[0]) * valid_mask).astype(jnp.bfloat16)
    hidden_three = jnp.dot(active_two, w_expand, preferred_element_type=jnp.float32)
    stats_three = norm_forward(hidden_three, gain_three, shift_three, valid_mask, pixel_count)
    before_act = stats_three[0] + inputs.astype(jnp.float32)
    shared = (jax.nn.gelu(before_act) * valid_mask).astype(jnp.bfloat16)
    proj_local = proj_weight[0]
    gain_local = head_gain[0]
    shift_local = head_shift[0]
    joined_weight = jnp.concatenate([branch_weight[0], rate_weight[0]], axis=1)
    pixel_sum = jnp.dot(
        valid_mask.reshape(1, pixels).astype(jnp.bfloat16),
        shared,
        preferred_element_type=jnp.float32,
    )[0]
    shared_image = shared.reshape(band_rows, cols_count, in_width)
    padded_sources = []
    for level in (1, 2, 3):
        reach = level * RATE
        bands_away = reach // band_rows
        triple = (
            far_rows(shared_image, bands_away, True),
            shared_image,
            far_rows(shared_image, bands_away, False),
        )
        padded_sources.append(
            [jnp.pad(source, ((0, 0), (reach, reach), (0, 0))) for source in triple]
        )
    zero_rows = jnp.zeros((pixels, head_width), jnp.float32)
    start_totals = (
        zero_rows,
        jnp.zeros((1, head_width), jnp.float32),
        zero_rows,
        zero_rows,
        zero_rows,
    )
    all_weights = lax.all_gather(joined_weight, "space", axis=0, tiled=True)
    width_now = all_weights.shape[0]
    one_acc = jnp.dot(shared, all_weights[:, :head_width], preferred_element_type=jnp.float32)
    pool_cols = pixel_sum[None]
    pool_acc = jnp.dot(
        pool_cols,
        all_weights[:, head_width : 2 * head_width].astype(jnp.float32),
        precision=PRECISE,
        preferred_element_type=jnp.float32,
    )
    rate_accs = []
    for fold_level_index in range(3):
        fold_reach = (fold_level_index + 1) * RATE
        running = start_totals[2 + fold_level_index]
        for fold_row_tap in range(3):
            fold_source = padded_sources[fold_level_index][fold_row_tap]
            for fold_col_tap in range(3):
                window = fold_source[
                    :, fold_col_tap * fold_reach : fold_col_tap * fold_reach + cols_count
                ].reshape(pixels, width_now)
                column = (2 + 9 * fold_level_index + 3 * fold_row_tap + fold_col_tap) * head_width
                running = running + jnp.dot(
                    window,
                    all_weights[:, column : column + head_width],
                    preferred_element_type=jnp.float32,
                )
        rate_accs.append(running)
    pre_both = jnp.concatenate([one_acc, rate_accs[0], rate_accs[1], rate_accs[2]], axis=1)
    gain_both, shift_both = (gain_local[: 4 * head_width], shift_local[: 4 * head_width])
    totals = channel_sums(
        (
            jnp.sum(pre_both * valid_mask, axis=0),
            jnp.sum(pre_both * pre_both * valid_mask, axis=0),
            pool_acc[0],
        )
    )
    stats_both = norm_values(pre_both, totals[0], totals[1], gain_both, shift_both, pixel_count)
    pooled = totals[2][None] / pixel_count
    active_both = (jax.nn.gelu(stats_both[0]) * valid_mask).astype(jnp.bfloat16)
    active_pool = jax.nn.gelu(pooled).astype(jnp.bfloat16)
    joined = jnp.concatenate(
        [active_both, (active_pool.astype(jnp.float32) * valid_mask).astype(jnp.bfloat16)], axis=1
    )
    projected = jnp.dot(joined, proj_local, preferred_element_type=jnp.float32)
    gain_proj = gain_local[4 * head_width :]
    stats_proj = norm_forward(
        projected, gain_proj, shift_local[4 * head_width :], valid_mask, pixel_count
    )
    head_result = (jax.nn.gelu(stats_proj[0]) * valid_mask).astype(jnp.bfloat16)
    cot_rows = head_cot[0].reshape(pixels, head_width).astype(jnp.float32)
    proj_upstream = gelu_back(stats_proj[0], cot_rows * valid_mask)
    proj_hidden, proj_gain_grad, proj_shift_grad = norm_backward(
        proj_upstream, stats_proj[1], stats_proj[2], gain_proj, valid_mask, pixel_count
    )
    proj_low = proj_hidden.astype(jnp.bfloat16)
    joined_grad = lax.dot_general(
        proj_low, proj_local, (((1,), (1,)), ((), ())), preferred_element_type=jnp.float32
    )
    proj_term = lax.dot_general(
        joined, proj_low, (((0,), (0,)), ((), ())), preferred_element_type=jnp.float32
    )
    both_upstream = gelu_back(stats_both[0], joined_grad[:, : 4 * head_width] * valid_mask)
    pool_total = jnp.sum(joined_grad[:, 4 * head_width :] * valid_mask, axis=0)
    back_totals = channel_sums(
        (
            proj_term,
            pool_total,
            jnp.sum(both_upstream * valid_mask, axis=0),
            jnp.sum(both_upstream * stats_both[1] * valid_mask, axis=0),
        )
    )
    pool_grad = gelu_back(pooled, back_totals[1][None]).astype(jnp.bfloat16)
    both_grad = norm_finish(
        both_upstream,
        stats_both[1],
        stats_both[2],
        gain_both,
        back_totals[3],
        back_totals[2],
        valid_mask,
        pixel_count,
    ).astype(jnp.bfloat16)
    tap_grads = []
    for level_index in range(3):
        reach = (level_index + 1) * RATE
        bands_away = reach // band_rows
        rate_image = both_grad[
            :, (1 + level_index) * head_width : (2 + level_index) * head_width
        ].reshape(band_rows, cols_count, head_width)
        back_sources = [
            jnp.pad(source, ((0, 0), (reach, reach), (0, 0)))
            for source in (
                far_rows(rate_image, bands_away, False),
                rate_image,
                far_rows(rate_image, bands_away, True),
            )
        ]
        for row_tap in range(3):
            for col_tap in range(3):
                tap_grads.append(
                    back_sources[row_tap][
                        :, (2 - col_tap) * reach : (2 - col_tap) * reach + cols_count
                    ].reshape(pixels, head_width)
                )
    right_side = jnp.concatenate([both_grad[:, :head_width]] + tap_grads, axis=1)
    used_rows = jnp.concatenate(
        [all_weights[:, :head_width], all_weights[:, 2 * head_width :]], axis=1
    )
    main_part = lax.dot_general(
        right_side, used_rows, (((1,), (1,)), ((), ())), preferred_element_type=jnp.float32
    )
    pool_part = lax.dot_general(
        pool_grad,
        all_weights[:, head_width : 2 * head_width],
        (((1,), (1,)), ((), ())),
        preferred_element_type=jnp.float32,
    )
    shared_grad = (main_part + valid_mask * pool_part / pixel_count).astype(jnp.bfloat16)
    head_term = lax.dot_general(
        shared, right_side, (((0,), (0,)), ((), ())), preferred_element_type=jnp.float32
    )
    pool_term = pixel_sum[:, None] * pool_grad.astype(jnp.float32) / pixel_count
    head_term = jnp.concatenate(
        [head_term[:, :head_width], pool_term, head_term[:, head_width:]], axis=1
    )
    all_grads = lax.all_gather(shared_grad[None], "task", axis=0, tiled=True)
    flat_grads = all_grads.reshape(all_grads.shape[0], -1)
    gram_matrix = lax.psum(
        lax.dot_general(
            flat_grads, flat_grads, (((1,), (1,)), ((), ())), preferred_element_type=jnp.float32
        ),
        "space",
    )
    task_weight = imtl_weights(gram_matrix)
    mixed_grad = task_weight[0] * all_grads[0].astype(jnp.float32)
    for task_index in range(1, all_grads.shape[0]):
        mixed_grad = mixed_grad + task_weight[task_index] * all_grads[task_index].astype(
            jnp.float32
        )
    combined = mixed_grad.astype(jnp.bfloat16)
    gate_grad = gelu_back(before_act, combined.astype(jnp.float32) * valid_mask)
    hidden_grad_three, gain_grad_three, shift_grad_three = norm_backward(
        gate_grad, stats_three[1], stats_three[2], gain_three, valid_mask, pixel_count
    )
    low_three = hidden_grad_three.astype(jnp.bfloat16)
    expand_term = lax.dot_general(
        active_two, low_three, (((0,), (0,)), ((), ())), preferred_element_type=jnp.float32
    )
    active_grad_two = lax.dot_general(
        low_three, w_expand, (((1,), (1,)), ((), ())), preferred_element_type=jnp.float32
    )
    upstream_two = gelu_back(stats_two[0], active_grad_two * valid_mask)
    hidden_grad_two, gain_grad_two, shift_grad_two = norm_backward(
        upstream_two, stats_two[1], stats_two[2], gain_two, valid_mask, pixel_count
    )
    low_two = hidden_grad_two.astype(jnp.bfloat16)
    dilated_term = jnp.einsum("pti,po->ito", patches, low_two, preferred_element_type=jnp.float32)
    back_patches = trunk_taps(
        band_rim(low_two.reshape(band_rows, cols_count, middle_width)),
        CONV_DILATION,
        band_rows,
        cols_count,
        True,
    )
    active_grad_one = jnp.einsum(
        "pto,ito->pi", back_patches, w_dilated, preferred_element_type=jnp.float32
    )
    upstream_one = gelu_back(stats_one[0], active_grad_one * valid_mask)
    hidden_grad_one, gain_grad_one, shift_grad_one = norm_backward(
        upstream_one, stats_one[1], stats_one[2], gain_one, valid_mask, pixel_count
    )
    low_one = hidden_grad_one.astype(jnp.bfloat16)
    reduce_term = lax.dot_general(
        inputs, low_one, (((0,), (0,)), ((), ())), preferred_element_type=jnp.float32
    )
    input_grad = (
        lax.dot_general(
            low_one, w_reduce, (((1,), (1,)), ((), ())), preferred_element_type=jnp.float32
        )
        + gate_grad
    )
    reduced = (
        lax.psum_scatter(head_term, "space", scatter_dimension=0, tiled=True),
        lax.psum_scatter(reduce_term, "space", scatter_dimension=0, tiled=True),
        lax.psum_scatter(dilated_term, "space", scatter_dimension=0, tiled=True),
        lax.psum_scatter(expand_term, "space", scatter_dimension=0, tiled=True),
    )
    means = jnp.concatenate([stats_one[3], stats_two[3], stats_three[3]])
    variances = (
        jnp.concatenate([stats_one[4], stats_two[4], stats_three[4]])
        * pixel_count
        / (pixel_count - 1.0)
    )
    batch_stats = jnp.stack([means, variances])
    head_gain_grad = jnp.concatenate([back_totals[3], proj_gain_grad])[None]
    head_shift_grad = jnp.concatenate([back_totals[2], proj_shift_grad])[None]
    return (
        head_result.reshape(1, band_rows, cols_count, head_width),
        input_grad.reshape(band_rows, cols_count, in_width).astype(jnp.bfloat16),
        reduced[1],
        reduced[2],
        reduced[3],
        jnp.concatenate([gain_grad_one, gain_grad_two, gain_grad_three]),
        jnp.concatenate([shift_grad_one, shift_grad_two, shift_grad_three]),
        batch_stats,
        reduced[0][:, : 2 * head_width][None],
        reduced[0][:, 2 * head_width :][None],
        back_totals[0][None],
        head_gain_grad,
        head_shift_grad,
        task_weight,
    )


MESH_ID = pl.DeviceIdType.MESH
LANE = 128


FAR_LAG = 2
SEND_LAG = 0
GELU_A = 0.7978845608028654
GELU_B = 0.044715


def gelu_of(value):
    return 0.5 * value * (1.0 + jnp.tanh(GELU_A * (value + GELU_B * value * value * value)))


def gelu_slope(value):
    square = value * value
    bend = jnp.tanh(GELU_A * value * (1.0 + GELU_B * square))
    return 0.5 * (1.0 + bend) + 0.5 * value * (1.0 - bend * bend) * (
        GELU_A * (1.0 + 3.0 * GELU_B * square)
    )


def gelu_both(value):
    square = value * value
    bend = jnp.tanh(GELU_A * value * (1.0 + GELU_B * square))
    lift = 0.5 * (1.0 + bend)
    slope = lift + 0.5 * value * (1.0 - bend * bend) * (GELU_A * (1.0 + 3.0 * GELU_B * square))
    return value * lift, slope


def dot_nn(left_side, right_side):
    return jnp.dot(left_side, right_side, preferred_element_type=jnp.float32)


def dot_nt(left_side, right_side):
    return lax.dot_general(
        left_side, right_side, (((1,), (1,)), ((), ())), preferred_element_type=jnp.float32
    )


def shift_pixels(value, by, cols):
    if by == 0:
        return value
    rows = value.shape[0]
    column = lax.rem(lax.broadcasted_iota(jnp.int32, value.shape, 0), cols) + by
    rolled = pltpu.roll(value, (-by) % rows, 0)
    return jnp.where((column >= 0) & (column < cols), rolled, 0.0)


def row_mask(widths_ref, first_row, rows, cols):
    column = lax.broadcasted_iota(jnp.int32, (cols, LANE), 0)
    return jnp.concatenate(
        [
            jnp.where(column < widths_ref[first_row + number], 1.0, 0.0).astype(jnp.float32)
            for number in range(rows)
        ],
        axis=0,
    )


def count_pixels(widths_ref):
    total = widths_ref[0]
    for number in range(1, widths_ref.shape[0]):
        total = total + widths_ref[number]
    return jnp.full((1, LANE), total.astype(jnp.float32), jnp.float32)


class Post:
    def __init__(self, send_sem, recv_sem):
        self.send_sem, self.recv_sem = send_sem, recv_sem
        self.used = 0
        self.sent = []

    def copy(self, source, target, device):
        made = pltpu.make_async_remote_copy(
            source,
            target,
            self.send_sem.at[self.used],
            self.recv_sem.at[self.used],
            device_id=device,
            device_id_type=MESH_ID,
        )
        self.used += 1
        return made

    def push(self, source, target, device):
        made = self.copy(source, target, device)
        made.start()
        self.sent.append(made)
        return made

    def close(self):
        for made in self.sent:
            made.wait_send()
        self.sent = []


class Place:
    def __init__(self, tasks, bands):
        self.tasks, self.bands, self.chips = tasks, bands, bands // 2
        self.task = lax.axis_index("task")
        self.band = lax.axis_index("space")
        self.chip = self.band // 2
        self.core = lax.rem(self.band, 2)
        self.twin = {"space": self.chip * 2 + 1 - self.core}
        low, high = lax.rem(self.task, 2), self.task // 2
        self.other_tasks = [(1 - high) * 2 + 1 - low, high * 2 + 1 - low, (1 - high) * 2 + low]
        self.other_bands = [lax.rem(self.band + step, bands) for step in range(1, bands)]

    def greet(self):
        barrier = pltpu.get_barrier_semaphore()
        greeted = [{"task": task} for task in self.other_tasks]
        greeted += [{"space": band} for band in self.other_bands]
        for device in greeted:
            pl.semaphore_signal(barrier, inc=1, device_id=device, device_id_type=MESH_ID)

    def meet(self):
        barrier = pltpu.get_barrier_semaphore()
        pl.semaphore_wait(barrier, len(self.other_tasks) + len(self.other_bands))

    def sum_begin(self, post, axis, own_ref, land_ref):
        mine = self.task if axis == "task" else self.band
        others = self.other_tasks if axis == "task" else self.other_bands
        copies = [post.push(own_ref, land_ref.at[mine], {axis: other}) for other in others]
        land_ref[pl.ds(mine, 1)] = own_ref[...][None]
        return copies, land_ref

    def sum_end(self, begun):
        copies, land_ref = begun
        for made in copies:
            made.wait_recv()
        total = land_ref[0]
        for slot in range(1, len(copies) + 1):
            total = total + land_ref[slot]
        return total

    def sum_over(self, post, axis, own_ref, land_ref):
        return self.sum_end(self.sum_begin(post, axis, own_ref, land_ref))


def back_phase(
    at,
    post,
    sizes,
    local_sem,
    part_copy,
    xg,
    h3q,
    v3_ref,
    h2_ref,
    v2_ref,
    h1_ref,
    v1_ref,
    act_ref,
    a2_ref,
    ps_ref,
    x_hbm,
    widths_ref,
    we_hbm,
    wd_hbm,
    wr_hbm,
    write,
    tw_hbm,
    ig_hbm,
    rg_hbm,
    dg_hbm,
    eg_hbm,
    s3_hbm,
    s2_hbm,
    s1_hbm,
    pg_hbm,
    tw_out,
    ig_out,
    rg_out,
    dg_out,
    eg_out,
    s3_out,
    s2_out,
    s1_out,
    pg_out,
    we,
    wd,
    wr,
    x_ref,
    mask_ref,
    gram_own,
    gram_land,
    gram_mid,
    gram_land_b,
    comb,
    comb_land,
    gate,
    scaled,
    gate_low,
    gate_band,
    st3,
    st3_land,
    st3_mid,
    st3_land_b,
    l3,
    l3x,
    st2,
    st2_land,
    st2_mid,
    st2_land_b,
    l2,
    l2_halo,
    ag1,
    st1,
    st1_land,
    l1,
    xt,
    a2t,
    e_term,
    e_twin,
    e_land,
    e_share,
    e_tasks,
    l2c,
    d_sum,
    d_share,
    d_tasks,
    r_term,
    r_twin,
    r_land,
    r_share,
    r_tasks,
    p_all,
):
    tasks, bands, cols, quarter, mid, wide, piece = sizes
    low = jnp.bfloat16
    f32 = jnp.float32
    task, band = at.task, at.band
    my_rows = pl.ds(pl.multiple_of(task * quarter, quarter), quarter)
    arrays = {
        "x": (x_hbm, x_ref),
        "we": (we_hbm, we),
        "wd": (wd_hbm, wd),
        "wr": (wr_hbm, wr),
    }
    loads = {
        name: pltpu.make_async_copy(source, target, local_sem.at[number])
        for number, (name, (source, target)) in enumerate(arrays.items())
    }

    def loaded(*names):
        for name in names:
            loads[name].wait()

    for load in loads.values():
        load.start()
    band_rows = x_ref.shape[0] // cols
    mask_ref[...] = row_mask(widths_ref, band * band_rows, band_rows, cols)

    pairs = [(a, b) for a in range(tasks) for b in range(a, tasks)]

    def gram_step(number, totals):
        grads = [xg[a, number].astype(f32) for a in range(tasks)]
        out = []
        for (a, b), total in zip(pairs, totals):
            product = grads[a] * grads[b]
            product = product.reshape(quarter // 8, 8, piece).sum(axis=0)
            for start in range(0, piece, LANE):
                total = total + product[:, start : start + LANE]
            out.append(total)
        return tuple(out)

    totals = lax.fori_loop(
        0, bands, gram_step, tuple(jnp.zeros((8, LANE), f32) for _ in pairs)
    )
    gram_own[...] = jnp.zeros_like(gram_own)
    for number, total in enumerate(totals):
        gram_own[number : number + 1] = jnp.sum(total, axis=0, keepdims=True)
    begun = at.sum_begin(post, "task", gram_own, gram_land)
    a2t[...] = a2_ref[...].T
    gram_mid[...] = at.sum_end(begun)
    begun = at.sum_begin(post, "space", gram_mid, gram_land_b)

    loaded("x")
    def turn_inputs(number, carry):
        lanes = pl.ds(pl.multiple_of(number * piece, piece), piece)
        xt[lanes, :] = x_ref[:, lanes].T
        return carry

    lax.fori_loop(0, wide // piece, turn_inputs, 0)
    gram_sum = at.sum_end(begun)
    gram_sum = jnp.broadcast_to(jnp.sum(gram_sum, axis=1, keepdims=True), gram_sum.shape)
    gram = [[None] * tasks for _ in range(tasks)]
    for number, (a, b) in enumerate(pairs):
        gram[a][b] = gram[b][a] = gram_sum[number : number + 1]
    norms = [jnp.sqrt(gram[a][a] + GRAM_EPS) for a in range(tasks)]
    cos = [[gram[a][b] / norms[b] for b in range(tasks)] for a in range(tasks)]
    rows_list = [
        [cos[0][0] - cos[0][l] - cos[k][0] + cos[k][l] for k in range(1, tasks)]
        for l in range(1, tasks)
    ]
    values = [cos[0][0] - cos[0][l] for l in range(1, tasks)]
    count = tasks - 1
    for pivot in range(count):
        for lower in range(pivot + 1, count):
            factor = rows_list[lower][pivot] / rows_list[pivot][pivot]
            rows_list[lower] = [
                under - factor * over for under, over in zip(rows_list[lower], rows_list[pivot])
            ]
            values[lower] = values[lower] - factor * values[pivot]
    answer = [None] * count
    for pivot in reversed(range(count)):
        running = values[pivot]
        for later in range(pivot + 1, count):
            running = running - rows_list[pivot][later] * answer[later]
        answer[pivot] = running / rows_list[pivot][pivot]
    rest = answer[0]
    for value in answer[1:]:
        rest = rest + value
    task_weight = [1.0 - rest] + answer
    for number in range(tasks):
        tw_out[number : number + 1] = task_weight[number]
    weights = [jnp.concatenate([value] * (piece // LANE), axis=1) for value in task_weight]

    def mixed(number):
        total = weights[0] * xg[0, number].astype(f32)
        for a in range(1, tasks):
            total = total + weights[a] * xg[a, number].astype(f32)
        return total.astype(low)

    comb_in = []
    for other in at.other_bands:
        comb[other] = mixed(other)
        comb_in.append(post.push(comb.at[other], comb_land.at[band], {"space": other}))
    comb_land[pl.ds(band, 1)] = mixed(band)[None]
    for made in comb_in:
        made.wait_recv()

    mask_quarter = mask_ref[my_rows]
    mask_piece = jnp.concatenate([mask_quarter] * (piece // LANE), axis=1)
    inv_count = 1.0 / count_pixels(widths_ref)
    inv_piece = jnp.concatenate([inv_count] * (piece // LANE), axis=1)
    per_row = st3.shape[1] // piece
    half = st3.shape[0] // 2

    def gate_step(number, carry):
        lanes = pl.ds(pl.multiple_of(number * piece, piece), piece)
        hat = (h3q[:, lanes] - v3_ref[0:1, lanes]) * v3_ref[1:2, lanes]
        before = v3_ref[2:3, lanes] * hat + v3_ref[3:4, lanes] + x_ref[my_rows, lanes].astype(f32)
        grad = gelu_slope(before) * comb_land[number].astype(f32) * mask_piece
        gate[number] = grad
        scaled[number] = hat
        gate_low[number] = grad.astype(low)
        row = number // per_row
        spot = pl.ds(pl.multiple_of(lax.rem(number, per_row) * piece, piece), piece)
        st3[pl.ds(row, 1), spot] = jnp.sum(grad, axis=0, keepdims=True)
        st3[pl.ds(half + row, 1), spot] = jnp.sum(grad * hat, axis=0, keepdims=True)
        return carry

    lax.fori_loop(0, bands, gate_step, 0)
    st3_mid[...] = at.sum_over(post, "task", st3, st3_land)
    s3_out[...] = at.sum_over(post, "space", st3_mid, st3_land_b)

    def third_step(number, carry):
        lanes = pl.ds(pl.multiple_of(number * piece, piece), piece)
        row = number // per_row
        spot = pl.ds(pl.multiple_of(lax.rem(number, per_row) * piece, piece), piece)
        shift_grad = s3_out[pl.ds(row, 1), spot] * inv_piece
        gain_grad = s3_out[pl.ds(half + row, 1), spot] * inv_piece
        l3[number] = (
            mask_piece
            * (v3_ref[2:3, lanes] * v3_ref[1:2, lanes])
            * (gate[number] - shift_grad - scaled[number] * gain_grad)
        ).astype(low)
        return carry

    lax.fori_loop(0, bands, third_step, 0)
    per_task = bands // tasks
    l3_in = []
    for other in at.other_tasks:
        l3_in.append(
            post.push(l3.at[pl.ds(other * per_task, per_task)], l3x.at[task], {"task": other})
        )
    l3x[pl.ds(task, 1)] = l3[pl.ds(task * per_task, per_task)][None]
    loaded("we")
    p_all[pl.ds(band, 1)] = ps_ref[...][None]
    p_block = p_all.at[band]
    p_near = post.push(p_block, p_block, at.twin)
    p_far = [
        post.push(
            p_block,
            p_block,
            {"space": lax.rem(at.chip + step, at.chips) * 2 + at.core},
        )
        for step in range(1, at.chips)
    ]

    def expand_step(number, total):
        lanes = pl.ds(pl.multiple_of(number * piece, piece), piece)
        return total + dot_nt(l3[number], we[:, lanes])

    ag2 = lax.fori_loop(0, bands, expand_step, jnp.zeros((quarter, mid), f32))

    mask_mid = jnp.concatenate([mask_quarter] * (mid // LANE), axis=1)
    inv_mid = jnp.concatenate([inv_count] * (mid // LANE), axis=1)
    hat = (h2_ref[my_rows] - v2_ref[0:1]) * v2_ref[1:2]
    grad = gelu_slope(v2_ref[2:3] * hat + v2_ref[3:4]) * ag2 * mask_mid
    spread = mid // LANE

    def put_sums(target, first, second):
        for number in range(spread):
            lanes = slice(number * LANE, (number + 1) * LANE)
            target[number : number + 1] = first[:, lanes]
            target[spread + number : spread + number + 1] = second[:, lanes]

    def get_sums(total):
        return [
            jnp.concatenate([total[base + k : base + k + 1] for k in range(spread)], axis=1)
            for base in (0, spread)
        ]

    def to_twin(term, landing):
        return post.push(term.at[1 - at.core], landing, at.twin)

    def both_cores(pair, term, twin):
        pair.wait_recv()
        for step in range(1, at.chips):
            other = lax.rem(at.chip + step, at.chips)
            both = term[at.core, other].astype(f32) + twin[other].astype(f32)
            twin[other] = both.astype(low)

    def along(twin, landing):
        return [
            post.push(
                twin.at[other], landing.at[at.chip], {"space": other * 2 + at.core}
            )
            for other in [lax.rem(at.chip + step, at.chips) for step in range(1, at.chips)]
        ]

    def settle(arrivals, term, twin, landing):
        total = term[at.core, at.chip].astype(f32) + twin[at.chip].astype(f32)
        for made in arrivals:
            made.wait_recv()
        for step in range(1, at.chips):
            total = total + landing[lax.rem(at.chip + step, at.chips)].astype(f32)
        return total.astype(low)

    def to_tasks(share, landing):
        arrivals = [post.push(share, landing.at[task], {"task": other}) for other in at.other_tasks]
        landing[pl.ds(task, 1)] = share[...][None]
        return arrivals

    def expand_part(number):
        share = jnp.concatenate([l3x[a, number] for a in range(tasks)], axis=0)
        part = dot_nn(a2t[...], share).astype(low)
        per_band = part.shape[0] // bands
        for target in range(bands):
            e_term[target % 2, target // 2, :, number * piece : (number + 1) * piece] = part[
                target * per_band : (target + 1) * per_band
            ]

    narrow = mid // tasks
    my_lanes = pl.ds(pl.multiple_of(task * narrow, narrow), narrow)
    put_sums(
        st2, jnp.sum(grad, axis=0, keepdims=True), jnp.sum(grad * hat, axis=0, keepdims=True)
    )
    begun = at.sum_begin(post, "task", st2, st2_land)
    for made in l3_in:
        made.wait_recv()
    expand_part(0)
    st2_mid[...] = at.sum_end(begun)
    begun = at.sum_begin(post, "space", st2_mid, st2_land_b)
    for number in range(1, per_task):
        expand_part(number)
    e_pair = to_twin(e_term, e_twin)
    s2_out[...] = at.sum_end(begun)
    shift_grad, gain_grad = get_sums(s2_out[...])
    l2[my_rows] = (
        mask_mid
        * (v2_ref[2:3] * v2_ref[1:2])
        * (grad - shift_grad * inv_mid - hat * (gain_grad * inv_mid))
    ).astype(low)
    l2_in = [post.push(l2.at[my_rows], l2.at[my_rows], {"task": other}) for other in at.other_tasks]
    both_cores(e_pair, e_term, e_twin)
    e_in = along(e_twin, e_land)
    for made in l2_in:
        made.wait_recv()
    gate_in = [
        post.push(gate_low, gate_band.at[task], {"task": other}) for other in at.other_tasks
    ]
    gate_band[pl.ds(task, 1)] = gate_low[...][None]
    has_above, has_below = band > 0, band < bands - 1
    up = post.copy(l2, l2_halo.at[1], {"space": lax.rem(band + bands - 1, bands)})
    down = post.copy(l2, l2_halo.at[0], {"space": lax.rem(band + 1, bands)})

    @pl.when(has_above)
    def _():
        up.start()

    @pl.when(has_below)
    def _():
        down.start()

    @pl.when(jnp.logical_not(has_above))
    def _():
        l2_halo[0] = jnp.zeros_like(l2)

    @pl.when(jnp.logical_not(has_below))
    def _():
        l2_halo[1] = jnp.zeros_like(l2)

    p_passed = []
    for step, made in enumerate(p_far, start=1):
        made.wait_recv()
        block = p_all.at[lax.rem(at.chip + at.chips - step, at.chips) * 2 + at.core]
        p_passed.append(post.push(block, block, at.twin))
    loaded("wd")
    halves = [slice(start, start + piece) for start in range(0, mid, piece)]
    for lanes in halves:
        total = None
        for col_tap in range(3):
            part = shift_pixels(
                dot_nt(l2[...], wd[3 + col_tap, lanes, :]), -CONV_DILATION * (col_tap - 1), cols
            )
            total = part if total is None else total + part
        ag1[:, lanes] = total

    @pl.when(has_below)
    def _():
        up.wait_recv()

    @pl.when(has_above)
    def _():
        down.wait_recv()

    for lanes in halves:
        total = None
        for col_tap in range(3):
            part = dot_nt(l2_halo[1], wd[col_tap, lanes, :]) + dot_nt(
                l2_halo[0], wd[6 + col_tap, lanes, :]
            )
            part = shift_pixels(part, -CONV_DILATION * (col_tap - 1), cols)
            total = part if total is None else total + part
        ag1[:, lanes] += total

    pixels = ag1.shape[0]
    chunk = pixels // 8

    def first_rows(number):
        return pl.ds(pl.multiple_of(number * chunk, chunk), chunk)

    def first_step(number, sums):
        rows = first_rows(number)
        hat = (h1_ref[rows] - v1_ref[0:1]) * v1_ref[1:2]
        keep = jnp.concatenate([mask_ref[rows]] * spread, axis=1)
        grad = gelu_slope(v1_ref[2:3] * hat + v1_ref[3:4]) * ag1[rows] * keep
        ag1[rows] = grad
        return (
            sums[0] + jnp.sum(grad, axis=0, keepdims=True),
            sums[1] + jnp.sum(grad * hat, axis=0, keepdims=True),
        )

    nothing = jnp.zeros((1, mid), f32)
    first, second = lax.fori_loop(0, 8, first_step, (nothing, nothing))
    put_sums(st1, first, second)
    begun = at.sum_begin(post, "space", st1, st1_land)
    l2c[pl.ds(band, 1)] = l2[:, my_lanes][None]
    l2_block = l2c.at[band]
    d_far = [
        post.push(
            l2_block,
            l2_block,
            {"space": lax.rem(at.chip + step, at.chips) * 2 + at.core},
        )
        for step in range(1, at.chips)
    ]
    d_near = [post.push(l2_block, l2_block, at.twin)]
    e_share[...] = settle(e_in, e_term, e_twin, e_land)
    s1_out[...] = at.sum_end(begun)
    shift_grad, gain_grad = get_sums(s1_out[...])
    shift_grad, gain_grad = shift_grad * inv_mid, gain_grad * inv_mid

    def first_finish(number, carry):
        rows = first_rows(number)
        hat = (h1_ref[rows] - v1_ref[0:1]) * v1_ref[1:2]
        keep = jnp.concatenate([mask_ref[rows]] * spread, axis=1)
        l1[rows] = (
            keep * (v1_ref[2:3] * v1_ref[1:2]) * (ag1[rows] - shift_grad - hat * gain_grad)
        ).astype(low)
        return carry

    lax.fori_loop(0, 8, first_finish, 0)

    share_r = l1[:, my_lanes]
    per_band_r = wide // bands

    def reduce_step(number, carry):
        rows = pl.ds(pl.multiple_of(number * per_band_r, per_band_r), per_band_r)
        r_term[lax.rem(number, 2), number // 2] = dot_nn(xt[rows, :], share_r).astype(low)
        return carry

    lax.fori_loop(0, bands, reduce_step, 0)
    r_pair = to_twin(r_term, r_twin)
    e_back = to_tasks(e_share, e_tasks)
    both_cores(r_pair, r_term, r_twin)
    r_in = along(r_twin, r_land)

    for step, made in enumerate(d_far, start=1):
        made.wait_recv()
        block = l2c.at[lax.rem(at.chip + at.chips - step, at.chips) * 2 + at.core]
        d_near.append(post.push(block, block, at.twin))

    loaded("wr")
    for made in gate_in:
        made.wait_recv()

    def input_step(number, carry):
        lanes = pl.ds(pl.multiple_of(number * piece, piece), piece)
        gates = jnp.concatenate([gate_band[a, number] for a in range(tasks)], axis=0).astype(f32)
        ig_out[:, lanes] = (dot_nt(l1[...], wr[lanes, :]) + gates).astype(low)
        return carry

    lax.fori_loop(0, bands, input_step, 0)
    write(ig_out, ig_hbm)
    for source, target in ((tw_out, tw_hbm), (s3_out, s3_hbm), (s2_out, s2_hbm), (s1_out, s1_hbm)):
        write(source, target)
    for step in range(bands - 1):
        part_copy(step).wait()
    for made in d_near:
        made.wait_recv()
    d_sum[...] = jnp.zeros_like(d_sum)

    def dilated_step(number, carry):
        left = jnp.concatenate([act_ref[number + row_tap] for row_tap in range(3)], axis=0)
        right = l2c[number].astype(f32)
        for col_tap in range(3):
            moved = shift_pixels(right, -CONV_DILATION * (col_tap - 1), cols).astype(low)
            d_sum[col_tap] += dot_nn(left, moved)
        return carry

    lax.fori_loop(0, bands, dilated_step, 0)
    part = d_share.shape[1]
    for row_tap in range(3):
        for col_tap in range(3):
            d_share[3 * row_tap + col_tap] = d_sum[
                col_tap, row_tap * part : (row_tap + 1) * part
            ].astype(low)
    d_back = to_tasks(d_share, d_tasks)
    r_share[...] = settle(r_in, r_term, r_twin, r_land)
    r_back = to_tasks(r_share, r_tasks)
    for made in [p_near] + p_passed:
        made.wait_recv()
    pg_out[...] = p_all[...]
    write(pg_out, pg_hbm)
    for made in e_back:
        made.wait_recv()
    broad = wide // tasks
    for a in range(tasks):
        eg_out[:, a * broad : (a + 1) * broad] = e_tasks[a].astype(f32)
    write(eg_out, eg_hbm)
    for made in d_back:
        made.wait_recv()
    for a in range(tasks):
        dg_out[:, :, a * narrow : (a + 1) * narrow] = d_tasks[a].astype(f32)
    write(dg_out, dg_hbm)
    for made in r_back:
        made.wait_recv()
    for a in range(tasks):
        rg_out[:, a * narrow : (a + 1) * narrow] = r_tasks[a].astype(f32)
    write(rg_out, rg_hbm)
    post.close()

    @pl.when(has_above)
    def _():
        up.wait_send()

    @pl.when(has_below)
    def _():
        down.wait_send()


def head_phase(
    at,
    post,
    plan,
    rate_loads,
    sh_ref,
    widths_ref,
    gain_ref,
    shift_ref,
    cot_ref,
    bw_ref,
    pw_ref,
    head_out,
    xg_out,
    grads_out,
    proj_share,
    both_sums_out,
    proj_sums_out,
    rate,
    turned,
    extra,
    term,
    twin_land,
    right_land,
    left_land,
    pre,
    joined,
    upstream,
    cot,
    out_rows,
    masks,
    projected,
    proj_up,
    proj_low,
    pixel_sum,
    st_both,
    st_both_sum,
    st_both_land,
    st_proj,
    st_proj_sum,
    st_proj_land,
    st_pback,
    st_pback_land,
    st_back,
    st_back_land,
    st_rim_sum,
    st_rim,
    st_rim_land,
    both_all,
    moved,
    grads,
    back,
    sg,
    proj_term,
    p_twin,
    p_land,
):
    tasks, bands, cols, pixels, width, taps, extras = plan
    low, f32 = jnp.bfloat16, jnp.float32
    send_sem, recv_sem = post.send_sem, post.recv_sem
    chips, chip, core, band = at.chips, at.chip, at.core, at.band
    last, half = chips - 1, chips // 2
    group = 2 * pixels
    band_rows = pixels // cols
    spread = width // LANE
    number_of = {tap[:3]: number for number, tap in enumerate(taps)}
    moved_levels = sorted({entry[0] for entry in extras})
    late = sorted({entry[2] for entry in extras})
    slots = moved_levels + [branch for branch in range(4) if branch not in moved_levels]
    side = chip // half
    is_end = (chip == 0) | (chip == last)
    next_chip = lax.rem(chip + 1, chips)
    prev_chip = lax.rem(chip + last, chips)
    own = side * (half - 1)

    def reserve(count):
        first = post.used
        post.used += count
        return first

    def hop(source, landing, device_chip, number):
        return pltpu.make_async_remote_copy(
            source,
            landing,
            send_sem.at[number],
            recv_sem.at[number],
            device_id={"space": device_chip * 2 + core},
            device_id_type=MESH_ID,
        )

    def to_twin(source, landing, number):
        return pltpu.make_async_remote_copy(
            source,
            landing,
            send_sem.at[number],
            recv_sem.at[number],
            device_id=at.twin,
            device_id_type=MESH_ID,
        )

    first_cot = reserve(half)

    def send_cot(number):
        return hop(cot_ref, cot.at[number], side * last, first_cot + number)

    for load in rate_loads:
        load.wait()
    cot[pl.ds(own, 1)] = cot_ref[...][None]

    @pl.when(jnp.logical_not(is_end))
    def _():
        send_cot(chip - side * half).start()

    def rows_of(ref, number):
        return jnp.concatenate([ref[2 * number], ref[2 * number + 1]], axis=0)

    def right_of(level, col_tap):
        return (col_tap - 1) * level * RATE

    def forward_taps(source, level, row_tap):
        total = None
        for col_tap in range(3):
            number = number_of.get((level, row_tap, col_tap))
            if number is None:
                continue
            part = shift_pixels(
                dot_nn(source, rate[number]), right_of(level, col_tap), cols
            )
            total = part if total is None else total + part
        return total

    extra[...] = jnp.zeros_like(extra)
    for level, target, source, row_tap in extras:
        extra[moved_levels.index(level), target // last] += forward_taps(
            rows_of(sh_ref, source), level, row_tap
        )

    first_twin = reserve(4 * chips)

    def twin_term(number, branch):
        return to_twin(
            term.at[number, 1 - core, branch],
            twin_land.at[number, branch],
            first_twin + 4 * number + branch,
        )

    def forward_group(step, carry):
        number = lax.rem(step + half * (1 - side), chips)
        at_rim = jnp.where(lax.rem(number, last) == 0, 1.0, 0.0)
        source = rows_of(sh_ref, number)
        for branch in slots:
            if branch == 0:
                value = dot_nn(source, bw_ref[:, :width])
            else:
                value = forward_taps(source, branch, 1)
                if branch in moved_levels:
                    value = value + at_rim * extra[moved_levels.index(branch), number // last]
            value = value.astype(low)
            term[number, 0, branch] = value[:pixels]
            term[number, 1, branch] = value[pixels:]
            twin_term(number, branch).start()
        return carry

    first_right, first_left = reserve(8 * half), reserve(8 * half)
    portion = pixels // 2

    def rows_at(part):
        return pl.ds(part * portion, portion)

    def go_right(number, branch, part):
        return hop(
            twin_land.at[half + number, branch, rows_at(part)],
            right_land.at[number, branch, rows_at(part)],
            next_chip,
            first_right + 8 * number + 2 * branch + part,
        )

    def go_left(number, branch, part):
        return hop(
            twin_land.at[number, branch, rows_at(part)],
            left_land.at[number, branch, rows_at(part)],
            prev_chip,
            first_left + 8 * number + 2 * branch + part,
        )

    def both_cores(number, branch):
        twin_term(number, branch).wait_recv()
        return term[number, core, branch].astype(f32) + twin_land[number, branch].astype(f32)

    def start_off(number, copy_of):
        for branch in slots:
            twin_land[number, branch] = both_cores(number, branch).astype(low)
            for part in range(2):
                copy_of(branch, part).start()

    for number in range(half):
        lax.fori_loop(number, number + 1, forward_group, 0)

        @pl.when(chip == 0)
        def _():
            start_off(half + number, functools.partial(go_right, number))

        @pl.when(chip == last)
        def _():
            start_off(number, functools.partial(go_left, number))

    lax.fori_loop(half, chips, forward_group, 0)

    def pass_on(number, branch, part, copy, landing):
        if part == 0:
            twin_term(number, branch).wait_recv()
        copy.wait_recv()
        rows = rows_at(part)
        twin_land[number, branch, rows] = (
            term[number, core, branch, rows].astype(f32)
            + twin_land[number, branch, rows].astype(f32)
            + landing[rows].astype(f32)
        ).astype(low)
        copy.start()

    def pass_right(number, branch, part):
        landing = right_land.at[number, branch]
        pass_on(half + number, branch, part, go_right(number, branch, part), landing)

    def pass_left(number, branch, part):
        landing = left_land.at[number, branch]
        pass_on(number, branch, part, go_left(number, branch, part), landing)

    order = [
        (number, branch, part) for number in range(half) for branch in slots for part in range(2)
    ]

    def pass_both(near, far):
        for step in range(len(order) + FAR_LAG):
            if step < len(order):
                near(*order[step])
            if step >= FAR_LAG:
                far(*order[step - FAR_LAG])

    @pl.when(jnp.logical_not(is_end) & (side == 0))
    def _():
        pass_both(pass_right, pass_left)

    @pl.when(jnp.logical_not(is_end) & (side == 1))
    def _():
        pass_both(pass_left, pass_right)

    pixel_sum[...] = jnp.zeros_like(pixel_sum)

    def turn_group(number, carry):
        source = rows_of(sh_ref, number)
        turned[:, pl.ds(pl.multiple_of(number * group, group), group)] = source.T
        pixel_sum[0:1] += jnp.sum(source.astype(f32), axis=0, keepdims=True)
        return carry

    lax.fori_loop(0, chips, turn_group, 0)
    inv_count = jnp.concatenate([1.0 / count_pixels(widths_ref)] * spread, axis=1)

    def put_rows(target, number, value):
        for part in range(spread):
            target[pl.ds(number * spread + part, 1), :] = value[:, part * LANE : (part + 1) * LANE]

    def add_rows(target, number, value):
        for part in range(spread):
            target[pl.ds(number * spread + part, 1), :] += value[
                :, part * LANE : (part + 1) * LANE
            ]

    def get_rows(target, number):
        return jnp.concatenate(
            [target[pl.ds(number * spread + part, 1), :] for part in range(spread)], axis=1
        )

    def column_sum(value):
        return jnp.sum(value, axis=0, keepdims=True)

    def mask_of(number):
        return jnp.concatenate([masks[number]] * spread, axis=1)

    for target in (st_both, st_proj, st_pback, st_back, st_rim):
        target[...] = jnp.zeros_like(target)
    for number in range(half):
        masks[number] = row_mask(
            widths_ref, (2 * (side * half + number) + core) * band_rows, band_rows, cols
        )

    def settle(copy_of, landing):
        def step_of(step, carry):
            number, branch = step // 4, lax.rem(step, 4)
            total = both_cores(side * half + number, branch)
            for part in range(2):
                copy_of(number, branch, part).wait_recv()
            value = total + landing[number, branch].astype(f32)
            pre[number, branch] = value
            kept = value * mask_of(number)
            add_rows(st_both, branch, column_sum(kept))
            add_rows(st_both, 4 + branch, column_sum(kept * value))
            return carry

        lax.fori_loop(0, 4 * half, step_of, 0)

    @pl.when(chip == 0)
    def _():
        settle(go_left, left_land)

    @pl.when(chip == last)
    def _():
        settle(go_right, right_land)

    sums_now = pixel_sum[0:1]
    high = sums_now.astype(low)
    rest = sums_now - high.astype(f32)
    middle = rest.astype(low)
    tail = (rest - middle.astype(f32)).astype(low)
    pieces = jnp.concatenate(
        [high.astype(f32), middle.astype(f32), tail.astype(f32), jnp.zeros((13, width), f32)],
        axis=0,
    ).astype(low)
    put_rows(st_both, 8, column_sum(dot_nn(pieces, bw_ref[:, width:])))
    st_both_sum[...] = at.sum_over(post, "space", st_both, st_both_land)
    pooled = get_rows(st_both_sum, 8) * inv_count

    def lanes_of(number):
        return pl.ds(pl.multiple_of(number * width, width), width)

    def scale_of(target, first, second):
        mean_value = get_rows(target, first) * inv_count
        variance = get_rows(target, second) * inv_count - mean_value * mean_value
        return mean_value, lax.rsqrt(variance + NORM_EPS)

    def at_ends(body, count):
        @pl.when(is_end)
        def _():
            lax.fori_loop(0, count, body, 0)

    pool_lanes = slice(4 * width, 5 * width)

    def pool_step(number, carry):
        joined[number, 4] = (
            gelu_of(pooled).astype(low).astype(f32) * mask_of(number)
        ).astype(low)
        projected[number] = dot_nn(joined[number, 4], pw_ref[pool_lanes, :])
        return carry

    at_ends(pool_step, half)

    def activate(step, carry):
        number, branch = step // 4, lax.rem(step, 4)
        mean_value, inv_std = scale_of(st_both_sum, branch, 4 + branch)
        hat = (pre[number, branch] - mean_value) * inv_std
        pre[number, branch] = hat
        normed = gain_ref[:, lanes_of(branch)] * hat + shift_ref[:, lanes_of(branch)]
        active, slope = gelu_both(normed)
        keep = mask_of(number)
        active = (active * keep).astype(low)
        upstream[number, branch] = slope * keep
        joined[number, branch] = active
        projected[number] += dot_nn(active, pw_ref[lanes_of(branch), :])
        return carry

    at_ends(activate, 4 * half)

    def project_sums(number, carry):
        value = projected[number]
        kept = value * mask_of(number)
        add_rows(st_proj, 0, column_sum(kept))
        add_rows(st_proj, 1, column_sum(kept * value))
        return carry

    at_ends(project_sums, half)
    st_proj_sum[...] = at.sum_over(post, "space", st_proj, st_proj_land)
    proj_mean, proj_inv = scale_of(st_proj_sum, 0, 1)
    gain_proj = gain_ref[:, pool_lanes]

    def proj_back(number, carry):
        hat = (projected[number] - proj_mean) * proj_inv
        projected[number] = hat
        normed = gain_proj * hat + shift_ref[:, pool_lanes]
        keep = mask_of(number)
        active, slope = gelu_both(normed)
        up = slope * cot[number].astype(f32) * keep
        proj_up[number] = up
        add_rows(st_pback, 0, column_sum(up))
        add_rows(st_pback, 1, column_sum(up * hat))
        out_rows[number] = (active * keep).astype(low)
        return carry

    @pl.when(is_end)
    def _():
        for number in range(half):

            @pl.when(own != number)
            def _():
                send_cot(number).wait_recv()

    at_ends(proj_back, half)
    proj_sums_out[...] = at.sum_over(post, "space", st_pback, st_pback_land)
    shift_proj, gain_grad_proj = get_rows(proj_sums_out, 0), get_rows(proj_sums_out, 1)

    def proj_finish(number, carry):
        keep = mask_of(number)
        proj_low[number] = (
            keep
            * (gain_proj * proj_inv)
            * (
                proj_up[number]
                - shift_proj * inv_count
                - projected[number] * (gain_grad_proj * inv_count)
            )
        ).astype(low)
        return carry

    def pool_back(number, carry):
        joined_grad = dot_nt(proj_low[number], pw_ref[pool_lanes, :])
        add_rows(st_back, 8, column_sum(joined_grad * mask_of(number)))
        return carry

    def back_step(branch):
        def step_of(number, carry):
            joined_grad = dot_nt(proj_low[number], pw_ref[lanes_of(branch), :])
            hat = pre[number, branch]
            up = upstream[number, branch] * joined_grad
            upstream[number, branch] = up
            shift_sum, gain_sum = column_sum(up), column_sum(up * hat)
            add_rows(st_back, branch, shift_sum)
            add_rows(st_back, 4 + branch, gain_sum)
            if branch == slots[0]:
                add_rows(st_rim, 0, shift_sum)
                add_rows(st_rim, 1, gain_sum)
            return carry

        return step_of

    at_ends(proj_finish, half)
    at_ends(back_step(slots[0]), half)
    begun_rim = at.sum_begin(post, "space", st_rim, st_rim_land)
    at_ends(pool_back, half)
    for branch in slots[1:]:
        at_ends(back_step(branch), half)
    begun_back = at.sum_begin(post, "space", st_back, st_back_land)
    st_rim_sum[...] = at.sum_end(begun_rim)

    order = [(number, branch) for branch in moved_levels for number in range(half)]
    order += [
        (number, branch)
        for number in range(half)
        for branch in slots
        if branch not in moved_levels
    ]
    first_right_all, first_left_all = reserve(8 * half), reserve(8 * half)
    first_twin_all, first_out = reserve(8 * chips), reserve(half)

    def block_of(number, branch, part):
        return both_all.at[number * 2 + core, branch, rows_at(part)]

    def along_right(number, branch, part):
        block = block_of(number, branch, part)
        return hop(block, block, next_chip, first_right_all + 8 * number + 2 * branch + part)

    def along_left(number, branch, part):
        block = block_of(half + number, branch, part)
        return hop(block, block, prev_chip, first_left_all + 8 * number + 2 * branch + part)

    def hand_over(number, branch, part):
        block = block_of(number, branch, part)
        return to_twin(block, block, first_twin_all + 8 * number + 2 * branch + part)

    def make_both(number, branch):
        _, inv_std = scale_of(st_both_sum, branch, 4 + branch)
        if branch == slots[0]:
            sums = get_rows(st_rim_sum, 0), get_rows(st_rim_sum, 1)
        else:
            sums = get_rows(both_sums_out, branch), get_rows(both_sums_out, 4 + branch)
        shift_grad, gain_grad = sums[0] * inv_count, sums[1] * inv_count
        both_all[2 * (side * half + number) + core, branch] = (
            mask_of(number)
            * (gain_ref[:, lanes_of(branch)] * inv_std)
            * (upstream[number, branch] - shift_grad - pre[number, branch] * gain_grad)
        ).astype(low)

    parts = [(number, branch, part) for number, branch in order for part in range(2)]
    by_halves = [entry for entry in order[half:] if entry[0] == half - 1]
    parts = parts[: -2 * len(by_halves)]
    parts += [entry + (part,) for part in range(2) for entry in by_halves]

    def send_out(number):
        return hop(out_rows.at[number], head_out, side * half + number, first_out + number)

    def send_parts(some):
        made = set()
        for number, branch, part in some:
            if (number, branch) not in made:
                make_both(number, branch)
                made.add((number, branch))

            @pl.when(chip == 0)
            def _():
                along_right(number, branch, part).start()
                hand_over(number, branch, part).start()

            @pl.when(chip == last)
            def _():
                along_left(number, branch, 1 - part).start()
                hand_over(half + number, branch, 1 - part).start()

    @pl.when(is_end)
    def _():
        send_parts([entry for entry in parts if entry[1] == slots[0]])

    both_sums_out[...] = at.sum_end(begun_back)
    pool_grad = (gelu_slope(pooled) * get_rows(both_sums_out, 8)).astype(low)

    @pl.when(is_end)
    def _():
        send_parts([entry for entry in parts if entry[1] != slots[0]])
        for number in range(half):

            @pl.when(own != number)
            def _():
                send_out(number).start()

        head_out[...] = out_rows[own]

    def proj_step(branch, carry):
        total = dot_nn(joined[0, branch].T, proj_low[0])
        for number in range(1, half):
            total = total + dot_nn(joined[number, branch].T, proj_low[number])
        proj_term[lanes_of(branch), :] = total.astype(low)
        return carry

    at_ends(proj_step, 5)

    rows_p = proj_share.shape[0]

    def proj_rows(number):
        return pl.ds(pl.multiple_of(number * rows_p, rows_p), rows_p)

    first_pair, first_p = reserve(chips), reserve(2 * chips)

    def p_pair(number):
        return to_twin(
            proj_term.at[proj_rows(2 * number + 1 - core)], p_twin.at[number], first_pair + number
        )

    def p_hop(end, number):
        return hop(p_twin.at[number], p_land.at[end], number, first_p + end * chips + number)

    @pl.when(is_end)
    def _():
        for number in range(chips):
            p_pair(number).start()

    def send_projection():
        for number in range(chips):
            p_pair(number).wait_recv()
            both = proj_term[proj_rows(2 * number + core)].astype(f32)
            p_twin[number] = (both + p_twin[number].astype(f32)).astype(low)

            @pl.when(chip != number)
            def _():
                p_hop(side, number).start()

    grads[...] = jnp.zeros_like(grads)
    pool_row = dot_nt(
        jnp.broadcast_to(pool_grad, (16, width)), bw_ref[:, width:]
    )[0:1] * inv_count
    quarter = pixels // tasks
    my_rows = pl.ds(pl.multiple_of(at.task * quarter, quarter), quarter)
    first_task = reserve(chips * len(at.other_tasks))

    def to_task(number, turn):
        other = at.other_tasks[turn]
        theirs = pl.ds(pl.multiple_of(other * quarter, quarter), quarter)
        two = pl.ds(2 * number, 2)
        spot = first_task + number * len(at.other_tasks) + turn
        return pltpu.make_async_remote_copy(
            sg.at[two, theirs],
            xg_out.at[at.task, two],
            send_sem.at[spot],
            recv_sem.at[spot],
            device_id={"task": other},
            device_id_type=MESH_ID,
        )

    def finish_group(number, part=None):
        some = band_rows if part is None else band_rows // 2
        for place in range(2):
            first = (2 * number + place) * band_rows + (0 if part is None else part * some)
            keep = row_mask(widths_ref, first, some, cols)
            keep = jnp.concatenate([keep] * spread, axis=1)
            start = 0 if part is None else part * portion
            rows = slice(start, start + some * cols)
            value = back[number, place * pixels + start : place * pixels + start + some * cols]
            sg[2 * number + place, rows] = (value + keep * pool_row).astype(low)

        def there(task):
            return task >= 0 if part is None else task // (tasks // 2) == part

        for turn, other in enumerate(at.other_tasks):

            @pl.when(there(other))
            def _():
                to_task(number, turn).start()

        @pl.when(there(at.task))
        def _():
            for place in range(2):
                xg_out[at.task, 2 * number + place] = sg[2 * number + place, my_rows]

    def back_part(number, branch, part=None):
        for piece in range(2) if part is None else (part,):
            hand_over(number, branch, piece).wait_recv()
        rows = slice(0, pixels) if part is None else slice(part * portion, (part + 1) * portion)
        count = rows.stop - rows.start
        starts = [(2 * number + place) * pixels + rows.start for place in range(2)]
        columns = jnp.concatenate([turned[:, start : start + count] for start in starts], axis=1)
        image = jnp.concatenate(
            [both_all[2 * number, branch, rows], both_all[2 * number + 1, branch, rows]], axis=0
        )
        if branch == 0:
            total = dot_nt(image, bw_ref[:, :width])
            grads[len(taps)] += dot_nn(columns, image)
        else:
            total = None
            image = image.astype(f32)
            for col_tap in range(3):
                tap = number_of.get((branch, 1, col_tap))
                if tap is None:
                    continue
                moved_now = shift_pixels(image, -right_of(branch, col_tap), cols).astype(low)
                if branch in moved_levels and number in late:
                    moved[moved_levels.index(branch), number // last, col_tap] = moved_now
                now = dot_nt(moved_now, rate[tap])
                total = now if total is None else total + now
                grads[tap] += dot_nn(columns, moved_now)
        for place in range(2):
            target = slice(place * pixels + rows.start, place * pixels + rows.stop)
            share = total[place * count : (place + 1) * count]
            if branch == slots[0]:
                back[number, target] = share
            else:
                back[number, target] += share

    def far_taps():
        for level, target, source, row_tap in extras:
            columns = turned[:, source * group : (source + 1) * group]
            total = back[source]
            for col_tap in range(3):
                tap = number_of.get((level, row_tap, col_tap))
                if tap is None:
                    continue
                part = moved[moved_levels.index(level), target // last, col_tap]
                total = total + dot_nt(part, rate[tap])
                grads[tap] += dot_nn(columns, part)
            back[source] = total

    def take_right(number, branch, part):
        along_right(number, branch, part).wait_recv()

        @pl.when(chip < last)
        def _():
            along_right(number, branch, part).start()

        hand_over(number, branch, part).start()

    def take_left(number, branch, part):
        along_left(number, branch, part).wait_recv()

        @pl.when(chip > 0)
        def _():
            along_left(number, branch, part).start()

        hand_over(half + number, branch, part).start()

    for step in range(len(parts) + FAR_LAG + 1):
        if step < len(parts):
            number, branch, part = parts[step]

            @pl.when(jnp.logical_not(is_end) & (side == 0))
            def _():
                take_right(number, branch, part)

            @pl.when(jnp.logical_not(is_end) & (side == 1))
            def _():
                take_left(number, branch, 1 - part)

        if FAR_LAG <= step < len(parts) + FAR_LAG:
            number, branch, part = parts[step - FAR_LAG]

            @pl.when(side == 0)
            def _():
                take_left(number, branch, 1 - part)

            @pl.when(side == 1)
            def _():
                take_right(number, branch, part)

        if step == len(parts) + SEND_LAG:

            @pl.when(is_end)
            def _():
                send_projection()

        done = step - FAR_LAG - 1
        if done < 0:
            continue
        number, branch, part = parts[done]
        if (number, branch) in by_halves:
            back_part(number, branch, part)
            back_part(half + number, branch, 1 - part)
            if (number, branch) == by_halves[-1]:
                finish_group(number, part)
                finish_group(half + number, 1 - part)
        elif part == 1:
            back_part(number, branch)
            back_part(half + number, branch)
            if (number, branch) == order[half - 1]:
                far_taps()
            if branch == slots[3]:
                finish_group(number)
                finish_group(half + number)

    column = jnp.broadcast_to(pixel_sum[0:1], (8, width)).T[:, 0:1]
    grads_out[len(taps) + 1] = (column * (pool_grad.astype(f32) * inv_count)).astype(low)

    def finish_tap(number, carry):
        grads_out[number] = grads[number].astype(low)
        return carry

    lax.fori_loop(0, len(taps) + 1, finish_tap, 0)
    for end in range(2):

        @pl.when(chip == end * last)
        def _():
            p_land[end] = p_twin[end * last]

        @pl.when(chip != end * last)
        def _():
            p_hop(end, chip).wait_recv()

    proj_share[...] = (p_land[0].astype(f32) + p_land[1].astype(f32)).astype(low)

    def tasks_in(number, carry):
        for turn in range(len(at.other_tasks)):
            to_task(number, turn).wait()
        return carry

    lax.fori_loop(0, chips, tasks_in, 0)

    @pl.when(jnp.logical_not(is_end))
    def _():
        send_out(chip - side * half).wait_recv()
        send_cot(chip - side * half).wait_send()

    post.close()

    def twin_left(number, carry):
        for branch in range(4):
            twin_term(number, branch).wait_send()
            for part in range(2):
                hand_over(number, branch, part).wait_send()
        return carry

    lax.fori_loop(0, chips, twin_left, 0)

    def line_left(number, carry):
        for branch in range(4):
            for part in range(2):

                @pl.when(chip < last)
                def _():
                    go_right(number, branch, part).wait_send()
                    along_right(number, branch, part).wait_send()

                @pl.when(chip > 0)
                def _():
                    go_left(number, branch, part).wait_send()
                    along_left(number, branch, part).wait_send()

        return carry

    lax.fori_loop(0, half, line_left, 0)

    @pl.when(is_end)
    def _():
        for number in range(half):

            @pl.when(own != number)
            def _():
                send_out(number).wait_send()

        for number in range(chips):
            p_pair(number).wait_send()

            @pl.when(chip != number)
            def _():
                p_hop(side, number).wait_send()


def trunk_phase(
    at,
    post,
    sizes,
    when_loaded,
    norm_loads,
    part_copy,
    x_hbm,
    widths_ref,
    gain_ref,
    shift_ref,
    wr_hbm,
    wd_hbm,
    we_hbm,
    sh_out,
    act,
    h1,
    h2,
    a2,
    h3q,
    v1,
    v2,
    v3,
    stats_out,
    x,
    wr,
    wd,
    we,
    rim,
    turned,
    h3,
    blocks,
    mask_own,
    st1,
    st1_land,
    st2,
    st2_land,
    st3,
    st3_land,
    local_sem,
):
    tasks, bands, cols, quarter, mid, wide, piece = sizes
    low, f32 = jnp.bfloat16, jnp.float32
    task, band = at.task, at.band
    my_rows = pl.ds(pl.multiple_of(task * quarter, quarter), quarter)
    depth = x.shape[1] // 4
    pieces = []
    for number in range(4):
        some = slice(number * depth, (number + 1) * depth)
        pieces.append(
            (
                some,
                pltpu.make_async_copy(x_hbm.at[:, some], x.at[:, some], local_sem.at[2 * number]),
                pltpu.make_async_copy(wr_hbm.at[some], wr.at[some], local_sem.at[2 * number + 1]),
            )
        )
    for _, of_x, of_weight in pieces:
        of_x.start()
        of_weight.start()
    loads = [
        pltpu.make_async_copy(wd_hbm, wd, local_sem.at[8]),
        pltpu.make_async_copy(we_hbm, we, local_sem.at[9]),
    ]
    at.greet()
    pixels = x.shape[0]
    band_rows = pixels // cols
    mask = row_mask(widths_ref, band * band_rows, band_rows, cols)
    count = count_pixels(widths_ref)
    spread = mid // LANE

    def across(value, lanes):
        return jnp.concatenate([value] * (lanes // LANE), axis=1)

    def put_sums(target, value, keep):
        kept = value * keep
        first = jnp.sum(kept, axis=0, keepdims=True)
        second = jnp.sum(kept * value, axis=0, keepdims=True)
        for number in range(spread):
            lanes = slice(number * LANE, (number + 1) * LANE)
            target[number : number + 1] = first[:, lanes]
            target[spread + number : spread + number + 1] = second[:, lanes]

    def get_sums(total):
        return [
            jnp.concatenate([total[base + k : base + k + 1] for k in range(spread)], axis=1)
            for base in (0, spread)
        ]

    def put_norm(vectors, lanes, first, second, start):
        width = first.shape[1]
        inv = across(1.0 / count, width)
        mean_value = first * inv
        variance = second * inv - mean_value * mean_value
        vectors[0:1, lanes] = mean_value
        vectors[1:2, lanes] = lax.rsqrt(variance + NORM_EPS)
        vectors[2:3, lanes] = gain_ref[:, start : start + width]
        vectors[3:4, lanes] = shift_ref[:, start : start + width]
        stats_out[0:1, start : start + width] = mean_value
        stats_out[1:2, start : start + width] = variance * across(count / (count - 1.0), width)

    def activate(hidden, vectors, keep):
        normed = vectors[2:3] * ((hidden - vectors[0:1]) * vectors[1:2]) + vectors[3:4]
        return (gelu_of(normed) * keep).astype(low)

    mask_mid = across(mask, mid)
    for number, (some, of_x, of_weight) in enumerate(pieces):
        of_x.wait()
        of_weight.wait()
        term = dot_nn(x[:, some], wr[some])
        if number == 0:
            h1[...] = term
        else:
            h1[...] += term
    for load in loads:
        load.start()
    at.meet()
    put_sums(st1, h1[...], mask_mid)
    begun = at.sum_begin(post, "space", st1, st1_land)
    for load in norm_loads:
        load.wait()
    first, second = get_sums(at.sum_end(begun))
    when_loaded()
    put_norm(v1, slice(0, mid), first, second, 0)
    rim[1] = activate(h1[...], v1, mask_mid)

    has_above, has_below = band > 0, band < bands - 1
    up = post.copy(rim.at[1], rim.at[2], {"space": lax.rem(band + bands - 1, bands)})
    down = post.copy(rim.at[1], rim.at[0], {"space": lax.rem(band + 1, bands)})

    @pl.when(has_above)
    def _():
        up.start()

    @pl.when(has_below)
    def _():
        down.start()

    @pl.when(jnp.logical_not(has_above))
    def _():
        rim[0] = jnp.zeros(rim.shape[1:], low)

    @pl.when(jnp.logical_not(has_below))
    def _():
        rim[2] = jnp.zeros(rim.shape[1:], low)

    loads[0].wait()
    halves = [slice(start, start + piece) for start in range(0, mid, piece)]

    def tap_sum(row_taps, lanes):
        total = None
        for col_tap in range(3):
            part = None
            for row_tap in row_taps:
                term = dot_nn(rim[row_tap], wd[3 * row_tap + col_tap, :, lanes])
                part = term if part is None else part + term
            part = shift_pixels(part, CONV_DILATION * (col_tap - 1), cols)
            total = part if total is None else total + part
        return total

    for lanes in halves:
        h2[:, lanes] = tap_sum((1,), lanes)

    turned[...] = rim[1].T

    @pl.when(has_below)
    def _():
        up.wait_recv()

    @pl.when(has_above)
    def _():
        down.wait_recv()

    for lanes in halves:
        h2[:, lanes] += tap_sum((0, 2), lanes)

    put_sums(st2, h2[...], mask_mid)
    first, second = get_sums(at.sum_over(post, "space", st2, st2_land))
    put_norm(v2, slice(0, mid), first, second, mid)
    a2[...] = activate(h2[...], v2, mask_mid)

    loads[1].wait()
    mask_piece = across(mask, piece)
    per_row = st3.shape[1] // piece
    half = st3.shape[0] // 2

    def expand_step(number, carry):
        lanes = pl.ds(pl.multiple_of(number * piece, piece), piece)
        value = dot_nn(a2[...], we[:, lanes])
        h3[:, lanes] = value
        kept = value * mask_piece
        row = number // per_row
        spot = pl.ds(pl.multiple_of(lax.rem(number, per_row) * piece, piece), piece)
        st3[pl.ds(row, 1), spot] = jnp.sum(kept, axis=0, keepdims=True)
        st3[pl.ds(half + row, 1), spot] = jnp.sum(kept * value, axis=0, keepdims=True)
        return carry

    lax.fori_loop(0, bands, expand_step, 0)
    begun = at.sum_begin(post, "space", st3, st3_land)
    h3q[...] = h3[my_rows]
    total = at.sum_end(begun)
    lanes_in = st3.shape[1]
    for row in range(half):
        put_norm(
            v3,
            slice(row * lanes_in, (row + 1) * lanes_in),
            total[row : row + 1],
            total[half + row : half + row + 1],
            2 * mid + row * lanes_in,
        )

    mask_own[...] = mask
    mask_quarter = across(mask_own[my_rows], piece)

    def shared_of(number):
        lanes = pl.ds(pl.multiple_of(number * piece, piece), piece)
        hat = (h3q[:, lanes] - v3[0:1, lanes]) * v3[1:2, lanes]
        before = v3[2:3, lanes] * hat + v3[3:4, lanes] + x[my_rows, lanes].astype(f32)
        return (gelu_of(before) * mask_quarter).astype(low)

    slices_in = []
    for other in at.other_bands:
        blocks[other] = shared_of(other)
        slices_in.append(
            post.push(blocks.at[other], sh_out.at[band, my_rows], {"space": other})
        )
    sh_out[band, my_rows] = shared_of(band)

    part = mid // bands

    def part_of(number):
        return turned.at[pl.ds(pl.multiple_of(number * part, part), part)]

    act[0] = jnp.zeros(act.shape[1:], low)
    act[bands + 1] = jnp.zeros(act.shape[1:], low)
    act[band + 1] = part_of(band)[...]
    for step in range(bands - 1):
        part_copy(step).start()

    def to_tasks(number):
        block = sh_out.at[number, my_rows]
        return [post.push(block, block, {"task": other}) for other in at.other_tasks]

    quarters_in = to_tasks(band)
    for step, made in enumerate(slices_in, start=1):
        made.wait_recv()
        quarters_in += to_tasks(lax.rem(band + bands - step, bands))
    for made in quarters_in:
        made.wait_recv()
    post.close()

    @pl.when(has_above)
    def _():
        up.wait_send()

    @pl.when(has_below)
    def _():
        down.wait_send()


class Held:
    def __init__(self, shape, dtype, passing=False):
        self.memory = pltpu.VMEM(shape, dtype)
        self.passing = passing


def with_phase(entries, refs, body):
    def run(*passing):
        passing, kept = list(passing), list(refs)
        body([(passing if entry.passing else kept).pop(0) for entry in entries])

    pl.run_scoped(run, *[entry.memory for entry in entries if entry.passing])


def whole_kernel(sizes, plan, phases, counts, *refs):
    refs = list(refs)

    def take(count):
        taken = refs[:count]
        del refs[:count]
        return taken

    x_hbm, widths, gain_hbm, shift_hbm, wr_hbm, wd_hbm, we_hbm = take(7)
    head_hbm_in = take(5)
    (rate_hbm,) = take(1)
    stats_hbm, head_hbm, grads_hbm, both_hbm, proj_hbm = take(5)
    back_hbm = take(counts[2])
    trunk_outs, head_outs = take(counts[0]), take(counts[1])
    gain, shift, *head_in = take(7)
    head_gain, head_shift, cot, bw, pw = head_in
    (shared,) = take(1)
    kept = [take(sum(not entry.passing for entry in entries)) for entries in phases]
    send_sem, recv_sem, local_sem, rate_sem, out_sem, in_sem = refs
    tasks, bands, width, taps = sizes[0], sizes[1], plan[4], plan[5]
    at = Place(tasks, bands)
    post = Post(send_sem, recv_sem)
    writes = []

    def write(source, target):
        copy = pltpu.make_async_copy(source, target, out_sem.at[len(writes)])
        copy.start()
        writes.append(copy)

    part = sizes[4] // bands
    first_part = post.used
    post.used += bands

    def part_copy(step):
        other = at.other_bands[step]
        return pltpu.make_async_remote_copy(
            kept[0][1].at[pl.ds(pl.multiple_of(other * part, part), part)],
            trunk_outs[0].at[at.band + 1],
            send_sem.at[first_part + step],
            recv_sem.at[first_part + step],
            device_id={"space": other},
            device_id_type=MESH_ID,
        )

    rate = kept[1][0]
    rate_loads = []
    for number, (level, row_tap, col_tap, _, _) in enumerate(taps):
        start = (9 * (level - 1) + 3 * row_tap + col_tap) * width
        rate_loads.append(
            pltpu.make_async_copy(
                rate_hbm.at[:, start : start + width], rate.at[number], rate_sem.at[number]
            )
        )

    norm_loads = [
        pltpu.make_async_copy(source, target, in_sem.at[number])
        for number, (source, target) in enumerate(((gain_hbm, gain), (shift_hbm, shift)))
    ]
    for load in norm_loads:
        load.start()
    rate_loads += [
        pltpu.make_async_copy(source, target, in_sem.at[2 + number])
        for number, (source, target) in enumerate(zip(head_hbm_in, head_in))
    ]

    def when_loaded():
        for load in rate_loads:
            load.start()

    def run_trunk(scratch):
        trunk_phase(
            at,
            post,
            sizes,
            when_loaded,
            norm_loads,
            part_copy,
            x_hbm,
            widths,
            gain,
            shift,
            wr_hbm,
            wd_hbm,
            we_hbm,
            shared,
            *trunk_outs,
            *scratch,
            local_sem,
        )

    def run_head(scratch):
        head_phase(
            at,
            post,
            plan,
            rate_loads,
            shared,
            widths,
            head_gain,
            head_shift,
            cot,
            bw,
            pw,
            *head_outs,
            *scratch,
        )

    with_phase(phases[0], kept[0], run_trunk)
    act, h1, h2, a2, h3q, v1, v2, v3, stats = trunk_outs
    write(stats, stats_hbm)
    with_phase(phases[1], kept[1], run_head)
    head_out, xg, grads_out, proj_share, both_sums, proj_sums = head_outs
    for source, target in (
        (head_out, head_hbm),
        (grads_out, grads_hbm),
        (both_sums, both_hbm),
        (proj_sums, proj_hbm),
    ):
        write(source, target)

    def run_back(scratch):
        back_phase(
            at,
            post,
            sizes,
            local_sem,
            part_copy,
            xg,
            h3q,
            v3,
            h2,
            v2,
            h1,
            v1,
            act,
            a2,
            proj_share,
            x_hbm,
            widths,
            we_hbm,
            wd_hbm,
            wr_hbm,
            write,
            *back_hbm,
            *scratch,
        )
        while len(writes) > before:
            writes.pop().wait()

    before = len(writes)
    with_phase(phases[2], kept[2], run_back)
    for copy in writes:
        copy.wait()


def whole(tasks, bands, cols, rows, collective, x, widths, gain, shift, wr, wd, we, *head_in):
    low, f32 = jnp.bfloat16, jnp.float32
    head_gain, head_shift, cot, bw, pw, rate = head_in
    pixels, wide = x.shape
    mid = wr.shape[1]
    quarter, piece = pixels // tasks, wide // bands
    width = pw.shape[1]
    chips = bands // 2
    group_rows = rows // chips
    taps = live_taps(rows, cols)
    extras = []
    for level in (1, 2, 3):
        for row_tap in (0, 2):
            if (level, row_tap, 1) in [tap[:3] for tap in taps]:
                away = (row_tap - 1) * level * RATE // group_rows
                extras += [
                    (level, target, target + away, row_tap)
                    for target in range(chips)
                    if 0 <= target + away < chips
                ]
    levels = max(len({entry[0] for entry in extras}), 1)
    anywhere = pl.BlockSpec(memory_space=pl.ANY)
    shape = jax.ShapeDtypeStruct
    block = (pixels, width)
    both_rows, proj_rows = -(-9 * width // LANE // 8) * 8, 8

    part, narrow, broad = mid // bands, mid // tasks, wide // tasks
    half = chips // 2
    pool_rows = pw.shape[0] // bands
    mid_rows, stat_wide = 2 * mid // LANE, wide // 4

    def kept(dims, dtype=low):
        return Held(tuple(dims), dtype)

    def passing(dims, dtype=low):
        return Held(tuple(dims), dtype, True)

    def over_bands(count, lanes=LANE):
        return [kept((count, lanes), f32), kept((bands, count, lanes), f32)]

    def over_all(count, lanes=LANE):
        return [kept((count, lanes), f32), kept((tasks, count, lanes), f32)] + over_bands(
            count, lanes
        )

    def terms(*dims):
        return [
            kept((2, chips) + dims),
            kept((chips,) + dims),
            kept((chips,) + dims),
            kept(dims),
            kept((tasks,) + dims),
        ]

    trunk_scratch = (
        [
            passing(x.shape),
            passing(wr.shape),
            passing(wd.shape),
            passing(we.shape),
            kept((3, pixels, mid)),
            kept((mid, pixels)),
            passing((pixels, wide), f32),
            kept((bands, quarter, piece)),
            passing((pixels, LANE), f32),
        ]
        + over_bands(mid_rows)
        + over_bands(mid_rows)
        + over_bands(8, stat_wide)
    )
    head_scratch = (
        [
            kept((len(taps), piece, width)),
            passing((piece, bands * pixels)),
            passing((levels, 2, 2 * pixels, width), f32),
            passing((chips, 2, 4) + block),
            kept((chips, 4) + block),
            kept((half, 4) + block),
            kept((half, 4) + block),
            passing((half, 4) + block, f32),
            passing((half, 5) + block),
            passing((half, 4) + block, f32),
            kept((half,) + block),
            passing((half,) + block),
            passing((half, pixels, LANE), f32),
            passing((half,) + block, f32),
            passing((half,) + block, f32),
            passing((half,) + block),
            passing((8, piece), f32),
            kept((both_rows, LANE), f32),
        ]
        + over_bands(both_rows)
        + [kept((proj_rows, LANE), f32)]
        + over_bands(proj_rows)
        + over_bands(proj_rows)
        + over_bands(both_rows)
        + [kept((proj_rows, LANE), f32)]
        + over_bands(proj_rows)
        + [
            kept((bands, 4) + block),
            passing((levels, 2, 3, 2 * pixels, width)),
            passing((len(taps) + 1, piece, width), f32),
            passing((chips, 2 * pixels, width), f32),
            passing((bands, pixels, piece)),
            passing(pw.shape),
            kept((chips, pool_rows, width)),
            kept((2, pool_rows, width)),
        ]
    )
    back_outs = (
        shape((8, LANE), f32),
        shape((pixels, wide), low),
        shape((piece, mid), f32),
        shape((9, part, mid), f32),
        shape((part, wide), f32),
        shape((8, stat_wide), f32),
        shape((mid_rows, LANE), f32),
        shape((mid_rows, LANE), f32),
        shape((bands, pool_rows, width), low),
    )
    back_scratch = (
        [kept(out.shape, out.dtype) for out in back_outs]
        + [
            passing(we.shape),
            passing(wd.shape),
            passing(wr.shape),
            passing(x.shape),
            passing((pixels, LANE), f32),
        ]
        + over_all(16)
        + [
            kept((bands, quarter, piece)),
            kept((bands, quarter, piece)),
            passing((bands, quarter, piece), f32),
            passing((bands, quarter, piece), f32),
            kept((bands, quarter, piece)),
            kept((tasks, bands, quarter, piece)),
        ]
        + over_all(8, stat_wide)
        + [
            kept((bands, quarter, piece)),
            kept((tasks, bands // tasks, quarter, piece)),
        ]
        + over_all(mid_rows)
        + [
            kept((pixels, mid)),
            kept((2, pixels, mid)),
            passing((pixels, mid), f32),
        ]
        + over_bands(mid_rows)
        + [
            passing((pixels, mid)),
            passing((wide, pixels)),
            passing((mid, pixels)),
        ]
        + terms(part, broad)
        + [
            kept((bands, pixels, narrow)),
            passing((3, 3 * part, narrow), f32),
            kept((9, part, narrow)),
            kept((tasks, 9, part, narrow)),
        ]
        + terms(piece, narrow)
        + [kept((bands, pool_rows, width))]
    )
    sizes = (tasks, bands, cols, quarter, mid, wide, piece)
    plan = (tasks, bands, cols, pixels, width, tuple(taps), tuple(extras))
    trunk_outs = (
        shape((bands + 2, part, pixels), low),
        shape((pixels, mid), f32),
        shape((pixels, mid), f32),
        shape((pixels, mid), low),
        shape((quarter, wide), f32),
        shape((8, mid), f32),
        shape((8, mid), f32),
        shape((8, wide), f32),
        shape((2, 2 * mid + wide), f32),
    )
    head_outs = (
        shape(block, low),
        shape((tasks, bands, quarter, piece), low),
        shape((len(taps) + 2, piece, width), low),
        shape((pool_rows, width), low),
        shape((both_rows, LANE), f32),
        shape((proj_rows, LANE), f32),
    )
    out_shapes = (trunk_outs[8], head_outs[0], head_outs[2], head_outs[4], head_outs[5])
    out_shapes += back_outs
    phases = (trunk_scratch, head_scratch, back_scratch)
    return taps, pl.pallas_call(
        functools.partial(
            whole_kernel, sizes, plan, phases, (len(trunk_outs), len(head_outs), len(back_outs))
        ),
        name="whole",
        out_shape=out_shapes,
        in_specs=[anywhere, pl.BlockSpec(memory_space=pltpu.SMEM)] + [anywhere] * 11,
        out_specs=(anywhere,) * len(out_shapes),
        scratch_shapes=[pltpu.VMEM(out.shape, out.dtype) for out in trunk_outs + head_outs]
        + [
            pltpu.VMEM(value.shape, value.dtype)
            for value in (gain, shift, head_gain, head_shift, cot, bw, pw)
        ]
        + [pltpu.VMEM((bands, pixels, piece), low)]
        + [entry.memory for entries in phases for entry in entries if not entry.passing]
        + [
            pltpu.SemaphoreType.DMA((352,)),
            pltpu.SemaphoreType.DMA((352,)),
            pltpu.SemaphoreType.DMA((10,)),
            pltpu.SemaphoreType.DMA((len(taps),)),
            pltpu.SemaphoreType.DMA((len(out_shapes),)),
            pltpu.SemaphoreType.DMA((7,)),
        ],
        compiler_params=pltpu.CompilerParams(
            collective_id=collective, has_side_effects=True, vmem_limit_bytes=60 << 20
        ),
    )(x, widths, gain, shift, wr, wd, we, *head_in)


def finish_kernel(
    places,
    tap_hbm,
    ho_in,
    ig_in,
    rg_in,
    dg_in,
    eg_in,
    bs_in,
    tw_hbm,
    pg_hbm,
    s3_hbm,
    s2_hbm,
    s1_hbm,
    both_hbm,
    proj_hbm,
    ho_out,
    ig_out,
    rg_out,
    dg_out,
    eg_out,
    bs_out,
    branch_out,
    rate_out,
    pg_hbm_out,
    tg_hbm_out,
    ts_hbm_out,
    hg_hbm_out,
    hs_hbm_out,
    tw_hbm_out,
    tap_ref,
    tw_ref,
    pg_ref,
    s3_ref,
    s2_ref,
    s1_ref,
    both_ref,
    proj_ref,
    ho_buf,
    ig_buf,
    rg_buf,
    dg_buf,
    eg_buf,
    bs_buf,
    branch,
    rate,
    pg_out,
    tg_out,
    ts_out,
    hg_out,
    hs_out,
    tw_out,
    sems,
    load_sems,
):
    f32 = jnp.float32
    width = tap_ref.shape[2]
    loads = [
        pltpu.make_async_copy(source, target, load_sems.at[number])
        for number, (source, target) in enumerate(
            (
                (tap_hbm, tap_ref),
                (pg_hbm, pg_ref),
                (tw_hbm, tw_ref),
                (s3_hbm, s3_ref),
                (s2_hbm, s2_ref),
                (s1_hbm, s1_ref),
                (both_hbm, both_ref),
                (proj_hbm, proj_ref),
            )
        )
    ]
    for load in loads:
        load.start()
    passed = [
        (ho_in, ho_buf, ho_out),
        (ig_in, ig_buf, ig_out),
        (rg_in, rg_buf, rg_out),
        (dg_in, dg_buf, dg_out),
        (eg_in, eg_buf, eg_out),
        (bs_in, bs_buf, bs_out),
    ]
    passes = [
        (
            pltpu.make_async_copy(source, buffer, load_sems.at[len(loads) + number]),
            pltpu.make_async_copy(buffer, target, sems.at[number]),
        )
        for number, (source, buffer, target) in enumerate(passed)
    ]
    for copy, _ in passes:
        copy.start()
    copies = [copy for _, copy in passes]
    per_level = len(places) // 3
    for number, place in enumerate(places):
        if place is None:
            rate[:, number * width : (number + 1) * width] = jnp.zeros(
                (rate.shape[0], width), f32
            )
    loads[0].wait()
    for level in range(3):
        for number in range(level * per_level, (level + 1) * per_level):
            lanes = slice(number * width, (number + 1) * width)
            if places[number] is not None:
                rate[:, lanes] = tap_ref[places[number]].astype(f32)
        lanes = slice(level * per_level * width, (level + 1) * per_level * width)
        copy = pltpu.make_async_copy(
            rate.at[:, lanes], rate_out.at[:, lanes], sems.at[len(copies)]
        )
        copy.start()
        copies.append(copy)
    for arrival, copy in passes:
        arrival.wait()
        copy.start()
    count = tap_ref.shape[0]
    branch[:, :width] = tap_ref[count - 2].astype(f32)
    branch[:, width:] = tap_ref[count - 1].astype(f32)
    copy = pltpu.make_async_copy(branch, branch_out, sems.at[len(copies)])
    copy.start()
    copies.append(copy)
    loads[1].wait()
    pg_out[...] = pg_ref[...].astype(f32)
    copy = pltpu.make_async_copy(pg_out, pg_hbm_out, sems.at[len(copies)])
    copy.start()
    copies.append(copy)
    for load in loads[2:]:
        load.wait()
    rows = s1_ref.shape[0] // 2
    ts_out[0:rows] = s1_ref[0:rows]
    tg_out[0:rows] = s1_ref[rows : 2 * rows]
    ts_out[rows : 2 * rows] = s2_ref[0:rows]
    tg_out[rows : 2 * rows] = s2_ref[rows : 2 * rows]
    half, lanes_in = s3_ref.shape[0] // 2, s3_ref.shape[1]
    for row in range(half):
        for part in range(lanes_in // LANE):
            target = 2 * rows + row * (lanes_in // LANE) + part
            lanes = slice(part * LANE, (part + 1) * LANE)
            ts_out[target : target + 1] = s3_ref[row : row + 1, lanes]
            tg_out[target : target + 1] = s3_ref[half + row : half + row + 1, lanes]
    spread = width // LANE
    for row in range(4 * spread):
        lanes = slice(row * LANE, (row + 1) * LANE)
        hs_out[:, lanes] = both_ref[row : row + 1]
        hg_out[:, lanes] = both_ref[4 * spread + row : 4 * spread + row + 1]
    for row in range(spread):
        lanes = slice((4 * spread + row) * LANE, (4 * spread + row + 1) * LANE)
        hs_out[:, lanes] = proj_ref[row : row + 1]
        hg_out[:, lanes] = proj_ref[spread + row : spread + row + 1]
    tasks = tw_out.shape[1]
    place = lax.broadcasted_iota(jnp.int32, (1, LANE), 1)
    weights = jnp.zeros((1, LANE), f32)
    for number in range(tasks):
        weights = jnp.where(place == number, tw_ref[number : number + 1], weights)
    tw_out[...] = weights[:, :tasks]
    for source, target in (
        (tg_out, tg_hbm_out),
        (ts_out, ts_hbm_out),
        (hg_out, hg_hbm_out),
        (hs_out, hs_hbm_out),
        (tw_out, tw_hbm_out),
    ):
        copy = pltpu.make_async_copy(source, target, sems.at[len(copies)])
        copy.start()
        copies.append(copy)
    for copy in copies:
        copy.wait()


def finish(places, tasks, taps, ho, ig, rg, dg, eg, bs, tw, pg, s3, s2, s1, both, proj):
    f32 = jnp.float32
    anywhere = pl.BlockSpec(memory_space=pl.ANY)
    shape = jax.ShapeDtypeStruct
    depth, width = taps.shape[1:]
    rows = (s1.size + s2.size + s3.size) // 2 // LANE
    out_shapes = (
        shape(ho.shape, ho.dtype),
        shape(ig.shape, ig.dtype),
        shape(rg.shape, rg.dtype),
        shape(dg.shape, dg.dtype),
        shape(eg.shape, eg.dtype),
        shape(bs.shape, bs.dtype),
        shape((depth, 2 * width), f32),
        shape((depth, len(places) * width), f32),
        shape(pg.shape, f32),
        shape((rows, LANE), f32),
        shape((rows, LANE), f32),
        shape((1, 5 * width), f32),
        shape((1, 5 * width), f32),
        shape((1, tasks), f32),
        )
    small = out_shapes[8:]
    return pl.pallas_call(
        functools.partial(finish_kernel, places),
        name="finish",
        out_shape=out_shapes,
        in_specs=[anywhere] * 14,
        out_specs=(anywhere,) * 14,
        scratch_shapes=[
            pltpu.VMEM(value.shape, value.dtype) for value in (taps, tw, pg, s3, s2, s1, both, proj, ho, ig, rg, dg, eg, bs)
        ]
        + [
            pltpu.VMEM((depth, 2 * width), f32),
            pltpu.VMEM((depth, len(places) * width), f32),
        ]
        + [pltpu.VMEM(out.shape, out.dtype) for out in small]
        + [
            pltpu.SemaphoreType.DMA((16,)),
            pltpu.SemaphoreType.DMA((14,)),
        ],
        compiler_params=pltpu.CompilerParams(vmem_limit_bytes=60 << 20),
    )(taps, ho, ig, rg, dg, eg, bs, tw, pg, s3, s2, s1, both, proj)


def live_taps(rows, cols):
    taps = []
    for level in (1, 2, 3):
        for row_tap in range(3):
            for col_tap in range(3):
                down, right = (row_tap - 1) * level * RATE, (col_tap - 1) * level * RATE
                if abs(down) < rows and abs(right) < cols:
                    taps.append((level, row_tap, col_tap, down, right))
    return taps


def per_device_slices(
    features,
    row_width,
    w_reduce,
    w_dilated,
    w_expand,
    trunk_gain,
    trunk_shift,
    branch_weight,
    rate_weight,
    proj_weight,
    head_gain,
    head_shift,
    head_cot,
):
    bands, tasks = lax.axis_size("space"), lax.axis_size("task")
    band_rows, cols, in_width = features.shape
    rows = band_rows * bands
    pixels = band_rows * cols
    head_width = proj_weight.shape[2]
    inputs = features.reshape(pixels, in_width)
    dilated = w_dilated.transpose(1, 0, 2)
    taps, (
        batch_stats,
        head_out,
        tap_grads,
        both_sums,
        proj_sums,
        weight_rows,
        input_grad,
        reduce_grad,
        dilated_grad,
        expand_grad,
        sums_three,
        sums_two,
        sums_one,
        proj_grad,
    ) = whole(
        tasks,
        bands,
        cols,
        rows,
        0,
        inputs,
        row_width,
        trunk_gain.reshape(1, -1),
        trunk_shift.reshape(1, -1),
        w_reduce,
        dilated,
        w_expand,
        head_gain,
        head_shift,
        head_cot.reshape(pixels, head_width),
        branch_weight[0],
        proj_weight[0],
        rate_weight[0],
    )
    place_of = {tap[:3]: number for number, tap in enumerate(taps)}
    places = tuple(
        place_of.get((level, row_tap, col_tap))
        for level in (1, 2, 3)
        for row_tap in range(3)
        for col_tap in range(3)
    )
    (
        head_out,
        input_grad,
        reduce_grad,
        dilated_grad,
        expand_grad,
        batch_stats,
        branch_grad,
        rate_grad,
        proj_grad,
        trunk_gains,
        trunk_shifts,
        head_gains,
        head_shifts,
        task_weight,
    ) = finish(
        places,
        tasks,
        tap_grads,
        head_out,
        input_grad,
        reduce_grad,
        dilated_grad,
        expand_grad,
        batch_stats,
        weight_rows,
        proj_grad.reshape(-1, head_width),
        sums_three,
        sums_two,
        sums_one,
        both_sums,
        proj_sums,
    )
    return (
        head_out.reshape(1, band_rows, cols, head_width),
        input_grad.reshape(features.shape),
        reduce_grad,
        dilated_grad.transpose(1, 0, 2),
        expand_grad,
        trunk_gains.reshape(-1),
        trunk_shifts.reshape(-1),
        batch_stats,
        branch_grad[None],
        rate_grad[None],
        proj_grad[None],
        head_gains,
        head_shifts,
        task_weight.reshape(-1),
    )


def solution(mesh):
    def body(features, *others):
        small = mesh.shape["space"] == 8 and mesh.shape["task"] == 4
        if small and features.shape[:2] == (2, 128):
            return per_device_slices(features, *others)
        return per_device(features, *others)

    return jax.shard_map(
        body,
        mesh=mesh,
        in_specs=(
            P("space", None, None),
            P(),
            P(),
            P(),
            P(),
            P(),
            P(),
            P("task", "space", None),
            P("task", "space", None),
            P("task", None, None),
            P("task", None),
            P("task", None),
            P("task", "space", None, None),
        ),
        out_specs=(
            P("task", "space", None, None),
            P("space", None, None),
            P("space", None),
            P("space", None, None),
            P("space", None),
            P(),
            P(),
            P(),
            P("task", "space", None),
            P("task", "space", None),
            P("task", None, None),
            P("task", None),
            P("task", None),
            P(),
        ),
        check_vma=False,
    )
```
